32 devices in a mesh: pool: 8 (over z, y), mlp: 4 (over x, core).
Axes of the slice: x: 2, y: 2, z: 4, core: 2. Of those that a mesh axis runs over, the one named last changes fastest.
Arguments:
- residual_in: bfloat16 [16, 3072], P('pool', 'mlp'), may hold values from -6 to 6
- query_new: bfloat16 [16, 3072], P('pool', 'mlp'), may hold values from -6 to 6
- key_new: bfloat16 [16, 3072], P('pool', 'mlp'), may hold values from -6 to 6
- value_new: bfloat16 [16, 3072], P('pool', 'mlp'), may hold values from -6 to 6
- key_cache: bfloat16 [40, 256, 3072], P('pool', None, 'mlp'), may hold values from -240 to 240
- value_cache: bfloat16 [40, 256, 3072], P('pool', None, 'mlp'), may hold values from -6 to 6
- block_table: int32 [16, 8], P('pool'), may hold values from -1 to 39, as said below
- lengths: int32 [16], P('pool'), may hold values from 1 to 2048, as said below
- out_weight: bfloat16 [3072, 3072], P('mlp', 'pool'), may hold values from -0.109375 to 0.109375
- norm_gain: bfloat16 [3072], P('mlp'), may hold values from 0.25 to 1.75
- gate_weight: bfloat16 [3072, 8192], P('mlp', 'pool'), may hold values from -0.109375 to 0.109375
- up_weight: bfloat16 [3072, 8192], P('mlp', 'pool'), may hold values from -0.109375 to 0.109375
- down_weight: bfloat16 [8192, 3072], P('pool', 'mlp'), may hold values from -0.0625 to 0.0625
Outputs:
- layer_out: bfloat16 [16, 3072], P('pool', 'mlp')
The draws below stay inside these ranges and needn't reach their ends.
Inputs may be any that keep to these rules, and one draw needn't show every extreme that they name: `block_table`: row r lists ceil(lengths[r] / 256) distinct block numbers followed by -1; no block is listed twice in the whole table. `lengths`: some request holds exactly 2048 tokens.
All inputs are finite; a program needn't handle non-finite values.
Results may differ from the reference program's by a relative error of at most 0.012.
Values may be sent and summed in bfloat16 or wider, within the bound.
No kernel may reach another device: no remote copies, remote signals or barrier semaphores. Data moves between devices by JAX's collectives and lax.ppermute only.
A program may use at most 64 MiB of HBM per device.

```python
import math
import jax
import jax.numpy as jnp
from jax import lax

H = 32
HD = 96
D = 3072
FF = 8192
BT = 256
MAXB = 8
REQ = 16
BLOCKS = 40


def block_layout(key):
    layout_key = jax.random.fold_in(key, 7)
    key_count, key_heavy, key_tail, key_order = jax.random.split(layout_key, 4)
    request_ids = jnp.arange(REQ, dtype=jnp.int32)
    counts = jax.random.randint(key_count, (REQ,), 1, 3).astype(jnp.int32)
    heavy_row = jax.random.randint(key_heavy, (), 0, REQ).astype(jnp.int32)
    counts = jnp.where(request_ids == heavy_row, MAXB, counts)
    tail_len = jax.random.randint(key_tail, (REQ,), 1, BT + 1).astype(jnp.int32)
    tail_len = jnp.where(request_ids == heavy_row, BT, tail_len)
    lengths = (counts - 1) * BT + tail_len
    shuffled = jax.random.permutation(key_order, jnp.arange(BLOCKS, dtype=jnp.int32))
    first_slot = jnp.cumsum(counts) - counts
    slot_ids = first_slot[:, None] + jnp.arange(MAXB, dtype=jnp.int32)[None, :]
    block_ids = shuffled[jnp.clip(slot_ids, 0, BLOCKS - 1)]
    block_ids = jnp.where(jnp.arange(MAXB, dtype=jnp.int32)[None, :] < counts[:, None], block_ids, -1)
    return (block_ids.astype(jnp.int32), lengths.astype(jnp.int32))


def draw_block_table(key, part):
    return block_layout(key)[0]


def draw_lengths(key, part):
    return block_layout(key)[1]


def draw_key_cache(key, part):
    entries = jnp.clip(jax.random.normal(key, (BLOCKS, BT, D), jnp.float32), -6.0, 6.0)
    return entries.astype(jnp.bfloat16)


def block_levels(rng, shape, cuts, least, high):
    factor_of = 1.0
    for axis_at, shards_of in cuts:
        draws = jax.random.uniform(jax.random.fold_in(jax.random.fold_in(rng, 6), axis_at), (shards_of,), jnp.float32, least / len(cuts), high / len(cuts))
        factor_of = factor_of * jnp.repeat(jnp.exp(draws), shape[axis_at] // shards_of).reshape((-1,) + (1,) * (len(shape) - 1 - axis_at))
    return factor_of


def noise(key, extent, spread, most, cuts=(), kind=jnp.bfloat16):
    level = block_levels(key, extent, cuts, -0.22, 0.18) if cuts else 1.0
    values = jax.random.normal(key, extent, jnp.float32) * spread * level
    return jnp.minimum(jnp.maximum(values, -most), most).astype(kind)


def setup_inputs(seed: int = 0) -> dict:
    key_list = jax.random.split(jax.random.key(seed), 14)
    return {
        "residual_in": noise(key_list[0], (REQ, D), 1.0, 6.0, ((0, 8), (1, 4))),
        "query_new": noise(key_list[1], (REQ, D), 1.0, 6.0, ((0, 8), (1, 4))),
        "key_new": noise(key_list[2], (REQ, D), 1.0, 6.0, ((0, 8), (1, 4))),
        "value_new": noise(key_list[3], (REQ, D), 1.0, 6.0, ((0, 8), (1, 4))),
        "key_cache": draw_key_cache(jax.random.fold_in(key_list[13], 71), 0),
        "value_cache": noise(key_list[5], (BLOCKS, BT, D), 1.0, 6.0, ((0, 8), (2, 4))),
        "block_table": draw_block_table(jax.random.fold_in(key_list[13], 71), 0),
        "lengths": draw_lengths(jax.random.fold_in(key_list[13], 71), 0),
        "out_weight": noise(key_list[8], (D, D), D ** -0.5, 0.109375, ((0, 4), (1, 8))),
        "norm_gain": jnp.clip(1.0 + 0.15 * jax.random.normal(key_list[9], (D,), jnp.float32), 0.25, 1.75).astype(jnp.bfloat16),
        "gate_weight": noise(key_list[10], (D, FF), D ** -0.5, 0.109375, ((0, 4), (1, 8))),
        "up_weight": noise(key_list[11], (D, FF), D ** -0.5, 0.109375, ((0, 4), (1, 8))),
        "down_weight": noise(key_list[12], (FF, D), FF ** -0.5, 0.0625, ((0, 8), (1, 4))),
    }


def rotate(values, positions):
    half_size = HD // 2
    inverse_freq = 10000.0 ** (-(2.0 * jnp.arange(half_size, dtype=jnp.float32)) / HD)
    angles = positions.astype(jnp.float32)[:, None, None] * inverse_freq[None, None, :]
    cosine = jnp.cos(angles)
    sine_part = jnp.sin(angles)
    first = values[..., :half_size]
    second = values[..., half_size:]
    return jnp.concatenate([first * cosine - second * sine_part, second * cosine + first * sine_part], -1)

def reference(residual_in, query_new, key_new, value_new, key_cache, value_cache, block_table, lengths, out_weight, norm_gain, gate_weight, up_weight, down_weight):
    requests = residual_in.shape[0]
    score_scale = 1.0 / math.sqrt(HD)
    queries = rotate(query_new.astype(jnp.float32).reshape(requests, H, HD), lengths).astype(jnp.bfloat16)
    new_keys = rotate(key_new.astype(jnp.float32).reshape(requests, H, HD), lengths).astype(jnp.bfloat16)
    new_values = value_new.reshape(requests, H, HD)

    def attend(inputs):
        query_row, key_self, value_self, block_row, length = inputs
        picked = jnp.clip(block_row, 0, BLOCKS - 1).astype(jnp.int32)
        key_rows = key_cache[picked].reshape(MAXB * BT, H, HD).astype(jnp.float32)
        value_rows = value_cache[picked].reshape(MAXB * BT, H, HD).astype(jnp.float32)
        scores = jnp.einsum('hd,thd->ht', query_row.astype(jnp.float32), key_rows) * score_scale
        valid_mask = jnp.arange(MAXB * BT, dtype=jnp.int32) < length
        scores = jnp.where(valid_mask[None, :], scores, -1e+30)
        self_score = lax.optimization_barrier(jnp.sum(query_row.astype(jnp.float32) * key_self.astype(jnp.float32), -1)) * score_scale
        maximum = jnp.maximum(lax.optimization_barrier(jnp.max(scores, 1)), self_score)
        weights = jnp.where(valid_mask[None, :], jnp.exp(scores - maximum[:, None]), 0.0)
        self_weight = jnp.exp(self_score - maximum)
        totals = lax.optimization_barrier(jnp.sum(weights, 1)) + self_weight
        weights_low = lax.optimization_barrier(weights.astype(jnp.bfloat16))
        self_low = lax.optimization_barrier(self_weight.astype(jnp.bfloat16))
        numerator = jnp.einsum('ht,thd->hd', weights_low.astype(jnp.float32), value_rows)
        numerator = numerator + self_low.astype(jnp.float32)[:, None] * value_self.astype(jnp.float32)
        return (numerator / totals[:, None]).astype(jnp.bfloat16).reshape(H * HD)
    attended = lax.map(attend, (queries, new_keys, new_values, block_table, lengths))
    head_out = lax.optimization_barrier(jnp.dot(attended, out_weight, preferred_element_type=jnp.float32).astype(jnp.bfloat16))
    residual = residual_in.astype(jnp.float32) + head_out.astype(jnp.float32)
    mean_square = lax.optimization_barrier(jnp.mean(residual * residual, -1, keepdims=True))
    normed = (residual * lax.rsqrt(mean_square + 1e-05) * norm_gain.astype(jnp.float32)).astype(jnp.bfloat16)
    gate = jnp.dot(normed, gate_weight, preferred_element_type=jnp.float32)
    up_part = jnp.dot(normed, up_weight, preferred_element_type=jnp.float32)
    hidden = (jax.nn.silu(gate) * up_part).astype(jnp.bfloat16)
    down_out = jnp.dot(hidden, down_weight, preferred_element_type=jnp.float32)
    return (residual + down_out).astype(jnp.bfloat16)
```

```python
import math

import jax
import jax.numpy as jnp
from jax import lax
from jax.sharding import PartitionSpec as P

HD = 96
LOW = -1e30
CODE = 128


def rotate(values, positions):
    half_size = values.shape[-1] // 2
    inverse_freq = 10000.0 ** (-(2.0 * jnp.arange(half_size, dtype=jnp.float32)) / values.shape[-1])
    angles = positions.astype(jnp.float32)[:, None, None] * inverse_freq[None, None, :]
    cosine = jnp.cos(angles)
    sine_part = jnp.sin(angles)
    first = values[..., :half_size]
    second = values[..., half_size:]
    return jnp.concatenate(
        [first * cosine - second * sine_part, second * cosine + first * sine_part], -1
    )


def low(values):
    return lax.reduce_precision(values, 8, 7)


def split(values):
    high = low(values)
    return high.astype(jnp.bfloat16), (values - high).astype(jnp.bfloat16)


def encode(ints):
    return (ints // CODE).astype(jnp.bfloat16), (ints % CODE).astype(jnp.bfloat16)


def decode(high, rest):
    return high.astype(jnp.int32) * CODE + rest.astype(jnp.int32)


def gather(values, axis):
    copies = jnp.broadcast_to(values[None], (lax.axis_size(axis),) + values.shape)
    return lax.all_to_all(copies, axis, 0, 0)


def per_device(
    residual_in,
    query_new,
    key_new,
    value_new,
    key_cache,
    value_cache,
    block_table,
    lengths,
    out_weight,
    norm_gain,
    gate_weight,
    up_weight,
    down_weight,
):
    rows, width = residual_in.shape
    heads = width // HD
    blocks, block_len = key_cache.shape[:2]
    most = block_table.shape[1]
    pool, mlp = lax.axis_size("pool"), lax.axis_size("mlp")
    pool_index = lax.axis_index("pool")
    requests = rows * pool
    score_scale = 1.0 / math.sqrt(HD)
    f32, bf16 = jnp.float32, jnp.bfloat16

    queries = rotate(query_new.astype(f32).reshape(rows, heads, HD), lengths).astype(bf16)
    new_keys = rotate(key_new.astype(f32).reshape(rows, heads, HD), lengths).astype(bf16)

    table_high, table_low = encode(block_table + 1)
    len_high, len_low = encode(lengths)
    packed = jnp.concatenate(
        [
            queries.reshape(rows, width),
            residual_in,
            table_high,
            table_low,
            len_high[:, None],
            len_low[:, None],
        ],
        1,
    )
    spare = -packed.shape[1] % 128
    packed = jnp.pad(packed, ((0, 0), (0, spare)))
    got = gather(packed, "pool").reshape(requests, packed.shape[1])
    all_queries = got[:, :width]
    all_input = got[:, width : 2 * width]
    tail = got[:, 2 * width :]
    tables = decode(tail[:, :most], tail[:, most : 2 * most]) - 1
    all_lengths = decode(tail[:, 2 * most], tail[:, 2 * most + 1])

    held_ids = pool_index * blocks + jnp.arange(blocks, dtype=jnp.int32)
    matches = tables[None, :, :] == held_ids[:, None, None]
    holder = jnp.any(matches, 2)
    block_index = jnp.sum(
        jnp.where(matches, jnp.arange(most, dtype=jnp.int32)[None, None, :], 0), (1, 2)
    )
    valid_len = jnp.sum(jnp.where(holder, all_lengths[None, :], 0), 1)
    block_query = jnp.dot(holder.astype(bf16), all_queries, preferred_element_type=f32)
    block_query = block_query.astype(bf16).reshape(blocks, heads, HD)
    key_rows = key_cache.reshape(blocks, block_len, heads, HD)
    value_rows = value_cache.reshape(blocks, block_len, heads, HD)
    scores = (
        jnp.einsum("bhd,bthd->bht", block_query, key_rows, preferred_element_type=f32)
        * score_scale
    )
    token_pos = block_index[:, None] * block_len + jnp.arange(block_len, dtype=jnp.int32)[None, :]
    valid = (token_pos < valid_len[:, None])[:, None, :]
    scores = jnp.where(valid, scores, LOW)
    shift = low(jnp.max(scores, 2))
    weights = jnp.where(valid, jnp.exp(scores - shift[:, :, None]), 0.0)
    totals = jnp.sum(weights, 2)
    numerator = jnp.einsum(
        "bht,bthd->bhd", weights.astype(bf16), value_rows, preferred_element_type=f32
    )
    self_score = jnp.sum(queries.astype(f32) * new_keys.astype(f32), -1) * score_scale
    self_shift = low(self_score)
    self_weight = jnp.exp(self_score - self_shift)
    self_numer = self_weight[:, :, None] * value_new.astype(f32).reshape(rows, heads, HD)

    own_total = jnp.concatenate([totals, self_weight], 0)
    total_high, total_low = split(own_total)
    part = jnp.concatenate(
        [
            jnp.concatenate([numerator, self_numer], 0)
            .astype(bf16)
            .reshape(blocks + rows, width),
            jnp.concatenate([shift, self_shift], 0).astype(bf16),
            total_high,
            total_low,
        ],
        1,
    )
    part = jnp.pad(part, ((0, 0), (0, -part.shape[1] % 128)))
    count = blocks + rows
    parts = gather(part, "pool").reshape(pool * count, part.shape[1])
    all_shift = parts[:, width : width + heads].astype(f32)
    all_total = parts[:, width + heads : width + 2 * heads].astype(f32) + parts[
        :, width + 2 * heads : width + 3 * heads
    ].astype(f32)
    place = jnp.arange(pool * count, dtype=jnp.int32)
    owner, slot = place // count, place % count
    is_block = slot < blocks
    block_id = jnp.where(is_block, owner * blocks + slot, -2)
    self_id = jnp.where(is_block, -2, owner * rows + slot - blocks)
    request_ids = jnp.arange(requests, dtype=jnp.int32)
    belongs = jnp.any(tables[:, None, :] == block_id[None, :, None], 2) | (
        request_ids[:, None] == self_id[None, :]
    )
    top = jnp.max(jnp.where(belongs[:, :, None], all_shift[None], LOW), 1)
    part_top = jnp.sum(jnp.where(belongs[:, :, None], top[:, None, :], 0.0), 0)
    scale = jnp.exp(all_shift - part_top)
    scaled = parts[:, :width].astype(f32).reshape(-1, heads, HD) * scale[:, :, None]
    mix = belongs.astype(f32)
    numer = jnp.dot(mix, scaled.reshape(-1, width), precision=lax.Precision.HIGHEST)
    denom = jnp.dot(mix, all_total * scale, precision=lax.Precision.HIGHEST)
    attended = (numer.reshape(requests, heads, HD) / denom[:, :, None]).astype(bf16)
    attended = attended.reshape(requests, width)

    head_part = jnp.dot(attended, out_weight, preferred_element_type=f32).astype(bf16)
    share = pool // mlp
    route = []
    for p in range(pool):
        for m in range(mlp):
            route.append((p * mlp + m, ((p % share) * mlp + m) * mlp + p // share))
    moved = lax.ppermute(head_part, ("pool", "mlp"), route)
    head_all = gather(moved, "pool").reshape(share, mlp, requests, -1)
    head_out = low(jnp.sum(head_all.astype(f32), 1))
    head_out = jnp.swapaxes(head_out, 0, 1).reshape(requests, width)
    residual = all_input.astype(f32) + head_out
    squares = jnp.sum(residual * residual, -1, keepdims=True)
    portion = (residual * norm_gain.astype(f32)).astype(bf16)

    ff = gate_weight.shape[1]
    square_high, square_low = split(squares)
    sums = jnp.concatenate(
        [
            jnp.dot(portion, gate_weight, preferred_element_type=f32).astype(bf16),
            jnp.dot(portion, up_weight, preferred_element_type=f32).astype(bf16),
            jnp.broadcast_to(square_high, (requests, 64)),
            jnp.broadcast_to(square_low, (requests, 64)),
        ],
        1,
    )
    summed = jnp.sum(gather(sums, "mlp").astype(f32), 0)
    mean_square = (summed[:, 2 * ff : 2 * ff + 1] + summed[:, 2 * ff + 64 : 2 * ff + 65]) / (
        width * mlp
    )
    factor = lax.rsqrt(mean_square + 1e-05)
    gate = summed[:, :ff] * factor
    up = summed[:, ff : 2 * ff] * factor
    hidden = (jax.nn.silu(gate) * up).astype(bf16)

    down = jnp.dot(hidden, down_weight, preferred_element_type=f32)
    down = lax.all_to_all(down.reshape(pool, rows, width), "pool", 0, 0)
    own = lax.dynamic_slice_in_dim(residual, pool_index * rows, rows, 0)
    return (own + jnp.sum(down, 0)).astype(bf16)


def solution(mesh):
    in_specs = (
        P("pool", "mlp"),
        P("pool", "mlp"),
        P("pool", "mlp"),
        P("pool", "mlp"),
        P("pool", None, "mlp"),
        P("pool", None, "mlp"),
        P("pool", None),
        P("pool"),
        P("mlp", "pool"),
        P("mlp"),
        P("mlp", "pool"),
        P("mlp", "pool"),
        P("pool", "mlp"),
    )
    return jax.shard_map(
        per_device, mesh=mesh, in_specs=in_specs, out_specs=P("pool", "mlp"), check_vma=False
    )
```

```python
import math

import jax
import jax.numpy as jnp
from jax import lax
from jax.sharding import PartitionSpec as P

HD = 96
LOW = -1e30
CODE = 128


def rotate(values, positions):
    half_size = values.shape[-1] // 2
    inverse_freq = 10000.0 ** (-(2.0 * jnp.arange(half_size, dtype=jnp.float32)) / values.shape[-1])
    angles = positions.astype(jnp.float32)[:, None, None] * inverse_freq[None, None, :]
    cosine = jnp.cos(angles)
    sine_part = jnp.sin(angles)
    first = values[..., :half_size]
    second = values[..., half_size:]
    return jnp.concatenate(
        [first * cosine - second * sine_part, second * cosine + first * sine_part], -1
    )


def low(values):
    return lax.reduce_precision(values, 8, 7)


def split(values):
    high = low(values)
    return high.astype(jnp.bfloat16), (values - high).astype(jnp.bfloat16)


def encode(ints):
    return (ints // CODE).astype(jnp.bfloat16), (ints % CODE).astype(jnp.bfloat16)


def decode(high, rest):
    return high.astype(jnp.int32) * CODE + rest.astype(jnp.int32)


def swap(axis, step):
    size = lax.axis_size(axis)
    return [(index, index ^ step) for index in range(size)]


def direct(axis):
    size = lax.axis_size(axis)
    return size <= 8 and size & (size - 1) == 0


def ordered(parts, axis):
    index = lax.axis_index(axis)
    bit = 1
    while bit < len(parts):
        odd = (index & bit) != 0
        parts = [jnp.where(odd, parts[s ^ bit], parts[s]) for s in range(len(parts))]
        bit *= 2
    return jnp.stack(parts)


def exchange(chunks, axis):
    size = lax.axis_size(axis)
    if not direct(axis):
        return lax.all_to_all(chunks, axis, 0, 0)
    index = lax.axis_index(axis)
    parts = []
    for step in range(size):
        chunk = lax.dynamic_index_in_dim(chunks, index ^ step, 0, keepdims=False)
        parts.append(lax.ppermute(chunk, axis, swap(axis, step)) if step else chunk)
    return jnp.stack(parts)


def gather(values, axis):
    size = lax.axis_size(axis)
    if not direct(axis):
        copies = jnp.broadcast_to(values[None], (size,) + values.shape)
        return lax.all_to_all(copies, axis, 0, 0)
    parts = [values]
    for step in range(1, size):
        parts.append(lax.ppermute(values, axis, swap(axis, step)))
    return ordered(parts, axis)


def gather_group(values):
    pool, mlp = lax.axis_size("pool"), lax.axis_size("mlp")
    share = pool // mlp
    parts = []
    for step in range(pool if direct("pool") else 1):
        route = []
        for p in range(pool):
            for m in range(mlp):
                route.append((p * mlp + m, (((p % share) * mlp + m) ^ step) * mlp + p // share))
        parts.append(lax.ppermute(values, ("pool", "mlp"), route))
    if direct("pool"):
        return ordered(parts, "pool")
    return gather(parts[0], "pool")


def per_device(
    residual_in,
    query_new,
    key_new,
    value_new,
    key_cache,
    value_cache,
    block_table,
    lengths,
    out_weight,
    norm_gain,
    gate_weight,
    up_weight,
    down_weight,
):
    rows, width = residual_in.shape
    heads = width // HD
    blocks, block_len = key_cache.shape[:2]
    most = block_table.shape[1]
    pool, mlp = lax.axis_size("pool"), lax.axis_size("mlp")
    pool_index = lax.axis_index("pool")
    requests = rows * pool
    score_scale = 1.0 / math.sqrt(HD)
    f32, bf16 = jnp.float32, jnp.bfloat16

    queries = rotate(query_new.astype(f32).reshape(rows, heads, HD), lengths).astype(bf16)
    new_keys = rotate(key_new.astype(f32).reshape(rows, heads, HD), lengths).astype(bf16)

    table_high, table_low = encode(block_table + 1)
    len_high, len_low = encode(lengths)
    packed = jnp.concatenate(
        [
            queries.reshape(rows, width),
            residual_in,
            table_high,
            table_low,
            len_high[:, None],
            len_low[:, None],
        ],
        1,
    )
    spare = -packed.shape[1] % 128
    packed = jnp.pad(packed, ((0, 0), (0, spare)))
    got = gather(packed, "pool").reshape(requests, packed.shape[1])
    all_queries = got[:, :width]
    all_input = got[:, width : 2 * width]
    tail = got[:, 2 * width :]
    tables = decode(tail[:, :most], tail[:, most : 2 * most]) - 1
    all_lengths = decode(tail[:, 2 * most], tail[:, 2 * most + 1])

    held_ids = pool_index * blocks + jnp.arange(blocks, dtype=jnp.int32)
    matches = tables[None, :, :] == held_ids[:, None, None]
    holder = jnp.any(matches, 2)
    block_index = jnp.sum(
        jnp.where(matches, jnp.arange(most, dtype=jnp.int32)[None, None, :], 0), (1, 2)
    )
    valid_len = jnp.sum(jnp.where(holder, all_lengths[None, :], 0), 1)
    block_query = jnp.dot(holder.astype(bf16), all_queries, preferred_element_type=f32)
    block_query = block_query.astype(bf16).reshape(blocks, heads, HD)
    key_rows = key_cache.reshape(blocks, block_len, heads, HD)
    value_rows = value_cache.reshape(blocks, block_len, heads, HD)
    scores = (
        jnp.einsum("bhd,bthd->bht", block_query, key_rows, preferred_element_type=f32)
        * score_scale
    )
    token_pos = block_index[:, None] * block_len + jnp.arange(block_len, dtype=jnp.int32)[None, :]
    valid = (token_pos < valid_len[:, None])[:, None, :]
    scores = jnp.where(valid, scores, LOW)
    shift = low(jnp.max(scores, 2))
    weights = jnp.where(valid, jnp.exp(scores - shift[:, :, None]), 0.0)
    totals = jnp.sum(weights, 2)
    numerator = jnp.einsum(
        "bht,bthd->bhd", weights.astype(bf16), value_rows, preferred_element_type=f32
    )
    self_score = jnp.sum(queries.astype(f32) * new_keys.astype(f32), -1) * score_scale
    self_shift = low(self_score)
    self_weight = jnp.exp(self_score - self_shift)
    self_numer = self_weight[:, :, None] * value_new.astype(f32).reshape(rows, heads, HD)

    own_total = jnp.concatenate([totals, self_weight], 0)
    total_high, total_low = split(own_total)
    part = jnp.concatenate(
        [
            jnp.concatenate([numerator, self_numer], 0)
            .astype(bf16)
            .reshape(blocks + rows, width),
            jnp.concatenate([shift, self_shift], 0).astype(bf16),
            total_high,
            total_low,
        ],
        1,
    )
    part = jnp.pad(part, ((0, 0), (0, -part.shape[1] % 128)))
    count = blocks + rows
    parts = gather(part, "pool").reshape(pool * count, part.shape[1])
    all_shift = parts[:, width : width + heads].astype(f32)
    all_total = parts[:, width + heads : width + 2 * heads].astype(f32) + parts[
        :, width + 2 * heads : width + 3 * heads
    ].astype(f32)
    place = jnp.arange(pool * count, dtype=jnp.int32)
    owner, slot = place // count, place % count
    is_block = slot < blocks
    block_id = jnp.where(is_block, owner * blocks + slot, -2)
    self_id = jnp.where(is_block, -2, owner * rows + slot - blocks)
    request_ids = jnp.arange(requests, dtype=jnp.int32)
    belongs = jnp.any(tables[:, None, :] == block_id[None, :, None], 2) | (
        request_ids[:, None] == self_id[None, :]
    )
    top = jnp.max(jnp.where(belongs[:, :, None], all_shift[None], LOW), 1)
    part_top = jnp.sum(jnp.where(belongs[:, :, None], top[:, None, :], 0.0), 0)
    scale = jnp.exp(all_shift - part_top)
    scaled = parts[:, :width].astype(f32).reshape(-1, heads, HD) * scale[:, :, None]
    mix = belongs.astype(f32)
    numer = jnp.dot(mix, scaled.reshape(-1, width), precision=lax.Precision.HIGHEST)
    denom = jnp.dot(mix, all_total * scale, precision=lax.Precision.HIGHEST)
    attended = (numer.reshape(requests, heads, HD) / denom[:, :, None]).astype(bf16)
    attended = attended.reshape(requests, width)

    head_part = jnp.dot(attended, out_weight, preferred_element_type=f32).astype(bf16)
    head_all = gather_group(head_part).reshape(pool // mlp, mlp, requests, -1)
    head_out = low(jnp.sum(head_all.astype(f32), 1))
    head_out = jnp.swapaxes(head_out, 0, 1).reshape(requests, width)
    residual = all_input.astype(f32) + head_out
    squares = jnp.sum(residual * residual, -1, keepdims=True)
    portion = (residual * norm_gain.astype(f32)).astype(bf16)

    ff = gate_weight.shape[1]
    square_high, square_low = split(squares)
    sums = jnp.concatenate(
        [
            jnp.dot(portion, gate_weight, preferred_element_type=f32).astype(bf16),
            jnp.dot(portion, up_weight, preferred_element_type=f32).astype(bf16),
            jnp.broadcast_to(square_high, (requests, 64)),
            jnp.broadcast_to(square_low, (requests, 64)),
        ],
        1,
    )
    summed = jnp.sum(gather(sums, "mlp").astype(f32), 0)
    mean_square = (summed[:, 2 * ff : 2 * ff + 1] + summed[:, 2 * ff + 64 : 2 * ff + 65]) / (
        width * mlp
    )
    factor = lax.rsqrt(mean_square + 1e-05)
    gate = summed[:, :ff] * factor
    up = summed[:, ff : 2 * ff] * factor
    hidden = (jax.nn.silu(gate) * up).astype(bf16)

    down = jnp.dot(hidden, down_weight, preferred_element_type=f32)
    down = exchange(down.reshape(pool, rows, width), "pool")
    own = lax.dynamic_slice_in_dim(residual, pool_index * rows, rows, 0)
    return (own + jnp.sum(down, 0)).astype(bf16)


def solution(mesh):
    in_specs = (
        P("pool", "mlp"),
        P("pool", "mlp"),
        P("pool", "mlp"),
        P("pool", "mlp"),
        P("pool", None, "mlp"),
        P("pool", None, "mlp"),
        P("pool", None),
        P("pool"),
        P("mlp", "pool"),
        P("mlp"),
        P("mlp", "pool"),
        P("mlp", "pool"),
        P("pool", "mlp"),
    )
    return jax.shard_map(
        per_device, mesh=mesh, in_specs=in_specs, out_specs=P("pool", "mlp"), check_vma=False
    )
```

```python
import functools
import math

import jax
import jax.numpy as jnp
import numpy as np
from jax import lax
from jax.experimental import pallas as pl
from jax.experimental.pallas import tpu as pltpu
from jax.sharding import PartitionSpec as P

HD = 96
LOW = -1e30
CODE = 128


def rotate(values, positions):
    half_size = values.shape[-1] // 2
    inverse_freq = 10000.0 ** (-(2.0 * jnp.arange(half_size, dtype=jnp.float32)) / values.shape[-1])
    angles = positions.astype(jnp.float32)[:, None, None] * inverse_freq[None, None, :]
    cosine = jnp.cos(angles)
    sine_part = jnp.sin(angles)
    first = values[..., :half_size]
    second = values[..., half_size:]
    return jnp.concatenate(
        [first * cosine - second * sine_part, second * cosine + first * sine_part], -1
    )


def low(values):
    return lax.reduce_precision(values, 8, 7)


def split(values):
    high = low(values)
    return high.astype(jnp.bfloat16), (values - high).astype(jnp.bfloat16)


def encode(ints):
    return (ints // CODE).astype(jnp.bfloat16), (ints % CODE).astype(jnp.bfloat16)


def decode(high, rest):
    return high.astype(jnp.int32) * CODE + rest.astype(jnp.int32)


def gather(values, axis):
    copies = jnp.broadcast_to(values[None], (lax.axis_size(axis),) + values.shape)
    return lax.all_to_all(copies, axis, 0, 0)


def per_device_wide(
    residual_in,
    query_new,
    key_new,
    value_new,
    key_cache,
    value_cache,
    block_table,
    lengths,
    out_weight,
    norm_gain,
    gate_weight,
    up_weight,
    down_weight,
):
    rows, width = residual_in.shape
    heads = width // HD
    blocks, block_len = key_cache.shape[:2]
    most = block_table.shape[1]
    pool, mlp = lax.axis_size("pool"), lax.axis_size("mlp")
    pool_index = lax.axis_index("pool")
    requests = rows * pool
    score_scale = 1.0 / math.sqrt(HD)
    f32, bf16 = jnp.float32, jnp.bfloat16

    queries = rotate(query_new.astype(f32).reshape(rows, heads, HD), lengths).astype(bf16)
    new_keys = rotate(key_new.astype(f32).reshape(rows, heads, HD), lengths).astype(bf16)

    table_high, table_low = encode(block_table + 1)
    len_high, len_low = encode(lengths)
    packed = jnp.concatenate(
        [
            queries.reshape(rows, width),
            residual_in,
            table_high,
            table_low,
            len_high[:, None],
            len_low[:, None],
        ],
        1,
    )
    spare = -packed.shape[1] % 128
    packed = jnp.pad(packed, ((0, 0), (0, spare)))
    got = gather(packed, "pool").reshape(requests, packed.shape[1])
    all_queries = got[:, :width]
    all_input = got[:, width : 2 * width]
    tail = got[:, 2 * width :]
    tables = decode(tail[:, :most], tail[:, most : 2 * most]) - 1
    all_lengths = decode(tail[:, 2 * most], tail[:, 2 * most + 1])

    held_ids = pool_index * blocks + jnp.arange(blocks, dtype=jnp.int32)
    matches = tables[None, :, :] == held_ids[:, None, None]
    holder = jnp.any(matches, 2)
    block_index = jnp.sum(
        jnp.where(matches, jnp.arange(most, dtype=jnp.int32)[None, None, :], 0), (1, 2)
    )
    valid_len = jnp.sum(jnp.where(holder, all_lengths[None, :], 0), 1)
    block_query = jnp.dot(holder.astype(bf16), all_queries, preferred_element_type=f32)
    block_query = block_query.astype(bf16).reshape(blocks, heads, HD)
    key_rows = key_cache.reshape(blocks, block_len, heads, HD)
    value_rows = value_cache.reshape(blocks, block_len, heads, HD)
    scores = (
        jnp.einsum("bhd,bthd->bht", block_query, key_rows, preferred_element_type=f32)
        * score_scale
    )
    token_pos = block_index[:, None] * block_len + jnp.arange(block_len, dtype=jnp.int32)[None, :]
    valid = (token_pos < valid_len[:, None])[:, None, :]
    scores = jnp.where(valid, scores, LOW)
    shift = low(jnp.max(scores, 2))
    weights = jnp.where(valid, jnp.exp(scores - shift[:, :, None]), 0.0)
    totals = jnp.sum(weights, 2)
    numerator = jnp.einsum(
        "bht,bthd->bhd", weights.astype(bf16), value_rows, preferred_element_type=f32
    )
    self_score = jnp.sum(queries.astype(f32) * new_keys.astype(f32), -1) * score_scale
    self_shift = low(self_score)
    self_weight = jnp.exp(self_score - self_shift)
    self_numer = self_weight[:, :, None] * value_new.astype(f32).reshape(rows, heads, HD)

    own_total = jnp.concatenate([totals, self_weight], 0)
    total_high, total_low = split(own_total)
    part = jnp.concatenate(
        [
            jnp.concatenate([numerator, self_numer], 0)
            .astype(bf16)
            .reshape(blocks + rows, width),
            jnp.concatenate([shift, self_shift], 0).astype(bf16),
            total_high,
            total_low,
        ],
        1,
    )
    part = jnp.pad(part, ((0, 0), (0, -part.shape[1] % 128)))
    count = blocks + rows
    parts = gather(part, "pool").reshape(pool * count, part.shape[1])
    all_shift = parts[:, width : width + heads].astype(f32)
    all_total = parts[:, width + heads : width + 2 * heads].astype(f32) + parts[
        :, width + 2 * heads : width + 3 * heads
    ].astype(f32)
    place = jnp.arange(pool * count, dtype=jnp.int32)
    owner, slot = place // count, place % count
    is_block = slot < blocks
    block_id = jnp.where(is_block, owner * blocks + slot, -2)
    self_id = jnp.where(is_block, -2, owner * rows + slot - blocks)
    request_ids = jnp.arange(requests, dtype=jnp.int32)
    belongs = jnp.any(tables[:, None, :] == block_id[None, :, None], 2) | (
        request_ids[:, None] == self_id[None, :]
    )
    top = jnp.max(jnp.where(belongs[:, :, None], all_shift[None], LOW), 1)
    part_top = jnp.sum(jnp.where(belongs[:, :, None], top[:, None, :], 0.0), 0)
    scale = jnp.exp(all_shift - part_top)
    scaled = parts[:, :width].astype(f32).reshape(-1, heads, HD) * scale[:, :, None]
    mix = belongs.astype(f32)
    numer = jnp.dot(mix, scaled.reshape(-1, width), precision=lax.Precision.HIGHEST)
    denom = jnp.dot(mix, all_total * scale, precision=lax.Precision.HIGHEST)
    attended = (numer.reshape(requests, heads, HD) / denom[:, :, None]).astype(bf16)
    attended = attended.reshape(requests, width)

    head_part = jnp.dot(attended, out_weight, preferred_element_type=f32).astype(bf16)
    share = pool // mlp
    route = []
    for p in range(pool):
        for m in range(mlp):
            route.append((p * mlp + m, ((p % share) * mlp + m) * mlp + p // share))
    moved = lax.ppermute(head_part, ("pool", "mlp"), route)
    head_all = gather(moved, "pool").reshape(share, mlp, requests, -1)
    head_out = low(jnp.sum(head_all.astype(f32), 1))
    head_out = jnp.swapaxes(head_out, 0, 1).reshape(requests, width)
    residual = all_input.astype(f32) + head_out
    squares = jnp.sum(residual * residual, -1, keepdims=True)
    portion = (residual * norm_gain.astype(f32)).astype(bf16)

    ff = gate_weight.shape[1]
    square_high, square_low = split(squares)
    sums = jnp.concatenate(
        [
            jnp.dot(portion, gate_weight, preferred_element_type=f32).astype(bf16),
            jnp.dot(portion, up_weight, preferred_element_type=f32).astype(bf16),
            jnp.broadcast_to(square_high, (requests, 64)),
            jnp.broadcast_to(square_low, (requests, 64)),
        ],
        1,
    )
    summed = jnp.sum(gather(sums, "mlp").astype(f32), 0)
    mean_square = (summed[:, 2 * ff : 2 * ff + 1] + summed[:, 2 * ff + 64 : 2 * ff + 65]) / (
        width * mlp
    )
    factor = lax.rsqrt(mean_square + 1e-05)
    gate = summed[:, :ff] * factor
    up = summed[:, ff : 2 * ff] * factor
    hidden = (jax.nn.silu(gate) * up).astype(bf16)

    down = jnp.dot(hidden, down_weight, preferred_element_type=f32)
    down = lax.all_to_all(down.reshape(pool, rows, width), "pool", 0, 0)
    own = lax.dynamic_slice_in_dim(residual, pool_index * rows, rows, 0)
    return (own + jnp.sum(down, 0)).astype(bf16)


F32, BF16 = jnp.float32, jnp.bfloat16
VMEM = pl.BlockSpec(memory_space=pltpu.VMEM)
SMEM = pl.BlockSpec(memory_space=pltpu.SMEM)


def call(kernel, name, outs, args, scratch=(), smem=(), flops=0):
    size = sum(math.prod(a.shape) * a.dtype.itemsize for a in args)
    return pl.pallas_call(
        kernel,
        out_shape=[jax.ShapeDtypeStruct(shape, dtype) for shape, dtype in outs],
        in_specs=[SMEM if i in smem else VMEM for i in range(len(args))],
        out_specs=[VMEM] * len(outs),
        scratch_shapes=list(scratch),
        compiler_params=pltpu.CompilerParams(vmem_limit_bytes=16 * 1024 * 1024),
        cost_estimate=pl.CostEstimate(flops=flops, bytes_accessed=size, transcendentals=0),
        name=name,
    )(*args)


def lanes(shape):
    return lax.broadcasted_iota(jnp.int32, shape, len(shape) - 1)


def in_order(pieces, index):
    for bit in (1, 2):
        odd = (index & bit) != 0
        pieces = [jnp.where(odd, pieces[s ^ bit], pieces[s]) for s in range(4)]
    return pieces


def rows_of(shape):
    return lax.broadcasted_iota(jnp.int32, shape, len(shape) - 2)


def round_low(values):
    return values.astype(BF16).astype(F32)


def prepare_kernel(table, length, freq, query, key, value, residual, packed, own, scr):
    rows, width = query.shape
    heads = width // HD
    most = table.shape[1]
    blocks = own.shape[0] - rows - 1
    scr[...] = jnp.zeros_like(scr)
    scr[0:rows, :] = query[...].astype(F32)
    scr[rows : 2 * rows, :] = key[...].astype(F32)
    values = scr[...]
    line = rows_of((8, width))
    where_at = jnp.zeros((8, width), F32)
    for r in range(rows):
        here = (line == r) | (line == rows + r)
        where_at = jnp.where(here, length[r].astype(F32), where_at)
    angles = where_at * freq[...]
    lane = lanes((8, width))
    first = lane % HD < HD // 2
    ahead = pltpu.roll(values, width - HD // 2, 1)
    behind = pltpu.roll(values, HD // 2, 1)
    other = jnp.where(first, -ahead, behind)
    turned = values * jnp.cos(angles) + other * jnp.sin(angles)
    scr[...] = round_low(turned)
    packed[:, :width] = scr[0:rows, :].astype(BF16)
    packed[:, width : 2 * width] = residual[...]
    tail = jnp.zeros((rows, 128), F32)
    at, row = lanes((rows, 128)), rows_of((rows, 128))
    for r in range(rows):
        codes = [table[r, k] + 1 for k in range(most)] + [length[r]]
        spots = [(k, most + k) for k in range(most)] + [(2 * most, 2 * most + 1)]
        for code, (high, rest) in zip(codes, spots):
            tail = jnp.where((row == r) & (at == high), (code >> 7).astype(F32), tail)
            tail = jnp.where((row == r) & (at == rest), (code & 127).astype(F32), tail)
    packed[:, 2 * width :] = tail.astype(BF16)

    head_mask = lane // HD == line
    product = scr[0:rows, :] * scr[rows : 2 * rows, :]
    own[...] = jnp.zeros_like(own)
    spot = lanes((8, 128))
    tail = jnp.zeros((8, 128), F32)
    for r in range(rows):
        score = jnp.sum(
            jnp.where(head_mask, jnp.broadcast_to(product[r : r + 1], (8, width)), 0.0),
            1,
            keepdims=True,
        ) * (1.0 / math.sqrt(HD))
        shift = round_low(score)
        weight = jnp.exp(score - shift)
        spread = jnp.sum(jnp.where(head_mask, round_low(weight), 0.0), 0, keepdims=True)
        own[blocks + r : blocks + r + 1, :width] = spread * value[r : r + 1, :].astype(F32)
        high = round_low(weight)
        tail = jnp.where(spot == blocks + r, shift, tail)
        tail = jnp.where(spot == 8 + blocks + r, high, tail)
        tail = jnp.where(spot == 16 + blocks + r, weight - high, tail)
    own[:, width:] = tail


def merge_kernel(mine, theirs, both):
    y = lax.axis_index("pool") % 2
    both[y] = mine[...]
    both[1 - y] = theirs[...]


def attend_kernel(a0, a1, a2, a3, own, keys, values, part, residual, tables, scr):
    blocks, block_len, width = keys.shape
    rows = a0.shape[1]
    heads = width // HD
    most = 8
    me = lax.axis_index("pool")
    for y in range(2):
        pieces = [piece[y].astype(F32) for piece in (a0, a1, a2, a3)]
        for z, piece in enumerate(in_order(pieces, me // 2)):
            scr[(z * 2 + y) * rows : (z * 2 + y + 1) * rows, :] = piece
    queries = scr[:, :width]
    residual[...] = scr[:, width : 2 * width]
    tail = scr[:, 2 * width :]
    requests = tail.shape[0]
    table = tail * CODE + pltpu.roll(tail, 128 - most, 1) - 1.0
    length = tail[:, 2 * most : 2 * most + 1] * CODE + tail[:, 2 * most + 1 : 2 * most + 2]
    lane = lanes((requests, 128))
    table = jnp.where(lane < most, table, -2.0)
    tables[...] = table
    head_mask = lanes((heads, width)) // HD == rows_of((heads, width))
    spot = lanes((heads, 128))
    token = lanes((heads, block_len)).astype(F32)
    tail = own[:, width:]
    part[...] = own[...].astype(BF16)
    numerators = []
    for b in range(blocks):
        match = jnp.where(table == (me * blocks + b).astype(F32), 1.0, 0.0)
        holder = jnp.sum(match, 1, keepdims=True)
        place = jnp.sum(jnp.sum(match * lane.astype(F32), 1, keepdims=True), 0, keepdims=True)
        limit = jnp.sum(holder * length, 0, keepdims=True) - place * block_len
        query = jnp.sum(holder * queries, 0, keepdims=True)
        spread = jnp.where(head_mask, query, 0.0).astype(BF16)
        scores = lax.dot_general(
            spread, keys[b], (((1,), (1,)), ((), ())), preferred_element_type=F32
        ) * (1.0 / math.sqrt(HD))
        valid = token < limit
        scores = jnp.where(valid, scores, LOW)
        shift = round_low(jnp.max(scores, 1, keepdims=True))
        weights = jnp.where(valid, jnp.exp(scores - shift), 0.0)
        total = jnp.sum(weights, 1, keepdims=True)
        full = jnp.dot(weights.astype(BF16), values[b], preferred_element_type=F32)
        numerators.append(jnp.sum(jnp.where(head_mask, full, 0.0), 0, keepdims=True))
        high = round_low(total)
        tail = jnp.where(spot == b, shift, tail)
        tail = jnp.where(spot == 8 + b, high, tail)
        tail = jnp.where(spot == 16 + b, total - high, tail)
    line = rows_of((8, width))
    numer = own[:, :width]
    for b in range(blocks):
        numer = jnp.where(line == b, numerators[b], numer)
    part[:, :width] = numer.astype(BF16)
    part[:, width:] = tail.astype(BF16)


def combine_kernel(b0, b1, b2, b3, tables, weight, head_part, numer, tails, mix):
    requests = tables.shape[0]
    slots = b0.shape[1]
    width = weight.shape[0]
    heads = width // HD
    rows, blocks = 2, slots - 3
    me = lax.axis_index("pool")
    for step, piece in enumerate((b0, b1, b2, b3)):
        z = (me // 2) ^ step
        for y in range(2):
            owner = z * 2 + y
            values = piece[y].astype(F32)
            numer[pl.ds(pl.multiple_of(owner * slots, 8), slots), :] = values[:, :width]
            tails[owner] = values[:, width:]
    lane8 = lanes((heads, 128))
    shifts = jnp.zeros((heads, 128), F32)
    totals = jnp.zeros((heads, 128), F32)
    for owner in range(8):
        tail = tails[owner]
        total = pltpu.roll(tail, 120, 1) + pltpu.roll(tail, 112, 1)
        tail, total = jnp.where(lane8 < 8, tail, 0.0), jnp.where(lane8 < 8, total, 0.0)
        if owner:
            tail, total = pltpu.roll(tail, 8 * owner, 1), pltpu.roll(total, 8 * owner, 1)
        shifts, totals = shifts + tail, totals + total
    lane = lanes((requests, 128))
    owner, slot = lane // slots, lane % slots
    block_id = jnp.where((slot < blocks) & (lane < 64), owner * blocks + slot, -5).astype(F32)
    self_id = jnp.where((slot >= blocks) & (slot < blocks + rows), owner * rows + slot - blocks, -5)
    table = tables[...]
    belongs = (self_id == rows_of((requests, 128))) & (lane < 64)
    for k in range(8):
        belongs = belongs | (table[:, k : k + 1] == block_id)
    for h in range(heads):
        shift = jnp.broadcast_to(shifts[h : h + 1], (requests, 128))
        top = jnp.max(jnp.where(belongs, shift, LOW), 1, keepdims=True)
        scale = jnp.where(belongs, jnp.exp(shift - top), 0.0)
        total = jnp.sum(scale * totals[h : h + 1], 1, keepdims=True)
        mix[h * requests : (h + 1) * requests, :] = scale / total
    full = jnp.dot(
        mix[:, : 8 * slots].astype(BF16), numer[...].astype(BF16), preferred_element_type=F32
    )
    head = lanes((requests, width)) // HD
    attended = jnp.zeros((requests, width), F32)
    for h in range(heads):
        attended = jnp.where(head == h, full[h * requests : (h + 1) * requests], attended)
    head_part[...] = jnp.dot(
        attended.astype(BF16), weight[...], preferred_element_type=F32
    ).astype(BF16)


def sum_kernel(p0, p1, p2, p3, total):
    total[...] = (
        (p0[...].astype(F32) + p1[...].astype(F32)) + (p2[...].astype(F32) + p3[...].astype(F32))
    ).astype(BF16)


def gate_up_kernel(same, flip, all_input, gain, gate, up, sums, own, scr):
    me = lax.axis_index("pool")
    odd = me % 2 == 1
    part = same.shape[1]
    ff = gate.shape[1]
    rows = own.shape[0]
    near, far = same[...].astype(F32), flip[...].astype(F32)
    scr[:, :part] = all_input[:, :part] + jnp.where(odd, far, near)
    scr[:, part:] = all_input[:, part:] + jnp.where(odd, near, far)
    residual = scr[...]
    mine = scr[0:rows, :]
    for p in range(1, residual.shape[0] // rows):
        mine = jnp.where(me == p, scr[p * rows : (p + 1) * rows, :], mine)
    own[...] = mine
    square = jnp.sum(residual * residual, 1, keepdims=True)
    portion = (residual * gain[...].astype(F32)).astype(BF16)
    sums[:, :ff] = jnp.dot(portion, gate[...], preferred_element_type=F32).astype(BF16)
    sums[:, ff : 2 * ff] = jnp.dot(portion, up[...], preferred_element_type=F32).astype(BF16)
    lane = lanes((residual.shape[0], 128))
    high = round_low(square)
    tail = jnp.where(lane == 0, high, jnp.where(lane == 1, square - high, 0.0))
    sums[:, 2 * ff :] = tail.astype(BF16)


def core_sum_kernel(mine, theirs, total):
    ff2 = mine.shape[1] - 128
    total[:, :ff2] = (mine[:, :ff2].astype(F32) + theirs[:, :ff2].astype(F32)).astype(BF16)
    tail = mine[:, ff2:].astype(F32) + theirs[:, ff2:].astype(F32)
    square = jnp.sum(tail, 1, keepdims=True)
    lane = lanes(tail.shape)
    high = round_low(square)
    tail = jnp.where(lane == 0, high, jnp.where(lane == 1, square - high, 0.0))
    total[:, ff2:] = tail.astype(BF16)


def down_kernel(features, mine, theirs, weight, send, keep, scr):
    y = lax.axis_index("pool") % 2
    ff = weight.shape[0]
    tail = mine[:, 2 * ff :].astype(F32) + theirs[:, 2 * ff :].astype(F32)
    square = jnp.sum(tail, 1, keepdims=True)
    factor = lax.rsqrt(square * (1.0 / features) + 1e-05)
    gate = (mine[:, :ff].astype(F32) + theirs[:, :ff].astype(F32)) * factor
    up = (mine[:, ff : 2 * ff].astype(F32) + theirs[:, ff : 2 * ff].astype(F32)) * factor
    hidden = (gate / (1.0 + jnp.exp(-gate)) * up).astype(BF16)
    scr[...] = jnp.dot(hidden, weight[...], preferred_element_type=F32)
    rows = scr.shape[0] // 8
    for z in range(4):
        even = scr[(2 * z) * rows : (2 * z + 1) * rows, :]
        odd = scr[(2 * z + 1) * rows : (2 * z + 2) * rows, :]
        keep[z * rows : (z + 1) * rows, :] = jnp.where(y == 0, even, odd)
        send[z * rows : (z + 1) * rows, :] = jnp.where(y == 0, odd, even)


def split_kernel(keep, got, c0, c1, c2, c3, scr):
    z = lax.axis_index("pool") // 2
    scr[...] = keep[...] + got[...]
    rows = c0.shape[0]
    chunks = in_order([scr[s * rows : (s + 1) * rows, :] for s in range(4)], z)
    for values, chunk in zip(chunks, (c0, c1, c2, c3)):
        chunk[...] = values


def final_kernel(own, c0, c1, c2, c3, out):
    out[...] = (own[...] + ((c0[...] + c1[...]) + (c2[...] + c3[...]))).astype(BF16)


def flip(values, axis, step):
    size = lax.axis_size(axis)
    return lax.ppermute(values, axis, [(index, index ^ step) for index in range(size)])


def per_device_small(
    residual_in,
    query_new,
    key_new,
    value_new,
    key_cache,
    value_cache,
    block_table,
    lengths,
    out_weight,
    norm_gain,
    gate_weight,
    up_weight,
    down_weight,
):
    rows, width = residual_in.shape
    blocks = key_cache.shape[0]
    pool, mlp = 8, 4
    requests = rows * pool
    ff = gate_weight.shape[1]
    part_cols = out_weight.shape[1]
    half = HD // 2
    freq = 10000.0 ** (-2.0 * (np.arange(width) % half) / HD)
    freq = jnp.asarray(np.broadcast_to(freq.astype(np.float32), (8, width)))
    packed_width = 2 * width + 128
    slots = blocks + rows + 1
    part_width = width + 128

    packed, own = call(
        prepare_kernel,
        "rotary",
        [((rows, packed_width), BF16), ((slots, part_width), F32)],
        [block_table, lengths, freq, query_new, key_new, value_new, residual_in],
        [pltpu.VMEM((8, width), F32)],
        smem=(0, 1),
    )

    def pool_gather(values):
        (both,) = call(
            merge_kernel,
            "merge",
            [((2,) + values.shape, values.dtype)],
            [values, flip(values, "pool", 1)],
        )
        return [both] + [flip(both, "pool", step) for step in (2, 4, 6)]

    part, all_input, tables = call(
        attend_kernel,
        "attend",
        [((slots, part_width), BF16), ((requests, width), F32), ((requests, 128), F32)],
        pool_gather(packed) + [own, key_cache, value_cache],
        [pltpu.VMEM((requests, packed_width), F32)],
    )
    (head_part,) = call(
        combine_kernel,
        "combine",
        [((requests, part_cols), BF16)],
        pool_gather(part) + [tables, out_weight],
        [
            pltpu.VMEM((pool * slots, width), F32),
            pltpu.VMEM((pool, slots, 128), F32),
            pltpu.VMEM((requests * width // HD, 128), F32),
        ],
    )
    (head_sum,) = call(
        sum_kernel,
        "head_sum",
        [((requests, part_cols), BF16)],
        [head_part] + [flip(head_part, "mlp", step) for step in (1, 2, 3)],
    )
    share = pool // mlp
    pieces = []
    for turn in range(share):
        route = []
        for p in range(pool):
            for m in range(mlp):
                target = m * share + (p % share ^ turn)
                route.append((p * mlp + m, target * mlp + p // share))
        pieces.append(lax.ppermute(head_sum, ("pool", "mlp"), route))
    sums, own_residual = call(
        gate_up_kernel,
        "gate_up",
        [((requests, 2 * ff + 128), BF16), ((rows, width), F32)],
        pieces + [all_input, norm_gain.reshape(1, width), gate_weight, up_weight],
        [pltpu.VMEM((requests, width), F32)],
    )
    (core_sums,) = call(
        core_sum_kernel,
        "core_sum",
        [((requests, 2 * ff + 128), BF16)],
        [sums, flip(sums, "mlp", 1)],
    )
    send, keep = call(
        functools.partial(down_kernel, width * mlp),
        "down",
        [((requests // 2, width), F32)] * 2,
        [core_sums, flip(core_sums, "mlp", 2), down_weight],
        [pltpu.VMEM((requests, width), F32)],
    )
    chunks = call(
        split_kernel,
        "pair_sum",
        [((rows, width), F32)] * 4,
        [keep, flip(send, "pool", 1)],
        [pltpu.VMEM((requests // 2, width), F32)],
    )
    (out,) = call(
        final_kernel,
        "final",
        [((rows, width), BF16)],
        [own_residual, chunks[0]]
        + [flip(chunks[step], "pool", 2 * step) for step in (1, 2, 3)],
    )
    return out


def solution(mesh):
    in_specs = (
        P("pool", "mlp"),
        P("pool", "mlp"),
        P("pool", "mlp"),
        P("pool", "mlp"),
        P("pool", None, "mlp"),
        P("pool", None, "mlp"),
        P("pool", None),
        P("pool"),
        P("mlp", "pool"),
        P("mlp"),
        P("mlp", "pool"),
        P("mlp", "pool"),
        P("pool", "mlp"),
    )
    small = mesh.shape["pool"] == 8 and mesh.shape["mlp"] == 4
    per_device = per_device_small if small else per_device_wide
    return jax.shard_map(
        per_device, mesh=mesh, in_specs=in_specs, out_specs=P("pool", "mlp"), check_vma=False
    )
```

```python
import functools
import math

import jax
import jax.numpy as jnp
import numpy as np
from jax import lax
from jax.experimental import pallas as pl
from jax.experimental.pallas import tpu as pltpu
from jax.sharding import PartitionSpec as P

HD = 96
LOW = -1e30
CODE = 128


def rotate(values, positions):
    half_size = values.shape[-1] // 2
    inverse_freq = 10000.0 ** (-(2.0 * jnp.arange(half_size, dtype=jnp.float32)) / values.shape[-1])
    angles = positions.astype(jnp.float32)[:, None, None] * inverse_freq[None, None, :]
    cosine = jnp.cos(angles)
    sine_part = jnp.sin(angles)
    first = values[..., :half_size]
    second = values[..., half_size:]
    return jnp.concatenate(
        [first * cosine - second * sine_part, second * cosine + first * sine_part], -1
    )


def low(values):
    return lax.reduce_precision(values, 8, 7)


def split(values):
    high = low(values)
    return high.astype(jnp.bfloat16), (values - high).astype(jnp.bfloat16)


def encode(ints):
    return (ints // CODE).astype(jnp.bfloat16), (ints % CODE).astype(jnp.bfloat16)


def decode(high, rest):
    return high.astype(jnp.int32) * CODE + rest.astype(jnp.int32)


def gather(values, axis):
    copies = jnp.broadcast_to(values[None], (lax.axis_size(axis),) + values.shape)
    return lax.all_to_all(copies, axis, 0, 0)


def per_device_wide(
    residual_in,
    query_new,
    key_new,
    value_new,
    key_cache,
    value_cache,
    block_table,
    lengths,
    out_weight,
    norm_gain,
    gate_weight,
    up_weight,
    down_weight,
):
    rows, width = residual_in.shape
    heads = width // HD
    blocks, block_len = key_cache.shape[:2]
    most = block_table.shape[1]
    pool, mlp = lax.axis_size("pool"), lax.axis_size("mlp")
    pool_index = lax.axis_index("pool")
    requests = rows * pool
    score_scale = 1.0 / math.sqrt(HD)
    f32, bf16 = jnp.float32, jnp.bfloat16

    queries = rotate(query_new.astype(f32).reshape(rows, heads, HD), lengths).astype(bf16)
    new_keys = rotate(key_new.astype(f32).reshape(rows, heads, HD), lengths).astype(bf16)

    table_high, table_low = encode(block_table + 1)
    len_high, len_low = encode(lengths)
    packed = jnp.concatenate(
        [
            queries.reshape(rows, width),
            residual_in,
            table_high,
            table_low,
            len_high[:, None],
            len_low[:, None],
        ],
        1,
    )
    spare = -packed.shape[1] % 128
    packed = jnp.pad(packed, ((0, 0), (0, spare)))
    got = gather(packed, "pool").reshape(requests, packed.shape[1])
    all_queries = got[:, :width]
    all_input = got[:, width : 2 * width]
    tail = got[:, 2 * width :]
    tables = decode(tail[:, :most], tail[:, most : 2 * most]) - 1
    all_lengths = decode(tail[:, 2 * most], tail[:, 2 * most + 1])

    held_ids = pool_index * blocks + jnp.arange(blocks, dtype=jnp.int32)
    matches = tables[None, :, :] == held_ids[:, None, None]
    holder = jnp.any(matches, 2)
    block_index = jnp.sum(
        jnp.where(matches, jnp.arange(most, dtype=jnp.int32)[None, None, :], 0), (1, 2)
    )
    valid_len = jnp.sum(jnp.where(holder, all_lengths[None, :], 0), 1)
    block_query = jnp.dot(holder.astype(bf16), all_queries, preferred_element_type=f32)
    block_query = block_query.astype(bf16).reshape(blocks, heads, HD)
    key_rows = key_cache.reshape(blocks, block_len, heads, HD)
    value_rows = value_cache.reshape(blocks, block_len, heads, HD)
    scores = (
        jnp.einsum("bhd,bthd->bht", block_query, key_rows, preferred_element_type=f32)
        * score_scale
    )
    token_pos = block_index[:, None] * block_len + jnp.arange(block_len, dtype=jnp.int32)[None, :]
    valid = (token_pos < valid_len[:, None])[:, None, :]
    scores = jnp.where(valid, scores, LOW)
    shift = low(jnp.max(scores, 2))
    weights = jnp.where(valid, jnp.exp(scores - shift[:, :, None]), 0.0)
    totals = jnp.sum(weights, 2)
    numerator = jnp.einsum(
        "bht,bthd->bhd", weights.astype(bf16), value_rows, preferred_element_type=f32
    )
    self_score = jnp.sum(queries.astype(f32) * new_keys.astype(f32), -1) * score_scale
    self_shift = low(self_score)
    self_weight = jnp.exp(self_score - self_shift)
    self_numer = self_weight[:, :, None] * value_new.astype(f32).reshape(rows, heads, HD)

    own_total = jnp.concatenate([totals, self_weight], 0)
    total_high, total_low = split(own_total)
    part = jnp.concatenate(
        [
            jnp.concatenate([numerator, self_numer], 0)
            .astype(bf16)
            .reshape(blocks + rows, width),
            jnp.concatenate([shift, self_shift], 0).astype(bf16),
            total_high,
            total_low,
        ],
        1,
    )
    part = jnp.pad(part, ((0, 0), (0, -part.shape[1] % 128)))
    count = blocks + rows
    parts = gather(part, "pool").reshape(pool * count, part.shape[1])
    all_shift = parts[:, width : width + heads].astype(f32)
    all_total = parts[:, width + heads : width + 2 * heads].astype(f32) + parts[
        :, width + 2 * heads : width + 3 * heads
    ].astype(f32)
    place = jnp.arange(pool * count, dtype=jnp.int32)
    owner, slot = place // count, place % count
    is_block = slot < blocks
    block_id = jnp.where(is_block, owner * blocks + slot, -2)
    self_id = jnp.where(is_block, -2, owner * rows + slot - blocks)
    request_ids = jnp.arange(requests, dtype=jnp.int32)
    belongs = jnp.any(tables[:, None, :] == block_id[None, :, None], 2) | (
        request_ids[:, None] == self_id[None, :]
    )
    top = jnp.max(jnp.where(belongs[:, :, None], all_shift[None], LOW), 1)
    part_top = jnp.sum(jnp.where(belongs[:, :, None], top[:, None, :], 0.0), 0)
    scale = jnp.exp(all_shift - part_top)
    scaled = parts[:, :width].astype(f32).reshape(-1, heads, HD) * scale[:, :, None]
    mix = belongs.astype(f32)
    numer = jnp.dot(mix, scaled.reshape(-1, width), precision=lax.Precision.HIGHEST)
    denom = jnp.dot(mix, all_total * scale, precision=lax.Precision.HIGHEST)
    attended = (numer.reshape(requests, heads, HD) / denom[:, :, None]).astype(bf16)
    attended = attended.reshape(requests, width)

    head_part = jnp.dot(attended, out_weight, preferred_element_type=f32).astype(bf16)
    share = pool // mlp
    route = []
    for p in range(pool):
        for m in range(mlp):
            route.append((p * mlp + m, ((p % share) * mlp + m) * mlp + p // share))
    moved = lax.ppermute(head_part, ("pool", "mlp"), route)
    head_all = gather(moved, "pool").reshape(share, mlp, requests, -1)
    head_out = low(jnp.sum(head_all.astype(f32), 1))
    head_out = jnp.swapaxes(head_out, 0, 1).reshape(requests, width)
    residual = all_input.astype(f32) + head_out
    squares = jnp.sum(residual * residual, -1, keepdims=True)
    portion = (residual * norm_gain.astype(f32)).astype(bf16)

    ff = gate_weight.shape[1]
    square_high, square_low = split(squares)
    sums = jnp.concatenate(
        [
            jnp.dot(portion, gate_weight, preferred_element_type=f32).astype(bf16),
            jnp.dot(portion, up_weight, preferred_element_type=f32).astype(bf16),
            jnp.broadcast_to(square_high, (requests, 64)),
            jnp.broadcast_to(square_low, (requests, 64)),
        ],
        1,
    )
    summed = jnp.sum(gather(sums, "mlp").astype(f32), 0)
    mean_square = (summed[:, 2 * ff : 2 * ff + 1] + summed[:, 2 * ff + 64 : 2 * ff + 65]) / (
        width * mlp
    )
    factor = lax.rsqrt(mean_square + 1e-05)
    gate = summed[:, :ff] * factor
    up = summed[:, ff : 2 * ff] * factor
    hidden = (jax.nn.silu(gate) * up).astype(bf16)

    down = jnp.dot(hidden, down_weight, preferred_element_type=f32)
    down = lax.all_to_all(down.reshape(pool, rows, width), "pool", 0, 0)
    own = lax.dynamic_slice_in_dim(residual, pool_index * rows, rows, 0)
    return (own + jnp.sum(down, 0)).astype(bf16)


F32, BF16 = jnp.float32, jnp.bfloat16
VMEM = pl.BlockSpec(memory_space=pltpu.VMEM)
HBM = pl.BlockSpec(memory_space=pl.ANY)


def call(kernel, name, outs, args, scratch=(), hbm=(), limit=16 * 2**20):
    size = sum(math.prod(a.shape) * a.dtype.itemsize for a in args)
    return pl.pallas_call(
        kernel,
        out_shape=[jax.ShapeDtypeStruct(shape, dtype) for shape, dtype in outs],
        in_specs=[HBM if i in hbm else VMEM for i in range(len(args))],
        out_specs=[VMEM] * len(outs),
        scratch_shapes=list(scratch),
        compiler_params=pltpu.CompilerParams(vmem_limit_bytes=limit),
        cost_estimate=pl.CostEstimate(flops=0, bytes_accessed=size, transcendentals=0),
        name=name,
    )(*args)


def lanes(shape):
    return lax.broadcasted_iota(jnp.int32, shape, len(shape) - 1)


def in_order(pieces, index):
    for bit in (1, 2):
        odd = (index & bit) != 0
        pieces = [jnp.where(odd, pieces[s ^ bit], pieces[s]) for s in range(4)]
    return pieces


def rows_of(shape):
    return lax.broadcasted_iota(jnp.int32, shape, len(shape) - 2)


def round_low(values):
    return values.astype(BF16).astype(F32)


def prepare_kernel(*refs):
    sources, (packed, own), held = refs[:6], refs[6:8], refs[8:14]
    scr, sems = refs[14:]
    copies = [
        pltpu.make_async_copy(source, target, sems.at[i])
        for i, (source, target) in enumerate(zip(sources, held))
    ]
    for copy in copies:
        copy.start()
    for copy in copies:
        copy.wait()
    table, length, query, key, value, residual = held
    rows, width = query.shape
    heads = width // HD
    most = table.shape[1]
    blocks = own.shape[0] - rows - 1
    scr[...] = jnp.zeros_like(scr)
    scr[0:rows, :] = query[...].astype(F32)
    scr[rows : 2 * rows, :] = key[...].astype(F32)
    values = scr[...]
    line = rows_of((8, width))
    where_at = jnp.zeros((8, width), F32)
    for r in range(rows):
        here = (line == r) | (line == rows + r)
        where_at = jnp.where(here, length[r].astype(F32), where_at)
    lane = lanes((8, width))
    turn = lanes((8, 384)) % (HD // 2)
    freq = jnp.zeros((8, 384), F32)
    for i in range(HD // 2):
        freq = jnp.where(turn == i, float(np.float32(10000.0 ** (-2.0 * i / HD))), freq)
    angles = where_at * jnp.concatenate([freq] * (width // 384), 1)
    first = lane % HD < HD // 2
    ahead = pltpu.roll(values, width - HD // 2, 1)
    behind = pltpu.roll(values, HD // 2, 1)
    other = jnp.where(first, -ahead, behind)
    turned = values * jnp.cos(angles) + other * jnp.sin(angles)
    scr[...] = round_low(turned)
    packed[:, :width] = scr[0:rows, :].astype(BF16)
    packed[:, width : 2 * width] = residual[...]
    tail = jnp.zeros((rows, 128), F32)
    at, row = lanes((rows, 128)), rows_of((rows, 128))
    for r in range(rows):
        codes = [table[r, k] + 1 for k in range(most)] + [length[r]]
        spots = [(k, most + k) for k in range(most)] + [(2 * most, 2 * most + 1)]
        for code, (high, rest) in zip(codes, spots):
            tail = jnp.where((row == r) & (at == high), (code >> 7).astype(F32), tail)
            tail = jnp.where((row == r) & (at == rest), (code & 127).astype(F32), tail)
    packed[:, 2 * width :] = tail.astype(BF16)

    head_mask = lane // HD == line
    product = scr[0:rows, :] * scr[rows : 2 * rows, :]
    own[...] = jnp.zeros_like(own)
    spot = lanes((8, 128))
    tail = jnp.zeros((8, 128), F32)
    for r in range(rows):
        score = jnp.sum(
            jnp.where(head_mask, jnp.broadcast_to(product[r : r + 1], (8, width)), 0.0),
            1,
            keepdims=True,
        ) * (1.0 / math.sqrt(HD))
        shift = round_low(score)
        weight = jnp.exp(score - shift)
        spread = jnp.sum(jnp.where(head_mask, round_low(weight), 0.0), 0, keepdims=True)
        own[blocks + r : blocks + r + 1, :width] = spread * value[r : r + 1, :].astype(F32)
        high = round_low(weight)
        tail = jnp.where(spot == blocks + r, shift, tail)
        tail = jnp.where(spot == 8 + blocks + r, high, tail)
        tail = jnp.where(spot == 16 + blocks + r, weight - high, tail)
    own[:, width:] = tail


def merge_kernel(mine, theirs, both):
    y = lax.axis_index("pool") % 2
    both[y] = mine[...]
    both[1 - y] = theirs[...]


def attend_kernel(
    a0, a1, a2, a3, own, far_keys, far_values, part, residual, tables, scr, keys, values, sems
):
    blocks, block_len, width = keys.shape
    copies = [
        pltpu.make_async_copy(far.at[b], near.at[b], sems.at[i, b])
        for i, (far, near) in enumerate(((far_keys, keys), (far_values, values)))
        for b in range(blocks)
    ]
    for copy in copies:
        copy.start()
    rows = a0.shape[1]
    heads = width // HD
    most = 8
    me = lax.axis_index("pool")
    for y in range(2):
        pieces = [piece[y].astype(F32) for piece in (a0, a1, a2, a3)]
        for z, piece in enumerate(in_order(pieces, me // 2)):
            scr[(z * 2 + y) * rows : (z * 2 + y + 1) * rows, :] = piece
    queries = scr[:, :width]
    residual[...] = scr[:, width : 2 * width]
    tail = scr[:, 2 * width :]
    requests = tail.shape[0]
    table = tail * CODE + pltpu.roll(tail, 128 - most, 1) - 1.0
    length = tail[:, 2 * most : 2 * most + 1] * CODE + tail[:, 2 * most + 1 : 2 * most + 2]
    lane = lanes((requests, 128))
    table = jnp.where(lane < most, table, -2.0)
    tables[...] = table
    head_mask = lanes((heads, width)) // HD == rows_of((heads, width))
    spot = lanes((heads, 128))
    tail = own[:, width:]
    part[...] = own[...].astype(BF16)
    scores, limits = [], []
    for b in range(blocks):
        match = jnp.where(table == (me * blocks + b).astype(F32), 1.0, 0.0)
        holder = jnp.sum(match, 1, keepdims=True)
        place = jnp.sum(jnp.sum(match * lane.astype(F32), 1, keepdims=True), 0, keepdims=True)
        limit = jnp.sum(holder * length, 0, keepdims=True) - place * block_len
        limits.append(jnp.broadcast_to(limit, (heads, block_len)))
        query = jnp.sum(holder * queries, 0, keepdims=True)
        spread = jnp.where(head_mask, query, 0.0).astype(BF16)
        copies[b].wait()
        scores.append(
            lax.dot_general(
                spread, keys[b], (((1,), (1,)), ((), ())), preferred_element_type=F32
            )
        )
    scores = jnp.concatenate(scores, 0) * (1.0 / math.sqrt(HD))
    token = lanes((blocks * heads, block_len)).astype(F32)
    valid = token < jnp.concatenate(limits, 0)
    scores = jnp.where(valid, scores, LOW)
    shift = round_low(jnp.max(scores, 1, keepdims=True))
    weights = jnp.where(valid, jnp.exp(scores - shift), 0.0)
    total = jnp.sum(weights, 1, keepdims=True)
    high = round_low(total)
    rest = total - high
    numerators = []
    for b in range(blocks):
        mine = slice(b * heads, (b + 1) * heads)
        copies[blocks + b].wait()
        full = jnp.dot(weights[mine].astype(BF16), values[b], preferred_element_type=F32)
        numerators.append(jnp.sum(jnp.where(head_mask, full, 0.0), 0, keepdims=True))
        tail = jnp.where(spot == b, shift[mine], tail)
        tail = jnp.where(spot == 8 + b, high[mine], tail)
        tail = jnp.where(spot == 16 + b, rest[mine], tail)
    line = rows_of((8, width))
    numer = own[:, :width]
    for b in range(blocks):
        numer = jnp.where(line == b, numerators[b], numer)
    part[:, :width] = numer.astype(BF16)
    part[:, width:] = tail.astype(BF16)


def combine_kernel(b0, b1, b2, b3, tables, weight, head_part, numer, tails, mix):
    requests = tables.shape[0]
    slots = b0.shape[1]
    width = weight.shape[0]
    heads = width // HD
    rows, blocks = 2, slots - 3
    me = lax.axis_index("pool")
    for step, piece in enumerate((b0, b1, b2, b3)):
        z = (me // 2) ^ step
        for y in range(2):
            owner = z * 2 + y
            values = piece[y].astype(F32)
            numer[pl.ds(pl.multiple_of(owner * slots, 8), slots), :] = values[:, :width]
            tails[owner] = values[:, width:]
    lane8 = lanes((heads, 128))
    shifts = jnp.zeros((heads, 128), F32)
    totals = jnp.zeros((heads, 128), F32)
    for owner in range(8):
        tail = tails[owner]
        total = pltpu.roll(tail, 120, 1) + pltpu.roll(tail, 112, 1)
        tail, total = jnp.where(lane8 < 8, tail, 0.0), jnp.where(lane8 < 8, total, 0.0)
        if owner:
            tail, total = pltpu.roll(tail, 8 * owner, 1), pltpu.roll(total, 8 * owner, 1)
        shifts, totals = shifts + tail, totals + total
    lane = lanes((requests, 128))
    owner, slot = lane // slots, lane % slots
    block_id = jnp.where((slot < blocks) & (lane < 64), owner * blocks + slot, -5).astype(F32)
    self_id = jnp.where((slot >= blocks) & (slot < blocks + rows), owner * rows + slot - blocks, -5)
    table = tables[...]
    belongs = (self_id == rows_of((requests, 128))) & (lane < 64)
    for k in range(8):
        belongs = belongs | (table[:, k : k + 1] == block_id)
    for h in range(heads):
        shift = jnp.broadcast_to(shifts[h : h + 1], (requests, 128))
        top = jnp.max(jnp.where(belongs, shift, LOW), 1, keepdims=True)
        scale = jnp.where(belongs, jnp.exp(shift - top), 0.0)
        total = jnp.sum(scale * totals[h : h + 1], 1, keepdims=True)
        mix[h * requests : (h + 1) * requests, :] = scale / total
    full = jnp.dot(
        mix[:, : 8 * slots].astype(BF16), numer[...].astype(BF16), preferred_element_type=F32
    )
    head = lanes((requests, width)) // HD
    attended = jnp.zeros((requests, width), F32)
    for h in range(heads):
        attended = jnp.where(head == h, full[h * requests : (h + 1) * requests], attended)
    head_part[...] = jnp.dot(
        attended.astype(BF16), weight[...], preferred_element_type=F32
    ).astype(BF16)


def sum_kernel(p0, p1, p2, p3, total):
    total[...] = (
        (p0[...].astype(F32) + p1[...].astype(F32)) + (p2[...].astype(F32) + p3[...].astype(F32))
    ).astype(BF16)


def gate_up_kernel(same, flip, all_input, gain, gate, up, sums, own, scr):
    me = lax.axis_index("pool")
    odd = me % 2 == 1
    part = same.shape[1]
    ff = gate.shape[1]
    rows = own.shape[0]
    near, far = same[...].astype(F32), flip[...].astype(F32)
    scr[:, :part] = all_input[:, :part] + jnp.where(odd, far, near)
    scr[:, part:] = all_input[:, part:] + jnp.where(odd, near, far)
    residual = scr[...]
    mine = scr[0:rows, :]
    for p in range(1, residual.shape[0] // rows):
        mine = jnp.where(me == p, scr[p * rows : (p + 1) * rows, :], mine)
    own[...] = mine
    square = jnp.sum(residual * residual, 1, keepdims=True)
    portion = (residual * gain[...].astype(F32)).astype(BF16)
    sums[:, :ff] = jnp.dot(portion, gate[...], preferred_element_type=F32).astype(BF16)
    sums[:, ff : 2 * ff] = jnp.dot(portion, up[...], preferred_element_type=F32).astype(BF16)
    lane = lanes((residual.shape[0], 128))
    high = round_low(square)
    tail = jnp.where(lane == 0, high, jnp.where(lane == 1, square - high, 0.0))
    sums[:, 2 * ff :] = tail.astype(BF16)


def core_sum_kernel(mine, theirs, total):
    ff2 = mine.shape[1] - 128
    total[:, :ff2] = (mine[:, :ff2].astype(F32) + theirs[:, :ff2].astype(F32)).astype(BF16)
    tail = mine[:, ff2:].astype(F32) + theirs[:, ff2:].astype(F32)
    square = jnp.sum(tail, 1, keepdims=True)
    lane = lanes(tail.shape)
    high = round_low(square)
    tail = jnp.where(lane == 0, high, jnp.where(lane == 1, square - high, 0.0))
    total[:, ff2:] = tail.astype(BF16)


def down_kernel(features, mine, theirs, weight, send, keep, scr):
    y = lax.axis_index("pool") % 2
    ff = weight.shape[0]
    tail = mine[:, 2 * ff :].astype(F32) + theirs[:, 2 * ff :].astype(F32)
    square = jnp.sum(tail, 1, keepdims=True)
    factor = lax.rsqrt(square * (1.0 / features) + 1e-05)
    gate = (mine[:, :ff].astype(F32) + theirs[:, :ff].astype(F32)) * factor
    up = (mine[:, ff : 2 * ff].astype(F32) + theirs[:, ff : 2 * ff].astype(F32)) * factor
    hidden = (gate / (1.0 + jnp.exp(-gate)) * up).astype(BF16)
    scr[...] = jnp.dot(hidden, weight[...], preferred_element_type=F32)
    rows = scr.shape[0] // 8
    for z in range(4):
        even = scr[(2 * z) * rows : (2 * z + 1) * rows, :]
        odd = scr[(2 * z + 1) * rows : (2 * z + 2) * rows, :]
        keep[z * rows : (z + 1) * rows, :] = jnp.where(y == 0, even, odd)
        send[z * rows : (z + 1) * rows, :] = jnp.where(y == 0, odd, even)


def split_kernel(keep, got, c0, c1, c2, c3, scr):
    z = lax.axis_index("pool") // 2
    scr[...] = keep[...] + got[...]
    rows = c0.shape[0]
    chunks = in_order([scr[s * rows : (s + 1) * rows, :] for s in range(4)], z)
    for values, chunk in zip(chunks, (c0, c1, c2, c3)):
        chunk[...] = values


def final_kernel(own, c0, c1, c2, c3, out):
    out[...] = (own[...] + ((c0[...] + c1[...]) + (c2[...] + c3[...]))).astype(BF16)


def flip(values, axis, step):
    size = lax.axis_size(axis)
    return lax.ppermute(values, axis, [(index, index ^ step) for index in range(size)])


def per_device_small(
    residual_in,
    query_new,
    key_new,
    value_new,
    key_cache,
    value_cache,
    block_table,
    lengths,
    out_weight,
    norm_gain,
    gate_weight,
    up_weight,
    down_weight,
):
    rows, width = residual_in.shape
    blocks = key_cache.shape[0]
    pool, mlp = 8, 4
    requests = rows * pool
    ff = gate_weight.shape[1]
    part_cols = out_weight.shape[1]
    packed_width = 2 * width + 128
    slots = blocks + rows + 1
    part_width = width + 128

    packed, own = call(
        prepare_kernel,
        "rotary",
        [((rows, packed_width), BF16), ((slots, part_width), F32)],
        [block_table, lengths, query_new, key_new, value_new, residual_in],
        [pltpu.SMEM(block_table.shape, jnp.int32), pltpu.SMEM(lengths.shape, jnp.int32)]
        + [pltpu.VMEM((rows, width), BF16)] * 4
        + [pltpu.VMEM((8, width), F32), pltpu.SemaphoreType.DMA((6,))],
        hbm=range(6),
        limit=52 * 2**20,
    )

    def pool_gather(values):
        (both,) = call(
            merge_kernel,
            "merge",
            [((2,) + values.shape, values.dtype)],
            [values, flip(values, "pool", 1)],
        )
        return [both] + [flip(both, "pool", step) for step in (2, 4, 6)]

    part, all_input, tables = call(
        attend_kernel,
        "attend",
        [((slots, part_width), BF16), ((requests, width), F32), ((requests, 128), F32)],
        pool_gather(packed) + [own, key_cache, value_cache],
        [
            pltpu.VMEM((requests, packed_width), F32),
            pltpu.VMEM(key_cache.shape, BF16),
            pltpu.VMEM(value_cache.shape, BF16),
            pltpu.SemaphoreType.DMA((2, blocks)),
        ],
        hbm=(5, 6),
        limit=52 * 2**20,
    )
    (head_part,) = call(
        combine_kernel,
        "combine",
        [((requests, part_cols), BF16)],
        pool_gather(part) + [tables, out_weight],
        [
            pltpu.VMEM((pool * slots, width), F32),
            pltpu.VMEM((pool, slots, 128), F32),
            pltpu.VMEM((requests * width // HD, 128), F32),
        ],
    )
    (head_sum,) = call(
        sum_kernel,
        "head_sum",
        [((requests, part_cols), BF16)],
        [head_part] + [flip(head_part, "mlp", step) for step in (1, 2, 3)],
    )
    pieces = []
    for turn in range(2):
        route = []
        for m in range(mlp):
            by_distance = sorted(range(4), key=lambda z: (-abs(z - m), z))
            for z, step in zip(by_distance, (0, 1, 2, 3)):
                for y in range(2):
                    source = (m * 2 + y) * mlp + (m ^ step)
                    route.append((source, (z * 2 + (y ^ turn)) * mlp + m))
        pieces.append(lax.ppermute(head_sum, ("pool", "mlp"), route))
    sums, own_residual = call(
        gate_up_kernel,
        "gate_up",
        [((requests, 2 * ff + 128), BF16), ((rows, width), F32)],
        pieces + [all_input, norm_gain.reshape(1, width), gate_weight, up_weight],
        [pltpu.VMEM((requests, width), F32)],
    )
    (core_sums,) = call(
        core_sum_kernel,
        "core_sum",
        [((requests, 2 * ff + 128), BF16)],
        [sums, flip(sums, "mlp", 1)],
    )
    send, keep = call(
        functools.partial(down_kernel, width * mlp),
        "down",
        [((requests // 2, width), F32)] * 2,
        [core_sums, flip(core_sums, "mlp", 2), down_weight],
        [pltpu.VMEM((requests, width), F32)],
    )
    chunks = call(
        split_kernel,
        "pair_sum",
        [((rows, width), F32)] * 4,
        [keep, flip(send, "pool", 1)],
        [pltpu.VMEM((requests // 2, width), F32)],
    )
    (out,) = call(
        final_kernel,
        "final",
        [((rows, width), BF16)],
        [own_residual, chunks[0]] + [flip(chunks[s], "pool", 2 * s) for s in (3, 2, 1)],
    )
    return out


def solution(mesh):
    in_specs = (
        P("pool", "mlp"),
        P("pool", "mlp"),
        P("pool", "mlp"),
        P("pool", "mlp"),
        P("pool", None, "mlp"),
        P("pool", None, "mlp"),
        P("pool", None),
        P("pool"),
        P("mlp", "pool"),
        P("mlp"),
        P("mlp", "pool"),
        P("mlp", "pool"),
        P("pool", "mlp"),
    )
    small = mesh.shape["pool"] == 8 and mesh.shape["mlp"] == 4
    per_device = per_device_small if small else per_device_wide
    return jax.shard_map(
        per_device, mesh=mesh, in_specs=in_specs, out_specs=P("pool", "mlp"), check_vma=False
    )
```

```python
import functools
import math

import jax
import jax.numpy as jnp
import numpy as np
from jax import lax
from jax.experimental import pallas as pl
from jax.experimental.pallas import tpu as pltpu
from jax.sharding import PartitionSpec as P

HD = 96
LOW = -1e30
CODE = 128


def rotate(values, positions):
    half_size = values.shape[-1] // 2
    inverse_freq = 10000.0 ** (-(2.0 * jnp.arange(half_size, dtype=jnp.float32)) / values.shape[-1])
    angles = positions.astype(jnp.float32)[:, None, None] * inverse_freq[None, None, :]
    cosine = jnp.cos(angles)
    sine_part = jnp.sin(angles)
    first = values[..., :half_size]
    second = values[..., half_size:]
    return jnp.concatenate(
        [first * cosine - second * sine_part, second * cosine + first * sine_part], -1
    )


def low(values):
    return lax.reduce_precision(values, 8, 7)


def split(values):
    high = low(values)
    return high.astype(jnp.bfloat16), (values - high).astype(jnp.bfloat16)


def encode(ints):
    return (ints // CODE).astype(jnp.bfloat16), (ints % CODE).astype(jnp.bfloat16)


def decode(high, rest):
    return high.astype(jnp.int32) * CODE + rest.astype(jnp.int32)


def gather(values, axis):
    copies = jnp.broadcast_to(values[None], (lax.axis_size(axis),) + values.shape)
    return lax.all_to_all(copies, axis, 0, 0)


def per_device_wide(
    residual_in,
    query_new,
    key_new,
    value_new,
    key_cache,
    value_cache,
    block_table,
    lengths,
    out_weight,
    norm_gain,
    gate_weight,
    up_weight,
    down_weight,
):
    rows, width = residual_in.shape
    heads = width // HD
    blocks, block_len = key_cache.shape[:2]
    most = block_table.shape[1]
    pool, mlp = lax.axis_size("pool"), lax.axis_size("mlp")
    pool_index = lax.axis_index("pool")
    requests = rows * pool
    score_scale = 1.0 / math.sqrt(HD)
    f32, bf16 = jnp.float32, jnp.bfloat16

    queries = rotate(query_new.astype(f32).reshape(rows, heads, HD), lengths).astype(bf16)
    new_keys = rotate(key_new.astype(f32).reshape(rows, heads, HD), lengths).astype(bf16)

    table_high, table_low = encode(block_table + 1)
    len_high, len_low = encode(lengths)
    packed = jnp.concatenate(
        [
            queries.reshape(rows, width),
            residual_in,
            table_high,
            table_low,
            len_high[:, None],
            len_low[:, None],
        ],
        1,
    )
    spare = -packed.shape[1] % 128
    packed = jnp.pad(packed, ((0, 0), (0, spare)))
    got = gather(packed, "pool").reshape(requests, packed.shape[1])
    all_queries = got[:, :width]
    all_input = got[:, width : 2 * width]
    tail = got[:, 2 * width :]
    tables = decode(tail[:, :most], tail[:, most : 2 * most]) - 1
    all_lengths = decode(tail[:, 2 * most], tail[:, 2 * most + 1])

    held_ids = pool_index * blocks + jnp.arange(blocks, dtype=jnp.int32)
    matches = tables[None, :, :] == held_ids[:, None, None]
    holder = jnp.any(matches, 2)
    block_index = jnp.sum(
        jnp.where(matches, jnp.arange(most, dtype=jnp.int32)[None, None, :], 0), (1, 2)
    )
    valid_len = jnp.sum(jnp.where(holder, all_lengths[None, :], 0), 1)
    block_query = jnp.dot(holder.astype(bf16), all_queries, preferred_element_type=f32)
    block_query = block_query.astype(bf16).reshape(blocks, heads, HD)
    key_rows = key_cache.reshape(blocks, block_len, heads, HD)
    value_rows = value_cache.reshape(blocks, block_len, heads, HD)
    scores = (
        jnp.einsum("bhd,bthd->bht", block_query, key_rows, preferred_element_type=f32)
        * score_scale
    )
    token_pos = block_index[:, None] * block_len + jnp.arange(block_len, dtype=jnp.int32)[None, :]
    valid = (token_pos < valid_len[:, None])[:, None, :]
    scores = jnp.where(valid, scores, LOW)
    shift = low(jnp.max(scores, 2))
    weights = jnp.where(valid, jnp.exp(scores - shift[:, :, None]), 0.0)
    totals = jnp.sum(weights, 2)
    numerator = jnp.einsum(
        "bht,bthd->bhd", weights.astype(bf16), value_rows, preferred_element_type=f32
    )
    self_score = jnp.sum(queries.astype(f32) * new_keys.astype(f32), -1) * score_scale
    self_shift = low(self_score)
    self_weight = jnp.exp(self_score - self_shift)
    self_numer = self_weight[:, :, None] * value_new.astype(f32).reshape(rows, heads, HD)

    own_total = jnp.concatenate([totals, self_weight], 0)
    total_high, total_low = split(own_total)
    part = jnp.concatenate(
        [
            jnp.concatenate([numerator, self_numer], 0)
            .astype(bf16)
            .reshape(blocks + rows, width),
            jnp.concatenate([shift, self_shift], 0).astype(bf16),
            total_high,
            total_low,
        ],
        1,
    )
    part = jnp.pad(part, ((0, 0), (0, -part.shape[1] % 128)))
    count = blocks + rows
    parts = gather(part, "pool").reshape(pool * count, part.shape[1])
    all_shift = parts[:, width : width + heads].astype(f32)
    all_total = parts[:, width + heads : width + 2 * heads].astype(f32) + parts[
        :, width + 2 * heads : width + 3 * heads
    ].astype(f32)
    place = jnp.arange(pool * count, dtype=jnp.int32)
    owner, slot = place // count, place % count
    is_block = slot < blocks
    block_id = jnp.where(is_block, owner * blocks + slot, -2)
    self_id = jnp.where(is_block, -2, owner * rows + slot - blocks)
    request_ids = jnp.arange(requests, dtype=jnp.int32)
    belongs = jnp.any(tables[:, None, :] == block_id[None, :, None], 2) | (
        request_ids[:, None] == self_id[None, :]
    )
    top = jnp.max(jnp.where(belongs[:, :, None], all_shift[None], LOW), 1)
    part_top = jnp.sum(jnp.where(belongs[:, :, None], top[:, None, :], 0.0), 0)
    scale = jnp.exp(all_shift - part_top)
    scaled = parts[:, :width].astype(f32).reshape(-1, heads, HD) * scale[:, :, None]
    mix = belongs.astype(f32)
    numer = jnp.dot(mix, scaled.reshape(-1, width), precision=lax.Precision.HIGHEST)
    denom = jnp.dot(mix, all_total * scale, precision=lax.Precision.HIGHEST)
    attended = (numer.reshape(requests, heads, HD) / denom[:, :, None]).astype(bf16)
    attended = attended.reshape(requests, width)

    head_part = jnp.dot(attended, out_weight, preferred_element_type=f32).astype(bf16)
    share = pool // mlp
    route = []
    for p in range(pool):
        for m in range(mlp):
            route.append((p * mlp + m, ((p % share) * mlp + m) * mlp + p // share))
    moved = lax.ppermute(head_part, ("pool", "mlp"), route)
    head_all = gather(moved, "pool").reshape(share, mlp, requests, -1)
    head_out = low(jnp.sum(head_all.astype(f32), 1))
    head_out = jnp.swapaxes(head_out, 0, 1).reshape(requests, width)
    residual = all_input.astype(f32) + head_out
    squares = jnp.sum(residual * residual, -1, keepdims=True)
    portion = (residual * norm_gain.astype(f32)).astype(bf16)

    ff = gate_weight.shape[1]
    square_high, square_low = split(squares)
    sums = jnp.concatenate(
        [
            jnp.dot(portion, gate_weight, preferred_element_type=f32).astype(bf16),
            jnp.dot(portion, up_weight, preferred_element_type=f32).astype(bf16),
            jnp.broadcast_to(square_high, (requests, 64)),
            jnp.broadcast_to(square_low, (requests, 64)),
        ],
        1,
    )
    summed = jnp.sum(gather(sums, "mlp").astype(f32), 0)
    mean_square = (summed[:, 2 * ff : 2 * ff + 1] + summed[:, 2 * ff + 64 : 2 * ff + 65]) / (
        width * mlp
    )
    factor = lax.rsqrt(mean_square + 1e-05)
    gate = summed[:, :ff] * factor
    up = summed[:, ff : 2 * ff] * factor
    hidden = (jax.nn.silu(gate) * up).astype(bf16)

    down = jnp.dot(hidden, down_weight, preferred_element_type=f32)
    down = lax.all_to_all(down.reshape(pool, rows, width), "pool", 0, 0)
    own = lax.dynamic_slice_in_dim(residual, pool_index * rows, rows, 0)
    return (own + jnp.sum(down, 0)).astype(bf16)


F32, BF16 = jnp.float32, jnp.bfloat16
VMEM = pl.BlockSpec(memory_space=pltpu.VMEM)
HBM = pl.BlockSpec(memory_space=pl.ANY)


def call(kernel, name, outs, args, scratch=(), hbm=(), limit=16 * 2**20):
    size = sum(math.prod(a.shape) * a.dtype.itemsize for a in args)
    return pl.pallas_call(
        kernel,
        out_shape=[jax.ShapeDtypeStruct(shape, dtype) for shape, dtype in outs],
        in_specs=[HBM if i in hbm else VMEM for i in range(len(args))],
        out_specs=[VMEM] * len(outs),
        scratch_shapes=list(scratch),
        compiler_params=pltpu.CompilerParams(vmem_limit_bytes=limit),
        cost_estimate=pl.CostEstimate(flops=0, bytes_accessed=size, transcendentals=0),
        name=name,
    )(*args)


def lanes(shape):
    return lax.broadcasted_iota(jnp.int32, shape, len(shape) - 1)


def in_order(pieces, index):
    for bit in (1, 2):
        odd = (index & bit) != 0
        pieces = [jnp.where(odd, pieces[s ^ bit], pieces[s]) for s in range(4)]
    return pieces


def rows_of(shape):
    return lax.broadcasted_iota(jnp.int32, shape, len(shape) - 2)


def round_low(values):
    return values.astype(BF16).astype(F32)


def prepare_kernel(*refs):
    sources, (packed, own), held = refs[:6], refs[8:10], refs[10:16]
    scr, sems = refs[16:]
    copies = [
        pltpu.make_async_copy(source, target, sems.at[i])
        for i, (source, target) in enumerate(zip(sources, held))
    ]
    for copy in copies:
        copy.start()
    for copy in copies:
        copy.wait()
    table, length, query, key, value, residual = held
    rows, width = query.shape
    heads = width // HD
    most = table.shape[1]
    blocks = own.shape[0] - rows - 1
    scr[...] = jnp.zeros_like(scr)
    scr[0:rows, :] = query[...].astype(F32)
    scr[rows : 2 * rows, :] = key[...].astype(F32)
    values = scr[...]
    line = rows_of((8, width))
    where_at = jnp.zeros((8, width), F32)
    for r in range(rows):
        here = (line == r) | (line == rows + r)
        where_at = jnp.where(here, length[r].astype(F32), where_at)
    lane = lanes((8, width))
    turn = lanes((8, 384)) % (HD // 2)
    freq = jnp.zeros((8, 384), F32)
    for i in range(HD // 2):
        freq = jnp.where(turn == i, float(np.float32(10000.0 ** (-2.0 * i / HD))), freq)
    angles = where_at * jnp.concatenate([freq] * (width // 384), 1)
    first = lane % HD < HD // 2
    ahead = pltpu.roll(values, width - HD // 2, 1)
    behind = pltpu.roll(values, HD // 2, 1)
    other = jnp.where(first, -ahead, behind)
    turned = values * jnp.cos(angles) + other * jnp.sin(angles)
    scr[...] = round_low(turned)
    packed[:, :width] = scr[0:rows, :].astype(BF16)
    packed[:, width : 2 * width] = residual[...]
    tail = jnp.zeros((rows, 128), F32)
    at, row = lanes((rows, 128)), rows_of((rows, 128))
    for r in range(rows):
        codes = [table[r, k] + 1 for k in range(most)] + [length[r]]
        spots = [(k, most + k) for k in range(most)] + [(2 * most, 2 * most + 1)]
        for code, (high, rest) in zip(codes, spots):
            tail = jnp.where((row == r) & (at == high), (code >> 7).astype(F32), tail)
            tail = jnp.where((row == r) & (at == rest), (code & 127).astype(F32), tail)
    packed[:, 2 * width :] = tail.astype(BF16)

    head_mask = lane // HD == line
    product = scr[0:rows, :] * scr[rows : 2 * rows, :]
    own[...] = jnp.zeros_like(own)
    spot = lanes((8, 128))
    tail = jnp.zeros((8, 128), F32)
    for r in range(rows):
        score = jnp.sum(
            jnp.where(head_mask, jnp.broadcast_to(product[r : r + 1], (8, width)), 0.0),
            1,
            keepdims=True,
        ) * (1.0 / math.sqrt(HD))
        shift = round_low(score)
        weight = jnp.exp(score - shift)
        spread = jnp.sum(jnp.where(head_mask, round_low(weight), 0.0), 0, keepdims=True)
        own[blocks + r : blocks + r + 1, :width] = spread * value[r : r + 1, :].astype(F32)
        high = round_low(weight)
        tail = jnp.where(spot == blocks + r, shift, tail)
        tail = jnp.where(spot == 8 + blocks + r, high, tail)
        tail = jnp.where(spot == 16 + blocks + r, weight - high, tail)
    own[:, width:] = tail


def merge_kernel(mine, theirs, both):
    y = lax.axis_index("pool") % 2
    both[y] = mine[...]
    both[1 - y] = theirs[...]


def attend_kernel(a0, a1, a2, a3, own, keys, values, part, residual, tables, scr):
    blocks, block_len, width = keys.shape
    rows = a0.shape[1]
    heads = width // HD
    most = 8
    me = lax.axis_index("pool")
    for y in range(2):
        pieces = [piece[y].astype(F32) for piece in (a0, a1, a2, a3)]
        for z, piece in enumerate(in_order(pieces, me // 2)):
            scr[(z * 2 + y) * rows : (z * 2 + y + 1) * rows, :] = piece
    queries = scr[:, :width]
    residual[...] = scr[:, width : 2 * width]
    tail = scr[:, 2 * width :]
    requests = tail.shape[0]
    table = tail * CODE + pltpu.roll(tail, 128 - most, 1) - 1.0
    length = tail[:, 2 * most : 2 * most + 1] * CODE + tail[:, 2 * most + 1 : 2 * most + 2]
    lane = lanes((requests, 128))
    table = jnp.where(lane < most, table, -2.0)
    tables[...] = table
    head_mask = lanes((heads, width)) // HD == rows_of((heads, width))
    spot = lanes((heads, 128))
    tail = own[:, width:]
    part[...] = own[...].astype(BF16)
    scores, limits = [], []
    for b in range(blocks):
        match = jnp.where(table == (me * blocks + b).astype(F32), 1.0, 0.0)
        holder = jnp.sum(match, 1, keepdims=True)
        place = jnp.sum(jnp.sum(match * lane.astype(F32), 1, keepdims=True), 0, keepdims=True)
        limit = jnp.sum(holder * length, 0, keepdims=True) - place * block_len
        limits.append(jnp.broadcast_to(limit, (heads, block_len)))
        query = jnp.sum(holder * queries, 0, keepdims=True)
        spread = jnp.where(head_mask, query, 0.0).astype(BF16)
        scores.append(
            lax.dot_general(
                spread, keys[b], (((1,), (1,)), ((), ())), preferred_element_type=F32
            )
        )
    scores = jnp.concatenate(scores, 0) * (1.0 / math.sqrt(HD))
    token = lanes((blocks * heads, block_len)).astype(F32)
    valid = token < jnp.concatenate(limits, 0)
    scores = jnp.where(valid, scores, LOW)
    shift = round_low(jnp.max(scores, 1, keepdims=True))
    weights = jnp.where(valid, jnp.exp(scores - shift), 0.0)
    total = jnp.sum(weights, 1, keepdims=True)
    high = round_low(total)
    rest = total - high
    numerators = []
    for b in range(blocks):
        mine = slice(b * heads, (b + 1) * heads)
        full = jnp.dot(weights[mine].astype(BF16), values[b], preferred_element_type=F32)
        numerators.append(jnp.sum(jnp.where(head_mask, full, 0.0), 0, keepdims=True))
        tail = jnp.where(spot == b, shift[mine], tail)
        tail = jnp.where(spot == 8 + b, high[mine], tail)
        tail = jnp.where(spot == 16 + b, rest[mine], tail)
    line = rows_of((8, width))
    numer = own[:, :width]
    for b in range(blocks):
        numer = jnp.where(line == b, numerators[b], numer)
    part[:, :width] = numer.astype(BF16)
    part[:, width:] = tail.astype(BF16)


def combine_kernel(b0, b1, b2, b3, tables, weight, head_part, numer, tails, mix):
    requests = tables.shape[0]
    slots = b0.shape[1]
    width = weight.shape[0]
    heads = width // HD
    rows, blocks = 2, slots - 3
    me = lax.axis_index("pool")
    for step, piece in enumerate((b0, b1, b2, b3)):
        z = (me // 2) ^ step
        for y in range(2):
            owner = z * 2 + y
            values = piece[y].astype(F32)
            numer[pl.ds(pl.multiple_of(owner * slots, 8), slots), :] = values[:, :width]
            tails[owner] = values[:, width:]
    lane8 = lanes((heads, 128))
    shifts = jnp.zeros((heads, 128), F32)
    totals = jnp.zeros((heads, 128), F32)
    for owner in range(8):
        tail = tails[owner]
        total = pltpu.roll(tail, 120, 1) + pltpu.roll(tail, 112, 1)
        tail, total = jnp.where(lane8 < 8, tail, 0.0), jnp.where(lane8 < 8, total, 0.0)
        if owner:
            tail, total = pltpu.roll(tail, 8 * owner, 1), pltpu.roll(total, 8 * owner, 1)
        shifts, totals = shifts + tail, totals + total
    lane = lanes((requests, 128))
    owner, slot = lane // slots, lane % slots
    block_id = jnp.where((slot < blocks) & (lane < 64), owner * blocks + slot, -5).astype(F32)
    self_id = jnp.where((slot >= blocks) & (slot < blocks + rows), owner * rows + slot - blocks, -5)
    table = tables[...]
    belongs = (self_id == rows_of((requests, 128))) & (lane < 64)
    for k in range(8):
        belongs = belongs | (table[:, k : k + 1] == block_id)
    for h in range(heads):
        shift = jnp.broadcast_to(shifts[h : h + 1], (requests, 128))
        top = jnp.max(jnp.where(belongs, shift, LOW), 1, keepdims=True)
        scale = jnp.where(belongs, jnp.exp(shift - top), 0.0)
        total = jnp.sum(scale * totals[h : h + 1], 1, keepdims=True)
        mix[h * requests : (h + 1) * requests, :] = scale / total
    full = jnp.dot(
        mix[:, : 8 * slots].astype(BF16), numer[...].astype(BF16), preferred_element_type=F32
    )
    head = lanes((requests, width)) // HD
    attended = jnp.zeros((requests, width), F32)
    for h in range(heads):
        attended = jnp.where(head == h, full[h * requests : (h + 1) * requests], attended)
    head_part[...] = jnp.dot(
        attended.astype(BF16), weight[...], preferred_element_type=F32
    ).astype(BF16)


def sum_kernel(p0, p1, p2, p3, total):
    total[...] = (
        (p0[...].astype(F32) + p1[...].astype(F32)) + (p2[...].astype(F32) + p3[...].astype(F32))
    ).astype(BF16)


def gate_up_kernel(same, flip, all_input, gain, gate, up, sums, own, scr):
    me = lax.axis_index("pool")
    odd = me % 2 == 1
    part = same.shape[1]
    ff = gate.shape[1]
    rows = own.shape[0]
    near, far = same[...].astype(F32), flip[...].astype(F32)
    scr[:, :part] = all_input[:, :part] + jnp.where(odd, far, near)
    scr[:, part:] = all_input[:, part:] + jnp.where(odd, near, far)
    residual = scr[...]
    mine = scr[0:rows, :]
    for p in range(1, residual.shape[0] // rows):
        mine = jnp.where(me == p, scr[p * rows : (p + 1) * rows, :], mine)
    own[...] = mine
    square = jnp.sum(residual * residual, 1, keepdims=True)
    portion = (residual * gain[...].astype(F32)).astype(BF16)
    sums[:, :ff] = jnp.dot(portion, gate[...], preferred_element_type=F32).astype(BF16)
    sums[:, ff : 2 * ff] = jnp.dot(portion, up[...], preferred_element_type=F32).astype(BF16)
    lane = lanes((residual.shape[0], 128))
    high = round_low(square)
    tail = jnp.where(lane == 0, high, jnp.where(lane == 1, square - high, 0.0))
    sums[:, 2 * ff :] = tail.astype(BF16)


def core_sum_kernel(mine, theirs, total):
    ff2 = mine.shape[1] - 128
    total[:, :ff2] = (mine[:, :ff2].astype(F32) + theirs[:, :ff2].astype(F32)).astype(BF16)
    tail = mine[:, ff2:].astype(F32) + theirs[:, ff2:].astype(F32)
    square = jnp.sum(tail, 1, keepdims=True)
    lane = lanes(tail.shape)
    high = round_low(square)
    tail = jnp.where(lane == 0, high, jnp.where(lane == 1, square - high, 0.0))
    total[:, ff2:] = tail.astype(BF16)


def down_kernel(features, mine, theirs, weight, send, keep, scr):
    y = lax.axis_index("pool") % 2
    ff = weight.shape[0]
    tail = mine[:, 2 * ff :].astype(F32) + theirs[:, 2 * ff :].astype(F32)
    square = jnp.sum(tail, 1, keepdims=True)
    factor = lax.rsqrt(square * (1.0 / features) + 1e-05)
    gate = (mine[:, :ff].astype(F32) + theirs[:, :ff].astype(F32)) * factor
    up = (mine[:, ff : 2 * ff].astype(F32) + theirs[:, ff : 2 * ff].astype(F32)) * factor
    hidden = (gate / (1.0 + jnp.exp(-gate)) * up).astype(BF16)
    scr[...] = jnp.dot(hidden, weight[...], preferred_element_type=F32)
    rows = scr.shape[0] // 8
    for z in range(4):
        even = scr[(2 * z) * rows : (2 * z + 1) * rows, :]
        odd = scr[(2 * z + 1) * rows : (2 * z + 2) * rows, :]
        keep[z * rows : (z + 1) * rows, :] = jnp.where(y == 0, even, odd)
        send[z * rows : (z + 1) * rows, :] = jnp.where(y == 0, odd, even)


def split_kernel(keep, got, c0, c1, c2, c3, scr):
    z = lax.axis_index("pool") // 2
    scr[...] = keep[...] + got[...]
    rows = c0.shape[0]
    chunks = in_order([scr[s * rows : (s + 1) * rows, :] for s in range(4)], z)
    for values, chunk in zip(chunks, (c0, c1, c2, c3)):
        chunk[...] = values


def final_kernel(own, c0, c1, c2, c3, out):
    out[...] = (own[...] + ((c0[...] + c1[...]) + (c2[...] + c3[...]))).astype(BF16)


def flip(values, axis, step):
    size = lax.axis_size(axis)
    return lax.ppermute(values, axis, [(index, index ^ step) for index in range(size)])


def per_device_small(
    residual_in,
    query_new,
    key_new,
    value_new,
    key_cache,
    value_cache,
    block_table,
    lengths,
    out_weight,
    norm_gain,
    gate_weight,
    up_weight,
    down_weight,
):
    rows, width = residual_in.shape
    blocks = key_cache.shape[0]
    pool, mlp = 8, 4
    requests = rows * pool
    ff = gate_weight.shape[1]
    part_cols = out_weight.shape[1]
    packed_width = 2 * width + 128
    slots = blocks + rows + 1
    part_width = width + 128

    packed, own = call(
        prepare_kernel,
        "rotary",
        [((rows, packed_width), BF16), ((slots, part_width), F32)],
        [block_table, lengths, query_new, key_new, value_new, residual_in, key_cache, value_cache],
        [pltpu.SMEM(block_table.shape, jnp.int32), pltpu.SMEM(lengths.shape, jnp.int32)]
        + [pltpu.VMEM((rows, width), BF16)] * 4
        + [pltpu.VMEM((8, width), F32), pltpu.SemaphoreType.DMA((6,))],
        hbm=range(8),
        limit=54 * 2**20,
    )

    def pool_gather(values):
        (both,) = call(
            merge_kernel,
            "merge",
            [((2,) + values.shape, values.dtype)],
            [values, flip(values, "pool", 1)],
        )
        return [both] + [flip(both, "pool", step) for step in (2, 4, 6)]

    part, all_input, tables = call(
        attend_kernel,
        "attend",
        [((slots, part_width), BF16), ((requests, width), F32), ((requests, 128), F32)],
        pool_gather(packed) + [own, key_cache, value_cache],
        [pltpu.VMEM((requests, packed_width), F32)],
    )
    (head_part,) = call(
        combine_kernel,
        "combine",
        [((requests, part_cols), BF16)],
        pool_gather(part) + [tables, out_weight],
        [
            pltpu.VMEM((pool * slots, width), F32),
            pltpu.VMEM((pool, slots, 128), F32),
            pltpu.VMEM((requests * width // HD, 128), F32),
        ],
    )
    (head_sum,) = call(
        sum_kernel,
        "head_sum",
        [((requests, part_cols), BF16)],
        [head_part] + [flip(head_part, "mlp", step) for step in (1, 2, 3)],
    )
    pieces = []
    for turn in range(2):
        route = []
        for m in range(mlp):
            by_distance = sorted(range(4), key=lambda z: (-abs(z - m), z))
            for z, step in zip(by_distance, (0, 1, 2, 3)):
                for y in range(2):
                    source = (m * 2 + y) * mlp + (m ^ step)
                    route.append((source, (z * 2 + (y ^ turn)) * mlp + m))
        pieces.append(lax.ppermute(head_sum, ("pool", "mlp"), route))
    sums, own_residual = call(
        gate_up_kernel,
        "gate_up",
        [((requests, 2 * ff + 128), BF16), ((rows, width), F32)],
        pieces + [all_input, norm_gain.reshape(1, width), gate_weight, up_weight],
        [pltpu.VMEM((requests, width), F32)],
    )
    (core_sums,) = call(
        core_sum_kernel,
        "core_sum",
        [((requests, 2 * ff + 128), BF16)],
        [sums, flip(sums, "mlp", 1)],
    )
    send, keep = call(
        functools.partial(down_kernel, width * mlp),
        "down",
        [((requests // 2, width), F32)] * 2,
        [core_sums, flip(core_sums, "mlp", 2), down_weight],
        [pltpu.VMEM((requests, width), F32)],
    )
    chunks = call(
        split_kernel,
        "pair_sum",
        [((rows, width), F32)] * 4,
        [keep, flip(send, "pool", 1)],
        [pltpu.VMEM((requests // 2, width), F32)],
    )
    (out,) = call(
        final_kernel,
        "final",
        [((rows, width), BF16)],
        [own_residual, chunks[0]] + [flip(chunks[s], "pool", 2 * s) for s in (3, 2, 1)],
    )
    return out


def solution(mesh):
    in_specs = (
        P("pool", "mlp"),
        P("pool", "mlp"),
        P("pool", "mlp"),
        P("pool", "mlp"),
        P("pool", None, "mlp"),
        P("pool", None, "mlp"),
        P("pool", None),
        P("pool"),
        P("mlp", "pool"),
        P("mlp"),
        P("mlp", "pool"),
        P("mlp", "pool"),
        P("pool", "mlp"),
    )
    small = mesh.shape["pool"] == 8 and mesh.shape["mlp"] == 4
    per_device = per_device_small if small else per_device_wide
    return jax.shard_map(
        per_device, mesh=mesh, in_specs=in_specs, out_specs=P("pool", "mlp"), check_vma=False
    )
```

```python
import functools
import math

import jax
import jax.numpy as jnp
import numpy as np
from jax import lax
from jax.experimental import pallas as pl
from jax.experimental.pallas import tpu as pltpu
from jax.sharding import PartitionSpec as P

HD = 96
LOW = -1e30
CODE = 128


def rotate(values, positions):
    half_size = values.shape[-1] // 2
    inverse_freq = 10000.0 ** (-(2.0 * jnp.arange(half_size, dtype=jnp.float32)) / values.shape[-1])
    angles = positions.astype(jnp.float32)[:, None, None] * inverse_freq[None, None, :]
    cosine = jnp.cos(angles)
    sine_part = jnp.sin(angles)
    first = values[..., :half_size]
    second = values[..., half_size:]
    return jnp.concatenate(
        [first * cosine - second * sine_part, second * cosine + first * sine_part], -1
    )


def low(values):
    return lax.reduce_precision(values, 8, 7)


def split(values):
    high = low(values)
    return high.astype(jnp.bfloat16), (values - high).astype(jnp.bfloat16)


def encode(ints):
    return (ints // CODE).astype(jnp.bfloat16), (ints % CODE).astype(jnp.bfloat16)


def decode(high, rest):
    return high.astype(jnp.int32) * CODE + rest.astype(jnp.int32)


def gather(values, axis):
    copies = jnp.broadcast_to(values[None], (lax.axis_size(axis),) + values.shape)
    return lax.all_to_all(copies, axis, 0, 0)


def per_device_wide(
    residual_in,
    query_new,
    key_new,
    value_new,
    key_cache,
    value_cache,
    block_table,
    lengths,
    out_weight,
    norm_gain,
    gate_weight,
    up_weight,
    down_weight,
):
    rows, width = residual_in.shape
    heads = width // HD
    blocks, block_len = key_cache.shape[:2]
    most = block_table.shape[1]
    pool, mlp = lax.axis_size("pool"), lax.axis_size("mlp")
    pool_index = lax.axis_index("pool")
    requests = rows * pool
    score_scale = 1.0 / math.sqrt(HD)
    f32, bf16 = jnp.float32, jnp.bfloat16

    queries = rotate(query_new.astype(f32).reshape(rows, heads, HD), lengths).astype(bf16)
    new_keys = rotate(key_new.astype(f32).reshape(rows, heads, HD), lengths).astype(bf16)

    table_high, table_low = encode(block_table + 1)
    len_high, len_low = encode(lengths)
    packed = jnp.concatenate(
        [
            queries.reshape(rows, width),
            residual_in,
            table_high,
            table_low,
            len_high[:, None],
            len_low[:, None],
        ],
        1,
    )
    spare = -packed.shape[1] % 128
    packed = jnp.pad(packed, ((0, 0), (0, spare)))
    got = gather(packed, "pool").reshape(requests, packed.shape[1])
    all_queries = got[:, :width]
    all_input = got[:, width : 2 * width]
    tail = got[:, 2 * width :]
    tables = decode(tail[:, :most], tail[:, most : 2 * most]) - 1
    all_lengths = decode(tail[:, 2 * most], tail[:, 2 * most + 1])

    held_ids = pool_index * blocks + jnp.arange(blocks, dtype=jnp.int32)
    matches = tables[None, :, :] == held_ids[:, None, None]
    holder = jnp.any(matches, 2)
    block_index = jnp.sum(
        jnp.where(matches, jnp.arange(most, dtype=jnp.int32)[None, None, :], 0), (1, 2)
    )
    valid_len = jnp.sum(jnp.where(holder, all_lengths[None, :], 0), 1)
    block_query = jnp.dot(holder.astype(bf16), all_queries, preferred_element_type=f32)
    block_query = block_query.astype(bf16).reshape(blocks, heads, HD)
    key_rows = key_cache.reshape(blocks, block_len, heads, HD)
    value_rows = value_cache.reshape(blocks, block_len, heads, HD)
    scores = (
        jnp.einsum("bhd,bthd->bht", block_query, key_rows, preferred_element_type=f32)
        * score_scale
    )
    token_pos = block_index[:, None] * block_len + jnp.arange(block_len, dtype=jnp.int32)[None, :]
    valid = (token_pos < valid_len[:, None])[:, None, :]
    scores = jnp.where(valid, scores, LOW)
    shift = low(jnp.max(scores, 2))
    weights = jnp.where(valid, jnp.exp(scores - shift[:, :, None]), 0.0)
    totals = jnp.sum(weights, 2)
    numerator = jnp.einsum(
        "bht,bthd->bhd", weights.astype(bf16), value_rows, preferred_element_type=f32
    )
    self_score = jnp.sum(queries.astype(f32) * new_keys.astype(f32), -1) * score_scale
    self_shift = low(self_score)
    self_weight = jnp.exp(self_score - self_shift)
    self_numer = self_weight[:, :, None] * value_new.astype(f32).reshape(rows, heads, HD)

    own_total = jnp.concatenate([totals, self_weight], 0)
    total_high, total_low = split(own_total)
    part = jnp.concatenate(
        [
            jnp.concatenate([numerator, self_numer], 0)
            .astype(bf16)
            .reshape(blocks + rows, width),
            jnp.concatenate([shift, self_shift], 0).astype(bf16),
            total_high,
            total_low,
        ],
        1,
    )
    part = jnp.pad(part, ((0, 0), (0, -part.shape[1] % 128)))
    count = blocks + rows
    parts = gather(part, "pool").reshape(pool * count, part.shape[1])
    all_shift = parts[:, width : width + heads].astype(f32)
    all_total = parts[:, width + heads : width + 2 * heads].astype(f32) + parts[
        :, width + 2 * heads : width + 3 * heads
    ].astype(f32)
    place = jnp.arange(pool * count, dtype=jnp.int32)
    owner, slot = place // count, place % count
    is_block = slot < blocks
    block_id = jnp.where(is_block, owner * blocks + slot, -2)
    self_id = jnp.where(is_block, -2, owner * rows + slot - blocks)
    request_ids = jnp.arange(requests, dtype=jnp.int32)
    belongs = jnp.any(tables[:, None, :] == block_id[None, :, None], 2) | (
        request_ids[:, None] == self_id[None, :]
    )
    top = jnp.max(jnp.where(belongs[:, :, None], all_shift[None], LOW), 1)
    part_top = jnp.sum(jnp.where(belongs[:, :, None], top[:, None, :], 0.0), 0)
    scale = jnp.exp(all_shift - part_top)
    scaled = parts[:, :width].astype(f32).reshape(-1, heads, HD) * scale[:, :, None]
    mix = belongs.astype(f32)
    numer = jnp.dot(mix, scaled.reshape(-1, width), precision=lax.Precision.HIGHEST)
    denom = jnp.dot(mix, all_total * scale, precision=lax.Precision.HIGHEST)
    attended = (numer.reshape(requests, heads, HD) / denom[:, :, None]).astype(bf16)
    attended = attended.reshape(requests, width)

    head_part = jnp.dot(attended, out_weight, preferred_element_type=f32).astype(bf16)
    share = pool // mlp
    route = []
    for p in range(pool):
        for m in range(mlp):
            route.append((p * mlp + m, ((p % share) * mlp + m) * mlp + p // share))
    moved = lax.ppermute(head_part, ("pool", "mlp"), route)
    head_all = gather(moved, "pool").reshape(share, mlp, requests, -1)
    head_out = low(jnp.sum(head_all.astype(f32), 1))
    head_out = jnp.swapaxes(head_out, 0, 1).reshape(requests, width)
    residual = all_input.astype(f32) + head_out
    squares = jnp.sum(residual * residual, -1, keepdims=True)
    portion = (residual * norm_gain.astype(f32)).astype(bf16)

    ff = gate_weight.shape[1]
    square_high, square_low = split(squares)
    sums = jnp.concatenate(
        [
            jnp.dot(portion, gate_weight, preferred_element_type=f32).astype(bf16),
            jnp.dot(portion, up_weight, preferred_element_type=f32).astype(bf16),
            jnp.broadcast_to(square_high, (requests, 64)),
            jnp.broadcast_to(square_low, (requests, 64)),
        ],
        1,
    )
    summed = jnp.sum(gather(sums, "mlp").astype(f32), 0)
    mean_square = (summed[:, 2 * ff : 2 * ff + 1] + summed[:, 2 * ff + 64 : 2 * ff + 65]) / (
        width * mlp
    )
    factor = lax.rsqrt(mean_square + 1e-05)
    gate = summed[:, :ff] * factor
    up = summed[:, ff : 2 * ff] * factor
    hidden = (jax.nn.silu(gate) * up).astype(bf16)

    down = jnp.dot(hidden, down_weight, preferred_element_type=f32)
    down = lax.all_to_all(down.reshape(pool, rows, width), "pool", 0, 0)
    own = lax.dynamic_slice_in_dim(residual, pool_index * rows, rows, 0)
    return (own + jnp.sum(down, 0)).astype(bf16)


F32, BF16 = jnp.float32, jnp.bfloat16
VMEM = pl.BlockSpec(memory_space=pltpu.VMEM)
HBM = pl.BlockSpec(memory_space=pl.ANY)


def call(kernel, name, outs, args, scratch=(), hbm=(), limit=16 * 2**20):
    size = sum(math.prod(a.shape) * a.dtype.itemsize for a in args)
    return pl.pallas_call(
        kernel,
        out_shape=[jax.ShapeDtypeStruct(shape, dtype) for shape, dtype in outs],
        in_specs=[HBM if i in hbm else VMEM for i in range(len(args))],
        out_specs=[VMEM] * len(outs),
        scratch_shapes=list(scratch),
        compiler_params=pltpu.CompilerParams(vmem_limit_bytes=limit),
        cost_estimate=pl.CostEstimate(flops=0, bytes_accessed=size, transcendentals=0),
        name=name,
    )(*args)


def lanes(shape):
    return lax.broadcasted_iota(jnp.int32, shape, len(shape) - 1)


def in_order(pieces, index):
    for bit in (1, 2):
        odd = (index & bit) != 0
        pieces = [jnp.where(odd, pieces[s ^ bit], pieces[s]) for s in range(4)]
    return pieces


def rows_of(shape):
    return lax.broadcasted_iota(jnp.int32, shape, len(shape) - 2)


def round_low(values):
    return values.astype(BF16).astype(F32)


def prepare_kernel(*refs):
    sources, (packed, own), held = refs[:6], refs[8:10], refs[10:16]
    scr, sems = refs[16:]
    copies = [
        pltpu.make_async_copy(source, target, sems.at[i])
        for i, (source, target) in enumerate(zip(sources, held))
    ]
    for copy in copies:
        copy.start()
    for copy in copies:
        copy.wait()
    table, length, query, key, value, residual = held
    rows, width = query.shape
    heads = width // HD
    most = table.shape[1]
    blocks = own.shape[0] - rows - 1
    scr[...] = jnp.zeros_like(scr)
    scr[0:rows, :] = query[...].astype(F32)
    scr[rows : 2 * rows, :] = key[...].astype(F32)
    values = scr[...]
    line = rows_of((8, width))
    where_at = jnp.zeros((8, width), F32)
    for r in range(rows):
        here = (line == r) | (line == rows + r)
        where_at = jnp.where(here, length[r].astype(F32), where_at)
    lane = lanes((8, width))
    turn = lanes((8, 384)) % (HD // 2)
    freq = jnp.zeros((8, 384), F32)
    for i in range(HD // 2):
        freq = jnp.where(turn == i, float(np.float32(10000.0 ** (-2.0 * i / HD))), freq)
    angles = where_at * jnp.concatenate([freq] * (width // 384), 1)
    first = lane % HD < HD // 2
    ahead = pltpu.roll(values, width - HD // 2, 1)
    behind = pltpu.roll(values, HD // 2, 1)
    other = jnp.where(first, -ahead, behind)
    turned = values * jnp.cos(angles) + other * jnp.sin(angles)
    scr[...] = round_low(turned)
    packed[:, :width] = scr[0:rows, :].astype(BF16)
    packed[:, width : 2 * width] = residual[...]
    tail = jnp.zeros((rows, 128), F32)
    at, row = lanes((rows, 128)), rows_of((rows, 128))
    for r in range(rows):
        codes = [table[r, k] + 1 for k in range(most)] + [length[r]]
        spots = [(k, most + k) for k in range(most)] + [(2 * most, 2 * most + 1)]
        for code, (high, rest) in zip(codes, spots):
            tail = jnp.where((row == r) & (at == high), (code >> 7).astype(F32), tail)
            tail = jnp.where((row == r) & (at == rest), (code & 127).astype(F32), tail)
    packed[:, 2 * width :] = tail.astype(BF16)

    head_mask = lane // HD == line
    product = scr[0:rows, :] * scr[rows : 2 * rows, :]
    own[...] = jnp.zeros_like(own)
    spot = lanes((8, 128))
    tail = jnp.zeros((8, 128), F32)
    for r in range(rows):
        score = jnp.sum(
            jnp.where(head_mask, jnp.broadcast_to(product[r : r + 1], (8, width)), 0.0),
            1,
            keepdims=True,
        ) * (1.0 / math.sqrt(HD))
        shift = round_low(score)
        weight = jnp.exp(score - shift)
        spread = jnp.sum(jnp.where(head_mask, round_low(weight), 0.0), 0, keepdims=True)
        own[blocks + r : blocks + r + 1, :width] = spread * value[r : r + 1, :].astype(F32)
        high = round_low(weight)
        tail = jnp.where(spot == blocks + r, shift, tail)
        tail = jnp.where(spot == 8 + blocks + r, high, tail)
        tail = jnp.where(spot == 16 + blocks + r, weight - high, tail)
    own[:, width:] = tail


def merge_kernel(mine, theirs, both):
    y = lax.axis_index("pool") % 2
    both[y] = mine[...]
    both[1 - y] = theirs[...]


def attend_kernel(a0, a1, a2, a3, own, keys, values, part, residual, tables, scr):
    blocks, block_len, width = keys.shape
    rows = a0.shape[1]
    heads = width // HD
    most = 8
    me = lax.axis_index("pool")
    for y in range(2):
        pieces = [piece[y].astype(F32) for piece in (a0, a1, a2, a3)]
        for z, piece in enumerate(in_order(pieces, me // 2)):
            scr[(z * 2 + y) * rows : (z * 2 + y + 1) * rows, :] = piece
    queries = scr[:, :width]
    residual[...] = scr[:, width : 2 * width]
    tail = scr[:, 2 * width :]
    requests = tail.shape[0]
    table = tail * CODE + pltpu.roll(tail, 128 - most, 1) - 1.0
    length = tail[:, 2 * most : 2 * most + 1] * CODE + tail[:, 2 * most + 1 : 2 * most + 2]
    lane = lanes((requests, 128))
    table = jnp.where(lane < most, table, -2.0)
    tables[...] = table
    head_mask = lanes((heads, width)) // HD == rows_of((heads, width))
    spot = lanes((heads, 128))
    tail = own[:, width:]
    part[...] = own[...].astype(BF16)
    scores, limits = [], []
    for b in range(blocks):
        match = jnp.where(table == (me * blocks + b).astype(F32), 1.0, 0.0)
        holder = jnp.sum(match, 1, keepdims=True)
        place = jnp.sum(jnp.sum(match * lane.astype(F32), 1, keepdims=True), 0, keepdims=True)
        limit = jnp.sum(holder * length, 0, keepdims=True) - place * block_len
        limits.append(jnp.broadcast_to(limit, (heads, block_len)))
        query = jnp.sum(holder * queries, 0, keepdims=True)
        spread = jnp.where(head_mask, query, 0.0).astype(BF16)
        scores.append(
            lax.dot_general(
                spread, keys[b], (((1,), (1,)), ((), ())), preferred_element_type=F32
            )
        )
    scores = jnp.concatenate(scores, 0) * (1.0 / math.sqrt(HD))
    token = lanes((blocks * heads, block_len)).astype(F32)
    valid = token < jnp.concatenate(limits, 0)
    scores = jnp.where(valid, scores, LOW)
    shift = round_low(jnp.max(scores, 1, keepdims=True))
    weights = jnp.where(valid, jnp.exp(scores - shift), 0.0)
    total = jnp.sum(weights, 1, keepdims=True)
    high = round_low(total)
    rest = total - high
    numerators = []
    for b in range(blocks):
        mine = slice(b * heads, (b + 1) * heads)
        full = jnp.dot(weights[mine].astype(BF16), values[b], preferred_element_type=F32)
        numerators.append(jnp.sum(jnp.where(head_mask, full, 0.0), 0, keepdims=True))
        tail = jnp.where(spot == b, shift[mine], tail)
        tail = jnp.where(spot == 8 + b, high[mine], tail)
        tail = jnp.where(spot == 16 + b, rest[mine], tail)
    line = rows_of((8, width))
    numer = own[:, :width]
    for b in range(blocks):
        numer = jnp.where(line == b, numerators[b], numer)
    part[:, :width] = numer.astype(BF16)
    part[:, width:] = tail.astype(BF16)


def combine_kernel(b0, b1, b2, b3, tables, weight, head_part, numer, tails, mix):
    requests = tables.shape[0]
    slots = b0.shape[1]
    width = weight.shape[0]
    heads = width // HD
    rows, blocks = 2, slots - 3
    me = lax.axis_index("pool")
    for step, piece in enumerate((b0, b1, b2, b3)):
        z = (me // 2) ^ step
        for y in range(2):
            owner = z * 2 + y
            values = piece[y].astype(F32)
            numer[pl.ds(pl.multiple_of(owner * slots, 8), slots), :] = values[:, :width]
            tails[owner] = values[:, width:]
    lane8 = lanes((heads, 128))
    shifts = jnp.zeros((heads, 128), F32)
    totals = jnp.zeros((heads, 128), F32)
    for owner in range(8):
        tail = tails[owner]
        total = pltpu.roll(tail, 120, 1) + pltpu.roll(tail, 112, 1)
        tail, total = jnp.where(lane8 < 8, tail, 0.0), jnp.where(lane8 < 8, total, 0.0)
        if owner:
            tail, total = pltpu.roll(tail, 8 * owner, 1), pltpu.roll(total, 8 * owner, 1)
        shifts, totals = shifts + tail, totals + total
    lane = lanes((requests, 128))
    owner, slot = lane // slots, lane % slots
    block_id = jnp.where((slot < blocks) & (lane < 64), owner * blocks + slot, -5).astype(F32)
    self_id = jnp.where((slot >= blocks) & (slot < blocks + rows), owner * rows + slot - blocks, -5)
    table = tables[...]
    belongs = (self_id == rows_of((requests, 128))) & (lane < 64)
    for k in range(8):
        belongs = belongs | (table[:, k : k + 1] == block_id)
    for h in range(heads):
        shift = jnp.broadcast_to(shifts[h : h + 1], (requests, 128))
        top = jnp.max(jnp.where(belongs, shift, LOW), 1, keepdims=True)
        scale = jnp.where(belongs, jnp.exp(shift - top), 0.0)
        total = jnp.sum(scale * totals[h : h + 1], 1, keepdims=True)
        mix[h * requests : (h + 1) * requests, :] = scale / total
    full = jnp.dot(
        mix[:, : 8 * slots].astype(BF16), numer[...].astype(BF16), preferred_element_type=F32
    )
    head = lanes((requests, width)) // HD
    attended = jnp.zeros((requests, width), F32)
    for h in range(heads):
        attended = jnp.where(head == h, full[h * requests : (h + 1) * requests], attended)
    head_part[...] = jnp.dot(
        attended.astype(BF16), weight[...], preferred_element_type=F32
    ).astype(BF16)


def sum_kernel(p0, p1, p2, p3, total):
    total[...] = (
        (p0[...].astype(F32) + p1[...].astype(F32)) + (p2[...].astype(F32) + p3[...].astype(F32))
    ).astype(BF16)


def gate_up_kernel(same, flip, all_input, gain, gate, up, sums, own, scr):
    me = lax.axis_index("pool")
    odd = me % 2 == 1
    part = same.shape[1]
    ff = gate.shape[1]
    rows = own.shape[0]
    near, far = same[...].astype(F32), flip[...].astype(F32)
    scr[:, :part] = all_input[:, :part] + jnp.where(odd, far, near)
    scr[:, part:] = all_input[:, part:] + jnp.where(odd, near, far)
    residual = scr[...]
    mine = scr[0:rows, :]
    for p in range(1, residual.shape[0] // rows):
        mine = jnp.where(me == p, scr[p * rows : (p + 1) * rows, :], mine)
    own[...] = mine
    square = jnp.sum(residual * residual, 1, keepdims=True)
    portion = (residual * gain[...].astype(F32)).astype(BF16)
    sums[:, :ff] = jnp.dot(portion, gate[...], preferred_element_type=F32).astype(BF16)
    sums[:, ff : 2 * ff] = jnp.dot(portion, up[...], preferred_element_type=F32).astype(BF16)
    lane = lanes((residual.shape[0], 128))
    high = round_low(square)
    tail = jnp.where(lane == 0, high, jnp.where(lane == 1, square - high, 0.0))
    sums[:, 2 * ff :] = tail.astype(BF16)


def core_sum_kernel(mine, theirs, total):
    ff2 = mine.shape[1] - 128
    total[:, :ff2] = (mine[:, :ff2].astype(F32) + theirs[:, :ff2].astype(F32)).astype(BF16)
    tail = mine[:, ff2:].astype(F32) + theirs[:, ff2:].astype(F32)
    square = jnp.sum(tail, 1, keepdims=True)
    lane = lanes(tail.shape)
    high = round_low(square)
    tail = jnp.where(lane == 0, high, jnp.where(lane == 1, square - high, 0.0))
    total[:, ff2:] = tail.astype(BF16)


def down_kernel(features, mine, theirs, weight, parts, scr):
    ff = weight.shape[0]
    tail = mine[:, 2 * ff :].astype(F32) + theirs[:, 2 * ff :].astype(F32)
    square = jnp.sum(tail, 1, keepdims=True)
    factor = lax.rsqrt(square * (1.0 / features) + 1e-05)
    gate = (mine[:, :ff].astype(F32) + theirs[:, :ff].astype(F32)) * factor
    up = (mine[:, ff : 2 * ff].astype(F32) + theirs[:, ff : 2 * ff].astype(F32)) * factor
    hidden = (gate / (1.0 + jnp.exp(-gate)) * up).astype(BF16)
    scr[...] = jnp.dot(hidden, weight[...], preferred_element_type=F32)
    rows = parts.shape[1]
    for p in range(parts.shape[0]):
        parts[p] = scr[p * rows : (p + 1) * rows, :].astype(BF16)


def final_kernel(own, parts, out):
    total = own[...]
    for p in range(parts.shape[0]):
        total = total + parts[p].astype(F32)
    out[...] = total.astype(BF16)


def flip(values, axis, step):
    size = lax.axis_size(axis)
    return lax.ppermute(values, axis, [(index, index ^ step) for index in range(size)])


def per_device_small(
    residual_in,
    query_new,
    key_new,
    value_new,
    key_cache,
    value_cache,
    block_table,
    lengths,
    out_weight,
    norm_gain,
    gate_weight,
    up_weight,
    down_weight,
):
    rows, width = residual_in.shape
    blocks = key_cache.shape[0]
    pool, mlp = 8, 4
    requests = rows * pool
    ff = gate_weight.shape[1]
    part_cols = out_weight.shape[1]
    packed_width = 2 * width + 128
    slots = blocks + rows + 1
    part_width = width + 128

    packed, own = call(
        prepare_kernel,
        "rotary",
        [((rows, packed_width), BF16), ((slots, part_width), F32)],
        [block_table, lengths, query_new, key_new, value_new, residual_in, key_cache, value_cache],
        [pltpu.SMEM(block_table.shape, jnp.int32), pltpu.SMEM(lengths.shape, jnp.int32)]
        + [pltpu.VMEM((rows, width), BF16)] * 4
        + [pltpu.VMEM((8, width), F32), pltpu.SemaphoreType.DMA((6,))],
        hbm=range(8),
        limit=54 * 2**20,
    )

    def pool_gather(values):
        (both,) = call(
            merge_kernel,
            "merge",
            [((2,) + values.shape, values.dtype)],
            [values, flip(values, "pool", 1)],
        )
        return [both] + [flip(both, "pool", step) for step in (2, 4, 6)]

    part, all_input, tables = call(
        attend_kernel,
        "attend",
        [((slots, part_width), BF16), ((requests, width), F32), ((requests, 128), F32)],
        pool_gather(packed) + [own, key_cache, value_cache],
        [pltpu.VMEM((requests, packed_width), F32)],
    )
    (head_part,) = call(
        combine_kernel,
        "combine",
        [((requests, part_cols), BF16)],
        pool_gather(part) + [tables, out_weight],
        [
            pltpu.VMEM((pool * slots, width), F32),
            pltpu.VMEM((pool, slots, 128), F32),
            pltpu.VMEM((requests * width // HD, 128), F32),
        ],
    )
    (head_sum,) = call(
        sum_kernel,
        "head_sum",
        [((requests, part_cols), BF16)],
        [head_part] + [flip(head_part, "mlp", step) for step in (1, 2, 3)],
    )
    pieces = []
    for turn in range(2):
        route = []
        for m in range(mlp):
            by_distance = sorted(range(4), key=lambda z: (-abs(z - m), z))
            for z, step in zip(by_distance, (0, 1, 2, 3)):
                for y in range(2):
                    source = (m * 2 + y) * mlp + (m ^ step)
                    route.append((source, (z * 2 + (y ^ turn)) * mlp + m))
        pieces.append(lax.ppermute(head_sum, ("pool", "mlp"), route))
    sums, own_residual = call(
        gate_up_kernel,
        "gate_up",
        [((requests, 2 * ff + 128), BF16), ((rows, width), F32)],
        pieces + [all_input, norm_gain.reshape(1, width), gate_weight, up_weight],
        [pltpu.VMEM((requests, width), F32)],
    )
    (core_sums,) = call(
        core_sum_kernel,
        "core_sum",
        [((requests, 2 * ff + 128), BF16)],
        [sums, flip(sums, "mlp", 1)],
    )
    (down,) = call(
        functools.partial(down_kernel, width * mlp),
        "down",
        [((pool, rows, width), BF16)],
        [core_sums, flip(core_sums, "mlp", 2), down_weight],
        [pltpu.VMEM((requests, width), F32)],
    )
    (out,) = call(
        final_kernel,
        "final",
        [((rows, width), BF16)],
        [own_residual, lax.all_to_all(down, "pool", 0, 0)],
    )
    return out


def solution(mesh):
    in_specs = (
        P("pool", "mlp"),
        P("pool", "mlp"),
        P("pool", "mlp"),
        P("pool", "mlp"),
        P("pool", None, "mlp"),
        P("pool", None, "mlp"),
        P("pool", None),
        P("pool"),
        P("mlp", "pool"),
        P("mlp"),
        P("mlp", "pool"),
        P("mlp", "pool"),
        P("pool", "mlp"),
    )
    small = mesh.shape["pool"] == 8 and mesh.shape["mlp"] == 4
    per_device = per_device_small if small else per_device_wide
    return jax.shard_map(
        per_device, mesh=mesh, in_specs=in_specs, out_specs=P("pool", "mlp"), check_vma=False
    )
```

```python
import functools
import math

import jax
import jax.numpy as jnp
import numpy as np
from jax import lax
from jax.experimental import pallas as pl
from jax.experimental.pallas import tpu as pltpu
from jax.sharding import PartitionSpec as P

HD = 96
LOW = -1e30
CODE = 128


def rotate(values, positions):
    half_size = values.shape[-1] // 2
    inverse_freq = 10000.0 ** (-(2.0 * jnp.arange(half_size, dtype=jnp.float32)) / values.shape[-1])
    angles = positions.astype(jnp.float32)[:, None, None] * inverse_freq[None, None, :]
    cosine = jnp.cos(angles)
    sine_part = jnp.sin(angles)
    first = values[..., :half_size]
    second = values[..., half_size:]
    return jnp.concatenate(
        [first * cosine - second * sine_part, second * cosine + first * sine_part], -1
    )


def low(values):
    return lax.reduce_precision(values, 8, 7)


def split(values):
    high = low(values)
    return high.astype(jnp.bfloat16), (values - high).astype(jnp.bfloat16)


def encode(ints):
    return (ints // CODE).astype(jnp.bfloat16), (ints % CODE).astype(jnp.bfloat16)


def decode(high, rest):
    return high.astype(jnp.int32) * CODE + rest.astype(jnp.int32)


def gather(values, axis):
    copies = jnp.broadcast_to(values[None], (lax.axis_size(axis),) + values.shape)
    return lax.all_to_all(copies, axis, 0, 0)


def per_device_wide(
    residual_in,
    query_new,
    key_new,
    value_new,
    key_cache,
    value_cache,
    block_table,
    lengths,
    out_weight,
    norm_gain,
    gate_weight,
    up_weight,
    down_weight,
):
    rows, width = residual_in.shape
    heads = width // HD
    blocks, block_len = key_cache.shape[:2]
    most = block_table.shape[1]
    pool, mlp = lax.axis_size("pool"), lax.axis_size("mlp")
    pool_index = lax.axis_index("pool")
    requests = rows * pool
    score_scale = 1.0 / math.sqrt(HD)
    f32, bf16 = jnp.float32, jnp.bfloat16

    queries = rotate(query_new.astype(f32).reshape(rows, heads, HD), lengths).astype(bf16)
    new_keys = rotate(key_new.astype(f32).reshape(rows, heads, HD), lengths).astype(bf16)

    table_high, table_low = encode(block_table + 1)
    len_high, len_low = encode(lengths)
    packed = jnp.concatenate(
        [
            queries.reshape(rows, width),
            residual_in,
            table_high,
            table_low,
            len_high[:, None],
            len_low[:, None],
        ],
        1,
    )
    spare = -packed.shape[1] % 128
    packed = jnp.pad(packed, ((0, 0), (0, spare)))
    got = gather(packed, "pool").reshape(requests, packed.shape[1])
    all_queries = got[:, :width]
    all_input = got[:, width : 2 * width]
    tail = got[:, 2 * width :]
    tables = decode(tail[:, :most], tail[:, most : 2 * most]) - 1
    all_lengths = decode(tail[:, 2 * most], tail[:, 2 * most + 1])

    held_ids = pool_index * blocks + jnp.arange(blocks, dtype=jnp.int32)
    matches = tables[None, :, :] == held_ids[:, None, None]
    holder = jnp.any(matches, 2)
    block_index = jnp.sum(
        jnp.where(matches, jnp.arange(most, dtype=jnp.int32)[None, None, :], 0), (1, 2)
    )
    valid_len = jnp.sum(jnp.where(holder, all_lengths[None, :], 0), 1)
    block_query = jnp.dot(holder.astype(bf16), all_queries, preferred_element_type=f32)
    block_query = block_query.astype(bf16).reshape(blocks, heads, HD)
    key_rows = key_cache.reshape(blocks, block_len, heads, HD)
    value_rows = value_cache.reshape(blocks, block_len, heads, HD)
    scores = (
        jnp.einsum("bhd,bthd->bht", block_query, key_rows, preferred_element_type=f32)
        * score_scale
    )
    token_pos = block_index[:, None] * block_len + jnp.arange(block_len, dtype=jnp.int32)[None, :]
    valid = (token_pos < valid_len[:, None])[:, None, :]
    scores = jnp.where(valid, scores, LOW)
    shift = low(jnp.max(scores, 2))
    weights = jnp.where(valid, jnp.exp(scores - shift[:, :, None]), 0.0)
    totals = jnp.sum(weights, 2)
    numerator = jnp.einsum(
        "bht,bthd->bhd", weights.astype(bf16), value_rows, preferred_element_type=f32
    )
    self_score = jnp.sum(queries.astype(f32) * new_keys.astype(f32), -1) * score_scale
    self_shift = low(self_score)
    self_weight = jnp.exp(self_score - self_shift)
    self_numer = self_weight[:, :, None] * value_new.astype(f32).reshape(rows, heads, HD)

    own_total = jnp.concatenate([totals, self_weight], 0)
    total_high, total_low = split(own_total)
    part = jnp.concatenate(
        [
            jnp.concatenate([numerator, self_numer], 0)
            .astype(bf16)
            .reshape(blocks + rows, width),
            jnp.concatenate([shift, self_shift], 0).astype(bf16),
            total_high,
            total_low,
        ],
        1,
    )
    part = jnp.pad(part, ((0, 0), (0, -part.shape[1] % 128)))
    count = blocks + rows
    parts = gather(part, "pool").reshape(pool * count, part.shape[1])
    all_shift = parts[:, width : width + heads].astype(f32)
    all_total = parts[:, width + heads : width + 2 * heads].astype(f32) + parts[
        :, width + 2 * heads : width + 3 * heads
    ].astype(f32)
    place = jnp.arange(pool * count, dtype=jnp.int32)
    owner, slot = place // count, place % count
    is_block = slot < blocks
    block_id = jnp.where(is_block, owner * blocks + slot, -2)
    self_id = jnp.where(is_block, -2, owner * rows + slot - blocks)
    request_ids = jnp.arange(requests, dtype=jnp.int32)
    belongs = jnp.any(tables[:, None, :] == block_id[None, :, None], 2) | (
        request_ids[:, None] == self_id[None, :]
    )
    top = jnp.max(jnp.where(belongs[:, :, None], all_shift[None], LOW), 1)
    part_top = jnp.sum(jnp.where(belongs[:, :, None], top[:, None, :], 0.0), 0)
    scale = jnp.exp(all_shift - part_top)
    scaled = parts[:, :width].astype(f32).reshape(-1, heads, HD) * scale[:, :, None]
    mix = belongs.astype(f32)
    numer = jnp.dot(mix, scaled.reshape(-1, width), precision=lax.Precision.HIGHEST)
    denom = jnp.dot(mix, all_total * scale, precision=lax.Precision.HIGHEST)
    attended = (numer.reshape(requests, heads, HD) / denom[:, :, None]).astype(bf16)
    attended = attended.reshape(requests, width)

    head_part = jnp.dot(attended, out_weight, preferred_element_type=f32).astype(bf16)
    share = pool // mlp
    route = []
    for p in range(pool):
        for m in range(mlp):
            route.append((p * mlp + m, ((p % share) * mlp + m) * mlp + p // share))
    moved = lax.ppermute(head_part, ("pool", "mlp"), route)
    head_all = gather(moved, "pool").reshape(share, mlp, requests, -1)
    head_out = low(jnp.sum(head_all.astype(f32), 1))
    head_out = jnp.swapaxes(head_out, 0, 1).reshape(requests, width)
    residual = all_input.astype(f32) + head_out
    squares = jnp.sum(residual * residual, -1, keepdims=True)
    portion = (residual * norm_gain.astype(f32)).astype(bf16)

    ff = gate_weight.shape[1]
    square_high, square_low = split(squares)
    sums = jnp.concatenate(
        [
            jnp.dot(portion, gate_weight, preferred_element_type=f32).astype(bf16),
            jnp.dot(portion, up_weight, preferred_element_type=f32).astype(bf16),
            jnp.broadcast_to(square_high, (requests, 64)),
            jnp.broadcast_to(square_low, (requests, 64)),
        ],
        1,
    )
    summed = jnp.sum(gather(sums, "mlp").astype(f32), 0)
    mean_square = (summed[:, 2 * ff : 2 * ff + 1] + summed[:, 2 * ff + 64 : 2 * ff + 65]) / (
        width * mlp
    )
    factor = lax.rsqrt(mean_square + 1e-05)
    gate = summed[:, :ff] * factor
    up = summed[:, ff : 2 * ff] * factor
    hidden = (jax.nn.silu(gate) * up).astype(bf16)

    down = jnp.dot(hidden, down_weight, preferred_element_type=f32)
    down = lax.all_to_all(down.reshape(pool, rows, width), "pool", 0, 0)
    own = lax.dynamic_slice_in_dim(residual, pool_index * rows, rows, 0)
    return (own + jnp.sum(down, 0)).astype(bf16)


F32, BF16 = jnp.float32, jnp.bfloat16
VMEM = pl.BlockSpec(memory_space=pltpu.VMEM)
HBM = pl.BlockSpec(memory_space=pl.ANY)


def call(kernel, name, outs, args, scratch=(), hbm=(), limit=16 * 2**20):
    size = sum(math.prod(a.shape) * a.dtype.itemsize for a in args)
    return pl.pallas_call(
        kernel,
        out_shape=[jax.ShapeDtypeStruct(shape, dtype) for shape, dtype in outs],
        in_specs=[HBM if i in hbm else VMEM for i in range(len(args))],
        out_specs=[VMEM] * len(outs),
        scratch_shapes=list(scratch),
        compiler_params=pltpu.CompilerParams(vmem_limit_bytes=limit),
        cost_estimate=pl.CostEstimate(flops=0, bytes_accessed=size, transcendentals=0),
        name=name,
    )(*args)


def lanes(shape):
    return lax.broadcasted_iota(jnp.int32, shape, len(shape) - 1)


def in_order(pieces, index):
    for bit in (1, 2):
        odd = (index & bit) != 0
        pieces = [jnp.where(odd, pieces[s ^ bit], pieces[s]) for s in range(4)]
    return pieces


def rows_of(shape):
    return lax.broadcasted_iota(jnp.int32, shape, len(shape) - 2)


def round_low(values):
    return values.astype(BF16).astype(F32)


def head_start(shape):
    return rows_of(shape) * HD % 128


def flatten(tail, width):
    heads = tail.shape[0]
    spread = jnp.zeros((heads, width), F32)
    start = head_start((heads, width))
    for k in (0, 32, 64, 96):
        moved = pltpu.roll(tail, k, 1) if k else tail
        spread = jnp.where(start == k, jnp.concatenate([moved] * (width // 128), 1), spread)
    lane = lanes((heads, width))
    used = (lane // HD == rows_of((heads, width))) & (lane % HD < 24)
    return jnp.sum(jnp.where(used, spread, 0.0), 0, keepdims=True)


def unflatten(row, heads):
    width = row.shape[1]
    lane = lanes((heads, width))
    used = (lane // HD == rows_of((heads, width))) & (lane % HD < 24)
    spread = jnp.where(used, jnp.broadcast_to(row, (heads, width)), 0.0)
    folded = spread[:, :128]
    for at in range(128, width, 128):
        folded = folded + spread[:, at : at + 128]
    start = head_start((heads, 128))
    tail = jnp.where(start == 0, folded, 0.0)
    for k in (32, 64, 96):
        tail = jnp.where(start == k, pltpu.roll(folded, 128 - k, 1), tail)
    return tail


def prepare_kernel(*refs):
    sources, (packed, own), held = refs[:6], refs[8:10], refs[10:16]
    scr, sems = refs[16:]
    copies = [
        pltpu.make_async_copy(source, target, sems.at[i])
        for i, (source, target) in enumerate(zip(sources, held))
    ]
    for copy in copies:
        copy.start()
    for copy in copies:
        copy.wait()
    table, length, query, key, value, residual = held
    rows, width = query.shape
    heads = width // HD
    most = table.shape[1]
    blocks = own.shape[0] - rows - 1
    scr[...] = jnp.zeros_like(scr)
    scr[0:rows, :] = query[...].astype(F32)
    scr[rows : 2 * rows, :] = key[...].astype(F32)
    values = scr[...]
    line = rows_of((8, width))
    where_at = jnp.zeros((8, width), F32)
    for r in range(rows):
        here = (line == r) | (line == rows + r)
        where_at = jnp.where(here, length[r].astype(F32), where_at)
    lane = lanes((8, width))
    turn = lanes((8, 384)) % (HD // 2)
    freq = jnp.zeros((8, 384), F32)
    for i in range(HD // 2):
        freq = jnp.where(turn == i, float(np.float32(10000.0 ** (-2.0 * i / HD))), freq)
    angles = where_at * jnp.concatenate([freq] * (width // 384), 1)
    first = lane % HD < HD // 2
    ahead = pltpu.roll(values, width - HD // 2, 1)
    behind = pltpu.roll(values, HD // 2, 1)
    other = jnp.where(first, -ahead, behind)
    turned = values * jnp.cos(angles) + other * jnp.sin(angles)
    scr[...] = round_low(turned)
    packed[:, :width] = scr[0:rows, :].astype(BF16)
    packed[:, width : 2 * width] = residual[...]
    tail = jnp.zeros((rows, 128), F32)
    at, row = lanes((rows, 128)), rows_of((rows, 128))
    for r in range(rows):
        codes = [table[r, k] + 1 for k in range(most)] + [length[r]]
        spots = [(k, most + k) for k in range(most)] + [(2 * most, 2 * most + 1)]
        for code, (high, rest) in zip(codes, spots):
            tail = jnp.where((row == r) & (at == high), (code >> 7).astype(F32), tail)
            tail = jnp.where((row == r) & (at == rest), (code & 127).astype(F32), tail)
    packed[:, 2 * width :] = tail.astype(BF16)

    head_mask = lane // HD == line
    product = scr[0:rows, :] * scr[rows : 2 * rows, :]
    own[...] = jnp.zeros_like(own)
    spot = lanes((8, 128))
    tail = jnp.zeros((8, 128), F32)
    for r in range(rows):
        score = jnp.sum(
            jnp.where(head_mask, jnp.broadcast_to(product[r : r + 1], (8, width)), 0.0),
            1,
            keepdims=True,
        ) * (1.0 / math.sqrt(HD))
        shift = round_low(score)
        weight = jnp.exp(score - shift)
        spread = jnp.sum(jnp.where(head_mask, round_low(weight), 0.0), 0, keepdims=True)
        own[blocks + r : blocks + r + 1, :width] = spread * value[r : r + 1, :].astype(F32)
        high = round_low(weight)
        tail = jnp.where(spot == blocks + r, shift, tail)
        tail = jnp.where(spot == 8 + blocks + r, high, tail)
        tail = jnp.where(spot == 16 + blocks + r, weight - high, tail)
    own[:, width:] = tail


def carry_kernel(packed, own, packed_near, own_near):
    packed_near[...] = packed[...]
    own_near[...] = own[...]


def merge_kernel(mine, theirs, both):
    y = lax.axis_index("pool") % 2
    both[y] = mine[...]
    both[1 - y] = theirs[...]


def attend_kernel(a0, a1, a2, a3, own, keys, values, part, residual, tables, scr):
    blocks, block_len, width = keys.shape
    rows = a0.shape[1]
    heads = width // HD
    most = 8
    me = lax.axis_index("pool")
    for y in range(2):
        pieces = [piece[y].astype(F32) for piece in (a0, a1, a2, a3)]
        for z, piece in enumerate(in_order(pieces, me // 2)):
            scr[(z * 2 + y) * rows : (z * 2 + y + 1) * rows, :] = piece
    queries = scr[:, :width]
    residual[...] = scr[:, width : 2 * width]
    tail = scr[:, 2 * width :]
    requests = tail.shape[0]
    table = tail * CODE + pltpu.roll(tail, 128 - most, 1) - 1.0
    length = tail[:, 2 * most : 2 * most + 1] * CODE + tail[:, 2 * most + 1 : 2 * most + 2]
    lane = lanes((requests, 128))
    table = jnp.where(lane < most, table, -2.0)
    tables[...] = table
    head_mask = lanes((heads, width)) // HD == rows_of((heads, width))
    spot = lanes((heads, 128))
    tail = own[:, width:]
    scores, limits = [], []
    for b in range(blocks):
        match = jnp.where(table == (me * blocks + b).astype(F32), 1.0, 0.0)
        holder = jnp.sum(match, 1, keepdims=True)
        place = jnp.sum(jnp.sum(match * lane.astype(F32), 1, keepdims=True), 0, keepdims=True)
        limit = jnp.sum(holder * length, 0, keepdims=True) - place * block_len
        limits.append(jnp.broadcast_to(limit, (heads, block_len)))
        query = jnp.sum(holder * queries, 0, keepdims=True)
        spread = jnp.where(head_mask, query, 0.0).astype(BF16)
        scores.append(
            lax.dot_general(
                spread, keys[b], (((1,), (1,)), ((), ())), preferred_element_type=F32
            )
        )
    scores = jnp.concatenate(scores, 0) * (1.0 / math.sqrt(HD))
    token = lanes((blocks * heads, block_len)).astype(F32)
    valid = token < jnp.concatenate(limits, 0)
    scores = jnp.where(valid, scores, LOW)
    shift = round_low(jnp.max(scores, 1, keepdims=True))
    weights = jnp.where(valid, jnp.exp(scores - shift), 0.0)
    total = jnp.sum(weights, 1, keepdims=True)
    high = round_low(total)
    rest = total - high
    numerators = []
    for b in range(blocks):
        mine = slice(b * heads, (b + 1) * heads)
        full = jnp.dot(weights[mine].astype(BF16), values[b], preferred_element_type=F32)
        numerators.append(jnp.sum(jnp.where(head_mask, full, 0.0), 0, keepdims=True))
        tail = jnp.where(spot == b, shift[mine], tail)
        tail = jnp.where(spot == 8 + b, high[mine], tail)
        tail = jnp.where(spot == 16 + b, rest[mine], tail)
    line = rows_of((8, width))
    numer = own[:, :width]
    for b in range(blocks):
        numer = jnp.where(line == b, numerators[b], numer)
    numer = jnp.where(line == 7, flatten(tail, width), numer)
    part[...] = numer.astype(BF16)


def combine_kernel(b0, b1, b2, b3, tables, weight, head_part, numer, tails, mix):
    requests = tables.shape[0]
    slots = b0.shape[1]
    width = weight.shape[0]
    heads = width // HD
    rows, blocks = 2, slots - 3
    me = lax.axis_index("pool")
    for step, piece in enumerate((b0, b1, b2, b3)):
        z = (me // 2) ^ step
        for y in range(2):
            owner = z * 2 + y
            values = piece[y].astype(F32)
            numer[pl.ds(pl.multiple_of(owner * slots, 8), slots), :] = values
            tails[owner] = unflatten(values[slots - 1 : slots], heads)
    lane8 = lanes((heads, 128))
    shifts = jnp.zeros((heads, 128), F32)
    totals = jnp.zeros((heads, 128), F32)
    for owner in range(8):
        tail = tails[owner]
        total = pltpu.roll(tail, 120, 1) + pltpu.roll(tail, 112, 1)
        tail, total = jnp.where(lane8 < 8, tail, 0.0), jnp.where(lane8 < 8, total, 0.0)
        if owner:
            tail, total = pltpu.roll(tail, 8 * owner, 1), pltpu.roll(total, 8 * owner, 1)
        shifts, totals = shifts + tail, totals + total
    lane = lanes((requests, 128))
    owner, slot = lane // slots, lane % slots
    block_id = jnp.where((slot < blocks) & (lane < 64), owner * blocks + slot, -5).astype(F32)
    self_id = jnp.where((slot >= blocks) & (slot < blocks + rows), owner * rows + slot - blocks, -5)
    table = tables[...]
    belongs = (self_id == rows_of((requests, 128))) & (lane < 64)
    for k in range(8):
        belongs = belongs | (table[:, k : k + 1] == block_id)
    for h in range(heads):
        shift = jnp.broadcast_to(shifts[h : h + 1], (requests, 128))
        top = jnp.max(jnp.where(belongs, shift, LOW), 1, keepdims=True)
        scale = jnp.where(belongs, jnp.exp(shift - top), 0.0)
        total = jnp.sum(scale * totals[h : h + 1], 1, keepdims=True)
        mix[h * requests : (h + 1) * requests, :] = scale / total
    full = jnp.dot(
        mix[:, : 8 * slots].astype(BF16), numer[...].astype(BF16), preferred_element_type=F32
    )
    head = lanes((requests, width)) // HD
    attended = jnp.zeros((requests, width), F32)
    for h in range(heads):
        attended = jnp.where(head == h, full[h * requests : (h + 1) * requests], attended)
    head_part[...] = jnp.dot(
        attended.astype(BF16), weight[...], preferred_element_type=F32
    ).astype(BF16)


def sum_kernel(p0, p1, p2, p3, total):
    total[...] = (
        (p0[...].astype(F32) + p1[...].astype(F32)) + (p2[...].astype(F32) + p3[...].astype(F32))
    ).astype(BF16)


def gate_up_kernel(same, flip, all_input, gain, gate, up, sums, own, scr):
    me = lax.axis_index("pool")
    odd = me % 2 == 1
    part = same.shape[1]
    ff = gate.shape[1]
    rows = own.shape[0]
    near, far = same[...].astype(F32), flip[...].astype(F32)
    scr[:, :part] = all_input[:, :part] + jnp.where(odd, far, near)
    scr[:, part:] = all_input[:, part:] + jnp.where(odd, near, far)
    residual = scr[...]
    mine = scr[0:rows, :]
    for p in range(1, residual.shape[0] // rows):
        mine = jnp.where(me == p, scr[p * rows : (p + 1) * rows, :], mine)
    own[...] = mine
    square = jnp.sum(residual * residual, 1, keepdims=True)
    portion = (residual * gain[...].astype(F32)).astype(BF16)
    sums[:, :ff] = jnp.dot(portion, gate[...], preferred_element_type=F32).astype(BF16)
    sums[:, ff : 2 * ff] = jnp.dot(portion, up[...], preferred_element_type=F32).astype(BF16)
    lane = lanes((residual.shape[0], 128))
    high = round_low(square)
    tail = jnp.where(lane == 0, high, jnp.where(lane == 1, square - high, 0.0))
    sums[:, 2 * ff :] = tail.astype(BF16)


def core_sum_kernel(mine, theirs, total):
    ff2 = mine.shape[1] - 128
    total[:, :ff2] = (mine[:, :ff2].astype(F32) + theirs[:, :ff2].astype(F32)).astype(BF16)
    tail = mine[:, ff2:].astype(F32) + theirs[:, ff2:].astype(F32)
    square = jnp.sum(tail, 1, keepdims=True)
    lane = lanes(tail.shape)
    high = round_low(square)
    tail = jnp.where(lane == 0, high, jnp.where(lane == 1, square - high, 0.0))
    total[:, ff2:] = tail.astype(BF16)


def down_kernel(features, mine, theirs, weight, parts, scr):
    ff = weight.shape[0]
    tail = mine[:, 2 * ff :].astype(F32) + theirs[:, 2 * ff :].astype(F32)
    square = jnp.sum(tail, 1, keepdims=True)
    factor = lax.rsqrt(square * (1.0 / features) + 1e-05)
    gate = (mine[:, :ff].astype(F32) + theirs[:, :ff].astype(F32)) * factor
    up = (mine[:, ff : 2 * ff].astype(F32) + theirs[:, ff : 2 * ff].astype(F32)) * factor
    hidden = (gate / (1.0 + jnp.exp(-gate)) * up).astype(BF16)
    scr[...] = jnp.dot(hidden, weight[...], preferred_element_type=F32)
    rows = parts.shape[1]
    for p in range(parts.shape[0]):
        parts[p] = scr[p * rows : (p + 1) * rows, :].astype(BF16)


def final_kernel(own, parts, out):
    total = own[...]
    for p in range(parts.shape[0]):
        total = total + parts[p].astype(F32)
    out[...] = total.astype(BF16)


def flip(values, axis, step):
    size = lax.axis_size(axis)
    return lax.ppermute(values, axis, [(index, index ^ step) for index in range(size)])


def per_device_small(
    residual_in,
    query_new,
    key_new,
    value_new,
    key_cache,
    value_cache,
    block_table,
    lengths,
    out_weight,
    norm_gain,
    gate_weight,
    up_weight,
    down_weight,
):
    rows, width = residual_in.shape
    blocks = key_cache.shape[0]
    pool, mlp = 8, 4
    requests = rows * pool
    ff = gate_weight.shape[1]
    part_cols = out_weight.shape[1]
    packed_width = 2 * width + 128
    slots = blocks + rows + 1
    part_width = width + 128

    packed, own = call(
        prepare_kernel,
        "rotary",
        [((rows, packed_width), BF16), ((slots, part_width), F32)],
        [block_table, lengths, query_new, key_new, value_new, residual_in, key_cache, value_cache],
        [pltpu.SMEM(block_table.shape, jnp.int32), pltpu.SMEM(lengths.shape, jnp.int32)]
        + [pltpu.VMEM((rows, width), BF16)] * 4
        + [pltpu.VMEM((8, width), F32), pltpu.SemaphoreType.DMA((6,))],
        hbm=range(8),
        limit=54 * 2**20,
    )

    packed_near, own = call(
        carry_kernel,
        "carry",
        [(packed.shape, BF16), (own.shape, F32)],
        [packed, own],
    )

    def pool_gather(values, near):
        (both,) = call(
            merge_kernel,
            "merge",
            [((2,) + values.shape, values.dtype)],
            [near, flip(values, "pool", 1)],
        )
        return [both] + [flip(both, "pool", step) for step in (2, 4, 6)]

    part, all_input, tables = call(
        attend_kernel,
        "attend",
        [((slots, width), BF16), ((requests, width), F32), ((requests, 128), F32)],
        pool_gather(packed, packed_near) + [own, key_cache, value_cache],
        [pltpu.VMEM((requests, packed_width), F32)],
    )
    (head_part,) = call(
        combine_kernel,
        "combine",
        [((requests, part_cols), BF16)],
        pool_gather(part, part) + [tables, out_weight],
        [
            pltpu.VMEM((pool * slots, width), F32),
            pltpu.VMEM((pool, slots, 128), F32),
            pltpu.VMEM((requests * width // HD, 128), F32),
        ],
    )
    (head_sum,) = call(
        sum_kernel,
        "head_sum",
        [((requests, part_cols), BF16)],
        [head_part] + [flip(head_part, "mlp", step) for step in (1, 2, 3)],
    )
    pieces = []
    for turn in range(2):
        route = []
        for m in range(mlp):
            by_distance = sorted(range(4), key=lambda z: (-abs(z - m), z))
            for z, step in zip(by_distance, (0, 1, 2, 3)):
                for y in range(2):
                    source = (m * 2 + y) * mlp + (m ^ step)
                    route.append((source, (z * 2 + (y ^ turn)) * mlp + m))
        pieces.append(lax.ppermute(head_sum, ("pool", "mlp"), route))
    sums, own_residual = call(
        gate_up_kernel,
        "gate_up",
        [((requests, 2 * ff + 128), BF16), ((rows, width), F32)],
        pieces + [all_input, norm_gain.reshape(1, width), gate_weight, up_weight],
        [pltpu.VMEM((requests, width), F32)],
    )
    (core_sums,) = call(
        core_sum_kernel,
        "core_sum",
        [((requests, 2 * ff + 128), BF16)],
        [sums, flip(sums, "mlp", 1)],
    )
    (down,) = call(
        functools.partial(down_kernel, width * mlp),
        "down",
        [((pool, rows, width), BF16)],
        [core_sums, flip(core_sums, "mlp", 2), down_weight],
        [pltpu.VMEM((requests, width), F32)],
    )
    (out,) = call(
        final_kernel,
        "final",
        [((rows, width), BF16)],
        [own_residual, lax.all_to_all(down, "pool", 0, 0)],
    )
    return out


def solution(mesh):
    in_specs = (
        P("pool", "mlp"),
        P("pool", "mlp"),
        P("pool", "mlp"),
        P("pool", "mlp"),
        P("pool", None, "mlp"),
        P("pool", None, "mlp"),
        P("pool", None),
        P("pool"),
        P("mlp", "pool"),
        P("mlp"),
        P("mlp", "pool"),
        P("mlp", "pool"),
        P("pool", "mlp"),
    )
    small = mesh.shape["pool"] == 8 and mesh.shape["mlp"] == 4
    per_device = per_device_small if small else per_device_wide
    return jax.shard_map(
        per_device, mesh=mesh, in_specs=in_specs, out_specs=P("pool", "mlp"), check_vma=False
    )
```

```python
import functools
import math

import jax
import jax.numpy as jnp
import numpy as np
from jax import lax
from jax.experimental import pallas as pl
from jax.experimental.pallas import tpu as pltpu
from jax.sharding import PartitionSpec as P

HD = 96
LOW = -1e30
CODE = 128


def rotate(values, positions):
    half_size = values.shape[-1] // 2
    inverse_freq = 10000.0 ** (-(2.0 * jnp.arange(half_size, dtype=jnp.float32)) / values.shape[-1])
    angles = positions.astype(jnp.float32)[:, None, None] * inverse_freq[None, None, :]
    cosine = jnp.cos(angles)
    sine_part = jnp.sin(angles)
    first = values[..., :half_size]
    second = values[..., half_size:]
    return jnp.concatenate(
        [first * cosine - second * sine_part, second * cosine + first * sine_part], -1
    )


def low(values):
    return lax.reduce_precision(values, 8, 7)


def split(values):
    high = low(values)
    return high.astype(jnp.bfloat16), (values - high).astype(jnp.bfloat16)


def encode(ints):
    return (ints // CODE).astype(jnp.bfloat16), (ints % CODE).astype(jnp.bfloat16)


def decode(high, rest):
    return high.astype(jnp.int32) * CODE + rest.astype(jnp.int32)


def gather(values, axis):
    copies = jnp.broadcast_to(values[None], (lax.axis_size(axis),) + values.shape)
    return lax.all_to_all(copies, axis, 0, 0)


def per_device_wide(
    residual_in,
    query_new,
    key_new,
    value_new,
    key_cache,
    value_cache,
    block_table,
    lengths,
    out_weight,
    norm_gain,
    gate_weight,
    up_weight,
    down_weight,
):
    rows, width = residual_in.shape
    heads = width // HD
    blocks, block_len = key_cache.shape[:2]
    most = block_table.shape[1]
    pool, mlp = lax.axis_size("pool"), lax.axis_size("mlp")
    pool_index = lax.axis_index("pool")
    requests = rows * pool
    score_scale = 1.0 / math.sqrt(HD)
    f32, bf16 = jnp.float32, jnp.bfloat16

    queries = rotate(query_new.astype(f32).reshape(rows, heads, HD), lengths).astype(bf16)
    new_keys = rotate(key_new.astype(f32).reshape(rows, heads, HD), lengths).astype(bf16)

    table_high, table_low = encode(block_table + 1)
    len_high, len_low = encode(lengths)
    packed = jnp.concatenate(
        [
            queries.reshape(rows, width),
            residual_in,
            table_high,
            table_low,
            len_high[:, None],
            len_low[:, None],
        ],
        1,
    )
    spare = -packed.shape[1] % 128
    packed = jnp.pad(packed, ((0, 0), (0, spare)))
    got = gather(packed, "pool").reshape(requests, packed.shape[1])
    all_queries = got[:, :width]
    all_input = got[:, width : 2 * width]
    tail = got[:, 2 * width :]
    tables = decode(tail[:, :most], tail[:, most : 2 * most]) - 1
    all_lengths = decode(tail[:, 2 * most], tail[:, 2 * most + 1])

    held_ids = pool_index * blocks + jnp.arange(blocks, dtype=jnp.int32)
    matches = tables[None, :, :] == held_ids[:, None, None]
    holder = jnp.any(matches, 2)
    block_index = jnp.sum(
        jnp.where(matches, jnp.arange(most, dtype=jnp.int32)[None, None, :], 0), (1, 2)
    )
    valid_len = jnp.sum(jnp.where(holder, all_lengths[None, :], 0), 1)
    block_query = jnp.dot(holder.astype(bf16), all_queries, preferred_element_type=f32)
    block_query = block_query.astype(bf16).reshape(blocks, heads, HD)
    key_rows = key_cache.reshape(blocks, block_len, heads, HD)
    value_rows = value_cache.reshape(blocks, block_len, heads, HD)
    scores = (
        jnp.einsum("bhd,bthd->bht", block_query, key_rows, preferred_element_type=f32)
        * score_scale
    )
    token_pos = block_index[:, None] * block_len + jnp.arange(block_len, dtype=jnp.int32)[None, :]
    valid = (token_pos < valid_len[:, None])[:, None, :]
    scores = jnp.where(valid, scores, LOW)
    shift = low(jnp.max(scores, 2))
    weights = jnp.where(valid, jnp.exp(scores - shift[:, :, None]), 0.0)
    totals = jnp.sum(weights, 2)
    numerator = jnp.einsum(
        "bht,bthd->bhd", weights.astype(bf16), value_rows, preferred_element_type=f32
    )
    self_score = jnp.sum(queries.astype(f32) * new_keys.astype(f32), -1) * score_scale
    self_shift = low(self_score)
    self_weight = jnp.exp(self_score - self_shift)
    self_numer = self_weight[:, :, None] * value_new.astype(f32).reshape(rows, heads, HD)

    own_total = jnp.concatenate([totals, self_weight], 0)
    total_high, total_low = split(own_total)
    part = jnp.concatenate(
        [
            jnp.concatenate([numerator, self_numer], 0)
            .astype(bf16)
            .reshape(blocks + rows, width),
            jnp.concatenate([shift, self_shift], 0).astype(bf16),
            total_high,
            total_low,
        ],
        1,
    )
    part = jnp.pad(part, ((0, 0), (0, -part.shape[1] % 128)))
    count = blocks + rows
    parts = gather(part, "pool").reshape(pool * count, part.shape[1])
    all_shift = parts[:, width : width + heads].astype(f32)
    all_total = parts[:, width + heads : width + 2 * heads].astype(f32) + parts[
        :, width + 2 * heads : width + 3 * heads
    ].astype(f32)
    place = jnp.arange(pool * count, dtype=jnp.int32)
    owner, slot = place // count, place % count
    is_block = slot < blocks
    block_id = jnp.where(is_block, owner * blocks + slot, -2)
    self_id = jnp.where(is_block, -2, owner * rows + slot - blocks)
    request_ids = jnp.arange(requests, dtype=jnp.int32)
    belongs = jnp.any(tables[:, None, :] == block_id[None, :, None], 2) | (
        request_ids[:, None] == self_id[None, :]
    )
    top = jnp.max(jnp.where(belongs[:, :, None], all_shift[None], LOW), 1)
    part_top = jnp.sum(jnp.where(belongs[:, :, None], top[:, None, :], 0.0), 0)
    scale = jnp.exp(all_shift - part_top)
    scaled = parts[:, :width].astype(f32).reshape(-1, heads, HD) * scale[:, :, None]
    mix = belongs.astype(f32)
    numer = jnp.dot(mix, scaled.reshape(-1, width), precision=lax.Precision.HIGHEST)
    denom = jnp.dot(mix, all_total * scale, precision=lax.Precision.HIGHEST)
    attended = (numer.reshape(requests, heads, HD) / denom[:, :, None]).astype(bf16)
    attended = attended.reshape(requests, width)

    head_part = jnp.dot(attended, out_weight, preferred_element_type=f32).astype(bf16)
    share = pool // mlp
    route = []
    for p in range(pool):
        for m in range(mlp):
            route.append((p * mlp + m, ((p % share) * mlp + m) * mlp + p // share))
    moved = lax.ppermute(head_part, ("pool", "mlp"), route)
    head_all = gather(moved, "pool").reshape(share, mlp, requests, -1)
    head_out = low(jnp.sum(head_all.astype(f32), 1))
    head_out = jnp.swapaxes(head_out, 0, 1).reshape(requests, width)
    residual = all_input.astype(f32) + head_out
    squares = jnp.sum(residual * residual, -1, keepdims=True)
    portion = (residual * norm_gain.astype(f32)).astype(bf16)

    ff = gate_weight.shape[1]
    square_high, square_low = split(squares)
    sums = jnp.concatenate(
        [
            jnp.dot(portion, gate_weight, preferred_element_type=f32).astype(bf16),
            jnp.dot(portion, up_weight, preferred_element_type=f32).astype(bf16),
            jnp.broadcast_to(square_high, (requests, 64)),
            jnp.broadcast_to(square_low, (requests, 64)),
        ],
        1,
    )
    summed = jnp.sum(gather(sums, "mlp").astype(f32), 0)
    mean_square = (summed[:, 2 * ff : 2 * ff + 1] + summed[:, 2 * ff + 64 : 2 * ff + 65]) / (
        width * mlp
    )
    factor = lax.rsqrt(mean_square + 1e-05)
    gate = summed[:, :ff] * factor
    up = summed[:, ff : 2 * ff] * factor
    hidden = (jax.nn.silu(gate) * up).astype(bf16)

    down = jnp.dot(hidden, down_weight, preferred_element_type=f32)
    down = lax.all_to_all(down.reshape(pool, rows, width), "pool", 0, 0)
    own = lax.dynamic_slice_in_dim(residual, pool_index * rows, rows, 0)
    return (own + jnp.sum(down, 0)).astype(bf16)


F32, BF16 = jnp.float32, jnp.bfloat16
VMEM = pl.BlockSpec(memory_space=pltpu.VMEM)
HBM = pl.BlockSpec(memory_space=pl.ANY)


def call(kernel, name, outs, args, scratch=(), hbm=(), limit=16 * 2**20):
    size = sum(math.prod(a.shape) * a.dtype.itemsize for a in args)
    return pl.pallas_call(
        kernel,
        out_shape=[jax.ShapeDtypeStruct(shape, dtype) for shape, dtype in outs],
        in_specs=[HBM if i in hbm else VMEM for i in range(len(args))],
        out_specs=[VMEM] * len(outs),
        scratch_shapes=list(scratch),
        compiler_params=pltpu.CompilerParams(vmem_limit_bytes=limit),
        cost_estimate=pl.CostEstimate(flops=0, bytes_accessed=size, transcendentals=0),
        name=name,
    )(*args)


def lanes(shape):
    return lax.broadcasted_iota(jnp.int32, shape, len(shape) - 1)


def in_order(pieces, index):
    for bit in (1, 2):
        odd = (index & bit) != 0
        pieces = [jnp.where(odd, pieces[s ^ bit], pieces[s]) for s in range(4)]
    return pieces


def rows_of(shape):
    return lax.broadcasted_iota(jnp.int32, shape, len(shape) - 2)


def round_low(values):
    return values.astype(BF16).astype(F32)


def head_start(shape):
    return rows_of(shape) * HD % 128


def flatten(tail, width):
    heads = tail.shape[0]
    spread = jnp.zeros((heads, width), F32)
    start = head_start((heads, width))
    for k in (0, 32, 64, 96):
        moved = pltpu.roll(tail, k, 1) if k else tail
        spread = jnp.where(start == k, jnp.concatenate([moved] * (width // 128), 1), spread)
    lane = lanes((heads, width))
    used = (lane // HD == rows_of((heads, width))) & (lane % HD < 24)
    return jnp.sum(jnp.where(used, spread, 0.0), 0, keepdims=True)


def unflatten(row, heads):
    width = row.shape[1]
    lane = lanes((heads, width))
    used = (lane // HD == rows_of((heads, width))) & (lane % HD < 24)
    spread = jnp.where(used, jnp.broadcast_to(row, (heads, width)), 0.0)
    folded = spread[:, :128]
    for at in range(128, width, 128):
        folded = folded + spread[:, at : at + 128]
    start = head_start((heads, 128))
    tail = jnp.where(start == 0, folded, 0.0)
    for k in (32, 64, 96):
        tail = jnp.where(start == k, pltpu.roll(folded, 128 - k, 1), tail)
    return tail


def prepare_kernel(*refs):
    sources, (packed, own), held = refs[:6], refs[8:10], refs[10:16]
    scr, sems = refs[16:]
    copies = [
        pltpu.make_async_copy(source, target, sems.at[i])
        for i, (source, target) in enumerate(zip(sources, held))
    ]
    for copy in copies:
        copy.start()
    for copy in copies:
        copy.wait()
    table, length, query, key, value, residual = held
    rows, width = query.shape
    heads = width // HD
    most = table.shape[1]
    blocks = own.shape[0] - rows - 1
    scr[...] = jnp.zeros_like(scr)
    scr[0:rows, :] = query[...].astype(F32)
    scr[rows : 2 * rows, :] = key[...].astype(F32)
    values = scr[...]
    line = rows_of((8, width))
    where_at = jnp.zeros((8, width), F32)
    for r in range(rows):
        here = (line == r) | (line == rows + r)
        where_at = jnp.where(here, length[r].astype(F32), where_at)
    lane = lanes((8, width))
    turn = lanes((8, 384)) % (HD // 2)
    freq = jnp.zeros((8, 384), F32)
    for i in range(HD // 2):
        freq = jnp.where(turn == i, float(np.float32(10000.0 ** (-2.0 * i / HD))), freq)
    angles = where_at * jnp.concatenate([freq] * (width // 384), 1)
    first = lane % HD < HD // 2
    ahead = pltpu.roll(values, width - HD // 2, 1)
    behind = pltpu.roll(values, HD // 2, 1)
    other = jnp.where(first, -ahead, behind)
    turned = values * jnp.cos(angles) + other * jnp.sin(angles)
    scr[...] = round_low(turned)
    packed[:, :width] = scr[0:rows, :].astype(BF16)
    packed[:, width : 2 * width] = residual[...]
    tail = jnp.zeros((rows, 128), F32)
    at, row = lanes((rows, 128)), rows_of((rows, 128))
    for r in range(rows):
        codes = [table[r, k] + 1 for k in range(most)] + [length[r]]
        spots = [(k, most + k) for k in range(most)] + [(2 * most, 2 * most + 1)]
        for code, (high, rest) in zip(codes, spots):
            tail = jnp.where((row == r) & (at == high), (code >> 7).astype(F32), tail)
            tail = jnp.where((row == r) & (at == rest), (code & 127).astype(F32), tail)
    packed[:, 2 * width :] = tail.astype(BF16)

    head_mask = lane // HD == line
    product = scr[0:rows, :] * scr[rows : 2 * rows, :]
    own[...] = jnp.zeros_like(own)
    spot = lanes((8, 128))
    tail = jnp.zeros((8, 128), F32)
    for r in range(rows):
        score = jnp.sum(
            jnp.where(head_mask, jnp.broadcast_to(product[r : r + 1], (8, width)), 0.0),
            1,
            keepdims=True,
        ) * (1.0 / math.sqrt(HD))
        shift = round_low(score)
        weight = jnp.exp(score - shift)
        spread = jnp.sum(jnp.where(head_mask, round_low(weight), 0.0), 0, keepdims=True)
        own[blocks + r : blocks + r + 1, :width] = spread * value[r : r + 1, :].astype(F32)
        high = round_low(weight)
        tail = jnp.where(spot == blocks + r, shift, tail)
        tail = jnp.where(spot == 8 + blocks + r, high, tail)
        tail = jnp.where(spot == 16 + blocks + r, weight - high, tail)
    own[:, width:] = tail


def carry_kernel(packed, own, packed_near, own_near):
    packed_near[...] = packed[...]
    own_near[...] = own[...]


def merge_kernel(mine, theirs, both):
    y = lax.axis_index("pool") % 2
    both[y] = mine[...]
    both[1 - y] = theirs[...]


def attend_kernel(a0, a1, a2, a3, own, keys, values, part, residual, tables, scr):
    blocks, block_len, width = keys.shape
    rows = a0.shape[1]
    heads = width // HD
    most = 8
    me = lax.axis_index("pool")
    for y in range(2):
        pieces = [piece[y].astype(F32) for piece in (a0, a1, a2, a3)]
        for z, piece in enumerate(in_order(pieces, me // 2)):
            scr[(z * 2 + y) * rows : (z * 2 + y + 1) * rows, :] = piece
    queries = scr[:, :width]
    residual[...] = scr[:, width : 2 * width]
    tail = scr[:, 2 * width :]
    requests = tail.shape[0]
    table = tail * CODE + pltpu.roll(tail, 128 - most, 1) - 1.0
    length = tail[:, 2 * most : 2 * most + 1] * CODE + tail[:, 2 * most + 1 : 2 * most + 2]
    lane = lanes((requests, 128))
    table = jnp.where(lane < most, table, -2.0)
    tables[...] = table
    head_mask = lanes((heads, width)) // HD == rows_of((heads, width))
    spot = lanes((heads, 128))
    tail = own[:, width:]
    scores, limits = [], []
    for b in range(blocks):
        match = jnp.where(table == (me * blocks + b).astype(F32), 1.0, 0.0)
        holder = jnp.sum(match, 1, keepdims=True)
        place = jnp.sum(jnp.sum(match * lane.astype(F32), 1, keepdims=True), 0, keepdims=True)
        limit = jnp.sum(holder * length, 0, keepdims=True) - place * block_len
        limits.append(jnp.broadcast_to(limit, (heads, block_len)))
        query = jnp.sum(holder * queries, 0, keepdims=True)
        spread = jnp.where(head_mask, query, 0.0).astype(BF16)
        scores.append(
            lax.dot_general(
                spread, keys[b], (((1,), (1,)), ((), ())), preferred_element_type=F32
            )
        )
    scores = jnp.concatenate(scores, 0) * (1.0 / math.sqrt(HD))
    token = lanes((blocks * heads, block_len)).astype(F32)
    valid = token < jnp.concatenate(limits, 0)
    scores = jnp.where(valid, scores, LOW)
    shift = round_low(jnp.max(scores, 1, keepdims=True))
    weights = jnp.where(valid, jnp.exp(scores - shift), 0.0)
    total = jnp.sum(weights, 1, keepdims=True)
    high = round_low(total)
    rest = total - high
    numerators = []
    for b in range(blocks):
        mine = slice(b * heads, (b + 1) * heads)
        full = jnp.dot(weights[mine].astype(BF16), values[b], preferred_element_type=F32)
        numerators.append(jnp.sum(jnp.where(head_mask, full, 0.0), 0, keepdims=True))
        tail = jnp.where(spot == b, shift[mine], tail)
        tail = jnp.where(spot == 8 + b, high[mine], tail)
        tail = jnp.where(spot == 16 + b, rest[mine], tail)
    line = rows_of((8, width))
    numer = own[:, :width]
    for b in range(blocks):
        numer = jnp.where(line == b, numerators[b], numer)
    numer = jnp.where(line == 7, flatten(tail, width), numer)
    part[...] = numer.astype(BF16)


def combine_kernel(b0, b1, b2, b3, tables, weight, head_part, numer, tails, mix):
    requests = tables.shape[0]
    slots = b0.shape[1]
    width = weight.shape[0]
    heads = width // HD
    rows, blocks = 2, slots - 3
    me = lax.axis_index("pool")
    for step, piece in enumerate((b0, b1, b2, b3)):
        z = (me // 2) ^ step
        for y in range(2):
            owner = z * 2 + y
            values = piece[y].astype(F32)
            numer[pl.ds(pl.multiple_of(owner * slots, 8), slots), :] = values
            tails[owner] = unflatten(values[slots - 1 : slots], heads)
    lane8 = lanes((heads, 128))
    shifts = jnp.zeros((heads, 128), F32)
    totals = jnp.zeros((heads, 128), F32)
    for owner in range(8):
        tail = tails[owner]
        total = pltpu.roll(tail, 120, 1) + pltpu.roll(tail, 112, 1)
        tail, total = jnp.where(lane8 < 8, tail, 0.0), jnp.where(lane8 < 8, total, 0.0)
        if owner:
            tail, total = pltpu.roll(tail, 8 * owner, 1), pltpu.roll(total, 8 * owner, 1)
        shifts, totals = shifts + tail, totals + total
    lane = lanes((requests, 128))
    owner, slot = lane // slots, lane % slots
    block_id = jnp.where((slot < blocks) & (lane < 64), owner * blocks + slot, -5).astype(F32)
    self_id = jnp.where((slot >= blocks) & (slot < blocks + rows), owner * rows + slot - blocks, -5)
    table = tables[...]
    belongs = (self_id == rows_of((requests, 128))) & (lane < 64)
    for k in range(8):
        belongs = belongs | (table[:, k : k + 1] == block_id)
    for h in range(heads):
        shift = jnp.broadcast_to(shifts[h : h + 1], (requests, 128))
        top = jnp.max(jnp.where(belongs, shift, LOW), 1, keepdims=True)
        scale = jnp.where(belongs, jnp.exp(shift - top), 0.0)
        total = jnp.sum(scale * totals[h : h + 1], 1, keepdims=True)
        mix[h * requests : (h + 1) * requests, :] = scale / total
    full = jnp.dot(
        mix[:, : 8 * slots].astype(BF16), numer[...].astype(BF16), preferred_element_type=F32
    )
    head = lanes((requests, width)) // HD
    attended = jnp.zeros((requests, width), F32)
    for h in range(heads):
        attended = jnp.where(head == h, full[h * requests : (h + 1) * requests], attended)
    head_part[...] = jnp.dot(
        attended.astype(BF16), weight[...], preferred_element_type=F32
    ).astype(BF16)


def sum_kernel(p0, p1, p2, p3, total):
    total[...] = (
        (p0[...].astype(F32) + p1[...].astype(F32)) + (p2[...].astype(F32) + p3[...].astype(F32))
    ).astype(BF16)


def gate_up_kernel(same, flip, all_input, gain, gate, up, sums, own, scr):
    me = lax.axis_index("pool")
    odd = me % 2 == 1
    part = same.shape[1]
    ff = gate.shape[1]
    rows = own.shape[0]
    near, far = same[...].astype(F32), flip[...].astype(F32)
    scr[:, :part] = all_input[:, :part] + jnp.where(odd, far, near)
    scr[:, part:] = all_input[:, part:] + jnp.where(odd, near, far)
    residual = scr[...]
    mine = scr[0:rows, :]
    for p in range(1, residual.shape[0] // rows):
        mine = jnp.where(me == p, scr[p * rows : (p + 1) * rows, :], mine)
    own[...] = mine
    square = jnp.sum(residual * residual, 1, keepdims=True)
    portion = (residual * gain[...].astype(F32)).astype(BF16)
    sums[:, :ff] = jnp.dot(portion, gate[...], preferred_element_type=F32).astype(BF16)
    sums[:, ff : 2 * ff] = jnp.dot(portion, up[...], preferred_element_type=F32).astype(BF16)
    lane = lanes((residual.shape[0], 128))
    high = round_low(square)
    tail = jnp.where(lane == 0, high, jnp.where(lane == 1, square - high, 0.0))
    sums[:, 2 * ff :] = tail.astype(BF16)


def core_sum_kernel(mine, theirs, total):
    ff2 = mine.shape[1] - 128
    total[:, :ff2] = (mine[:, :ff2].astype(F32) + theirs[:, :ff2].astype(F32)).astype(BF16)
    tail = mine[:, ff2:].astype(F32) + theirs[:, ff2:].astype(F32)
    square = jnp.sum(tail, 1, keepdims=True)
    lane = lanes(tail.shape)
    high = round_low(square)
    tail = jnp.where(lane == 0, high, jnp.where(lane == 1, square - high, 0.0))
    total[:, ff2:] = tail.astype(BF16)


def down_kernel(features, mine, theirs, weight, parts, scr):
    ff = weight.shape[0]
    tail = mine[:, 2 * ff :].astype(F32) + theirs[:, 2 * ff :].astype(F32)
    square = jnp.sum(tail, 1, keepdims=True)
    factor = lax.rsqrt(square * (1.0 / features) + 1e-05)
    gate = (mine[:, :ff].astype(F32) + theirs[:, :ff].astype(F32)) * factor
    up = (mine[:, ff : 2 * ff].astype(F32) + theirs[:, ff : 2 * ff].astype(F32)) * factor
    hidden = (gate / (1.0 + jnp.exp(-gate)) * up).astype(BF16)
    scr[...] = jnp.dot(hidden, weight[...], preferred_element_type=F32)
    rows = parts.shape[1]
    pool = parts.shape[0]
    for p in range(pool):
        parts[pool - 1 - p] = scr[p * rows : (p + 1) * rows, :].astype(BF16)


def final_kernel(own, parts, out):
    total = own[...]
    for p in range(parts.shape[0]):
        total = total + parts[p].astype(F32)
    out[...] = total.astype(BF16)


def flip(values, axis, step):
    size = lax.axis_size(axis)
    return lax.ppermute(values, axis, [(index, index ^ step) for index in range(size)])


def per_device_small(
    residual_in,
    query_new,
    key_new,
    value_new,
    key_cache,
    value_cache,
    block_table,
    lengths,
    out_weight,
    norm_gain,
    gate_weight,
    up_weight,
    down_weight,
):
    rows, width = residual_in.shape
    blocks = key_cache.shape[0]
    pool, mlp = 8, 4
    requests = rows * pool
    ff = gate_weight.shape[1]
    part_cols = out_weight.shape[1]
    packed_width = 2 * width + 128
    slots = blocks + rows + 1
    part_width = width + 128

    packed, own = call(
        prepare_kernel,
        "rotary",
        [((rows, packed_width), BF16), ((slots, part_width), F32)],
        [block_table, lengths, query_new, key_new, value_new, residual_in, key_cache, value_cache],
        [pltpu.SMEM(block_table.shape, jnp.int32), pltpu.SMEM(lengths.shape, jnp.int32)]
        + [pltpu.VMEM((rows, width), BF16)] * 4
        + [pltpu.VMEM((8, width), F32), pltpu.SemaphoreType.DMA((6,))],
        hbm=range(8),
        limit=54 * 2**20,
    )

    packed_near, own = call(
        carry_kernel,
        "carry",
        [(packed.shape, BF16), (own.shape, F32)],
        [packed, own],
    )

    def pool_gather(values, near):
        (both,) = call(
            merge_kernel,
            "merge",
            [((2,) + values.shape, values.dtype)],
            [near, flip(values, "pool", 1)],
        )
        return [both] + [flip(both, "pool", step) for step in (2, 4, 6)]

    part, all_input, tables = call(
        attend_kernel,
        "attend",
        [((slots, width), BF16), ((requests, width), F32), ((requests, 128), F32)],
        pool_gather(packed, packed_near) + [own, key_cache, value_cache],
        [pltpu.VMEM((requests, packed_width), F32)],
    )
    (head_part,) = call(
        combine_kernel,
        "combine",
        [((requests, part_cols), BF16)],
        pool_gather(part, part) + [tables, out_weight],
        [
            pltpu.VMEM((pool * slots, width), F32),
            pltpu.VMEM((pool, slots, 128), F32),
            pltpu.VMEM((requests * width // HD, 128), F32),
        ],
    )
    (head_sum,) = call(
        sum_kernel,
        "head_sum",
        [((requests, part_cols), BF16)],
        [head_part] + [flip(head_part, "mlp", step) for step in (1, 2, 3)],
    )
    pieces = []
    for turn in range(2):
        route = []
        for m in range(mlp):
            by_distance = sorted(range(4), key=lambda z: (-abs(z - m), z))
            for z, step in zip(by_distance, (0, 1, 2, 3)):
                for y in range(2):
                    source = (m * 2 + y) * mlp + (m ^ step)
                    route.append((source, (z * 2 + (y ^ turn)) * mlp + m))
        pieces.append(lax.ppermute(head_sum, ("pool", "mlp"), route))
    sums, own_residual = call(
        gate_up_kernel,
        "gate_up",
        [((requests, 2 * ff + 128), BF16), ((rows, width), F32)],
        pieces + [all_input, norm_gain.reshape(1, width), gate_weight, up_weight],
        [pltpu.VMEM((requests, width), F32)],
    )
    (core_sums,) = call(
        core_sum_kernel,
        "core_sum",
        [((requests, 2 * ff + 128), BF16)],
        [sums, flip(sums, "mlp", 1)],
    )
    (down,) = call(
        functools.partial(down_kernel, width * mlp),
        "down",
        [((pool, rows, width), BF16)],
        [core_sums, flip(core_sums, "mlp", 2), down_weight],
        [pltpu.VMEM((requests, width), F32)],
    )
    backwards = list(range(pool))[::-1]
    (out,) = call(
        final_kernel,
        "final",
        [((rows, width), BF16)],
        [own_residual, lax.all_to_all(down, "pool", 0, 0, axis_index_groups=[backwards])],
    )
    return out


def solution(mesh):
    in_specs = (
        P("pool", "mlp"),
        P("pool", "mlp"),
        P("pool", "mlp"),
        P("pool", "mlp"),
        P("pool", None, "mlp"),
        P("pool", None, "mlp"),
        P("pool", None),
        P("pool"),
        P("mlp", "pool"),
        P("mlp"),
        P("mlp", "pool"),
        P("mlp", "pool"),
        P("pool", "mlp"),
    )
    small = mesh.shape["pool"] == 8 and mesh.shape["mlp"] == 4
    per_device = per_device_small if small else per_device_wide
    return jax.shard_map(
        per_device, mesh=mesh, in_specs=in_specs, out_specs=P("pool", "mlp"), check_vma=False
    )
```

```python
import functools
import math

import jax
import jax.numpy as jnp
import numpy as np
from jax import lax
from jax.experimental import pallas as pl
from jax.experimental.pallas import tpu as pltpu
from jax.sharding import PartitionSpec as P

HD = 96
LOW = -1e30
CODE = 128


def rotate(values, positions):
    half_size = values.shape[-1] // 2
    inverse_freq = 10000.0 ** (-(2.0 * jnp.arange(half_size, dtype=jnp.float32)) / values.shape[-1])
    angles = positions.astype(jnp.float32)[:, None, None] * inverse_freq[None, None, :]
    cosine = jnp.cos(angles)
    sine_part = jnp.sin(angles)
    first = values[..., :half_size]
    second = values[..., half_size:]
    return jnp.concatenate(
        [first * cosine - second * sine_part, second * cosine + first * sine_part], -1
    )


def low(values):
    return lax.reduce_precision(values, 8, 7)


def split(values):
    high = low(values)
    return high.astype(jnp.bfloat16), (values - high).astype(jnp.bfloat16)


def encode(ints):
    return (ints // CODE).astype(jnp.bfloat16), (ints % CODE).astype(jnp.bfloat16)


def decode(high, rest):
    return high.astype(jnp.int32) * CODE + rest.astype(jnp.int32)


def gather(values, axis):
    copies = jnp.broadcast_to(values[None], (lax.axis_size(axis),) + values.shape)
    return lax.all_to_all(copies, axis, 0, 0)


def per_device_wide(
    residual_in,
    query_new,
    key_new,
    value_new,
    key_cache,
    value_cache,
    block_table,
    lengths,
    out_weight,
    norm_gain,
    gate_weight,
    up_weight,
    down_weight,
):
    rows, width = residual_in.shape
    heads = width // HD
    blocks, block_len = key_cache.shape[:2]
    most = block_table.shape[1]
    pool, mlp = lax.axis_size("pool"), lax.axis_size("mlp")
    pool_index = lax.axis_index("pool")
    requests = rows * pool
    score_scale = 1.0 / math.sqrt(HD)
    f32, bf16 = jnp.float32, jnp.bfloat16

    queries = rotate(query_new.astype(f32).reshape(rows, heads, HD), lengths).astype(bf16)
    new_keys = rotate(key_new.astype(f32).reshape(rows, heads, HD), lengths).astype(bf16)

    table_high, table_low = encode(block_table + 1)
    len_high, len_low = encode(lengths)
    packed = jnp.concatenate(
        [
            queries.reshape(rows, width),
            residual_in,
            table_high,
            table_low,
            len_high[:, None],
            len_low[:, None],
        ],
        1,
    )
    spare = -packed.shape[1] % 128
    packed = jnp.pad(packed, ((0, 0), (0, spare)))
    got = gather(packed, "pool").reshape(requests, packed.shape[1])
    all_queries = got[:, :width]
    all_input = got[:, width : 2 * width]
    tail = got[:, 2 * width :]
    tables = decode(tail[:, :most], tail[:, most : 2 * most]) - 1
    all_lengths = decode(tail[:, 2 * most], tail[:, 2 * most + 1])

    held_ids = pool_index * blocks + jnp.arange(blocks, dtype=jnp.int32)
    matches = tables[None, :, :] == held_ids[:, None, None]
    holder = jnp.any(matches, 2)
    block_index = jnp.sum(
        jnp.where(matches, jnp.arange(most, dtype=jnp.int32)[None, None, :], 0), (1, 2)
    )
    valid_len = jnp.sum(jnp.where(holder, all_lengths[None, :], 0), 1)
    block_query = jnp.dot(holder.astype(bf16), all_queries, preferred_element_type=f32)
    block_query = block_query.astype(bf16).reshape(blocks, heads, HD)
    key_rows = key_cache.reshape(blocks, block_len, heads, HD)
    value_rows = value_cache.reshape(blocks, block_len, heads, HD)
    scores = (
        jnp.einsum("bhd,bthd->bht", block_query, key_rows, preferred_element_type=f32)
        * score_scale
    )
    token_pos = block_index[:, None] * block_len + jnp.arange(block_len, dtype=jnp.int32)[None, :]
    valid = (token_pos < valid_len[:, None])[:, None, :]
    scores = jnp.where(valid, scores, LOW)
    shift = low(jnp.max(scores, 2))
    weights = jnp.where(valid, jnp.exp(scores - shift[:, :, None]), 0.0)
    totals = jnp.sum(weights, 2)
    numerator = jnp.einsum(
        "bht,bthd->bhd", weights.astype(bf16), value_rows, preferred_element_type=f32
    )
    self_score = jnp.sum(queries.astype(f32) * new_keys.astype(f32), -1) * score_scale
    self_shift = low(self_score)
    self_weight = jnp.exp(self_score - self_shift)
    self_numer = self_weight[:, :, None] * value_new.astype(f32).reshape(rows, heads, HD)

    own_total = jnp.concatenate([totals, self_weight], 0)
    total_high, total_low = split(own_total)
    part = jnp.concatenate(
        [
            jnp.concatenate([numerator, self_numer], 0)
            .astype(bf16)
            .reshape(blocks + rows, width),
            jnp.concatenate([shift, self_shift], 0).astype(bf16),
            total_high,
            total_low,
        ],
        1,
    )
    part = jnp.pad(part, ((0, 0), (0, -part.shape[1] % 128)))
    count = blocks + rows
    parts = gather(part, "pool").reshape(pool * count, part.shape[1])
    all_shift = parts[:, width : width + heads].astype(f32)
    all_total = parts[:, width + heads : width + 2 * heads].astype(f32) + parts[
        :, width + 2 * heads : width + 3 * heads
    ].astype(f32)
    place = jnp.arange(pool * count, dtype=jnp.int32)
    owner, slot = place // count, place % count
    is_block = slot < blocks
    block_id = jnp.where(is_block, owner * blocks + slot, -2)
    self_id = jnp.where(is_block, -2, owner * rows + slot - blocks)
    request_ids = jnp.arange(requests, dtype=jnp.int32)
    belongs = jnp.any(tables[:, None, :] == block_id[None, :, None], 2) | (
        request_ids[:, None] == self_id[None, :]
    )
    top = jnp.max(jnp.where(belongs[:, :, None], all_shift[None], LOW), 1)
    part_top = jnp.sum(jnp.where(belongs[:, :, None], top[:, None, :], 0.0), 0)
    scale = jnp.exp(all_shift - part_top)
    scaled = parts[:, :width].astype(f32).reshape(-1, heads, HD) * scale[:, :, None]
    mix = belongs.astype(f32)
    numer = jnp.dot(mix, scaled.reshape(-1, width), precision=lax.Precision.HIGHEST)
    denom = jnp.dot(mix, all_total * scale, precision=lax.Precision.HIGHEST)
    attended = (numer.reshape(requests, heads, HD) / denom[:, :, None]).astype(bf16)
    attended = attended.reshape(requests, width)

    head_part = jnp.dot(attended, out_weight, preferred_element_type=f32).astype(bf16)
    share = pool // mlp
    route = []
    for p in range(pool):
        for m in range(mlp):
            route.append((p * mlp + m, ((p % share) * mlp + m) * mlp + p // share))
    moved = lax.ppermute(head_part, ("pool", "mlp"), route)
    head_all = gather(moved, "pool").reshape(share, mlp, requests, -1)
    head_out = low(jnp.sum(head_all.astype(f32), 1))
    head_out = jnp.swapaxes(head_out, 0, 1).reshape(requests, width)
    residual = all_input.astype(f32) + head_out
    squares = jnp.sum(residual * residual, -1, keepdims=True)
    portion = (residual * norm_gain.astype(f32)).astype(bf16)

    ff = gate_weight.shape[1]
    square_high, square_low = split(squares)
    sums = jnp.concatenate(
        [
            jnp.dot(portion, gate_weight, preferred_element_type=f32).astype(bf16),
            jnp.dot(portion, up_weight, preferred_element_type=f32).astype(bf16),
            jnp.broadcast_to(square_high, (requests, 64)),
            jnp.broadcast_to(square_low, (requests, 64)),
        ],
        1,
    )
    summed = jnp.sum(gather(sums, "mlp").astype(f32), 0)
    mean_square = (summed[:, 2 * ff : 2 * ff + 1] + summed[:, 2 * ff + 64 : 2 * ff + 65]) / (
        width * mlp
    )
    factor = lax.rsqrt(mean_square + 1e-05)
    gate = summed[:, :ff] * factor
    up = summed[:, ff : 2 * ff] * factor
    hidden = (jax.nn.silu(gate) * up).astype(bf16)

    down = jnp.dot(hidden, down_weight, preferred_element_type=f32)
    down = lax.all_to_all(down.reshape(pool, rows, width), "pool", 0, 0)
    own = lax.dynamic_slice_in_dim(residual, pool_index * rows, rows, 0)
    return (own + jnp.sum(down, 0)).astype(bf16)


F32, BF16 = jnp.float32, jnp.bfloat16
VMEM = pl.BlockSpec(memory_space=pltpu.VMEM)
HBM = pl.BlockSpec(memory_space=pl.ANY)


def call(kernel, name, outs, args, scratch=(), hbm=(), limit=16 * 2**20):
    size = sum(math.prod(a.shape) * a.dtype.itemsize for a in args)
    return pl.pallas_call(
        kernel,
        out_shape=[jax.ShapeDtypeStruct(shape, dtype) for shape, dtype in outs],
        in_specs=[HBM if i in hbm else VMEM for i in range(len(args))],
        out_specs=[VMEM] * len(outs),
        scratch_shapes=list(scratch),
        compiler_params=pltpu.CompilerParams(vmem_limit_bytes=limit),
        cost_estimate=pl.CostEstimate(flops=0, bytes_accessed=size, transcendentals=0),
        name=name,
    )(*args)


def lanes(shape):
    return lax.broadcasted_iota(jnp.int32, shape, len(shape) - 1)


def in_order(pieces, index):
    for bit in (1, 2):
        odd = (index & bit) != 0
        pieces = [jnp.where(odd, pieces[s ^ bit], pieces[s]) for s in range(4)]
    return pieces


def rows_of(shape):
    return lax.broadcasted_iota(jnp.int32, shape, len(shape) - 2)


def round_low(values):
    return values.astype(BF16).astype(F32)


def head_start(shape):
    return rows_of(shape) * HD % 128


def flatten(tail, width):
    heads = tail.shape[0]
    spread = jnp.zeros((heads, width), F32)
    start = head_start((heads, width))
    for k in (0, 32, 64, 96):
        moved = pltpu.roll(tail, k, 1) if k else tail
        spread = jnp.where(start == k, jnp.concatenate([moved] * (width // 128), 1), spread)
    lane = lanes((heads, width))
    used = (lane // HD == rows_of((heads, width))) & (lane % HD < 24)
    return jnp.sum(jnp.where(used, spread, 0.0), 0, keepdims=True)


def unflatten(row, heads):
    width = row.shape[1]
    lane = lanes((heads, width))
    used = (lane // HD == rows_of((heads, width))) & (lane % HD < 24)
    spread = jnp.where(used, jnp.broadcast_to(row, (heads, width)), 0.0)
    folded = spread[:, :128]
    for at in range(128, width, 128):
        folded = folded + spread[:, at : at + 128]
    start = head_start((heads, 128))
    tail = jnp.where(start == 0, folded, 0.0)
    for k in (32, 64, 96):
        tail = jnp.where(start == k, pltpu.roll(folded, 128 - k, 1), tail)
    return tail


def prepare_kernel(*refs):
    sources, (packed, own), held = refs[:6], refs[8:10], refs[10:16]
    scr, sems = refs[16:]
    copies = [
        pltpu.make_async_copy(source, target, sems.at[i])
        for i, (source, target) in enumerate(zip(sources, held))
    ]
    for copy in copies:
        copy.start()
    for copy in copies:
        copy.wait()
    table, length, query, key, value, residual = held
    rows, width = query.shape
    heads = width // HD
    most = table.shape[1]
    blocks = own.shape[0] - rows - 1
    scr[...] = jnp.zeros_like(scr)
    scr[0:rows, :] = query[...].astype(F32)
    scr[rows : 2 * rows, :] = key[...].astype(F32)
    values = scr[...]
    line = rows_of((8, width))
    where_at = jnp.zeros((8, width), F32)
    for r in range(rows):
        here = (line == r) | (line == rows + r)
        where_at = jnp.where(here, length[r].astype(F32), where_at)
    lane = lanes((8, width))
    turn = lanes((8, 384)) % (HD // 2)
    freq = jnp.zeros((8, 384), F32)
    for i in range(HD // 2):
        freq = jnp.where(turn == i, float(np.float32(10000.0 ** (-2.0 * i / HD))), freq)
    angles = where_at * jnp.concatenate([freq] * (width // 384), 1)
    first = lane % HD < HD // 2
    ahead = pltpu.roll(values, width - HD // 2, 1)
    behind = pltpu.roll(values, HD // 2, 1)
    other = jnp.where(first, -ahead, behind)
    turned = values * jnp.cos(angles) + other * jnp.sin(angles)
    scr[...] = round_low(turned)
    packed[:, :width] = scr[0:rows, :].astype(BF16)
    packed[:, width : 2 * width] = residual[...]
    tail = jnp.zeros((rows, 128), F32)
    at, row = lanes((rows, 128)), rows_of((rows, 128))
    for r in range(rows):
        codes = [table[r, k] + 1 for k in range(most)] + [length[r]]
        spots = [(k, most + k) for k in range(most)] + [(2 * most, 2 * most + 1)]
        for code, (high, rest) in zip(codes, spots):
            tail = jnp.where((row == r) & (at == high), (code >> 7).astype(F32), tail)
            tail = jnp.where((row == r) & (at == rest), (code & 127).astype(F32), tail)
    packed[:, 2 * width :] = tail.astype(BF16)

    head_mask = lane // HD == line
    product = scr[0:rows, :] * scr[rows : 2 * rows, :]
    own[...] = jnp.zeros_like(own)
    spot = lanes((8, 128))
    tail = jnp.zeros((8, 128), F32)
    for r in range(rows):
        score = jnp.sum(
            jnp.where(head_mask, jnp.broadcast_to(product[r : r + 1], (8, width)), 0.0),
            1,
            keepdims=True,
        ) * (1.0 / math.sqrt(HD))
        shift = round_low(score)
        weight = jnp.exp(score - shift)
        spread = jnp.sum(jnp.where(head_mask, round_low(weight), 0.0), 0, keepdims=True)
        own[blocks + r : blocks + r + 1, :width] = spread * value[r : r + 1, :].astype(F32)
        high = round_low(weight)
        tail = jnp.where(spot == blocks + r, shift, tail)
        tail = jnp.where(spot == 8 + blocks + r, high, tail)
        tail = jnp.where(spot == 16 + blocks + r, weight - high, tail)
    own[:, width:] = tail


def carry_kernel(packed, own, packed_near, own_near):
    packed_near[...] = packed[...]
    own_near[...] = own[...]


def merge_kernel(mine, theirs, both):
    y = lax.axis_index("pool") % 2
    both[y] = mine[...]
    both[1 - y] = theirs[...]


def attend_kernel(a0, a1, a2, a3, own, keys, values, part, residual, tables, scr):
    blocks, block_len, width = keys.shape
    rows = a0.shape[1]
    heads = width // HD
    most = 8
    me = lax.axis_index("pool")
    for y in range(2):
        pieces = [piece[y].astype(F32) for piece in (a0, a1, a2, a3)]
        for z, piece in enumerate(in_order(pieces, me // 2)):
            scr[(z * 2 + y) * rows : (z * 2 + y + 1) * rows, :] = piece
    queries = scr[:, :width]
    residual[...] = scr[:, width : 2 * width]
    tail = scr[:, 2 * width :]
    requests = tail.shape[0]
    table = tail * CODE + pltpu.roll(tail, 128 - most, 1) - 1.0
    length = tail[:, 2 * most : 2 * most + 1] * CODE + tail[:, 2 * most + 1 : 2 * most + 2]
    lane = lanes((requests, 128))
    table = jnp.where(lane < most, table, -2.0)
    tables[...] = table
    head_mask = lanes((heads, width)) // HD == rows_of((heads, width))
    spot = lanes((heads, 128))
    tail = own[:, width:]
    scores, limits = [], []
    for b in range(blocks):
        match = jnp.where(table == (me * blocks + b).astype(F32), 1.0, 0.0)
        holder = jnp.sum(match, 1, keepdims=True)
        place = jnp.sum(jnp.sum(match * lane.astype(F32), 1, keepdims=True), 0, keepdims=True)
        limit = jnp.sum(holder * length, 0, keepdims=True) - place * block_len
        limits.append(jnp.broadcast_to(limit, (heads, block_len)))
        query = jnp.sum(holder * queries, 0, keepdims=True)
        spread = jnp.where(head_mask, query, 0.0).astype(BF16)
        scores.append(
            lax.dot_general(
                spread, keys[b], (((1,), (1,)), ((), ())), preferred_element_type=F32
            )
        )
    scores = jnp.concatenate(scores, 0) * (1.0 / math.sqrt(HD))
    token = lanes((blocks * heads, block_len)).astype(F32)
    valid = token < jnp.concatenate(limits, 0)
    scores = jnp.where(valid, scores, LOW)
    shift = round_low(jnp.max(scores, 1, keepdims=True))
    weights = jnp.where(valid, jnp.exp(scores - shift), 0.0)
    total = jnp.sum(weights, 1, keepdims=True)
    high = round_low(total)
    rest = total - high
    numerators = []
    for b in range(blocks):
        mine = slice(b * heads, (b + 1) * heads)
        full = jnp.dot(weights[mine].astype(BF16), values[b], preferred_element_type=F32)
        numerators.append(jnp.sum(jnp.where(head_mask, full, 0.0), 0, keepdims=True))
        tail = jnp.where(spot == b, shift[mine], tail)
        tail = jnp.where(spot == 8 + b, high[mine], tail)
        tail = jnp.where(spot == 16 + b, rest[mine], tail)
    line = rows_of((8, width))
    numer = own[:, :width]
    for b in range(blocks):
        numer = jnp.where(line == b, numerators[b], numer)
    numer = jnp.where(line == 7, flatten(tail, width), numer)
    part[...] = numer.astype(BF16)


def combine_kernel(b0, b1, b2, b3, tables, weight, head_part, numer, tails, mix):
    requests = tables.shape[0]
    slots = b0.shape[1]
    width = weight.shape[0]
    heads = width // HD
    rows, blocks = 2, slots - 3
    me = lax.axis_index("pool")
    for step, piece in enumerate((b0, b1, b2, b3)):
        z = (me // 2) ^ step
        for y in range(2):
            owner = z * 2 + y
            values = piece[y].astype(F32)
            numer[pl.ds(pl.multiple_of(owner * slots, 8), slots), :] = values
            tails[owner] = unflatten(values[slots - 1 : slots], heads)
    lane8 = lanes((heads, 128))
    shifts = jnp.zeros((heads, 128), F32)
    totals = jnp.zeros((heads, 128), F32)
    for owner in range(8):
        tail = tails[owner]
        total = pltpu.roll(tail, 120, 1) + pltpu.roll(tail, 112, 1)
        tail, total = jnp.where(lane8 < 8, tail, 0.0), jnp.where(lane8 < 8, total, 0.0)
        if owner:
            tail, total = pltpu.roll(tail, 8 * owner, 1), pltpu.roll(total, 8 * owner, 1)
        shifts, totals = shifts + tail, totals + total
    lane = lanes((requests, 128))
    owner, slot = lane // slots, lane % slots
    block_id = jnp.where((slot < blocks) & (lane < 64), owner * blocks + slot, -5).astype(F32)
    self_id = jnp.where((slot >= blocks) & (slot < blocks + rows), owner * rows + slot - blocks, -5)
    table = tables[...]
    belongs = (self_id == rows_of((requests, 128))) & (lane < 64)
    for k in range(8):
        belongs = belongs | (table[:, k : k + 1] == block_id)
    for h in range(heads):
        shift = jnp.broadcast_to(shifts[h : h + 1], (requests, 128))
        top = jnp.max(jnp.where(belongs, shift, LOW), 1, keepdims=True)
        scale = jnp.where(belongs, jnp.exp(shift - top), 0.0)
        total = jnp.sum(scale * totals[h : h + 1], 1, keepdims=True)
        mix[h * requests : (h + 1) * requests, :] = scale / total
    full = jnp.dot(
        mix[:, : 8 * slots].astype(BF16), numer[...].astype(BF16), preferred_element_type=F32
    )
    head = lanes((requests, width)) // HD
    attended = jnp.zeros((requests, width), F32)
    for h in range(heads):
        attended = jnp.where(head == h, full[h * requests : (h + 1) * requests], attended)
    head_part[...] = jnp.dot(
        attended.astype(BF16), weight[...], preferred_element_type=F32
    ).astype(BF16)


def sum_kernel(p0, p1, p2, p3, total):
    total[...] = (
        (p0[...].astype(F32) + p1[...].astype(F32)) + (p2[...].astype(F32) + p3[...].astype(F32))
    ).astype(BF16)


def gate_up_kernel(same, flip, all_input, gain, gate, up, send, keep, own, scr):
    me = lax.axis_index("pool")
    core = lax.axis_index("mlp") % 2
    odd = me % 2 == 1
    part = same.shape[1]
    half = gate.shape[1] // 2
    rows = own.shape[0]
    near, far = same[...].astype(F32), flip[...].astype(F32)
    scr[:, :part] = all_input[:, :part] + jnp.where(odd, far, near)
    scr[:, part:] = all_input[:, part:] + jnp.where(odd, near, far)
    residual = scr[...]
    mine = scr[0:rows, :]
    for p in range(1, residual.shape[0] // rows):
        mine = jnp.where(me == p, scr[p * rows : (p + 1) * rows, :], mine)
    own[...] = mine
    square = jnp.sum(residual * residual, 1, keepdims=True)
    portion = (residual * gain[...].astype(F32)).astype(BF16)
    for at, weight in ((0, gate), (half, up)):
        low_half = jnp.dot(portion, weight[:, :half], preferred_element_type=F32)
        high_half = jnp.dot(portion, weight[:, half:], preferred_element_type=F32)
        keep[:, at : at + half] = jnp.where(core == 0, low_half, high_half).astype(BF16)
        send[:, at : at + half] = jnp.where(core == 0, high_half, low_half).astype(BF16)
    tail = square_tail(square)
    keep[:, 2 * half :] = tail
    send[:, 2 * half :] = tail


def square_tail(square):
    lane = lanes((square.shape[0], 128))
    high = round_low(square)
    return jnp.where(lane == 0, high, jnp.where(lane == 1, square - high, 0.0)).astype(BF16)


def core_sum_kernel(mine, theirs, total):
    ff = mine.shape[1] - 128
    total[:, :ff] = (mine[:, :ff].astype(F32) + theirs[:, :ff].astype(F32)).astype(BF16)
    tail = mine[:, ff:].astype(F32) + theirs[:, ff:].astype(F32)
    total[:, ff:] = square_tail(jnp.sum(tail, 1, keepdims=True))


def hidden_kernel(features, mine, theirs, hidden):
    half = hidden.shape[1]
    tail = mine[:, 2 * half :].astype(F32) + theirs[:, 2 * half :].astype(F32)
    square = jnp.sum(tail, 1, keepdims=True)
    factor = lax.rsqrt(square * (1.0 / features) + 1e-05)
    gate = (mine[:, :half].astype(F32) + theirs[:, :half].astype(F32)) * factor
    up = (mine[:, half : 2 * half].astype(F32) + theirs[:, half : 2 * half].astype(F32)) * factor
    hidden[...] = (gate / (1.0 + jnp.exp(-gate)) * up).astype(BF16)


def down_kernel(mine, theirs, weight, parts, scr):
    half = weight.shape[0] // 2
    first = lax.axis_index("mlp") % 2 == 0
    mine, theirs = mine[...].astype(F32), theirs[...].astype(F32)
    low_half = jnp.where(first, mine, theirs).astype(BF16)
    high_half = jnp.where(first, theirs, mine).astype(BF16)
    scr[...] = jnp.dot(low_half, weight[:half], preferred_element_type=F32) + jnp.dot(
        high_half, weight[half:], preferred_element_type=F32
    )
    rows = parts.shape[1]
    pool = parts.shape[0]
    for p in range(pool):
        parts[pool - 1 - p] = scr[p * rows : (p + 1) * rows, :].astype(BF16)


def final_kernel(own, parts, out):
    total = own[...]
    for p in range(parts.shape[0]):
        total = total + parts[p].astype(F32)
    out[...] = total.astype(BF16)


def flip(values, axis, step):
    size = lax.axis_size(axis)
    return lax.ppermute(values, axis, [(index, index ^ step) for index in range(size)])


def per_device_small(
    residual_in,
    query_new,
    key_new,
    value_new,
    key_cache,
    value_cache,
    block_table,
    lengths,
    out_weight,
    norm_gain,
    gate_weight,
    up_weight,
    down_weight,
):
    rows, width = residual_in.shape
    blocks = key_cache.shape[0]
    pool, mlp = 8, 4
    requests = rows * pool
    ff = gate_weight.shape[1]
    part_cols = out_weight.shape[1]
    packed_width = 2 * width + 128
    slots = blocks + rows + 1
    part_width = width + 128

    packed, own = call(
        prepare_kernel,
        "rotary",
        [((rows, packed_width), BF16), ((slots, part_width), F32)],
        [block_table, lengths, query_new, key_new, value_new, residual_in, key_cache, value_cache],
        [pltpu.SMEM(block_table.shape, jnp.int32), pltpu.SMEM(lengths.shape, jnp.int32)]
        + [pltpu.VMEM((rows, width), BF16)] * 4
        + [pltpu.VMEM((8, width), F32), pltpu.SemaphoreType.DMA((6,))],
        hbm=range(8),
        limit=54 * 2**20,
    )

    packed_near, own = call(
        carry_kernel,
        "carry",
        [(packed.shape, BF16), (own.shape, F32)],
        [packed, own],
    )

    def pool_gather(values, near):
        (both,) = call(
            merge_kernel,
            "merge",
            [((2,) + values.shape, values.dtype)],
            [near, flip(values, "pool", 1)],
        )
        return [both] + [flip(both, "pool", step) for step in (2, 4, 6)]

    part, all_input, tables = call(
        attend_kernel,
        "attend",
        [((slots, width), BF16), ((requests, width), F32), ((requests, 128), F32)],
        pool_gather(packed, packed_near) + [own, key_cache, value_cache],
        [pltpu.VMEM((requests, packed_width), F32)],
    )
    (head_part,) = call(
        combine_kernel,
        "combine",
        [((requests, part_cols), BF16)],
        pool_gather(part, part) + [tables, out_weight],
        [
            pltpu.VMEM((pool * slots, width), F32),
            pltpu.VMEM((pool, slots, 128), F32),
            pltpu.VMEM((requests * width // HD, 128), F32),
        ],
    )
    (head_sum,) = call(
        sum_kernel,
        "head_sum",
        [((requests, part_cols), BF16)],
        [head_part] + [flip(head_part, "mlp", step) for step in (1, 2, 3)],
    )
    pieces = []
    for turn in range(2):
        route = []
        for m in range(mlp):
            by_distance = sorted(range(4), key=lambda z: (-abs(z - m), z))
            for z, step in zip(by_distance, (0, 1, 2, 3)):
                for y in range(2):
                    source = (m * 2 + y) * mlp + (m ^ step)
                    route.append((source, (z * 2 + (y ^ turn)) * mlp + m))
        pieces.append(lax.ppermute(head_sum, ("pool", "mlp"), route))
    send, keep, own_residual = call(
        gate_up_kernel,
        "gate_up",
        [((requests, ff + 128), BF16)] * 2 + [((rows, width), F32)],
        pieces + [all_input, norm_gain.reshape(1, width), gate_weight, up_weight],
        [pltpu.VMEM((requests, width), F32)],
    )
    (core_sums,) = call(
        core_sum_kernel,
        "core_sum",
        [((requests, ff + 128), BF16)],
        [keep, flip(send, "mlp", 1)],
    )
    (hidden,) = call(
        functools.partial(hidden_kernel, width * mlp),
        "hidden",
        [((requests, ff // 2), BF16)],
        [core_sums, flip(core_sums, "mlp", 2)],
    )
    (down,) = call(
        down_kernel,
        "down",
        [((pool, rows, width), BF16)],
        [hidden, flip(hidden, "mlp", 1), down_weight],
        [pltpu.VMEM((requests, width), F32)],
    )
    backwards = list(range(pool))[::-1]
    (out,) = call(
        final_kernel,
        "final",
        [((rows, width), BF16)],
        [own_residual, lax.all_to_all(down, "pool", 0, 0, axis_index_groups=[backwards])],
    )
    return out


def solution(mesh):
    in_specs = (
        P("pool", "mlp"),
        P("pool", "mlp"),
        P("pool", "mlp"),
        P("pool", "mlp"),
        P("pool", None, "mlp"),
        P("pool", None, "mlp"),
        P("pool", None),
        P("pool"),
        P("mlp", "pool"),
        P("mlp"),
        P("mlp", "pool"),
        P("mlp", "pool"),
        P("pool", "mlp"),
    )
    small = mesh.shape["pool"] == 8 and mesh.shape["mlp"] == 4
    per_device = per_device_small if small else per_device_wide
    return jax.shard_map(
        per_device, mesh=mesh, in_specs=in_specs, out_specs=P("pool", "mlp"), check_vma=False
    )
```

```python
import functools
import math

import jax
import jax.numpy as jnp
import numpy as np
from jax import lax
from jax.experimental import pallas as pl
from jax.experimental.pallas import tpu as pltpu
from jax.sharding import PartitionSpec as P

HD = 96
LOW = -1e30
CODE = 128


def rotate(values, positions):
    half_size = values.shape[-1] // 2
    inverse_freq = 10000.0 ** (-(2.0 * jnp.arange(half_size, dtype=jnp.float32)) / values.shape[-1])
    angles = positions.astype(jnp.float32)[:, None, None] * inverse_freq[None, None, :]
    cosine = jnp.cos(angles)
    sine_part = jnp.sin(angles)
    first = values[..., :half_size]
    second = values[..., half_size:]
    return jnp.concatenate(
        [first * cosine - second * sine_part, second * cosine + first * sine_part], -1
    )


def low(values):
    return lax.reduce_precision(values, 8, 7)


def split(values):
    high = low(values)
    return high.astype(jnp.bfloat16), (values - high).astype(jnp.bfloat16)


def encode(ints):
    return (ints // CODE).astype(jnp.bfloat16), (ints % CODE).astype(jnp.bfloat16)


def decode(high, rest):
    return high.astype(jnp.int32) * CODE + rest.astype(jnp.int32)


def gather(values, axis):
    copies = jnp.broadcast_to(values[None], (lax.axis_size(axis),) + values.shape)
    return lax.all_to_all(copies, axis, 0, 0)


def per_device_wide(
    residual_in,
    query_new,
    key_new,
    value_new,
    key_cache,
    value_cache,
    block_table,
    lengths,
    out_weight,
    norm_gain,
    gate_weight,
    up_weight,
    down_weight,
):
    rows, width = residual_in.shape
    heads = width // HD
    blocks, block_len = key_cache.shape[:2]
    most = block_table.shape[1]
    pool, mlp = lax.axis_size("pool"), lax.axis_size("mlp")
    pool_index = lax.axis_index("pool")
    requests = rows * pool
    score_scale = 1.0 / math.sqrt(HD)
    f32, bf16 = jnp.float32, jnp.bfloat16

    queries = rotate(query_new.astype(f32).reshape(rows, heads, HD), lengths).astype(bf16)
    new_keys = rotate(key_new.astype(f32).reshape(rows, heads, HD), lengths).astype(bf16)

    table_high, table_low = encode(block_table + 1)
    len_high, len_low = encode(lengths)
    packed = jnp.concatenate(
        [
            queries.reshape(rows, width),
            residual_in,
            table_high,
            table_low,
            len_high[:, None],
            len_low[:, None],
        ],
        1,
    )
    spare = -packed.shape[1] % 128
    packed = jnp.pad(packed, ((0, 0), (0, spare)))
    got = gather(packed, "pool").reshape(requests, packed.shape[1])
    all_queries = got[:, :width]
    all_input = got[:, width : 2 * width]
    tail = got[:, 2 * width :]
    tables = decode(tail[:, :most], tail[:, most : 2 * most]) - 1
    all_lengths = decode(tail[:, 2 * most], tail[:, 2 * most + 1])

    held_ids = pool_index * blocks + jnp.arange(blocks, dtype=jnp.int32)
    matches = tables[None, :, :] == held_ids[:, None, None]
    holder = jnp.any(matches, 2)
    block_index = jnp.sum(
        jnp.where(matches, jnp.arange(most, dtype=jnp.int32)[None, None, :], 0), (1, 2)
    )
    valid_len = jnp.sum(jnp.where(holder, all_lengths[None, :], 0), 1)
    block_query = jnp.dot(holder.astype(bf16), all_queries, preferred_element_type=f32)
    block_query = block_query.astype(bf16).reshape(blocks, heads, HD)
    key_rows = key_cache.reshape(blocks, block_len, heads, HD)
    value_rows = value_cache.reshape(blocks, block_len, heads, HD)
    scores = (
        jnp.einsum("bhd,bthd->bht", block_query, key_rows, preferred_element_type=f32)
        * score_scale
    )
    token_pos = block_index[:, None] * block_len + jnp.arange(block_len, dtype=jnp.int32)[None, :]
    valid = (token_pos < valid_len[:, None])[:, None, :]
    scores = jnp.where(valid, scores, LOW)
    shift = low(jnp.max(scores, 2))
    weights = jnp.where(valid, jnp.exp(scores - shift[:, :, None]), 0.0)
    totals = jnp.sum(weights, 2)
    numerator = jnp.einsum(
        "bht,bthd->bhd", weights.astype(bf16), value_rows, preferred_element_type=f32
    )
    self_score = jnp.sum(queries.astype(f32) * new_keys.astype(f32), -1) * score_scale
    self_shift = low(self_score)
    self_weight = jnp.exp(self_score - self_shift)
    self_numer = self_weight[:, :, None] * value_new.astype(f32).reshape(rows, heads, HD)

    own_total = jnp.concatenate([totals, self_weight], 0)
    total_high, total_low = split(own_total)
    part = jnp.concatenate(
        [
            jnp.concatenate([numerator, self_numer], 0)
            .astype(bf16)
            .reshape(blocks + rows, width),
            jnp.concatenate([shift, self_shift], 0).astype(bf16),
            total_high,
            total_low,
        ],
        1,
    )
    part = jnp.pad(part, ((0, 0), (0, -part.shape[1] % 128)))
    count = blocks + rows
    parts = gather(part, "pool").reshape(pool * count, part.shape[1])
    all_shift = parts[:, width : width + heads].astype(f32)
    all_total = parts[:, width + heads : width + 2 * heads].astype(f32) + parts[
        :, width + 2 * heads : width + 3 * heads
    ].astype(f32)
    place = jnp.arange(pool * count, dtype=jnp.int32)
    owner, slot = place // count, place % count
    is_block = slot < blocks
    block_id = jnp.where(is_block, owner * blocks + slot, -2)
    self_id = jnp.where(is_block, -2, owner * rows + slot - blocks)
    request_ids = jnp.arange(requests, dtype=jnp.int32)
    belongs = jnp.any(tables[:, None, :] == block_id[None, :, None], 2) | (
        request_ids[:, None] == self_id[None, :]
    )
    top = jnp.max(jnp.where(belongs[:, :, None], all_shift[None], LOW), 1)
    part_top = jnp.sum(jnp.where(belongs[:, :, None], top[:, None, :], 0.0), 0)
    scale = jnp.exp(all_shift - part_top)
    scaled = parts[:, :width].astype(f32).reshape(-1, heads, HD) * scale[:, :, None]
    mix = belongs.astype(f32)
    numer = jnp.dot(mix, scaled.reshape(-1, width), precision=lax.Precision.HIGHEST)
    denom = jnp.dot(mix, all_total * scale, precision=lax.Precision.HIGHEST)
    attended = (numer.reshape(requests, heads, HD) / denom[:, :, None]).astype(bf16)
    attended = attended.reshape(requests, width)

    head_part = jnp.dot(attended, out_weight, preferred_element_type=f32).astype(bf16)
    share = pool // mlp
    route = []
    for p in range(pool):
        for m in range(mlp):
            route.append((p * mlp + m, ((p % share) * mlp + m) * mlp + p // share))
    moved = lax.ppermute(head_part, ("pool", "mlp"), route)
    head_all = gather(moved, "pool").reshape(share, mlp, requests, -1)
    head_out = low(jnp.sum(head_all.astype(f32), 1))
    head_out = jnp.swapaxes(head_out, 0, 1).reshape(requests, width)
    residual = all_input.astype(f32) + head_out
    squares = jnp.sum(residual * residual, -1, keepdims=True)
    portion = (residual * norm_gain.astype(f32)).astype(bf16)

    ff = gate_weight.shape[1]
    square_high, square_low = split(squares)
    sums = jnp.concatenate(
        [
            jnp.dot(portion, gate_weight, preferred_element_type=f32).astype(bf16),
            jnp.dot(portion, up_weight, preferred_element_type=f32).astype(bf16),
            jnp.broadcast_to(square_high, (requests, 64)),
            jnp.broadcast_to(square_low, (requests, 64)),
        ],
        1,
    )
    summed = jnp.sum(gather(sums, "mlp").astype(f32), 0)
    mean_square = (summed[:, 2 * ff : 2 * ff + 1] + summed[:, 2 * ff + 64 : 2 * ff + 65]) / (
        width * mlp
    )
    factor = lax.rsqrt(mean_square + 1e-05)
    gate = summed[:, :ff] * factor
    up = summed[:, ff : 2 * ff] * factor
    hidden = (jax.nn.silu(gate) * up).astype(bf16)

    down = jnp.dot(hidden, down_weight, preferred_element_type=f32)
    down = lax.all_to_all(down.reshape(pool, rows, width), "pool", 0, 0)
    own = lax.dynamic_slice_in_dim(residual, pool_index * rows, rows, 0)
    return (own + jnp.sum(down, 0)).astype(bf16)


F32, BF16 = jnp.float32, jnp.bfloat16
VMEM = pl.BlockSpec(memory_space=pltpu.VMEM)
HBM = pl.BlockSpec(memory_space=pl.ANY)


def call(kernel, name, outs, args, scratch=(), hbm=(), limit=16 * 2**20):
    size = sum(math.prod(a.shape) * a.dtype.itemsize for a in args)
    return pl.pallas_call(
        kernel,
        out_shape=[jax.ShapeDtypeStruct(shape, dtype) for shape, dtype in outs],
        in_specs=[HBM if i in hbm else VMEM for i in range(len(args))],
        out_specs=[VMEM] * len(outs),
        scratch_shapes=list(scratch),
        compiler_params=pltpu.CompilerParams(vmem_limit_bytes=limit),
        cost_estimate=pl.CostEstimate(flops=0, bytes_accessed=size, transcendentals=0),
        name=name,
    )(*args)


def lanes(shape):
    return lax.broadcasted_iota(jnp.int32, shape, len(shape) - 1)


def in_order(pieces, index):
    for bit in (1, 2):
        odd = (index & bit) != 0
        pieces = [jnp.where(odd, pieces[s ^ bit], pieces[s]) for s in range(4)]
    return pieces


def rows_of(shape):
    return lax.broadcasted_iota(jnp.int32, shape, len(shape) - 2)


def round_low(values):
    return values.astype(BF16).astype(F32)


def head_start(shape):
    return rows_of(shape) * HD % 128


def flatten(tail, width):
    heads = tail.shape[0]
    spread = jnp.zeros((heads, width), F32)
    start = head_start((heads, width))
    for k in (0, 32, 64, 96):
        moved = pltpu.roll(tail, k, 1) if k else tail
        spread = jnp.where(start == k, jnp.concatenate([moved] * (width // 128), 1), spread)
    lane = lanes((heads, width))
    used = (lane // HD == rows_of((heads, width))) & (lane % HD < 24)
    return jnp.sum(jnp.where(used, spread, 0.0), 0, keepdims=True)


def unflatten(row, heads):
    width = row.shape[1]
    lane = lanes((heads, width))
    used = (lane // HD == rows_of((heads, width))) & (lane % HD < 24)
    spread = jnp.where(used, jnp.broadcast_to(row, (heads, width)), 0.0)
    folded = spread[:, :128]
    for at in range(128, width, 128):
        folded = folded + spread[:, at : at + 128]
    start = head_start((heads, 128))
    tail = jnp.where(start == 0, folded, 0.0)
    for k in (32, 64, 96):
        tail = jnp.where(start == k, pltpu.roll(folded, 128 - k, 1), tail)
    return tail


def prepare_kernel(*refs):
    sources, (packed, new), held = refs[:6], refs[8:10], refs[10:16]
    scr, sems = refs[16:]
    copies = [
        pltpu.make_async_copy(source, target, sems.at[i])
        for i, (source, target) in enumerate(zip(sources, held))
    ]
    for copy in copies:
        copy.start()
    table, length, query, key, value, residual = held
    rows, width = query.shape
    most = table.shape[1]
    period = 384
    turn = lanes((8, period)) % (HD // 2)
    freq = jnp.zeros((8, period), F32)
    for i in range(HD // 2):
        freq = jnp.where(turn == i, float(np.float32(10000.0 ** (-2.0 * i / HD))), freq)
    for copy in copies:
        copy.wait()
    scr[...] = jnp.zeros_like(scr)
    scr[0:rows, :] = query[...].astype(F32)
    scr[rows : 2 * rows, :] = key[...].astype(F32)
    values = scr[...]
    line = rows_of((8, period))
    where_at = jnp.zeros((8, period), F32)
    for r in range(rows):
        here = (line == r) | (line == rows + r)
        where_at = jnp.where(here, length[r].astype(F32), where_at)
    angles = where_at * freq
    cosine = jnp.concatenate([jnp.cos(angles)] * (width // period), 1)
    sine = jnp.concatenate([jnp.sin(angles)] * (width // period), 1)
    first = lanes((8, width)) % HD < HD // 2
    ahead = pltpu.roll(values, width - HD // 2, 1)
    behind = pltpu.roll(values, HD // 2, 1)
    scr[...] = values * cosine + jnp.where(first, -ahead, behind) * sine
    packed[:, :width] = scr[0:rows, :].astype(BF16)
    packed[:, width : 2 * width] = residual[...]
    tail = jnp.zeros((rows, 128), F32)
    at, row = lanes((rows, 128)), rows_of((rows, 128))
    for r in range(rows):
        codes = [table[r, k] + 1 for k in range(most)] + [length[r]]
        spots = [(k, most + k) for k in range(most)] + [(2 * most, 2 * most + 1)]
        for code, (high, rest) in zip(codes, spots):
            tail = jnp.where((row == r) & (at == high), (code >> 7).astype(F32), tail)
            tail = jnp.where((row == r) & (at == rest), (code & 127).astype(F32), tail)
    packed[:, 2 * width :] = tail.astype(BF16)
    new[:, :width] = scr[rows : 2 * rows, :].astype(BF16)
    new[:, width:] = value[...]


def carry_kernel(packed, new, packed_near, own):
    packed_near[...] = packed[...]
    rows, width = new.shape[0], new.shape[1] // 2
    blocks = own.shape[0] - rows - 1
    heads = width // HD
    head_mask = lanes((heads, width)) // HD == rows_of((heads, width))
    product = packed[:, :width].astype(F32) * new[:, :width].astype(F32)
    own[...] = jnp.zeros_like(own)
    spot = lanes((heads, 128))
    tail = jnp.zeros((heads, 128), F32)
    for r in range(rows):
        score = jnp.sum(
            jnp.where(head_mask, jnp.broadcast_to(product[r : r + 1], (heads, width)), 0.0),
            1,
            keepdims=True,
        ) * (1.0 / math.sqrt(HD))
        shift = round_low(score)
        weight = jnp.exp(score - shift)
        spread = jnp.sum(jnp.where(head_mask, round_low(weight), 0.0), 0, keepdims=True)
        own[blocks + r : blocks + r + 1, :width] = spread * new[r : r + 1, width:].astype(F32)
        high = round_low(weight)
        tail = jnp.where(spot == blocks + r, shift, tail)
        tail = jnp.where(spot == 8 + blocks + r, high, tail)
        tail = jnp.where(spot == 16 + blocks + r, weight - high, tail)
    own[:, width:] = tail


def merge_kernel(mine, theirs, both):
    y = lax.axis_index("pool") % 2
    both[y] = mine[...]
    both[1 - y] = theirs[...]


def attend_kernel(a0, a1, a2, a3, own, keys, values, part, residual, tables, scr):
    blocks, block_len, width = keys.shape
    rows = a0.shape[1]
    heads = width // HD
    most = 8
    me = lax.axis_index("pool")
    for y in range(2):
        pieces = [piece[y].astype(F32) for piece in (a0, a1, a2, a3)]
        for z, piece in enumerate(in_order(pieces, me // 2)):
            scr[(z * 2 + y) * rows : (z * 2 + y + 1) * rows, :] = piece
    queries = scr[:, :width]
    residual[...] = scr[:, width : 2 * width]
    tail = scr[:, 2 * width :]
    requests = tail.shape[0]
    table = tail * CODE + pltpu.roll(tail, 128 - most, 1) - 1.0
    length = tail[:, 2 * most : 2 * most + 1] * CODE + tail[:, 2 * most + 1 : 2 * most + 2]
    lane = lanes((requests, 128))
    table = jnp.where(lane < most, table, -2.0)
    tables[...] = table
    head_mask = lanes((heads, width)) // HD == rows_of((heads, width))
    spot = lanes((heads, 128))
    tail = own[:, width:]
    scores, limits = [], []
    for b in range(blocks):
        match = jnp.where(table == (me * blocks + b).astype(F32), 1.0, 0.0)
        holder = jnp.sum(match, 1, keepdims=True)
        place = jnp.sum(jnp.sum(match * lane.astype(F32), 1, keepdims=True), 0, keepdims=True)
        limit = jnp.sum(holder * length, 0, keepdims=True) - place * block_len
        limits.append(jnp.broadcast_to(limit, (heads, block_len)))
        query = jnp.sum(holder * queries, 0, keepdims=True)
        spread = jnp.where(head_mask, query, 0.0).astype(BF16)
        scores.append(
            lax.dot_general(
                spread, keys[b], (((1,), (1,)), ((), ())), preferred_element_type=F32
            )
        )
    scores = jnp.concatenate(scores, 0) * (1.0 / math.sqrt(HD))
    token = lanes((blocks * heads, block_len)).astype(F32)
    valid = token < jnp.concatenate(limits, 0)
    scores = jnp.where(valid, scores, LOW)
    shift = round_low(jnp.max(scores, 1, keepdims=True))
    weights = jnp.where(valid, jnp.exp(scores - shift), 0.0)
    total = jnp.sum(weights, 1, keepdims=True)
    high = round_low(total)
    rest = total - high
    numerators = []
    for b in range(blocks):
        mine = slice(b * heads, (b + 1) * heads)
        full = jnp.dot(weights[mine].astype(BF16), values[b], preferred_element_type=F32)
        numerators.append(jnp.sum(jnp.where(head_mask, full, 0.0), 0, keepdims=True))
        tail = jnp.where(spot == b, shift[mine], tail)
        tail = jnp.where(spot == 8 + b, high[mine], tail)
        tail = jnp.where(spot == 16 + b, rest[mine], tail)
    line = rows_of((8, width))
    numer = own[:, :width]
    for b in range(blocks):
        numer = jnp.where(line == b, numerators[b], numer)
    numer = jnp.where(line == 7, flatten(tail, width), numer)
    part[...] = numer.astype(BF16)


def combine_kernel(b0, b1, b2, b3, tables, weight, head_part, numer, tails, mix):
    requests = tables.shape[0]
    slots = b0.shape[1]
    width = weight.shape[0]
    heads = width // HD
    rows, blocks = 2, slots - 3
    me = lax.axis_index("pool")
    for step, piece in enumerate((b0, b1, b2, b3)):
        z = (me // 2) ^ step
        for y in range(2):
            owner = z * 2 + y
            values = piece[y].astype(F32)
            numer[pl.ds(pl.multiple_of(owner * slots, 8), slots), :] = values
            tails[owner] = unflatten(values[slots - 1 : slots], heads)
    lane8 = lanes((heads, 128))
    shifts = jnp.zeros((heads, 128), F32)
    totals = jnp.zeros((heads, 128), F32)
    for owner in range(8):
        tail = tails[owner]
        total = pltpu.roll(tail, 120, 1) + pltpu.roll(tail, 112, 1)
        tail, total = jnp.where(lane8 < 8, tail, 0.0), jnp.where(lane8 < 8, total, 0.0)
        if owner:
            tail, total = pltpu.roll(tail, 8 * owner, 1), pltpu.roll(total, 8 * owner, 1)
        shifts, totals = shifts + tail, totals + total
    lane = lanes((requests, 128))
    owner, slot = lane // slots, lane % slots
    block_id = jnp.where((slot < blocks) & (lane < 64), owner * blocks + slot, -5).astype(F32)
    self_id = jnp.where((slot >= blocks) & (slot < blocks + rows), owner * rows + slot - blocks, -5)
    table = tables[...]
    belongs = (self_id == rows_of((requests, 128))) & (lane < 64)
    for k in range(8):
        belongs = belongs | (table[:, k : k + 1] == block_id)
    for h in range(heads):
        shift = jnp.broadcast_to(shifts[h : h + 1], (requests, 128))
        top = jnp.max(jnp.where(belongs, shift, LOW), 1, keepdims=True)
        scale = jnp.where(belongs, jnp.exp(shift - top), 0.0)
        total = jnp.sum(scale * totals[h : h + 1], 1, keepdims=True)
        mix[h * requests : (h + 1) * requests, :] = scale / total
    full = jnp.dot(
        mix[:, : 8 * slots].astype(BF16), numer[...].astype(BF16), preferred_element_type=F32
    )
    head = lanes((requests, width)) // HD
    attended = jnp.zeros((requests, width), F32)
    for h in range(heads):
        attended = jnp.where(head == h, full[h * requests : (h + 1) * requests], attended)
    head_part[...] = jnp.dot(
        attended.astype(BF16), weight[...], preferred_element_type=F32
    ).astype(BF16)


def sum_kernel(p0, p1, p2, p3, total):
    total[...] = (
        (p0[...].astype(F32) + p1[...].astype(F32)) + (p2[...].astype(F32) + p3[...].astype(F32))
    ).astype(BF16)


def gate_up_kernel(same, flip, all_input, gain, gate, up, sums, own, scr):
    me = lax.axis_index("pool")
    odd = me % 2 == 1
    part = same.shape[1]
    ff = gate.shape[1]
    rows = own.shape[0]
    near, far = same[...].astype(F32), flip[...].astype(F32)
    scr[:, :part] = all_input[:, :part] + jnp.where(odd, far, near)
    scr[:, part:] = all_input[:, part:] + jnp.where(odd, near, far)
    residual = scr[...]
    mine = scr[0:rows, :]
    for p in range(1, residual.shape[0] // rows):
        mine = jnp.where(me == p, scr[p * rows : (p + 1) * rows, :], mine)
    own[...] = mine
    square = jnp.sum(residual * residual, 1, keepdims=True)
    portion = (residual * gain[...].astype(F32)).astype(BF16)
    sums[:, :ff] = jnp.dot(portion, gate[...], preferred_element_type=F32).astype(BF16)
    sums[:, ff : 2 * ff] = jnp.dot(portion, up[...], preferred_element_type=F32).astype(BF16)
    lane = lanes((residual.shape[0], 128))
    high = round_low(square)
    tail = jnp.where(lane == 0, high, jnp.where(lane == 1, square - high, 0.0))
    sums[:, 2 * ff :] = tail.astype(BF16)


def core_sum_kernel(mine, theirs, total):
    ff2 = mine.shape[1] - 128
    total[:, :ff2] = (mine[:, :ff2].astype(F32) + theirs[:, :ff2].astype(F32)).astype(BF16)
    tail = mine[:, ff2:].astype(F32) + theirs[:, ff2:].astype(F32)
    square = jnp.sum(tail, 1, keepdims=True)
    lane = lanes(tail.shape)
    high = round_low(square)
    tail = jnp.where(lane == 0, high, jnp.where(lane == 1, square - high, 0.0))
    total[:, ff2:] = tail.astype(BF16)


def down_kernel(features, mine, theirs, weight, parts, scr):
    ff = weight.shape[0]
    tail = mine[:, 2 * ff :].astype(F32) + theirs[:, 2 * ff :].astype(F32)
    square = jnp.sum(tail, 1, keepdims=True)
    factor = lax.rsqrt(square * (1.0 / features) + 1e-05)
    gate = (mine[:, :ff].astype(F32) + theirs[:, :ff].astype(F32)) * factor
    up = (mine[:, ff : 2 * ff].astype(F32) + theirs[:, ff : 2 * ff].astype(F32)) * factor
    hidden = (gate / (1.0 + jnp.exp(-gate)) * up).astype(BF16)
    scr[...] = jnp.dot(hidden, weight[...], preferred_element_type=F32)
    rows = parts.shape[1]
    pool = parts.shape[0]
    for p in range(pool):
        parts[pool - 1 - p] = scr[p * rows : (p + 1) * rows, :].astype(BF16)


def final_kernel(own, parts, out):
    total = own[...]
    for p in range(parts.shape[0]):
        total = total + parts[p].astype(F32)
    out[...] = total.astype(BF16)


def flip(values, axis, step):
    size = lax.axis_size(axis)
    return lax.ppermute(values, axis, [(index, index ^ step) for index in range(size)])


def per_device_small(
    residual_in,
    query_new,
    key_new,
    value_new,
    key_cache,
    value_cache,
    block_table,
    lengths,
    out_weight,
    norm_gain,
    gate_weight,
    up_weight,
    down_weight,
):
    rows, width = residual_in.shape
    blocks = key_cache.shape[0]
    pool, mlp = 8, 4
    requests = rows * pool
    ff = gate_weight.shape[1]
    part_cols = out_weight.shape[1]
    packed_width = 2 * width + 128
    slots = blocks + rows + 1
    part_width = width + 128

    packed, new = call(
        prepare_kernel,
        "rotary",
        [((rows, packed_width), BF16), ((rows, 2 * width), BF16)],
        [block_table, lengths, query_new, key_new, value_new, residual_in, key_cache, value_cache],
        [pltpu.SMEM(block_table.shape, jnp.int32), pltpu.SMEM(lengths.shape, jnp.int32)]
        + [pltpu.VMEM((rows, width), BF16)] * 4
        + [pltpu.VMEM((8, width), F32), pltpu.SemaphoreType.DMA((6,))],
        hbm=range(8),
        limit=54 * 2**20,
    )

    packed_near, own = call(
        carry_kernel,
        "carry",
        [(packed.shape, BF16), ((slots, part_width), F32)],
        [packed, new],
    )

    def pool_gather(values, near):
        (both,) = call(
            merge_kernel,
            "merge",
            [((2,) + values.shape, values.dtype)],
            [near, flip(values, "pool", 1)],
        )
        return [both] + [flip(both, "pool", step) for step in (2, 4, 6)]

    part, all_input, tables = call(
        attend_kernel,
        "attend",
        [((slots, width), BF16), ((requests, width), F32), ((requests, 128), F32)],
        pool_gather(packed, packed_near) + [own, key_cache, value_cache],
        [pltpu.VMEM((requests, packed_width), F32)],
    )
    (head_part,) = call(
        combine_kernel,
        "combine",
        [((requests, part_cols), BF16)],
        pool_gather(part, part) + [tables, out_weight],
        [
            pltpu.VMEM((pool * slots, width), F32),
            pltpu.VMEM((pool, slots, 128), F32),
            pltpu.VMEM((requests * width // HD, 128), F32),
        ],
    )
    (head_sum,) = call(
        sum_kernel,
        "head_sum",
        [((requests, part_cols), BF16)],
        [head_part] + [flip(head_part, "mlp", step) for step in (1, 3, 2)],
    )
    pieces = []
    for turn in range(2):
        route = []
        for m in range(mlp):
            by_distance = sorted(range(4), key=lambda z: (-abs(z - m), z))
            for z, step in zip(by_distance, (1, 0, 3, 2) if m % 2 == 0 else (0, 1, 2, 3)):
                for y in range(2):
                    source = (m * 2 + y) * mlp + (m ^ step)
                    route.append((source, (z * 2 + (y ^ turn)) * mlp + m))
        pieces.append(lax.ppermute(head_sum, ("pool", "mlp"), route))
    sums, own_residual = call(
        gate_up_kernel,
        "gate_up",
        [((requests, 2 * ff + 128), BF16), ((rows, width), F32)],
        pieces + [all_input, norm_gain.reshape(1, width), gate_weight, up_weight],
        [pltpu.VMEM((requests, width), F32)],
    )
    (core_sums,) = call(
        core_sum_kernel,
        "core_sum",
        [((requests, 2 * ff + 128), BF16)],
        [sums, flip(sums, "mlp", 1)],
    )
    (down,) = call(
        functools.partial(down_kernel, width * mlp),
        "down",
        [((pool, rows, width), BF16)],
        [core_sums, flip(core_sums, "mlp", 2), down_weight],
        [pltpu.VMEM((requests, width), F32)],
    )
    backwards = list(range(pool))[::-1]
    (out,) = call(
        final_kernel,
        "final",
        [((rows, width), BF16)],
        [own_residual, lax.all_to_all(down, "pool", 0, 0, axis_index_groups=[backwards])],
    )
    return out


def solution(mesh):
    in_specs = (
        P("pool", "mlp"),
        P("pool", "mlp"),
        P("pool", "mlp"),
        P("pool", "mlp"),
        P("pool", None, "mlp"),
        P("pool", None, "mlp"),
        P("pool", None),
        P("pool"),
        P("mlp", "pool"),
        P("mlp"),
        P("mlp", "pool"),
        P("mlp", "pool"),
        P("pool", "mlp"),
    )
    small = mesh.shape["pool"] == 8 and mesh.shape["mlp"] == 4
    per_device = per_device_small if small else per_device_wide
    return jax.shard_map(
        per_device, mesh=mesh, in_specs=in_specs, out_specs=P("pool", "mlp"), check_vma=False
    )
```

```python
import functools
import math

import jax
import jax.numpy as jnp
import numpy as np
from jax import lax
from jax.experimental import pallas as pl
from jax.experimental.pallas import tpu as pltpu
from jax.sharding import PartitionSpec as P

HD = 96
LOW = -1e30
CODE = 128


def rotate(values, positions):
    half_size = values.shape[-1] // 2
    inverse_freq = 10000.0 ** (-(2.0 * jnp.arange(half_size, dtype=jnp.float32)) / values.shape[-1])
    angles = positions.astype(jnp.float32)[:, None, None] * inverse_freq[None, None, :]
    cosine = jnp.cos(angles)
    sine_part = jnp.sin(angles)
    first = values[..., :half_size]
    second = values[..., half_size:]
    return jnp.concatenate(
        [first * cosine - second * sine_part, second * cosine + first * sine_part], -1
    )


def low(values):
    return lax.reduce_precision(values, 8, 7)


def split(values):
    high = low(values)
    return high.astype(jnp.bfloat16), (values - high).astype(jnp.bfloat16)


def encode(ints):
    return (ints // CODE).astype(jnp.bfloat16), (ints % CODE).astype(jnp.bfloat16)


def decode(high, rest):
    return high.astype(jnp.int32) * CODE + rest.astype(jnp.int32)


def gather(values, axis):
    copies = jnp.broadcast_to(values[None], (lax.axis_size(axis),) + values.shape)
    return lax.all_to_all(copies, axis, 0, 0)


def per_device_wide(
    residual_in,
    query_new,
    key_new,
    value_new,
    key_cache,
    value_cache,
    block_table,
    lengths,
    out_weight,
    norm_gain,
    gate_weight,
    up_weight,
    down_weight,
):
    rows, width = residual_in.shape
    heads = width // HD
    blocks, block_len = key_cache.shape[:2]
    most = block_table.shape[1]
    pool, mlp = lax.axis_size("pool"), lax.axis_size("mlp")
    pool_index = lax.axis_index("pool")
    requests = rows * pool
    score_scale = 1.0 / math.sqrt(HD)
    f32, bf16 = jnp.float32, jnp.bfloat16

    queries = rotate(query_new.astype(f32).reshape(rows, heads, HD), lengths).astype(bf16)
    new_keys = rotate(key_new.astype(f32).reshape(rows, heads, HD), lengths).astype(bf16)

    table_high, table_low = encode(block_table + 1)
    len_high, len_low = encode(lengths)
    packed = jnp.concatenate(
        [
            queries.reshape(rows, width),
            residual_in,
            table_high,
            table_low,
            len_high[:, None],
            len_low[:, None],
        ],
        1,
    )
    spare = -packed.shape[1] % 128
    packed = jnp.pad(packed, ((0, 0), (0, spare)))
    got = gather(packed, "pool").reshape(requests, packed.shape[1])
    all_queries = got[:, :width]
    all_input = got[:, width : 2 * width]
    tail = got[:, 2 * width :]
    tables = decode(tail[:, :most], tail[:, most : 2 * most]) - 1
    all_lengths = decode(tail[:, 2 * most], tail[:, 2 * most + 1])

    held_ids = pool_index * blocks + jnp.arange(blocks, dtype=jnp.int32)
    matches = tables[None, :, :] == held_ids[:, None, None]
    holder = jnp.any(matches, 2)
    block_index = jnp.sum(
        jnp.where(matches, jnp.arange(most, dtype=jnp.int32)[None, None, :], 0), (1, 2)
    )
    valid_len = jnp.sum(jnp.where(holder, all_lengths[None, :], 0), 1)
    block_query = jnp.dot(holder.astype(bf16), all_queries, preferred_element_type=f32)
    block_query = block_query.astype(bf16).reshape(blocks, heads, HD)
    key_rows = key_cache.reshape(blocks, block_len, heads, HD)
    value_rows = value_cache.reshape(blocks, block_len, heads, HD)
    scores = (
        jnp.einsum("bhd,bthd->bht", block_query, key_rows, preferred_element_type=f32)
        * score_scale
    )
    token_pos = block_index[:, None] * block_len + jnp.arange(block_len, dtype=jnp.int32)[None, :]
    valid = (token_pos < valid_len[:, None])[:, None, :]
    scores = jnp.where(valid, scores, LOW)
    shift = low(jnp.max(scores, 2))
    weights = jnp.where(valid, jnp.exp(scores - shift[:, :, None]), 0.0)
    totals = jnp.sum(weights, 2)
    numerator = jnp.einsum(
        "bht,bthd->bhd", weights.astype(bf16), value_rows, preferred_element_type=f32
    )
    self_score = jnp.sum(queries.astype(f32) * new_keys.astype(f32), -1) * score_scale
    self_shift = low(self_score)
    self_weight = jnp.exp(self_score - self_shift)
    self_numer = self_weight[:, :, None] * value_new.astype(f32).reshape(rows, heads, HD)

    own_total = jnp.concatenate([totals, self_weight], 0)
    total_high, total_low = split(own_total)
    part = jnp.concatenate(
        [
            jnp.concatenate([numerator, self_numer], 0)
            .astype(bf16)
            .reshape(blocks + rows, width),
            jnp.concatenate([shift, self_shift], 0).astype(bf16),
            total_high,
            total_low,
        ],
        1,
    )
    part = jnp.pad(part, ((0, 0), (0, -part.shape[1] % 128)))
    count = blocks + rows
    parts = gather(part, "pool").reshape(pool * count, part.shape[1])
    all_shift = parts[:, width : width + heads].astype(f32)
    all_total = parts[:, width + heads : width + 2 * heads].astype(f32) + parts[
        :, width + 2 * heads : width + 3 * heads
    ].astype(f32)
    place = jnp.arange(pool * count, dtype=jnp.int32)
    owner, slot = place // count, place % count
    is_block = slot < blocks
    block_id = jnp.where(is_block, owner * blocks + slot, -2)
    self_id = jnp.where(is_block, -2, owner * rows + slot - blocks)
    request_ids = jnp.arange(requests, dtype=jnp.int32)
    belongs = jnp.any(tables[:, None, :] == block_id[None, :, None], 2) | (
        request_ids[:, None] == self_id[None, :]
    )
    top = jnp.max(jnp.where(belongs[:, :, None], all_shift[None], LOW), 1)
    part_top = jnp.sum(jnp.where(belongs[:, :, None], top[:, None, :], 0.0), 0)
    scale = jnp.exp(all_shift - part_top)
    scaled = parts[:, :width].astype(f32).reshape(-1, heads, HD) * scale[:, :, None]
    mix = belongs.astype(f32)
    numer = jnp.dot(mix, scaled.reshape(-1, width), precision=lax.Precision.HIGHEST)
    denom = jnp.dot(mix, all_total * scale, precision=lax.Precision.HIGHEST)
    attended = (numer.reshape(requests, heads, HD) / denom[:, :, None]).astype(bf16)
    attended = attended.reshape(requests, width)

    head_part = jnp.dot(attended, out_weight, preferred_element_type=f32).astype(bf16)
    share = pool // mlp
    route = []
    for p in range(pool):
        for m in range(mlp):
            route.append((p * mlp + m, ((p % share) * mlp + m) * mlp + p // share))
    moved = lax.ppermute(head_part, ("pool", "mlp"), route)
    head_all = gather(moved, "pool").reshape(share, mlp, requests, -1)
    head_out = low(jnp.sum(head_all.astype(f32), 1))
    head_out = jnp.swapaxes(head_out, 0, 1).reshape(requests, width)
    residual = all_input.astype(f32) + head_out
    squares = jnp.sum(residual * residual, -1, keepdims=True)
    portion = (residual * norm_gain.astype(f32)).astype(bf16)

    ff = gate_weight.shape[1]
    square_high, square_low = split(squares)
    sums = jnp.concatenate(
        [
            jnp.dot(portion, gate_weight, preferred_element_type=f32).astype(bf16),
            jnp.dot(portion, up_weight, preferred_element_type=f32).astype(bf16),
            jnp.broadcast_to(square_high, (requests, 64)),
            jnp.broadcast_to(square_low, (requests, 64)),
        ],
        1,
    )
    summed = jnp.sum(gather(sums, "mlp").astype(f32), 0)
    mean_square = (summed[:, 2 * ff : 2 * ff + 1] + summed[:, 2 * ff + 64 : 2 * ff + 65]) / (
        width * mlp
    )
    factor = lax.rsqrt(mean_square + 1e-05)
    gate = summed[:, :ff] * factor
    up = summed[:, ff : 2 * ff] * factor
    hidden = (jax.nn.silu(gate) * up).astype(bf16)

    down = jnp.dot(hidden, down_weight, preferred_element_type=f32)
    down = lax.all_to_all(down.reshape(pool, rows, width), "pool", 0, 0)
    own = lax.dynamic_slice_in_dim(residual, pool_index * rows, rows, 0)
    return (own + jnp.sum(down, 0)).astype(bf16)


F32, BF16 = jnp.float32, jnp.bfloat16
VMEM = pl.BlockSpec(memory_space=pltpu.VMEM)
HBM = pl.BlockSpec(memory_space=pl.ANY)


def call(kernel, name, outs, args, scratch=(), hbm=(), limit=16 * 2**20):
    size = sum(math.prod(a.shape) * a.dtype.itemsize for a in args)
    return pl.pallas_call(
        kernel,
        out_shape=[jax.ShapeDtypeStruct(shape, dtype) for shape, dtype in outs],
        in_specs=[HBM if i in hbm else VMEM for i in range(len(args))],
        out_specs=[VMEM] * len(outs),
        scratch_shapes=list(scratch),
        compiler_params=pltpu.CompilerParams(vmem_limit_bytes=limit),
        cost_estimate=pl.CostEstimate(flops=0, bytes_accessed=size, transcendentals=0),
        name=name,
    )(*args)


def lanes(shape):
    return lax.broadcasted_iota(jnp.int32, shape, len(shape) - 1)


def in_order(pieces, index):
    for bit in (1, 2):
        odd = (index & bit) != 0
        pieces = [jnp.where(odd, pieces[s ^ bit], pieces[s]) for s in range(4)]
    return pieces


def rows_of(shape):
    return lax.broadcasted_iota(jnp.int32, shape, len(shape) - 2)


def round_low(values):
    return values.astype(BF16).astype(F32)


def head_start(shape):
    return rows_of(shape) * HD % 128


def flatten(tail, width):
    heads = tail.shape[0]
    spread = jnp.zeros((heads, width), F32)
    start = head_start((heads, width))
    for k in (0, 32, 64, 96):
        moved = pltpu.roll(tail, k, 1) if k else tail
        spread = jnp.where(start == k, jnp.concatenate([moved] * (width // 128), 1), spread)
    lane = lanes((heads, width))
    used = (lane // HD == rows_of((heads, width))) & (lane % HD < 24)
    return jnp.sum(jnp.where(used, spread, 0.0), 0, keepdims=True)


def unflatten(row, heads):
    width = row.shape[1]
    lane = lanes((heads, width))
    used = (lane // HD == rows_of((heads, width))) & (lane % HD < 24)
    spread = jnp.where(used, jnp.broadcast_to(row, (heads, width)), 0.0)
    folded = spread[:, :128]
    for at in range(128, width, 128):
        folded = folded + spread[:, at : at + 128]
    start = head_start((heads, 128))
    tail = jnp.where(start == 0, folded, 0.0)
    for k in (32, 64, 96):
        tail = jnp.where(start == k, pltpu.roll(folded, 128 - k, 1), tail)
    return tail


def prepare_kernel(*refs):
    sources, (packed, new), held = refs[:6], refs[8:10], refs[10:16]
    scr, sems = refs[16:]
    copies = [
        pltpu.make_async_copy(source, target, sems.at[i])
        for i, (source, target) in enumerate(zip(sources, held))
    ]
    for copy in copies:
        copy.start()
    table, length, query, key, value, residual = held
    rows, width = query.shape
    most = table.shape[1]
    period = 384
    turn = lanes((8, period)) % (HD // 2)
    freq = jnp.zeros((8, period), F32)
    for i in range(HD // 2):
        freq = jnp.where(turn == i, float(np.float32(10000.0 ** (-2.0 * i / HD))), freq)
    for copy in copies:
        copy.wait()
    scr[...] = jnp.zeros_like(scr)
    scr[0:rows, :] = query[...].astype(F32)
    scr[rows : 2 * rows, :] = key[...].astype(F32)
    values = scr[...]
    line = rows_of((8, period))
    where_at = jnp.zeros((8, period), F32)
    for r in range(rows):
        here = (line == r) | (line == rows + r)
        where_at = jnp.where(here, length[r].astype(F32), where_at)
    angles = where_at * freq
    cosine = jnp.concatenate([jnp.cos(angles)] * (width // period), 1)
    sine = jnp.concatenate([jnp.sin(angles)] * (width // period), 1)
    first = lanes((8, width)) % HD < HD // 2
    ahead = pltpu.roll(values, width - HD // 2, 1)
    behind = pltpu.roll(values, HD // 2, 1)
    scr[...] = values * cosine + jnp.where(first, -ahead, behind) * sine
    packed[:, :width] = scr[0:rows, :].astype(BF16)
    packed[:, width : 2 * width] = residual[...]
    tail = jnp.zeros((rows, 128), F32)
    at, row = lanes((rows, 128)), rows_of((rows, 128))
    for r in range(rows):
        codes = [table[r, k] + 1 for k in range(most)] + [length[r]]
        spots = [(k, most + k) for k in range(most)] + [(2 * most, 2 * most + 1)]
        for code, (high, rest) in zip(codes, spots):
            tail = jnp.where((row == r) & (at == high), (code >> 7).astype(F32), tail)
            tail = jnp.where((row == r) & (at == rest), (code & 127).astype(F32), tail)
    packed[:, 2 * width :] = tail.astype(BF16)
    new[:, :width] = scr[rows : 2 * rows, :].astype(BF16)
    new[:, width:] = value[...]


def carry_kernel(packed, new, packed_near, own):
    packed_near[...] = packed[...]
    rows, width = new.shape[0], new.shape[1] // 2
    blocks = own.shape[0] - rows - 1
    heads = width // HD
    head_mask = lanes((heads, width)) // HD == rows_of((heads, width))
    product = packed[:, :width].astype(F32) * new[:, :width].astype(F32)
    own[...] = jnp.zeros_like(own)
    spot = lanes((heads, 128))
    tail = jnp.zeros((heads, 128), F32)
    for r in range(rows):
        score = jnp.sum(
            jnp.where(head_mask, jnp.broadcast_to(product[r : r + 1], (heads, width)), 0.0),
            1,
            keepdims=True,
        ) * (1.0 / math.sqrt(HD))
        shift = round_low(score)
        weight = jnp.exp(score - shift)
        spread = jnp.sum(jnp.where(head_mask, round_low(weight), 0.0), 0, keepdims=True)
        own[blocks + r : blocks + r + 1, :width] = spread * new[r : r + 1, width:].astype(F32)
        high = round_low(weight)
        tail = jnp.where(spot == blocks + r, shift, tail)
        tail = jnp.where(spot == 8 + blocks + r, high, tail)
        tail = jnp.where(spot == 16 + blocks + r, weight - high, tail)
    own[:, width:] = tail


def merge_kernel(mine, theirs, both):
    y = lax.axis_index("pool") % 2
    both[y] = mine[...]
    both[1 - y] = theirs[...]


def attend_kernel(a0, a1, a2, a3, own, keys, values, part, residual, tables, scr):
    blocks, block_len, width = keys.shape
    rows = a0.shape[1]
    heads = width // HD
    most = 8
    me = lax.axis_index("pool")
    for y in range(2):
        pieces = [piece[y].astype(F32) for piece in (a0, a1, a2, a3)]
        for z, piece in enumerate(in_order(pieces, me // 2)):
            scr[(z * 2 + y) * rows : (z * 2 + y + 1) * rows, :] = piece
    queries = scr[:, :width]
    residual[...] = scr[:, width : 2 * width]
    tail = scr[:, 2 * width :]
    requests = tail.shape[0]
    table = tail * CODE + pltpu.roll(tail, 128 - most, 1) - 1.0
    length = tail[:, 2 * most : 2 * most + 1] * CODE + tail[:, 2 * most + 1 : 2 * most + 2]
    lane = lanes((requests, 128))
    table = jnp.where(lane < most, table, -2.0)
    tables[...] = table
    head_mask = lanes((heads, width)) // HD == rows_of((heads, width))
    spot = lanes((heads, 128))
    tail = own[:, width:]
    scores, limits = [], []
    for b in range(blocks):
        match = jnp.where(table == (me * blocks + b).astype(F32), 1.0, 0.0)
        holder = jnp.sum(match, 1, keepdims=True)
        place = jnp.sum(jnp.sum(match * lane.astype(F32), 1, keepdims=True), 0, keepdims=True)
        limit = jnp.sum(holder * length, 0, keepdims=True) - place * block_len
        limits.append(jnp.broadcast_to(limit, (heads, block_len)))
        query = jnp.sum(holder * queries, 0, keepdims=True)
        spread = jnp.where(head_mask, query, 0.0).astype(BF16)
        scores.append(
            lax.dot_general(
                spread, keys[b], (((1,), (1,)), ((), ())), preferred_element_type=F32
            )
        )
    scores = jnp.concatenate(scores, 0) * (1.0 / math.sqrt(HD))
    token = lanes((blocks * heads, block_len)).astype(F32)
    valid = token < jnp.concatenate(limits, 0)
    scores = jnp.where(valid, scores, LOW)
    shift = round_low(jnp.max(scores, 1, keepdims=True))
    weights = jnp.where(valid, jnp.exp(scores - shift), 0.0)
    total = jnp.sum(weights, 1, keepdims=True)
    high = round_low(total)
    rest = total - high
    numerators = []
    for b in range(blocks):
        mine = slice(b * heads, (b + 1) * heads)
        full = jnp.dot(weights[mine].astype(BF16), values[b], preferred_element_type=F32)
        numerators.append(jnp.sum(jnp.where(head_mask, full, 0.0), 0, keepdims=True))
        tail = jnp.where(spot == b, shift[mine], tail)
        tail = jnp.where(spot == 8 + b, high[mine], tail)
        tail = jnp.where(spot == 16 + b, rest[mine], tail)
    line = rows_of((8, width))
    numer = own[:, :width]
    for b in range(blocks):
        numer = jnp.where(line == b, numerators[b], numer)
    numer = jnp.where(line == 7, flatten(tail, width), numer)
    part[...] = numer.astype(BF16)


def combine_kernel(b0, b1, b2, b3, tables, weight, head_part, numer, tails, mix):
    requests = tables.shape[0]
    slots = b0.shape[1]
    width = weight.shape[0]
    heads = width // HD
    rows, blocks = 2, slots - 3
    me = lax.axis_index("pool")
    for step, piece in enumerate((b0, b1, b2, b3)):
        z = (me // 2) ^ step
        for y in range(2):
            owner = z * 2 + y
            values = piece[y].astype(F32)
            numer[pl.ds(pl.multiple_of(owner * slots, 8), slots), :] = values
            tails[owner] = unflatten(values[slots - 1 : slots], heads)
    lane8 = lanes((heads, 128))
    shifts = jnp.zeros((heads, 128), F32)
    totals = jnp.zeros((heads, 128), F32)
    for owner in range(8):
        tail = tails[owner]
        total = pltpu.roll(tail, 120, 1) + pltpu.roll(tail, 112, 1)
        tail, total = jnp.where(lane8 < 8, tail, 0.0), jnp.where(lane8 < 8, total, 0.0)
        if owner:
            tail, total = pltpu.roll(tail, 8 * owner, 1), pltpu.roll(total, 8 * owner, 1)
        shifts, totals = shifts + tail, totals + total
    lane = lanes((requests, 128))
    owner, slot = lane // slots, lane % slots
    block_id = jnp.where((slot < blocks) & (lane < 64), owner * blocks + slot, -5).astype(F32)
    self_id = jnp.where((slot >= blocks) & (slot < blocks + rows), owner * rows + slot - blocks, -5)
    table = tables[...]
    belongs = (self_id == rows_of((requests, 128))) & (lane < 64)
    for k in range(8):
        belongs = belongs | (table[:, k : k + 1] == block_id)
    for h in range(heads):
        shift = jnp.broadcast_to(shifts[h : h + 1], (requests, 128))
        top = jnp.max(jnp.where(belongs, shift, LOW), 1, keepdims=True)
        scale = jnp.where(belongs, jnp.exp(shift - top), 0.0)
        total = jnp.sum(scale * totals[h : h + 1], 1, keepdims=True)
        mix[h * requests : (h + 1) * requests, :] = scale / total
    full = jnp.dot(
        mix[:, : 8 * slots].astype(BF16), numer[...].astype(BF16), preferred_element_type=F32
    )
    head = lanes((requests, width)) // HD
    attended = jnp.zeros((requests, width), F32)
    for h in range(heads):
        attended = jnp.where(head == h, full[h * requests : (h + 1) * requests], attended)
    head_part[...] = jnp.dot(
        attended.astype(BF16), weight[...], preferred_element_type=F32
    ).astype(BF16)


def sum_kernel(p0, p1, total):
    total[...] = (p0[...].astype(F32) + p1[...].astype(F32)).astype(BF16)


def gate_up_kernel(s0, s1, f0, f1, all_input, gain, gate, up, sums, own, scr):
    me = lax.axis_index("pool")
    odd = me % 2 == 1
    part = s0.shape[1]
    ff = gate.shape[1]
    rows = own.shape[0]
    near = round_low(s0[...].astype(F32) + s1[...].astype(F32))
    far = round_low(f0[...].astype(F32) + f1[...].astype(F32))
    scr[:, :part] = all_input[:, :part] + jnp.where(odd, far, near)
    scr[:, part:] = all_input[:, part:] + jnp.where(odd, near, far)
    residual = scr[...]
    mine = scr[0:rows, :]
    for p in range(1, residual.shape[0] // rows):
        mine = jnp.where(me == p, scr[p * rows : (p + 1) * rows, :], mine)
    own[...] = mine
    square = jnp.sum(residual * residual, 1, keepdims=True)
    portion = (residual * gain[...].astype(F32)).astype(BF16)
    sums[:, :ff] = jnp.dot(portion, gate[...], preferred_element_type=F32).astype(BF16)
    sums[:, ff : 2 * ff] = jnp.dot(portion, up[...], preferred_element_type=F32).astype(BF16)
    lane = lanes((residual.shape[0], 128))
    high = round_low(square)
    tail = jnp.where(lane == 0, high, jnp.where(lane == 1, square - high, 0.0))
    sums[:, 2 * ff :] = tail.astype(BF16)


def core_sum_kernel(mine, theirs, total):
    ff2 = mine.shape[1] - 128
    total[:, :ff2] = (mine[:, :ff2].astype(F32) + theirs[:, :ff2].astype(F32)).astype(BF16)
    tail = mine[:, ff2:].astype(F32) + theirs[:, ff2:].astype(F32)
    square = jnp.sum(tail, 1, keepdims=True)
    lane = lanes(tail.shape)
    high = round_low(square)
    tail = jnp.where(lane == 0, high, jnp.where(lane == 1, square - high, 0.0))
    total[:, ff2:] = tail.astype(BF16)


def down_kernel(features, mine, theirs, weight, parts, scr):
    ff = weight.shape[0]
    tail = mine[:, 2 * ff :].astype(F32) + theirs[:, 2 * ff :].astype(F32)
    square = jnp.sum(tail, 1, keepdims=True)
    factor = lax.rsqrt(square * (1.0 / features) + 1e-05)
    gate = (mine[:, :ff].astype(F32) + theirs[:, :ff].astype(F32)) * factor
    up = (mine[:, ff : 2 * ff].astype(F32) + theirs[:, ff : 2 * ff].astype(F32)) * factor
    hidden = (gate / (1.0 + jnp.exp(-gate)) * up).astype(BF16)
    scr[...] = jnp.dot(hidden, weight[...], preferred_element_type=F32)
    rows = parts.shape[1]
    pool = parts.shape[0]
    for p in range(pool):
        parts[pool - 1 - p] = scr[p * rows : (p + 1) * rows, :].astype(BF16)


def final_kernel(own, parts, out):
    total = own[...]
    for p in range(parts.shape[0]):
        total = total + parts[p].astype(F32)
    out[...] = total.astype(BF16)


def flip(values, axis, step):
    size = lax.axis_size(axis)
    return lax.ppermute(values, axis, [(index, index ^ step) for index in range(size)])


def per_device_small(
    residual_in,
    query_new,
    key_new,
    value_new,
    key_cache,
    value_cache,
    block_table,
    lengths,
    out_weight,
    norm_gain,
    gate_weight,
    up_weight,
    down_weight,
):
    rows, width = residual_in.shape
    blocks = key_cache.shape[0]
    pool, mlp = 8, 4
    requests = rows * pool
    ff = gate_weight.shape[1]
    part_cols = out_weight.shape[1]
    packed_width = 2 * width + 128
    slots = blocks + rows + 1
    part_width = width + 128

    packed, new = call(
        prepare_kernel,
        "rotary",
        [((rows, packed_width), BF16), ((rows, 2 * width), BF16)],
        [block_table, lengths, query_new, key_new, value_new, residual_in, key_cache, value_cache],
        [pltpu.SMEM(block_table.shape, jnp.int32), pltpu.SMEM(lengths.shape, jnp.int32)]
        + [pltpu.VMEM((rows, width), BF16)] * 4
        + [pltpu.VMEM((8, width), F32), pltpu.SemaphoreType.DMA((6,))],
        hbm=range(8),
        limit=54 * 2**20,
    )

    packed_near, own = call(
        carry_kernel,
        "carry",
        [(packed.shape, BF16), ((slots, part_width), F32)],
        [packed, new],
    )

    def pool_gather(values, near):
        (both,) = call(
            merge_kernel,
            "merge",
            [((2,) + values.shape, values.dtype)],
            [near, flip(values, "pool", 1)],
        )
        return [both] + [flip(both, "pool", step) for step in (2, 4, 6)]

    part, all_input, tables = call(
        attend_kernel,
        "attend",
        [((slots, width), BF16), ((requests, width), F32), ((requests, 128), F32)],
        pool_gather(packed, packed_near) + [own, key_cache, value_cache],
        [pltpu.VMEM((requests, packed_width), F32)],
    )
    (head_part,) = call(
        combine_kernel,
        "combine",
        [((requests, part_cols), BF16)],
        pool_gather(part, part) + [tables, out_weight],
        [
            pltpu.VMEM((pool * slots, width), F32),
            pltpu.VMEM((pool, slots, 128), F32),
            pltpu.VMEM((requests * width // HD, 128), F32),
        ],
    )
    (head_sum,) = call(
        sum_kernel,
        "head_sum",
        [((requests, part_cols), BF16)],
        [head_part, flip(head_part, "mlp", 1)],
    )
    pieces = []
    for turn_y in range(2):
        for turn_x in range(2):
            route = []
            for m in range(mlp):
                by_distance = sorted(range(4), key=lambda z: (-abs(z - m), z))
                for place, z in enumerate(by_distance):
                    x = m // 2 ^ turn_x ^ place // 2
                    core = 1 - place % 2
                    for y in range(2):
                        source = (m * 2 + y) * mlp + x * 2 + core
                        route.append((source, (z * 2 + (y ^ turn_y)) * mlp + m))
            pieces.append(lax.ppermute(head_sum, ("pool", "mlp"), route))
    sums, own_residual = call(
        gate_up_kernel,
        "gate_up",
        [((requests, 2 * ff + 128), BF16), ((rows, width), F32)],
        pieces + [all_input, norm_gain.reshape(1, width), gate_weight, up_weight],
        [pltpu.VMEM((requests, width), F32)],
    )
    (core_sums,) = call(
        core_sum_kernel,
        "core_sum",
        [((requests, 2 * ff + 128), BF16)],
        [sums, flip(sums, "mlp", 1)],
    )
    (down,) = call(
        functools.partial(down_kernel, width * mlp),
        "down",
        [((pool, rows, width), BF16)],
        [core_sums, flip(core_sums, "mlp", 2), down_weight],
        [pltpu.VMEM((requests, width), F32)],
    )
    backwards = list(range(pool))[::-1]
    (out,) = call(
        final_kernel,
        "final",
        [((rows, width), BF16)],
        [own_residual, lax.all_to_all(down, "pool", 0, 0, axis_index_groups=[backwards])],
    )
    return out


def solution(mesh):
    in_specs = (
        P("pool", "mlp"),
        P("pool", "mlp"),
        P("pool", "mlp"),
        P("pool", "mlp"),
        P("pool", None, "mlp"),
        P("pool", None, "mlp"),
        P("pool", None),
        P("pool"),
        P("mlp", "pool"),
        P("mlp"),
        P("mlp", "pool"),
        P("mlp", "pool"),
        P("pool", "mlp"),
    )
    small = mesh.shape["pool"] == 8 and mesh.shape["mlp"] == 4
    per_device = per_device_small if small else per_device_wide
    return jax.shard_map(
        per_device, mesh=mesh, in_specs=in_specs, out_specs=P("pool", "mlp"), check_vma=False
    )
```

```python
import functools
import math

import jax
import jax.numpy as jnp
import numpy as np
from jax import lax
from jax.experimental import pallas as pl
from jax.experimental.pallas import tpu as pltpu
from jax.sharding import PartitionSpec as P

HD = 96
LOW = -1e30
CODE = 128


def rotate(values, positions):
    half_size = values.shape[-1] // 2
    inverse_freq = 10000.0 ** (-(2.0 * jnp.arange(half_size, dtype=jnp.float32)) / values.shape[-1])
    angles = positions.astype(jnp.float32)[:, None, None] * inverse_freq[None, None, :]
    cosine = jnp.cos(angles)
    sine_part = jnp.sin(angles)
    first = values[..., :half_size]
    second = values[..., half_size:]
    return jnp.concatenate(
        [first * cosine - second * sine_part, second * cosine + first * sine_part], -1
    )


def low(values):
    return lax.reduce_precision(values, 8, 7)


def split(values):
    high = low(values)
    return high.astype(jnp.bfloat16), (values - high).astype(jnp.bfloat16)


def encode(ints):
    return (ints // CODE).astype(jnp.bfloat16), (ints % CODE).astype(jnp.bfloat16)


def decode(high, rest):
    return high.astype(jnp.int32) * CODE + rest.astype(jnp.int32)


def gather(values, axis):
    copies = jnp.broadcast_to(values[None], (lax.axis_size(axis),) + values.shape)
    return lax.all_to_all(copies, axis, 0, 0)


def per_device_wide(
    residual_in,
    query_new,
    key_new,
    value_new,
    key_cache,
    value_cache,
    block_table,
    lengths,
    out_weight,
    norm_gain,
    gate_weight,
    up_weight,
    down_weight,
):
    rows, width = residual_in.shape
    heads = width // HD
    blocks, block_len = key_cache.shape[:2]
    most = block_table.shape[1]
    pool, mlp = lax.axis_size("pool"), lax.axis_size("mlp")
    pool_index = lax.axis_index("pool")
    requests = rows * pool
    score_scale = 1.0 / math.sqrt(HD)
    f32, bf16 = jnp.float32, jnp.bfloat16

    queries = rotate(query_new.astype(f32).reshape(rows, heads, HD), lengths).astype(bf16)
    new_keys = rotate(key_new.astype(f32).reshape(rows, heads, HD), lengths).astype(bf16)

    table_high, table_low = encode(block_table + 1)
    len_high, len_low = encode(lengths)
    packed = jnp.concatenate(
        [
            queries.reshape(rows, width),
            residual_in,
            table_high,
            table_low,
            len_high[:, None],
            len_low[:, None],
        ],
        1,
    )
    spare = -packed.shape[1] % 128
    packed = jnp.pad(packed, ((0, 0), (0, spare)))
    got = gather(packed, "pool").reshape(requests, packed.shape[1])
    all_queries = got[:, :width]
    all_input = got[:, width : 2 * width]
    tail = got[:, 2 * width :]
    tables = decode(tail[:, :most], tail[:, most : 2 * most]) - 1
    all_lengths = decode(tail[:, 2 * most], tail[:, 2 * most + 1])

    held_ids = pool_index * blocks + jnp.arange(blocks, dtype=jnp.int32)
    matches = tables[None, :, :] == held_ids[:, None, None]
    holder = jnp.any(matches, 2)
    block_index = jnp.sum(
        jnp.where(matches, jnp.arange(most, dtype=jnp.int32)[None, None, :], 0), (1, 2)
    )
    valid_len = jnp.sum(jnp.where(holder, all_lengths[None, :], 0), 1)
    block_query = jnp.dot(holder.astype(bf16), all_queries, preferred_element_type=f32)
    block_query = block_query.astype(bf16).reshape(blocks, heads, HD)
    key_rows = key_cache.reshape(blocks, block_len, heads, HD)
    value_rows = value_cache.reshape(blocks, block_len, heads, HD)
    scores = (
        jnp.einsum("bhd,bthd->bht", block_query, key_rows, preferred_element_type=f32)
        * score_scale
    )
    token_pos = block_index[:, None] * block_len + jnp.arange(block_len, dtype=jnp.int32)[None, :]
    valid = (token_pos < valid_len[:, None])[:, None, :]
    scores = jnp.where(valid, scores, LOW)
    shift = low(jnp.max(scores, 2))
    weights = jnp.where(valid, jnp.exp(scores - shift[:, :, None]), 0.0)
    totals = jnp.sum(weights, 2)
    numerator = jnp.einsum(
        "bht,bthd->bhd", weights.astype(bf16), value_rows, preferred_element_type=f32
    )
    self_score = jnp.sum(queries.astype(f32) * new_keys.astype(f32), -1) * score_scale
    self_shift = low(self_score)
    self_weight = jnp.exp(self_score - self_shift)
    self_numer = self_weight[:, :, None] * value_new.astype(f32).reshape(rows, heads, HD)

    own_total = jnp.concatenate([totals, self_weight], 0)
    total_high, total_low = split(own_total)
    part = jnp.concatenate(
        [
            jnp.concatenate([numerator, self_numer], 0)
            .astype(bf16)
            .reshape(blocks + rows, width),
            jnp.concatenate([shift, self_shift], 0).astype(bf16),
            total_high,
            total_low,
        ],
        1,
    )
    part = jnp.pad(part, ((0, 0), (0, -part.shape[1] % 128)))
    count = blocks + rows
    parts = gather(part, "pool").reshape(pool * count, part.shape[1])
    all_shift = parts[:, width : width + heads].astype(f32)
    all_total = parts[:, width + heads : width + 2 * heads].astype(f32) + parts[
        :, width + 2 * heads : width + 3 * heads
    ].astype(f32)
    place = jnp.arange(pool * count, dtype=jnp.int32)
    owner, slot = place // count, place % count
    is_block = slot < blocks
    block_id = jnp.where(is_block, owner * blocks + slot, -2)
    self_id = jnp.where(is_block, -2, owner * rows + slot - blocks)
    request_ids = jnp.arange(requests, dtype=jnp.int32)
    belongs = jnp.any(tables[:, None, :] == block_id[None, :, None], 2) | (
        request_ids[:, None] == self_id[None, :]
    )
    top = jnp.max(jnp.where(belongs[:, :, None], all_shift[None], LOW), 1)
    part_top = jnp.sum(jnp.where(belongs[:, :, None], top[:, None, :], 0.0), 0)
    scale = jnp.exp(all_shift - part_top)
    scaled = parts[:, :width].astype(f32).reshape(-1, heads, HD) * scale[:, :, None]
    mix = belongs.astype(f32)
    numer = jnp.dot(mix, scaled.reshape(-1, width), precision=lax.Precision.HIGHEST)
    denom = jnp.dot(mix, all_total * scale, precision=lax.Precision.HIGHEST)
    attended = (numer.reshape(requests, heads, HD) / denom[:, :, None]).astype(bf16)
    attended = attended.reshape(requests, width)

    head_part = jnp.dot(attended, out_weight, preferred_element_type=f32).astype(bf16)
    share = pool // mlp
    route = []
    for p in range(pool):
        for m in range(mlp):
            route.append((p * mlp + m, ((p % share) * mlp + m) * mlp + p // share))
    moved = lax.ppermute(head_part, ("pool", "mlp"), route)
    head_all = gather(moved, "pool").reshape(share, mlp, requests, -1)
    head_out = low(jnp.sum(head_all.astype(f32), 1))
    head_out = jnp.swapaxes(head_out, 0, 1).reshape(requests, width)
    residual = all_input.astype(f32) + head_out
    squares = jnp.sum(residual * residual, -1, keepdims=True)
    portion = (residual * norm_gain.astype(f32)).astype(bf16)

    ff = gate_weight.shape[1]
    square_high, square_low = split(squares)
    sums = jnp.concatenate(
        [
            jnp.dot(portion, gate_weight, preferred_element_type=f32).astype(bf16),
            jnp.dot(portion, up_weight, preferred_element_type=f32).astype(bf16),
            jnp.broadcast_to(square_high, (requests, 64)),
            jnp.broadcast_to(square_low, (requests, 64)),
        ],
        1,
    )
    summed = jnp.sum(gather(sums, "mlp").astype(f32), 0)
    mean_square = (summed[:, 2 * ff : 2 * ff + 1] + summed[:, 2 * ff + 64 : 2 * ff + 65]) / (
        width * mlp
    )
    factor = lax.rsqrt(mean_square + 1e-05)
    gate = summed[:, :ff] * factor
    up = summed[:, ff : 2 * ff] * factor
    hidden = (jax.nn.silu(gate) * up).astype(bf16)

    down = jnp.dot(hidden, down_weight, preferred_element_type=f32)
    down = lax.all_to_all(down.reshape(pool, rows, width), "pool", 0, 0)
    own = lax.dynamic_slice_in_dim(residual, pool_index * rows, rows, 0)
    return (own + jnp.sum(down, 0)).astype(bf16)


F32, BF16 = jnp.float32, jnp.bfloat16
VMEM = pl.BlockSpec(memory_space=pltpu.VMEM)
HBM = pl.BlockSpec(memory_space=pl.ANY)


def call(kernel, name, outs, args, scratch=(), hbm=(), limit=16 * 2**20):
    size = sum(math.prod(a.shape) * a.dtype.itemsize for a in args)
    return pl.pallas_call(
        kernel,
        out_shape=[jax.ShapeDtypeStruct(shape, dtype) for shape, dtype in outs],
        in_specs=[HBM if i in hbm else VMEM for i in range(len(args))],
        out_specs=[VMEM] * len(outs),
        scratch_shapes=list(scratch),
        compiler_params=pltpu.CompilerParams(vmem_limit_bytes=limit),
        cost_estimate=pl.CostEstimate(flops=0, bytes_accessed=size, transcendentals=0),
        name=name,
    )(*args)


def lanes(shape):
    return lax.broadcasted_iota(jnp.int32, shape, len(shape) - 1)


def in_order(pieces, index):
    for bit in (1, 2):
        odd = (index & bit) != 0
        pieces = [jnp.where(odd, pieces[s ^ bit], pieces[s]) for s in range(4)]
    return pieces


def rows_of(shape):
    return lax.broadcasted_iota(jnp.int32, shape, len(shape) - 2)


def round_low(values):
    return values.astype(BF16).astype(F32)


def head_start(shape):
    return rows_of(shape) * HD % 128


def flatten(tail, width):
    heads = tail.shape[0]
    spread = jnp.zeros((heads, width), F32)
    start = head_start((heads, width))
    for k in (0, 32, 64, 96):
        moved = pltpu.roll(tail, k, 1) if k else tail
        spread = jnp.where(start == k, jnp.concatenate([moved] * (width // 128), 1), spread)
    lane = lanes((heads, width))
    used = (lane // HD == rows_of((heads, width))) & (lane % HD < 24)
    return jnp.sum(jnp.where(used, spread, 0.0), 0, keepdims=True)


def unflatten(row, heads):
    width = row.shape[1]
    lane = lanes((heads, width))
    used = (lane // HD == rows_of((heads, width))) & (lane % HD < 24)
    spread = jnp.where(used, jnp.broadcast_to(row, (heads, width)), 0.0)
    folded = spread[:, :128]
    for at in range(128, width, 128):
        folded = folded + spread[:, at : at + 128]
    start = head_start((heads, 128))
    tail = jnp.where(start == 0, folded, 0.0)
    for k in (32, 64, 96):
        tail = jnp.where(start == k, pltpu.roll(folded, 128 - k, 1), tail)
    return tail


def prepare_kernel(*refs):
    sources, (packed, new), held = refs[:6], refs[8:10], refs[10:16]
    scr, sems = refs[16:]
    copies = [
        pltpu.make_async_copy(source, target, sems.at[i])
        for i, (source, target) in enumerate(zip(sources, held))
    ]
    for copy in copies:
        copy.start()
    table, length, query, key, value, residual = held
    rows, width = query.shape
    most = table.shape[1]
    period = 384
    turn = lanes((8, period)) % (HD // 2)
    freq = jnp.zeros((8, period), F32)
    for i in range(HD // 2):
        freq = jnp.where(turn == i, float(np.float32(10000.0 ** (-2.0 * i / HD))), freq)
    for copy in copies:
        copy.wait()
    scr[...] = jnp.zeros_like(scr)
    scr[0:rows, :] = query[...].astype(F32)
    scr[rows : 2 * rows, :] = key[...].astype(F32)
    values = scr[...]
    line = rows_of((8, period))
    where_at = jnp.zeros((8, period), F32)
    for r in range(rows):
        here = (line == r) | (line == rows + r)
        where_at = jnp.where(here, length[r].astype(F32), where_at)
    angles = where_at * freq
    cosine = jnp.concatenate([jnp.cos(angles)] * (width // period), 1)
    sine = jnp.concatenate([jnp.sin(angles)] * (width // period), 1)
    first = lanes((8, width)) % HD < HD // 2
    ahead = pltpu.roll(values, width - HD // 2, 1)
    behind = pltpu.roll(values, HD // 2, 1)
    scr[...] = values * cosine + jnp.where(first, -ahead, behind) * sine
    packed[:, :width] = scr[0:rows, :].astype(BF16)
    packed[:, width : 2 * width] = residual[...]
    tail = jnp.zeros((rows, 128), F32)
    at, row = lanes((rows, 128)), rows_of((rows, 128))
    for r in range(rows):
        codes = [table[r, k] + 1 for k in range(most)] + [length[r]]
        spots = [(k, most + k) for k in range(most)] + [(2 * most, 2 * most + 1)]
        for code, (high, rest) in zip(codes, spots):
            tail = jnp.where((row == r) & (at == high), (code >> 7).astype(F32), tail)
            tail = jnp.where((row == r) & (at == rest), (code & 127).astype(F32), tail)
    packed[:, 2 * width :] = tail.astype(BF16)
    new[:, :width] = scr[rows : 2 * rows, :].astype(BF16)
    new[:, width:] = value[...]


def carry_kernel(packed, new, packed_near, own):
    packed_near[...] = packed[...]
    rows, width = new.shape[0], new.shape[1] // 2
    blocks = own.shape[0] - rows - 1
    heads = width // HD
    head_mask = lanes((heads, width)) // HD == rows_of((heads, width))
    product = packed[:, :width].astype(F32) * new[:, :width].astype(F32)
    own[...] = jnp.zeros_like(own)
    spot = lanes((heads, 128))
    tail = jnp.zeros((heads, 128), F32)
    for r in range(rows):
        score = jnp.sum(
            jnp.where(head_mask, jnp.broadcast_to(product[r : r + 1], (heads, width)), 0.0),
            1,
            keepdims=True,
        ) * (1.0 / math.sqrt(HD))
        shift = round_low(score)
        weight = jnp.exp(score - shift)
        spread = jnp.sum(jnp.where(head_mask, round_low(weight), 0.0), 0, keepdims=True)
        own[blocks + r : blocks + r + 1, :width] = spread * new[r : r + 1, width:].astype(F32)
        high = round_low(weight)
        tail = jnp.where(spot == blocks + r, shift, tail)
        tail = jnp.where(spot == 8 + blocks + r, high, tail)
        tail = jnp.where(spot == 16 + blocks + r, weight - high, tail)
    own[:, width:] = tail


def merge_kernel(mine, theirs, both):
    y = lax.axis_index("pool") % 2
    both[y] = mine[...]
    both[1 - y] = theirs[...]


def attend_kernel(a0, a1, a2, a3, own, keys, values, part, residual, tables, scr):
    blocks, block_len, width = keys.shape
    rows = a0.shape[1]
    heads = width // HD
    most = 8
    me = lax.axis_index("pool")
    for y in range(2):
        pieces = [piece[y].astype(F32) for piece in (a0, a1, a2, a3)]
        for z, piece in enumerate(in_order(pieces, me // 2)):
            scr[(z * 2 + y) * rows : (z * 2 + y + 1) * rows, :] = piece
    queries = scr[:, :width]
    residual[...] = scr[:, width : 2 * width]
    tail = scr[:, 2 * width :]
    requests = tail.shape[0]
    table = tail * CODE + pltpu.roll(tail, 128 - most, 1) - 1.0
    length = tail[:, 2 * most : 2 * most + 1] * CODE + tail[:, 2 * most + 1 : 2 * most + 2]
    lane = lanes((requests, 128))
    table = jnp.where(lane < most, table, -2.0)
    tables[...] = table
    head_mask = lanes((heads, width)) // HD == rows_of((heads, width))
    spot = lanes((heads, 128))
    tail = own[:, width:]
    scores, limits = [], []
    for b in range(blocks):
        match = jnp.where(table == (me * blocks + b).astype(F32), 1.0, 0.0)
        holder = jnp.sum(match, 1, keepdims=True)
        place = jnp.sum(jnp.sum(match * lane.astype(F32), 1, keepdims=True), 0, keepdims=True)
        limit = jnp.sum(holder * length, 0, keepdims=True) - place * block_len
        limits.append(jnp.broadcast_to(limit, (heads, block_len)))
        query = jnp.sum(holder * queries, 0, keepdims=True)
        spread = jnp.where(head_mask, query, 0.0).astype(BF16)
        scores.append(
            lax.dot_general(
                spread, keys[b], (((1,), (1,)), ((), ())), preferred_element_type=F32
            )
        )
    scores = jnp.concatenate(scores, 0) * (1.0 / math.sqrt(HD))
    token = lanes((blocks * heads, block_len)).astype(F32)
    valid = token < jnp.concatenate(limits, 0)
    scores = jnp.where(valid, scores, LOW)
    shift = round_low(jnp.max(scores, 1, keepdims=True))
    weights = jnp.where(valid, jnp.exp(scores - shift), 0.0)
    total = jnp.sum(weights, 1, keepdims=True)
    high = round_low(total)
    rest = total - high
    numerators = []
    for b in range(blocks):
        mine = slice(b * heads, (b + 1) * heads)
        full = jnp.dot(weights[mine].astype(BF16), values[b], preferred_element_type=F32)
        numerators.append(jnp.sum(jnp.where(head_mask, full, 0.0), 0, keepdims=True))
        tail = jnp.where(spot == b, shift[mine], tail)
        tail = jnp.where(spot == 8 + b, high[mine], tail)
        tail = jnp.where(spot == 16 + b, rest[mine], tail)
    line = rows_of((8, width))
    numer = own[:, :width]
    for b in range(blocks):
        numer = jnp.where(line == b, numerators[b], numer)
    numer = jnp.where(line == 7, flatten(tail, width), numer)
    part[...] = numer.astype(BF16)


def combine_kernel(b0, b1, b2, b3, tables, weight, head_part, numer, tails, mix):
    requests = tables.shape[0]
    slots = b0.shape[1]
    width = weight.shape[0]
    heads = width // HD
    rows, blocks = 2, slots - 3
    me = lax.axis_index("pool")
    for step, piece in enumerate((b0, b1, b2, b3)):
        z = (me // 2) ^ step
        for y in range(2):
            owner = z * 2 + y
            values = piece[y].astype(F32)
            numer[pl.ds(pl.multiple_of(owner * slots, 8), slots), :] = values
            tails[owner] = unflatten(values[slots - 1 : slots], heads)
    lane8 = lanes((heads, 128))
    shifts = jnp.zeros((heads, 128), F32)
    totals = jnp.zeros((heads, 128), F32)
    for owner in range(8):
        tail = tails[owner]
        total = pltpu.roll(tail, 120, 1) + pltpu.roll(tail, 112, 1)
        tail, total = jnp.where(lane8 < 8, tail, 0.0), jnp.where(lane8 < 8, total, 0.0)
        if owner:
            tail, total = pltpu.roll(tail, 8 * owner, 1), pltpu.roll(total, 8 * owner, 1)
        shifts, totals = shifts + tail, totals + total
    lane = lanes((requests, 128))
    owner, slot = lane // slots, lane % slots
    block_id = jnp.where((slot < blocks) & (lane < 64), owner * blocks + slot, -5).astype(F32)
    self_id = jnp.where((slot >= blocks) & (slot < blocks + rows), owner * rows + slot - blocks, -5)
    table = tables[...]
    belongs = (self_id == rows_of((requests, 128))) & (lane < 64)
    for k in range(8):
        belongs = belongs | (table[:, k : k + 1] == block_id)
    for h in range(heads):
        shift = jnp.broadcast_to(shifts[h : h + 1], (requests, 128))
        top = jnp.max(jnp.where(belongs, shift, LOW), 1, keepdims=True)
        scale = jnp.where(belongs, jnp.exp(shift - top), 0.0)
        total = jnp.sum(scale * totals[h : h + 1], 1, keepdims=True)
        mix[h * requests : (h + 1) * requests, :] = scale / total
    full = jnp.dot(
        mix[:, : 8 * slots].astype(BF16), numer[...].astype(BF16), preferred_element_type=F32
    )
    head = lanes((requests, width)) // HD
    attended = jnp.zeros((requests, width), F32)
    for h in range(heads):
        attended = jnp.where(head == h, full[h * requests : (h + 1) * requests], attended)
    head_part[...] = jnp.dot(
        attended.astype(BF16), weight[...], preferred_element_type=F32
    ).astype(BF16)


def sum_kernel(p0, p1, p2, p3, total):
    total[...] = (
        (p0[...].astype(F32) + p1[...].astype(F32)) + (p2[...].astype(F32) + p3[...].astype(F32))
    ).astype(BF16)


def gate_up_kernel(same, flip, all_input, gain, gate, up, sums, own, scr):
    me = lax.axis_index("pool")
    odd = me % 2 == 1
    part = same.shape[1]
    ff = gate.shape[1]
    rows = own.shape[0]
    near, far = same[...].astype(F32), flip[...].astype(F32)
    scr[:, :part] = all_input[:, :part] + jnp.where(odd, far, near)
    scr[:, part:] = all_input[:, part:] + jnp.where(odd, near, far)
    residual = scr[...]
    mine = scr[0:rows, :]
    for p in range(1, residual.shape[0] // rows):
        mine = jnp.where(me == p, scr[p * rows : (p + 1) * rows, :], mine)
    own[...] = mine
    square = jnp.sum(residual * residual, 1, keepdims=True)
    portion = (residual * gain[...].astype(F32)).astype(BF16)
    sums[:, :ff] = jnp.dot(portion, gate[...], preferred_element_type=F32).astype(BF16)
    sums[:, ff : 2 * ff] = jnp.dot(portion, up[...], preferred_element_type=F32).astype(BF16)
    lane = lanes((residual.shape[0], 128))
    high = round_low(square)
    tail = jnp.where(lane == 0, high, jnp.where(lane == 1, square - high, 0.0))
    sums[:, 2 * ff :] = tail.astype(BF16)


def core_sum_kernel(mine, theirs, total):
    ff2 = mine.shape[1] - 128
    total[:, :ff2] = (mine[:, :ff2].astype(F32) + theirs[:, :ff2].astype(F32)).astype(BF16)
    tail = mine[:, ff2:].astype(F32) + theirs[:, ff2:].astype(F32)
    square = jnp.sum(tail, 1, keepdims=True)
    lane = lanes(tail.shape)
    high = round_low(square)
    tail = jnp.where(lane == 0, high, jnp.where(lane == 1, square - high, 0.0))
    total[:, ff2:] = tail.astype(BF16)


def down_kernel(features, mine, theirs, weight, parts, scr):
    ff = weight.shape[0]
    tail = mine[:, 2 * ff :].astype(F32) + theirs[:, 2 * ff :].astype(F32)
    square = jnp.sum(tail, 1, keepdims=True)
    factor = lax.rsqrt(square * (1.0 / features) + 1e-05)
    gate = (mine[:, :ff].astype(F32) + theirs[:, :ff].astype(F32)) * factor
    up = (mine[:, ff : 2 * ff].astype(F32) + theirs[:, ff : 2 * ff].astype(F32)) * factor
    hidden = (gate / (1.0 + jnp.exp(-gate)) * up).astype(BF16)
    scr[...] = jnp.dot(hidden, weight[...], preferred_element_type=F32)
    rows = parts.shape[1]
    pool = parts.shape[0]
    for p in range(pool):
        parts[pool - 1 - p] = scr[p * rows : (p + 1) * rows, :].astype(BF16)


def final_kernel(own, parts, out):
    total = own[...]
    for p in range(parts.shape[0]):
        total = total + parts[p].astype(F32)
    out[...] = total.astype(BF16)


def flip(values, axis, step):
    size = lax.axis_size(axis)
    return lax.ppermute(values, axis, [(index, index ^ step) for index in range(size)])


def per_device_small(
    residual_in,
    query_new,
    key_new,
    value_new,
    key_cache,
    value_cache,
    block_table,
    lengths,
    out_weight,
    norm_gain,
    gate_weight,
    up_weight,
    down_weight,
):
    rows, width = residual_in.shape
    blocks = key_cache.shape[0]
    pool, mlp = 8, 4
    requests = rows * pool
    ff = gate_weight.shape[1]
    part_cols = out_weight.shape[1]
    packed_width = 2 * width + 128
    slots = blocks + rows + 1
    part_width = width + 128

    packed, new = call(
        prepare_kernel,
        "rotary",
        [((rows, packed_width), BF16), ((rows, 2 * width), BF16)],
        [block_table, lengths, query_new, key_new, value_new, residual_in, key_cache, value_cache],
        [pltpu.SMEM(block_table.shape, jnp.int32), pltpu.SMEM(lengths.shape, jnp.int32)]
        + [pltpu.VMEM((rows, width), BF16)] * 4
        + [pltpu.VMEM((8, width), F32), pltpu.SemaphoreType.DMA((6,))],
        hbm=range(8),
        limit=54 * 2**20,
    )

    packed_near, own = call(
        carry_kernel,
        "carry",
        [(packed.shape, BF16), ((slots, part_width), F32)],
        [packed, new],
    )

    def pool_gather(values, near):
        (both,) = call(
            merge_kernel,
            "merge",
            [((2,) + values.shape, values.dtype)],
            [near, flip(values, "pool", 1)],
        )
        return [both] + [flip(both, "pool", step) for step in (2, 4, 6)]

    part, all_input, tables = call(
        attend_kernel,
        "attend",
        [((slots, width), BF16), ((requests, width), F32), ((requests, 128), F32)],
        pool_gather(packed, packed_near) + [own, key_cache, value_cache],
        [pltpu.VMEM((requests, packed_width), F32)],
    )
    (head_part,) = call(
        combine_kernel,
        "combine",
        [((requests, part_cols), BF16)],
        pool_gather(part, part) + [tables, out_weight],
        [
            pltpu.VMEM((pool * slots, width), F32),
            pltpu.VMEM((pool, slots, 128), F32),
            pltpu.VMEM((requests * width // HD, 128), F32),
        ],
    )
    (head_sum,) = call(
        sum_kernel,
        "head_sum",
        [((requests, part_cols), BF16)],
        [head_part] + [flip(head_part, "mlp", step) for step in (1, 2, 3)],
    )
    pieces = []
    for turn in range(2):
        route = []
        for m in range(mlp):
            by_distance = sorted(range(4), key=lambda z: (-abs(z - m), z))
            for z, step in zip(by_distance, (1, 0, 3, 2) if m % 2 == 0 else (0, 1, 2, 3)):
                for y in range(2):
                    source = (m * 2 + y) * mlp + (m ^ step)
                    route.append((source, (z * 2 + (y ^ turn)) * mlp + m))
        pieces.append(lax.ppermute(head_sum, ("pool", "mlp"), route))
    sums, own_residual = call(
        gate_up_kernel,
        "gate_up",
        [((requests, 2 * ff + 128), BF16), ((rows, width), F32)],
        pieces + [all_input, norm_gain.reshape(1, width), gate_weight, up_weight],
        [pltpu.VMEM((requests, width), F32)],
    )
    (core_sums,) = call(
        core_sum_kernel,
        "core_sum",
        [((requests, 2 * ff + 128), BF16)],
        [sums, flip(sums, "mlp", 1)],
    )
    (down,) = call(
        functools.partial(down_kernel, width * mlp),
        "down",
        [((pool, rows, width), BF16)],
        [core_sums, flip(core_sums, "mlp", 3), down_weight],
        [pltpu.VMEM((requests, width), F32)],
    )
    backwards = list(range(pool))[::-1]
    (out,) = call(
        final_kernel,
        "final",
        [((rows, width), BF16)],
        [own_residual, lax.all_to_all(down, "pool", 0, 0, axis_index_groups=[backwards])],
    )
    return out


def solution(mesh):
    in_specs = (
        P("pool", "mlp"),
        P("pool", "mlp"),
        P("pool", "mlp"),
        P("pool", "mlp"),
        P("pool", None, "mlp"),
        P("pool", None, "mlp"),
        P("pool", None),
        P("pool"),
        P("mlp", "pool"),
        P("mlp"),
        P("mlp", "pool"),
        P("mlp", "pool"),
        P("pool", "mlp"),
    )
    small = mesh.shape["pool"] == 8 and mesh.shape["mlp"] == 4
    per_device = per_device_small if small else per_device_wide
    return jax.shard_map(
        per_device, mesh=mesh, in_specs=in_specs, out_specs=P("pool", "mlp"), check_vma=False
    )
```

```python
import functools
import math

import jax
import jax.numpy as jnp
import numpy as np
from jax import lax
from jax.experimental import pallas as pl
from jax.experimental.pallas import tpu as pltpu
from jax.sharding import PartitionSpec as P

HD = 96
LOW = -1e30
CODE = 128


def rotate(values, positions):
    half_size = values.shape[-1] // 2
    inverse_freq = 10000.0 ** (-(2.0 * jnp.arange(half_size, dtype=jnp.float32)) / values.shape[-1])
    angles = positions.astype(jnp.float32)[:, None, None] * inverse_freq[None, None, :]
    cosine = jnp.cos(angles)
    sine_part = jnp.sin(angles)
    first = values[..., :half_size]
    second = values[..., half_size:]
    return jnp.concatenate(
        [first * cosine - second * sine_part, second * cosine + first * sine_part], -1
    )


def low(values):
    return lax.reduce_precision(values, 8, 7)


def split(values):
    high = low(values)
    return high.astype(jnp.bfloat16), (values - high).astype(jnp.bfloat16)


def encode(ints):
    return (ints // CODE).astype(jnp.bfloat16), (ints % CODE).astype(jnp.bfloat16)


def decode(high, rest):
    return high.astype(jnp.int32) * CODE + rest.astype(jnp.int32)


def gather(values, axis):
    copies = jnp.broadcast_to(values[None], (lax.axis_size(axis),) + values.shape)
    return lax.all_to_all(copies, axis, 0, 0)


def per_device_wide(
    residual_in,
    query_new,
    key_new,
    value_new,
    key_cache,
    value_cache,
    block_table,
    lengths,
    out_weight,
    norm_gain,
    gate_weight,
    up_weight,
    down_weight,
):
    rows, width = residual_in.shape
    heads = width // HD
    blocks, block_len = key_cache.shape[:2]
    most = block_table.shape[1]
    pool, mlp = lax.axis_size("pool"), lax.axis_size("mlp")
    pool_index = lax.axis_index("pool")
    requests = rows * pool
    score_scale = 1.0 / math.sqrt(HD)
    f32, bf16 = jnp.float32, jnp.bfloat16

    queries = rotate(query_new.astype(f32).reshape(rows, heads, HD), lengths).astype(bf16)
    new_keys = rotate(key_new.astype(f32).reshape(rows, heads, HD), lengths).astype(bf16)

    table_high, table_low = encode(block_table + 1)
    len_high, len_low = encode(lengths)
    packed = jnp.concatenate(
        [
            queries.reshape(rows, width),
            residual_in,
            table_high,
            table_low,
            len_high[:, None],
            len_low[:, None],
        ],
        1,
    )
    spare = -packed.shape[1] % 128
    packed = jnp.pad(packed, ((0, 0), (0, spare)))
    got = gather(packed, "pool").reshape(requests, packed.shape[1])
    all_queries = got[:, :width]
    all_input = got[:, width : 2 * width]
    tail = got[:, 2 * width :]
    tables = decode(tail[:, :most], tail[:, most : 2 * most]) - 1
    all_lengths = decode(tail[:, 2 * most], tail[:, 2 * most + 1])

    held_ids = pool_index * blocks + jnp.arange(blocks, dtype=jnp.int32)
    matches = tables[None, :, :] == held_ids[:, None, None]
    holder = jnp.any(matches, 2)
    block_index = jnp.sum(
        jnp.where(matches, jnp.arange(most, dtype=jnp.int32)[None, None, :], 0), (1, 2)
    )
    valid_len = jnp.sum(jnp.where(holder, all_lengths[None, :], 0), 1)
    block_query = jnp.dot(holder.astype(bf16), all_queries, preferred_element_type=f32)
    block_query = block_query.astype(bf16).reshape(blocks, heads, HD)
    key_rows = key_cache.reshape(blocks, block_len, heads, HD)
    value_rows = value_cache.reshape(blocks, block_len, heads, HD)
    scores = (
        jnp.einsum("bhd,bthd->bht", block_query, key_rows, preferred_element_type=f32)
        * score_scale
    )
    token_pos = block_index[:, None] * block_len + jnp.arange(block_len, dtype=jnp.int32)[None, :]
    valid = (token_pos < valid_len[:, None])[:, None, :]
    scores = jnp.where(valid, scores, LOW)
    shift = low(jnp.max(scores, 2))
    weights = jnp.where(valid, jnp.exp(scores - shift[:, :, None]), 0.0)
    totals = jnp.sum(weights, 2)
    numerator = jnp.einsum(
        "bht,bthd->bhd", weights.astype(bf16), value_rows, preferred_element_type=f32
    )
    self_score = jnp.sum(queries.astype(f32) * new_keys.astype(f32), -1) * score_scale
    self_shift = low(self_score)
    self_weight = jnp.exp(self_score - self_shift)
    self_numer = self_weight[:, :, None] * value_new.astype(f32).reshape(rows, heads, HD)

    own_total = jnp.concatenate([totals, self_weight], 0)
    total_high, total_low = split(own_total)
    part = jnp.concatenate(
        [
            jnp.concatenate([numerator, self_numer], 0)
            .astype(bf16)
            .reshape(blocks + rows, width),
            jnp.concatenate([shift, self_shift], 0).astype(bf16),
            total_high,
            total_low,
        ],
        1,
    )
    part = jnp.pad(part, ((0, 0), (0, -part.shape[1] % 128)))
    count = blocks + rows
    parts = gather(part, "pool").reshape(pool * count, part.shape[1])
    all_shift = parts[:, width : width + heads].astype(f32)
    all_total = parts[:, width + heads : width + 2 * heads].astype(f32) + parts[
        :, width + 2 * heads : width + 3 * heads
    ].astype(f32)
    place = jnp.arange(pool * count, dtype=jnp.int32)
    owner, slot = place // count, place % count
    is_block = slot < blocks
    block_id = jnp.where(is_block, owner * blocks + slot, -2)
    self_id = jnp.where(is_block, -2, owner * rows + slot - blocks)
    request_ids = jnp.arange(requests, dtype=jnp.int32)
    belongs = jnp.any(tables[:, None, :] == block_id[None, :, None], 2) | (
        request_ids[:, None] == self_id[None, :]
    )
    top = jnp.max(jnp.where(belongs[:, :, None], all_shift[None], LOW), 1)
    part_top = jnp.sum(jnp.where(belongs[:, :, None], top[:, None, :], 0.0), 0)
    scale = jnp.exp(all_shift - part_top)
    scaled = parts[:, :width].astype(f32).reshape(-1, heads, HD) * scale[:, :, None]
    mix = belongs.astype(f32)
    numer = jnp.dot(mix, scaled.reshape(-1, width), precision=lax.Precision.HIGHEST)
    denom = jnp.dot(mix, all_total * scale, precision=lax.Precision.HIGHEST)
    attended = (numer.reshape(requests, heads, HD) / denom[:, :, None]).astype(bf16)
    attended = attended.reshape(requests, width)

    head_part = jnp.dot(attended, out_weight, preferred_element_type=f32).astype(bf16)
    share = pool // mlp
    route = []
    for p in range(pool):
        for m in range(mlp):
            route.append((p * mlp + m, ((p % share) * mlp + m) * mlp + p // share))
    moved = lax.ppermute(head_part, ("pool", "mlp"), route)
    head_all = gather(moved, "pool").reshape(share, mlp, requests, -1)
    head_out = low(jnp.sum(head_all.astype(f32), 1))
    head_out = jnp.swapaxes(head_out, 0, 1).reshape(requests, width)
    residual = all_input.astype(f32) + head_out
    squares = jnp.sum(residual * residual, -1, keepdims=True)
    portion = (residual * norm_gain.astype(f32)).astype(bf16)

    ff = gate_weight.shape[1]
    square_high, square_low = split(squares)
    sums = jnp.concatenate(
        [
            jnp.dot(portion, gate_weight, preferred_element_type=f32).astype(bf16),
            jnp.dot(portion, up_weight, preferred_element_type=f32).astype(bf16),
            jnp.broadcast_to(square_high, (requests, 64)),
            jnp.broadcast_to(square_low, (requests, 64)),
        ],
        1,
    )
    summed = jnp.sum(gather(sums, "mlp").astype(f32), 0)
    mean_square = (summed[:, 2 * ff : 2 * ff + 1] + summed[:, 2 * ff + 64 : 2 * ff + 65]) / (
        width * mlp
    )
    factor = lax.rsqrt(mean_square + 1e-05)
    gate = summed[:, :ff] * factor
    up = summed[:, ff : 2 * ff] * factor
    hidden = (jax.nn.silu(gate) * up).astype(bf16)

    down = jnp.dot(hidden, down_weight, preferred_element_type=f32)
    down = lax.all_to_all(down.reshape(pool, rows, width), "pool", 0, 0)
    own = lax.dynamic_slice_in_dim(residual, pool_index * rows, rows, 0)
    return (own + jnp.sum(down, 0)).astype(bf16)


F32, BF16 = jnp.float32, jnp.bfloat16
VMEM = pl.BlockSpec(memory_space=pltpu.VMEM)
HBM = pl.BlockSpec(memory_space=pl.ANY)


def call(kernel, name, outs, args, scratch=(), hbm=(), limit=16 * 2**20):
    size = sum(math.prod(a.shape) * a.dtype.itemsize for a in args)
    return pl.pallas_call(
        kernel,
        out_shape=[jax.ShapeDtypeStruct(shape, dtype) for shape, dtype in outs],
        in_specs=[HBM if i in hbm else VMEM for i in range(len(args))],
        out_specs=[VMEM] * len(outs),
        scratch_shapes=list(scratch),
        compiler_params=pltpu.CompilerParams(vmem_limit_bytes=limit),
        cost_estimate=pl.CostEstimate(flops=0, bytes_accessed=size, transcendentals=0),
        name=name,
    )(*args)


def lanes(shape):
    return lax.broadcasted_iota(jnp.int32, shape, len(shape) - 1)


def rows_of(shape):
    return lax.broadcasted_iota(jnp.int32, shape, len(shape) - 2)


def round_low(values):
    return values.astype(BF16).astype(F32)


def head_start(shape):
    return rows_of(shape) * HD % 128


def flatten(tail, width):
    heads = tail.shape[0]
    spread = jnp.zeros((heads, width), F32)
    start = head_start((heads, width))
    for k in (0, 32, 64, 96):
        moved = pltpu.roll(tail, k, 1) if k else tail
        spread = jnp.where(start == k, jnp.concatenate([moved] * (width // 128), 1), spread)
    lane = lanes((heads, width))
    used = (lane // HD == rows_of((heads, width))) & (lane % HD < 24)
    return jnp.sum(jnp.where(used, spread, 0.0), 0, keepdims=True)


def unflatten(row, heads):
    width = row.shape[1]
    lane = lanes((heads, width))
    used = (lane // HD == rows_of((heads, width))) & (lane % HD < 24)
    spread = jnp.where(used, jnp.broadcast_to(row, (heads, width)), 0.0)
    folded = spread[:, :128]
    for at in range(128, width, 128):
        folded = folded + spread[:, at : at + 128]
    start = head_start((heads, 128))
    tail = jnp.where(start == 0, folded, 0.0)
    for k in (32, 64, 96):
        tail = jnp.where(start == k, pltpu.roll(folded, 128 - k, 1), tail)
    return tail


def prepare_kernel(*refs):
    sources, (packed, new), held = refs[:6], refs[8:10], refs[10:16]
    scr, sems = refs[16:]
    copies = [
        pltpu.make_async_copy(source, target, sems.at[i])
        for i, (source, target) in enumerate(zip(sources, held))
    ]
    for copy in copies:
        copy.start()
    table, length, query, key, value, residual = held
    rows, width = query.shape
    most = table.shape[1]
    period = 384
    turn = lanes((8, period)) % (HD // 2)
    freq = jnp.zeros((8, period), F32)
    for i in range(HD // 2):
        freq = jnp.where(turn == i, float(np.float32(10000.0 ** (-2.0 * i / HD))), freq)
    for copy in copies:
        copy.wait()
    scr[...] = jnp.zeros_like(scr)
    scr[0:rows, :] = query[...].astype(F32)
    scr[rows : 2 * rows, :] = key[...].astype(F32)
    values = scr[...]
    line = rows_of((8, period))
    where_at = jnp.zeros((8, period), F32)
    for r in range(rows):
        here = (line == r) | (line == rows + r)
        where_at = jnp.where(here, length[r].astype(F32), where_at)
    angles = where_at * freq
    cosine = jnp.concatenate([jnp.cos(angles)] * (width // period), 1)
    sine = jnp.concatenate([jnp.sin(angles)] * (width // period), 1)
    first = lanes((8, width)) % HD < HD // 2
    ahead = pltpu.roll(values, width - HD // 2, 1)
    behind = pltpu.roll(values, HD // 2, 1)
    scr[...] = values * cosine + jnp.where(first, -ahead, behind) * sine
    packed[:, :width] = scr[0:rows, :].astype(BF16)
    packed[:, width : 2 * width] = residual[...]
    tail = jnp.zeros((rows, 128), F32)
    at, row = lanes((rows, 128)), rows_of((rows, 128))
    for r in range(rows):
        codes = [table[r, k] + 1 for k in range(most)] + [length[r]]
        spots = [(k, most + k) for k in range(most)] + [(2 * most, 2 * most + 1)]
        for code, (high, rest) in zip(codes, spots):
            tail = jnp.where((row == r) & (at == high), (code >> 7).astype(F32), tail)
            tail = jnp.where((row == r) & (at == rest), (code & 127).astype(F32), tail)
    packed[:, 2 * width :] = tail.astype(BF16)
    new[:, :width] = scr[rows : 2 * rows, :].astype(BF16)
    new[:, width:] = value[...]


def carry_kernel(packed, new, packed_near, own):
    packed_near[...] = packed[...]
    rows, width = new.shape[0], new.shape[1] // 2
    blocks = own.shape[0] - rows - 1
    heads = width // HD
    head_mask = lanes((heads, width)) // HD == rows_of((heads, width))
    product = packed[:, :width].astype(F32) * new[:, :width].astype(F32)
    own[...] = jnp.zeros_like(own)
    spot = lanes((heads, 128))
    tail = jnp.zeros((heads, 128), F32)
    for r in range(rows):
        score = jnp.sum(
            jnp.where(head_mask, jnp.broadcast_to(product[r : r + 1], (heads, width)), 0.0),
            1,
            keepdims=True,
        ) * (1.0 / math.sqrt(HD))
        shift = round_low(score)
        weight = jnp.exp(score - shift)
        spread = jnp.sum(jnp.where(head_mask, round_low(weight), 0.0), 0, keepdims=True)
        own[blocks + r : blocks + r + 1, :width] = spread * new[r : r + 1, width:].astype(F32)
        high = round_low(weight)
        tail = jnp.where(spot == blocks + r, shift, tail)
        tail = jnp.where(spot == 8 + blocks + r, high, tail)
        tail = jnp.where(spot == 16 + blocks + r, weight - high, tail)
    own[:, width:] = tail


def merge_kernel(mine, theirs, both):
    y = lax.axis_index("pool") % 2
    for z in range(both.shape[0]):
        both[z, y] = mine[...]
        both[z, 1 - y] = theirs[...]


def attend_kernel(pieces, own, keys, values, part, residual, tables, scr):
    blocks, block_len, width = keys.shape
    rows = pieces.shape[2]
    heads = width // HD
    most = 8
    me = lax.axis_index("pool")
    for p in range(8):
        scr[p * rows : (p + 1) * rows, :] = pieces[p // 2, p % 2].astype(F32)
    queries = scr[:, :width]
    residual[...] = scr[:, width : 2 * width]
    tail = scr[:, 2 * width :]
    requests = tail.shape[0]
    table = tail * CODE + pltpu.roll(tail, 128 - most, 1) - 1.0
    length = tail[:, 2 * most : 2 * most + 1] * CODE + tail[:, 2 * most + 1 : 2 * most + 2]
    lane = lanes((requests, 128))
    table = jnp.where(lane < most, table, -2.0)
    tables[...] = table
    head_mask = lanes((heads, width)) // HD == rows_of((heads, width))
    spot = lanes((heads, 128))
    tail = own[:, width:]
    scores, limits = [], []
    for b in range(blocks):
        match = jnp.where(table == (me * blocks + b).astype(F32), 1.0, 0.0)
        holder = jnp.sum(match, 1, keepdims=True)
        place = jnp.sum(jnp.sum(match * lane.astype(F32), 1, keepdims=True), 0, keepdims=True)
        limit = jnp.sum(holder * length, 0, keepdims=True) - place * block_len
        limits.append(jnp.broadcast_to(limit, (heads, block_len)))
        query = jnp.sum(holder * queries, 0, keepdims=True)
        spread = jnp.where(head_mask, query, 0.0).astype(BF16)
        scores.append(
            lax.dot_general(
                spread, keys[b], (((1,), (1,)), ((), ())), preferred_element_type=F32
            )
        )
    scores = jnp.concatenate(scores, 0) * (1.0 / math.sqrt(HD))
    token = lanes((blocks * heads, block_len)).astype(F32)
    valid = token < jnp.concatenate(limits, 0)
    scores = jnp.where(valid, scores, LOW)
    shift = round_low(jnp.max(scores, 1, keepdims=True))
    weights = jnp.where(valid, jnp.exp(scores - shift), 0.0)
    total = jnp.sum(weights, 1, keepdims=True)
    high = round_low(total)
    rest = total - high
    numerators = []
    for b in range(blocks):
        mine = slice(b * heads, (b + 1) * heads)
        full = jnp.dot(weights[mine].astype(BF16), values[b], preferred_element_type=F32)
        numerators.append(jnp.sum(jnp.where(head_mask, full, 0.0), 0, keepdims=True))
        tail = jnp.where(spot == b, shift[mine], tail)
        tail = jnp.where(spot == 8 + b, high[mine], tail)
        tail = jnp.where(spot == 16 + b, rest[mine], tail)
    line = rows_of((8, width))
    numer = own[:, :width]
    for b in range(blocks):
        numer = jnp.where(line == b, numerators[b], numer)
    numer = jnp.where(line == 7, flatten(tail, width), numer)
    part[...] = numer.astype(BF16)


def combine_kernel(pieces, tables, weight, head_part, numer, tails, mix):
    requests = tables.shape[0]
    slots = pieces.shape[2]
    width = weight.shape[0]
    heads = width // HD
    rows, blocks = 2, slots - 3
    for owner in range(8):
        values = pieces[owner // 2, owner % 2].astype(F32)
        numer[owner * slots : (owner + 1) * slots, :] = values
        tails[owner] = unflatten(values[slots - 1 : slots], heads)
    lane8 = lanes((heads, 128))
    shifts = jnp.zeros((heads, 128), F32)
    totals = jnp.zeros((heads, 128), F32)
    for owner in range(8):
        tail = tails[owner]
        total = pltpu.roll(tail, 120, 1) + pltpu.roll(tail, 112, 1)
        tail, total = jnp.where(lane8 < 8, tail, 0.0), jnp.where(lane8 < 8, total, 0.0)
        if owner:
            tail, total = pltpu.roll(tail, 8 * owner, 1), pltpu.roll(total, 8 * owner, 1)
        shifts, totals = shifts + tail, totals + total
    lane = lanes((requests, 128))
    owner, slot = lane // slots, lane % slots
    block_id = jnp.where((slot < blocks) & (lane < 64), owner * blocks + slot, -5).astype(F32)
    self_id = jnp.where((slot >= blocks) & (slot < blocks + rows), owner * rows + slot - blocks, -5)
    table = tables[...]
    belongs = (self_id == rows_of((requests, 128))) & (lane < 64)
    for k in range(8):
        belongs = belongs | (table[:, k : k + 1] == block_id)
    for h in range(heads):
        shift = jnp.broadcast_to(shifts[h : h + 1], (requests, 128))
        top = jnp.max(jnp.where(belongs, shift, LOW), 1, keepdims=True)
        scale = jnp.where(belongs, jnp.exp(shift - top), 0.0)
        total = jnp.sum(scale * totals[h : h + 1], 1, keepdims=True)
        mix[h * requests : (h + 1) * requests, :] = scale / total
    full = jnp.dot(
        mix[:, : 8 * slots].astype(BF16), numer[...].astype(BF16), preferred_element_type=F32
    )
    head = lanes((requests, width)) // HD
    attended = jnp.zeros((requests, width), F32)
    for h in range(heads):
        attended = jnp.where(head == h, full[h * requests : (h + 1) * requests], attended)
    head_part[...] = jnp.dot(
        attended.astype(BF16), weight[...], preferred_element_type=F32
    ).astype(BF16)


def sum_kernel(p0, p1, p2, p3, total):
    total[...] = (
        (p0[...].astype(F32) + p1[...].astype(F32)) + (p2[...].astype(F32) + p3[...].astype(F32))
    ).astype(BF16)


def gate_up_kernel(flip, same, all_input, gain, gate, up, sums, own, scr):
    me = lax.axis_index("pool")
    odd = me % 2 == 1
    part = same.shape[1]
    ff = gate.shape[1]
    rows = own.shape[0]
    near, far = same[...].astype(F32), flip[...].astype(F32)
    scr[:, :part] = all_input[:, :part] + jnp.where(odd, far, near)
    scr[:, part:] = all_input[:, part:] + jnp.where(odd, near, far)
    residual = scr[...]
    mine = scr[0:rows, :]
    for p in range(1, residual.shape[0] // rows):
        mine = jnp.where(me == p, scr[p * rows : (p + 1) * rows, :], mine)
    own[...] = mine
    square = jnp.sum(residual * residual, 1, keepdims=True)
    portion = (residual * gain[...].astype(F32)).astype(BF16)
    sums[:, :ff] = jnp.dot(portion, gate[...], preferred_element_type=F32).astype(BF16)
    sums[:, ff : 2 * ff] = jnp.dot(portion, up[...], preferred_element_type=F32).astype(BF16)
    lane = lanes((residual.shape[0], 128))
    high = round_low(square)
    tail = jnp.where(lane == 0, high, jnp.where(lane == 1, square - high, 0.0))
    sums[:, 2 * ff :] = tail.astype(BF16)


def core_sum_kernel(mine, theirs, total):
    ff2 = mine.shape[1] - 128
    total[:, :ff2] = (mine[:, :ff2].astype(F32) + theirs[:, :ff2].astype(F32)).astype(BF16)
    tail = mine[:, ff2:].astype(F32) + theirs[:, ff2:].astype(F32)
    square = jnp.sum(tail, 1, keepdims=True)
    lane = lanes(tail.shape)
    high = round_low(square)
    tail = jnp.where(lane == 0, high, jnp.where(lane == 1, square - high, 0.0))
    total[:, ff2:] = tail.astype(BF16)


def down_kernel(features, mine, theirs, weight, parts, scr):
    ff = weight.shape[0]
    tail = mine[:, 2 * ff :].astype(F32) + theirs[:, 2 * ff :].astype(F32)
    square = jnp.sum(tail, 1, keepdims=True)
    factor = lax.rsqrt(square * (1.0 / features) + 1e-05)
    gate = (mine[:, :ff].astype(F32) + theirs[:, :ff].astype(F32)) * factor
    up = (mine[:, ff : 2 * ff].astype(F32) + theirs[:, ff : 2 * ff].astype(F32)) * factor
    hidden = (gate / (1.0 + jnp.exp(-gate)) * up).astype(BF16)
    scr[...] = jnp.dot(hidden, weight[...], preferred_element_type=F32)
    rows = parts.shape[1]
    pool = parts.shape[0]
    for p in range(pool):
        parts[pool - 1 - p] = scr[p * rows : (p + 1) * rows, :].astype(BF16)


def final_kernel(own, parts, out):
    total = own[...]
    for p in range(parts.shape[0]):
        total = total + parts[p].astype(F32)
    out[...] = total.astype(BF16)


def flip(values, axis, step):
    size = lax.axis_size(axis)
    return lax.ppermute(values, axis, [(index, index ^ step) for index in range(size)])


def per_device_small(
    residual_in,
    query_new,
    key_new,
    value_new,
    key_cache,
    value_cache,
    block_table,
    lengths,
    out_weight,
    norm_gain,
    gate_weight,
    up_weight,
    down_weight,
):
    rows, width = residual_in.shape
    blocks = key_cache.shape[0]
    pool, mlp = 8, 4
    requests = rows * pool
    ff = gate_weight.shape[1]
    part_cols = out_weight.shape[1]
    packed_width = 2 * width + 128
    slots = blocks + rows + 1
    part_width = width + 128

    packed, new = call(
        prepare_kernel,
        "rotary",
        [((rows, packed_width), BF16), ((rows, 2 * width), BF16)],
        [block_table, lengths, query_new, key_new, value_new, residual_in, key_cache, value_cache],
        [pltpu.SMEM(block_table.shape, jnp.int32), pltpu.SMEM(lengths.shape, jnp.int32)]
        + [pltpu.VMEM((rows, width), BF16)] * 4
        + [pltpu.VMEM((8, width), F32), pltpu.SemaphoreType.DMA((6,))],
        hbm=range(8),
        limit=54 * 2**20,
    )

    packed_near, own = call(
        carry_kernel,
        "carry",
        [(packed.shape, BF16), ((slots, part_width), F32)],
        [packed, new],
    )

    def pool_gather(values, near):
        (both,) = call(
            merge_kernel,
            "merge",
            [((pool // 2, 2) + values.shape, values.dtype)],
            [near, flip(values, "pool", 1)],
        )
        lines = [[y + 2 * z for z in range(pool // 2)] for y in range(2)]
        return [lax.all_to_all(both, "pool", 0, 0, axis_index_groups=lines)]

    part, all_input, tables = call(
        attend_kernel,
        "attend",
        [((slots, width), BF16), ((requests, width), F32), ((requests, 128), F32)],
        pool_gather(packed, packed_near) + [own, key_cache, value_cache],
        [pltpu.VMEM((requests, packed_width), F32)],
    )
    (head_part,) = call(
        combine_kernel,
        "combine",
        [((requests, part_cols), BF16)],
        pool_gather(part, part) + [tables, out_weight],
        [
            pltpu.VMEM((pool * slots, width), F32),
            pltpu.VMEM((pool, slots, 128), F32),
            pltpu.VMEM((requests * width // HD, 128), F32),
        ],
    )
    (head_sum,) = call(
        sum_kernel,
        "head_sum",
        [((requests, part_cols), BF16)],
        [head_part] + [flip(head_part, "mlp", step) for step in (3, 2, 1)],
    )
    pieces = []
    for turn in (1, 0):
        route = []
        for m in range(mlp):
            by_distance = sorted(range(4), key=lambda z: (-abs(z - m), z))
            for z, step in zip(by_distance, (1, 0, 3, 2) if m % 2 == 0 else (0, 1, 2, 3)):
                for y in range(2):
                    source = (m * 2 + y) * mlp + (m ^ step)
                    route.append((source, (z * 2 + (y ^ turn)) * mlp + m))
        pieces.append(lax.ppermute(head_sum, ("pool", "mlp"), route))
    sums, own_residual = call(
        gate_up_kernel,
        "gate_up",
        [((requests, 2 * ff + 128), BF16), ((rows, width), F32)],
        pieces + [all_input, norm_gain.reshape(1, width), gate_weight, up_weight],
        [pltpu.VMEM((requests, width), F32)],
    )
    (core_sums,) = call(
        core_sum_kernel,
        "core_sum",
        [((requests, 2 * ff + 128), BF16)],
        [sums, flip(sums, "mlp", 1)],
    )
    (down,) = call(
        functools.partial(down_kernel, width * mlp),
        "down",
        [((pool, rows, width), BF16)],
        [core_sums, flip(core_sums, "mlp", 3), down_weight],
        [pltpu.VMEM((requests, width), F32)],
    )
    backwards = list(range(pool))[::-1]
    (out,) = call(
        final_kernel,
        "final",
        [((rows, width), BF16)],
        [own_residual, lax.all_to_all(down, "pool", 0, 0, axis_index_groups=[backwards])],
    )
    return out


def solution(mesh):
    in_specs = (
        P("pool", "mlp"),
        P("pool", "mlp"),
        P("pool", "mlp"),
        P("pool", "mlp"),
        P("pool", None, "mlp"),
        P("pool", None, "mlp"),
        P("pool", None),
        P("pool"),
        P("mlp", "pool"),
        P("mlp"),
        P("mlp", "pool"),
        P("mlp", "pool"),
        P("pool", "mlp"),
    )
    small = mesh.shape["pool"] == 8 and mesh.shape["mlp"] == 4
    per_device = per_device_small if small else per_device_wide
    return jax.shard_map(
        per_device, mesh=mesh, in_specs=in_specs, out_specs=P("pool", "mlp"), check_vma=False
    )
```

```python
import functools
import math

import jax
import jax.numpy as jnp
import numpy as np
from jax import lax
from jax.experimental import pallas as pl
from jax.experimental.pallas import tpu as pltpu
from jax.sharding import PartitionSpec as P

HD = 96
LOW = -1e30
CODE = 128


def rotate(values, positions):
    half_size = values.shape[-1] // 2
    inverse_freq = 10000.0 ** (-(2.0 * jnp.arange(half_size, dtype=jnp.float32)) / values.shape[-1])
    angles = positions.astype(jnp.float32)[:, None, None] * inverse_freq[None, None, :]
    cosine = jnp.cos(angles)
    sine_part = jnp.sin(angles)
    first = values[..., :half_size]
    second = values[..., half_size:]
    return jnp.concatenate(
        [first * cosine - second * sine_part, second * cosine + first * sine_part], -1
    )


def low(values):
    return lax.reduce_precision(values, 8, 7)


def split(values):
    high = low(values)
    return high.astype(jnp.bfloat16), (values - high).astype(jnp.bfloat16)


def encode(ints):
    return (ints // CODE).astype(jnp.bfloat16), (ints % CODE).astype(jnp.bfloat16)


def decode(high, rest):
    return high.astype(jnp.int32) * CODE + rest.astype(jnp.int32)


def gather(values, axis):
    copies = jnp.broadcast_to(values[None], (lax.axis_size(axis),) + values.shape)
    return lax.all_to_all(copies, axis, 0, 0)


def per_device_wide(
    residual_in,
    query_new,
    key_new,
    value_new,
    key_cache,
    value_cache,
    block_table,
    lengths,
    out_weight,
    norm_gain,
    gate_weight,
    up_weight,
    down_weight,
):
    rows, width = residual_in.shape
    heads = width // HD
    blocks, block_len = key_cache.shape[:2]
    most = block_table.shape[1]
    pool, mlp = lax.axis_size("pool"), lax.axis_size("mlp")
    pool_index = lax.axis_index("pool")
    requests = rows * pool
    score_scale = 1.0 / math.sqrt(HD)
    f32, bf16 = jnp.float32, jnp.bfloat16

    queries = rotate(query_new.astype(f32).reshape(rows, heads, HD), lengths).astype(bf16)
    new_keys = rotate(key_new.astype(f32).reshape(rows, heads, HD), lengths).astype(bf16)

    table_high, table_low = encode(block_table + 1)
    len_high, len_low = encode(lengths)
    packed = jnp.concatenate(
        [
            queries.reshape(rows, width),
            residual_in,
            table_high,
            table_low,
            len_high[:, None],
            len_low[:, None],
        ],
        1,
    )
    spare = -packed.shape[1] % 128
    packed = jnp.pad(packed, ((0, 0), (0, spare)))
    got = gather(packed, "pool").reshape(requests, packed.shape[1])
    all_queries = got[:, :width]
    all_input = got[:, width : 2 * width]
    tail = got[:, 2 * width :]
    tables = decode(tail[:, :most], tail[:, most : 2 * most]) - 1
    all_lengths = decode(tail[:, 2 * most], tail[:, 2 * most + 1])

    held_ids = pool_index * blocks + jnp.arange(blocks, dtype=jnp.int32)
    matches = tables[None, :, :] == held_ids[:, None, None]
    holder = jnp.any(matches, 2)
    block_index = jnp.sum(
        jnp.where(matches, jnp.arange(most, dtype=jnp.int32)[None, None, :], 0), (1, 2)
    )
    valid_len = jnp.sum(jnp.where(holder, all_lengths[None, :], 0), 1)
    block_query = jnp.dot(holder.astype(bf16), all_queries, preferred_element_type=f32)
    block_query = block_query.astype(bf16).reshape(blocks, heads, HD)
    key_rows = key_cache.reshape(blocks, block_len, heads, HD)
    value_rows = value_cache.reshape(blocks, block_len, heads, HD)
    scores = (
        jnp.einsum("bhd,bthd->bht", block_query, key_rows, preferred_element_type=f32)
        * score_scale
    )
    token_pos = block_index[:, None] * block_len + jnp.arange(block_len, dtype=jnp.int32)[None, :]
    valid = (token_pos < valid_len[:, None])[:, None, :]
    scores = jnp.where(valid, scores, LOW)
    shift = low(jnp.max(scores, 2))
    weights = jnp.where(valid, jnp.exp(scores - shift[:, :, None]), 0.0)
    totals = jnp.sum(weights, 2)
    numerator = jnp.einsum(
        "bht,bthd->bhd", weights.astype(bf16), value_rows, preferred_element_type=f32
    )
    self_score = jnp.sum(queries.astype(f32) * new_keys.astype(f32), -1) * score_scale
    self_shift = low(self_score)
    self_weight = jnp.exp(self_score - self_shift)
    self_numer = self_weight[:, :, None] * value_new.astype(f32).reshape(rows, heads, HD)

    own_total = jnp.concatenate([totals, self_weight], 0)
    total_high, total_low = split(own_total)
    part = jnp.concatenate(
        [
            jnp.concatenate([numerator, self_numer], 0)
            .astype(bf16)
            .reshape(blocks + rows, width),
            jnp.concatenate([shift, self_shift], 0).astype(bf16),
            total_high,
            total_low,
        ],
        1,
    )
    part = jnp.pad(part, ((0, 0), (0, -part.shape[1] % 128)))
    count = blocks + rows
    parts = gather(part, "pool").reshape(pool * count, part.shape[1])
    all_shift = parts[:, width : width + heads].astype(f32)
    all_total = parts[:, width + heads : width + 2 * heads].astype(f32) + parts[
        :, width + 2 * heads : width + 3 * heads
    ].astype(f32)
    place = jnp.arange(pool * count, dtype=jnp.int32)
    owner, slot = place // count, place % count
    is_block = slot < blocks
    block_id = jnp.where(is_block, owner * blocks + slot, -2)
    self_id = jnp.where(is_block, -2, owner * rows + slot - blocks)
    request_ids = jnp.arange(requests, dtype=jnp.int32)
    belongs = jnp.any(tables[:, None, :] == block_id[None, :, None], 2) | (
        request_ids[:, None] == self_id[None, :]
    )
    top = jnp.max(jnp.where(belongs[:, :, None], all_shift[None], LOW), 1)
    part_top = jnp.sum(jnp.where(belongs[:, :, None], top[:, None, :], 0.0), 0)
    scale = jnp.exp(all_shift - part_top)
    scaled = parts[:, :width].astype(f32).reshape(-1, heads, HD) * scale[:, :, None]
    mix = belongs.astype(f32)
    numer = jnp.dot(mix, scaled.reshape(-1, width), precision=lax.Precision.HIGHEST)
    denom = jnp.dot(mix, all_total * scale, precision=lax.Precision.HIGHEST)
    attended = (numer.reshape(requests, heads, HD) / denom[:, :, None]).astype(bf16)
    attended = attended.reshape(requests, width)

    head_part = jnp.dot(attended, out_weight, preferred_element_type=f32).astype(bf16)
    share = pool // mlp
    route = []
    for p in range(pool):
        for m in range(mlp):
            route.append((p * mlp + m, ((p % share) * mlp + m) * mlp + p // share))
    moved = lax.ppermute(head_part, ("pool", "mlp"), route)
    head_all = gather(moved, "pool").reshape(share, mlp, requests, -1)
    head_out = low(jnp.sum(head_all.astype(f32), 1))
    head_out = jnp.swapaxes(head_out, 0, 1).reshape(requests, width)
    residual = all_input.astype(f32) + head_out
    squares = jnp.sum(residual * residual, -1, keepdims=True)
    portion = (residual * norm_gain.astype(f32)).astype(bf16)

    ff = gate_weight.shape[1]
    square_high, square_low = split(squares)
    sums = jnp.concatenate(
        [
            jnp.dot(portion, gate_weight, preferred_element_type=f32).astype(bf16),
            jnp.dot(portion, up_weight, preferred_element_type=f32).astype(bf16),
            jnp.broadcast_to(square_high, (requests, 64)),
            jnp.broadcast_to(square_low, (requests, 64)),
        ],
        1,
    )
    summed = jnp.sum(gather(sums, "mlp").astype(f32), 0)
    mean_square = (summed[:, 2 * ff : 2 * ff + 1] + summed[:, 2 * ff + 64 : 2 * ff + 65]) / (
        width * mlp
    )
    factor = lax.rsqrt(mean_square + 1e-05)
    gate = summed[:, :ff] * factor
    up = summed[:, ff : 2 * ff] * factor
    hidden = (jax.nn.silu(gate) * up).astype(bf16)

    down = jnp.dot(hidden, down_weight, preferred_element_type=f32)
    down = lax.all_to_all(down.reshape(pool, rows, width), "pool", 0, 0)
    own = lax.dynamic_slice_in_dim(residual, pool_index * rows, rows, 0)
    return (own + jnp.sum(down, 0)).astype(bf16)


F32, BF16 = jnp.float32, jnp.bfloat16
VMEM = pl.BlockSpec(memory_space=pltpu.VMEM)
HBM = pl.BlockSpec(memory_space=pl.ANY)


def call(kernel, name, outs, args, scratch=(), hbm=(), limit=16 * 2**20):
    size = sum(math.prod(a.shape) * a.dtype.itemsize for a in args)
    return pl.pallas_call(
        kernel,
        out_shape=[jax.ShapeDtypeStruct(shape, dtype) for shape, dtype in outs],
        in_specs=[HBM if i in hbm else VMEM for i in range(len(args))],
        out_specs=[VMEM] * len(outs),
        scratch_shapes=list(scratch),
        compiler_params=pltpu.CompilerParams(vmem_limit_bytes=limit),
        cost_estimate=pl.CostEstimate(flops=0, bytes_accessed=size, transcendentals=0),
        name=name,
    )(*args)


def lanes(shape):
    return lax.broadcasted_iota(jnp.int32, shape, len(shape) - 1)


def in_order(pieces, index):
    for bit in (1, 2):
        odd = (index & bit) != 0
        pieces = [jnp.where(odd, pieces[s ^ bit], pieces[s]) for s in range(4)]
    return pieces


def rows_of(shape):
    return lax.broadcasted_iota(jnp.int32, shape, len(shape) - 2)


def round_low(values):
    return values.astype(BF16).astype(F32)


def head_start(shape):
    return rows_of(shape) * HD % 128


def flatten(tail, width):
    heads = tail.shape[0]
    spread = jnp.zeros((heads, width), F32)
    start = head_start((heads, width))
    for k in (0, 32, 64, 96):
        moved = pltpu.roll(tail, k, 1) if k else tail
        spread = jnp.where(start == k, jnp.concatenate([moved] * (width // 128), 1), spread)
    lane = lanes((heads, width))
    used = (lane // HD == rows_of((heads, width))) & (lane % HD < 24)
    return jnp.sum(jnp.where(used, spread, 0.0), 0, keepdims=True)


def unflatten(row, heads):
    width = row.shape[1]
    lane = lanes((heads, width))
    used = (lane // HD == rows_of((heads, width))) & (lane % HD < 24)
    spread = jnp.where(used, jnp.broadcast_to(row, (heads, width)), 0.0)
    folded = spread[:, :128]
    for at in range(128, width, 128):
        folded = folded + spread[:, at : at + 128]
    start = head_start((heads, 128))
    tail = jnp.where(start == 0, folded, 0.0)
    for k in (32, 64, 96):
        tail = jnp.where(start == k, pltpu.roll(folded, 128 - k, 1), tail)
    return tail


def prepare_kernel(*refs):
    sources, (packed, new), held = refs[:6], refs[8:10], refs[10:16]
    scr, sems = refs[16:]
    copies = [
        pltpu.make_async_copy(source, target, sems.at[i])
        for i, (source, target) in enumerate(zip(sources, held))
    ]
    for copy in copies:
        copy.start()
    table, length, query, key, value, residual = held
    rows, width = query.shape
    most = table.shape[1]
    period = 384
    turn = lanes((8, period)) % (HD // 2)
    freq = jnp.zeros((8, period), F32)
    for i in range(HD // 2):
        freq = jnp.where(turn == i, float(np.float32(10000.0 ** (-2.0 * i / HD))), freq)
    for copy in copies[:2]:
        copy.wait()
    line = rows_of((8, period))
    where_at = jnp.zeros((8, period), F32)
    for r in range(rows):
        here = (line == r) | (line == rows + r)
        where_at = jnp.where(here, length[r].astype(F32), where_at)
    angles = where_at * freq
    cosine = jnp.concatenate([jnp.cos(angles)] * (width // period), 1)
    sine = jnp.concatenate([jnp.sin(angles)] * (width // period), 1)
    for copy in copies[2:]:
        copy.wait()
    scr[...] = jnp.zeros_like(scr)
    scr[0:rows, :] = query[...].astype(F32)
    scr[rows : 2 * rows, :] = key[...].astype(F32)
    values = scr[...]
    first = lanes((8, width)) % HD < HD // 2
    ahead = pltpu.roll(values, width - HD // 2, 1)
    behind = pltpu.roll(values, HD // 2, 1)
    scr[...] = values * cosine + jnp.where(first, -ahead, behind) * sine
    packed[:, :width] = scr[0:rows, :].astype(BF16)
    packed[:, width : 2 * width] = residual[...]
    tail = jnp.zeros((rows, 128), F32)
    at, row = lanes((rows, 128)), rows_of((rows, 128))
    for r in range(rows):
        codes = [table[r, k] + 1 for k in range(most)] + [length[r]]
        spots = [(k, most + k) for k in range(most)] + [(2 * most, 2 * most + 1)]
        for code, (high, rest) in zip(codes, spots):
            tail = jnp.where((row == r) & (at == high), (code >> 7).astype(F32), tail)
            tail = jnp.where((row == r) & (at == rest), (code & 127).astype(F32), tail)
    packed[:, 2 * width :] = tail.astype(BF16)
    new[:, :width] = scr[rows : 2 * rows, :].astype(BF16)
    new[:, width:] = value[...]


def carry_kernel(packed, new, packed_near, own):
    packed_near[...] = packed[...]
    rows, width = new.shape[0], new.shape[1] // 2
    blocks = own.shape[0] - rows - 1
    heads = width // HD
    head_mask = lanes((heads, width)) // HD == rows_of((heads, width))
    product = packed[:, :width].astype(F32) * new[:, :width].astype(F32)
    own[...] = jnp.zeros_like(own)
    spot = lanes((heads, 128))
    tail = jnp.zeros((heads, 128), F32)
    for r in range(rows):
        score = jnp.sum(
            jnp.where(head_mask, jnp.broadcast_to(product[r : r + 1], (heads, width)), 0.0),
            1,
            keepdims=True,
        ) * (1.0 / math.sqrt(HD))
        shift = round_low(score)
        weight = jnp.exp(score - shift)
        spread = jnp.sum(jnp.where(head_mask, round_low(weight), 0.0), 0, keepdims=True)
        own[blocks + r : blocks + r + 1, :width] = spread * new[r : r + 1, width:].astype(F32)
        high = round_low(weight)
        tail = jnp.where(spot == blocks + r, shift, tail)
        tail = jnp.where(spot == 8 + blocks + r, high, tail)
        tail = jnp.where(spot == 16 + blocks + r, weight - high, tail)
    own[:, width:] = tail


def merge_kernel(mine, theirs, both):
    y = lax.axis_index("pool") % 2
    both[y] = mine[...]
    both[1 - y] = theirs[...]


def attend_kernel(a0, a1, a3, a2, own, keys, values, part, residual, tables, scr):
    blocks, block_len, width = keys.shape
    rows = a0.shape[1]
    heads = width // HD
    most = 8
    me = lax.axis_index("pool")
    for y in range(2):
        pieces = [piece[y].astype(F32) for piece in (a0, a1, a2, a3)]
        for z, piece in enumerate(in_order(pieces, me // 2)):
            scr[(z * 2 + y) * rows : (z * 2 + y + 1) * rows, :] = piece
    queries = scr[:, :width]
    residual[...] = scr[:, width : 2 * width]
    tail = scr[:, 2 * width :]
    requests = tail.shape[0]
    table = tail * CODE + pltpu.roll(tail, 128 - most, 1) - 1.0
    length = tail[:, 2 * most : 2 * most + 1] * CODE + tail[:, 2 * most + 1 : 2 * most + 2]
    lane = lanes((requests, 128))
    table = jnp.where(lane < most, table, -2.0)
    tables[...] = table
    head_mask = lanes((heads, width)) // HD == rows_of((heads, width))
    spot = lanes((heads, 128))
    tail = own[:, width:]
    scores, limits = [], []
    for b in range(blocks):
        match = jnp.where(table == (me * blocks + b).astype(F32), 1.0, 0.0)
        holder = jnp.sum(match, 1, keepdims=True)
        place = jnp.sum(jnp.sum(match * lane.astype(F32), 1, keepdims=True), 0, keepdims=True)
        limit = jnp.sum(holder * length, 0, keepdims=True) - place * block_len
        limits.append(jnp.broadcast_to(limit, (heads, block_len)))
        query = jnp.sum(holder * queries, 0, keepdims=True)
        spread = jnp.where(head_mask, query, 0.0).astype(BF16)
        scores.append(
            lax.dot_general(
                spread, keys[b], (((1,), (1,)), ((), ())), preferred_element_type=F32
            )
        )
    scores = jnp.concatenate(scores, 0) * (1.0 / math.sqrt(HD))
    token = lanes((blocks * heads, block_len)).astype(F32)
    valid = token < jnp.concatenate(limits, 0)
    scores = jnp.where(valid, scores, LOW)
    shift = round_low(jnp.max(scores, 1, keepdims=True))
    weights = jnp.where(valid, jnp.exp(scores - shift), 0.0)
    total = jnp.sum(weights, 1, keepdims=True)
    high = round_low(total)
    rest = total - high
    numerators = []
    for b in range(blocks):
        mine = slice(b * heads, (b + 1) * heads)
        full = jnp.dot(weights[mine].astype(BF16), values[b], preferred_element_type=F32)
        numerators.append(jnp.sum(jnp.where(head_mask, full, 0.0), 0, keepdims=True))
        tail = jnp.where(spot == b, shift[mine], tail)
        tail = jnp.where(spot == 8 + b, high[mine], tail)
        tail = jnp.where(spot == 16 + b, rest[mine], tail)
    line = rows_of((8, width))
    numer = own[:, :width]
    for b in range(blocks):
        numer = jnp.where(line == b, numerators[b], numer)
    numer = jnp.where(line == 7, flatten(tail, width), numer)
    part[...] = numer.astype(BF16)


def combine_kernel(b0, b1, b2, b3, tables, weight, head_part, numer, tails):
    requests = tables.shape[0]
    slots = b0.shape[1]
    width = weight.shape[0]
    heads = width // HD
    rows, blocks = 2, slots - 3
    me = lax.axis_index("pool")
    for step, piece in enumerate((b0, b1, b2, b3)):
        z = (me // 2) ^ step
        for y in range(2):
            owner = z * 2 + y
            values = piece[y].astype(F32)
            numer[pl.ds(pl.multiple_of(owner * slots, 8), slots), :] = values
            tails[owner] = unflatten(values[slots - 1 : slots], heads)
    lane8 = lanes((heads, 128))
    shifts = jnp.zeros((heads, 128), F32)
    totals = jnp.zeros((heads, 128), F32)
    for owner in range(8):
        tail = tails[owner]
        total = pltpu.roll(tail, 120, 1) + pltpu.roll(tail, 112, 1)
        tail, total = jnp.where(lane8 < 8, tail, 0.0), jnp.where(lane8 < 8, total, 0.0)
        if owner:
            tail, total = pltpu.roll(tail, 8 * owner, 1), pltpu.roll(total, 8 * owner, 1)
        shifts, totals = shifts + tail, totals + total
    lane = lanes((requests, 128))
    owner, slot = lane // slots, lane % slots
    block_id = jnp.where((slot < blocks) & (lane < 64), owner * blocks + slot, -5).astype(F32)
    self_id = jnp.where((slot >= blocks) & (slot < blocks + rows), owner * rows + slot - blocks, -5)
    table = tables[...]
    belongs = (self_id == rows_of((requests, 128))) & (lane < 64)
    for k in range(8):
        belongs = belongs | (table[:, k : k + 1] == block_id)
    def spread(values):
        rows_each = [jnp.broadcast_to(values[h : h + 1], (requests, 128)) for h in range(heads)]
        return jnp.concatenate(rows_each, 0)

    outside = jnp.concatenate([jnp.where(belongs, 0.0, LOW)] * heads, 0)
    shift = spread(shifts) + outside
    scale = jnp.exp(shift - jnp.max(shift, 1, keepdims=True))
    total = jnp.sum(scale * spread(totals), 1, keepdims=True)
    mix = (scale / total)[:, : 8 * slots].astype(BF16)
    full = jnp.dot(mix, numer[...].astype(BF16), preferred_element_type=F32)
    head = lanes((requests, width)) // HD
    attended = jnp.zeros((requests, width), F32)
    for h in range(heads):
        attended = jnp.where(head == h, full[h * requests : (h + 1) * requests], attended)
    head_part[...] = jnp.dot(
        attended.astype(BF16), weight[...], preferred_element_type=F32
    ).astype(BF16)


def sum_kernel(p0, p1, p2, p3, total):
    total[...] = (
        (p0[...].astype(F32) + p1[...].astype(F32)) + (p2[...].astype(F32) + p3[...].astype(F32))
    ).astype(BF16)


def gate_up_kernel(same, flip, all_input, gain, gate, up, sums, own, scr):
    me = lax.axis_index("pool")
    odd = me % 2 == 1
    part = same.shape[1]
    ff = gate.shape[1]
    rows = own.shape[0]
    near, far = same[...].astype(F32), flip[...].astype(F32)
    scr[:, :part] = all_input[:, :part] + jnp.where(odd, far, near)
    scr[:, part:] = all_input[:, part:] + jnp.where(odd, near, far)
    residual = scr[...]
    mine = scr[0:rows, :]
    for p in range(1, residual.shape[0] // rows):
        mine = jnp.where(me == p, scr[p * rows : (p + 1) * rows, :], mine)
    own[...] = mine
    square = jnp.sum(residual * residual, 1, keepdims=True)
    portion = (residual * gain[...].astype(F32)).astype(BF16)
    sums[:, :ff] = jnp.dot(portion, gate[...], preferred_element_type=F32).astype(BF16)
    sums[:, ff : 2 * ff] = jnp.dot(portion, up[...], preferred_element_type=F32).astype(BF16)
    lane = lanes((residual.shape[0], 128))
    high = round_low(square)
    tail = jnp.where(lane == 0, high, jnp.where(lane == 1, square - high, 0.0))
    sums[:, 2 * ff :] = tail.astype(BF16)


def core_sum_kernel(mine, theirs, total):
    ff2 = mine.shape[1] - 128
    total[:, :ff2] = (mine[:, :ff2].astype(F32) + theirs[:, :ff2].astype(F32)).astype(BF16)
    tail = mine[:, ff2:].astype(F32) + theirs[:, ff2:].astype(F32)
    square = jnp.sum(tail, 1, keepdims=True)
    lane = lanes(tail.shape)
    high = round_low(square)
    tail = jnp.where(lane == 0, high, jnp.where(lane == 1, square - high, 0.0))
    total[:, ff2:] = tail.astype(BF16)


def down_kernel(features, mine, theirs, weight, parts, scr):
    ff = weight.shape[0]
    tail = mine[:, 2 * ff :].astype(F32) + theirs[:, 2 * ff :].astype(F32)
    square = jnp.sum(tail, 1, keepdims=True)
    factor = lax.rsqrt(square * (1.0 / features) + 1e-05)
    gate = (mine[:, :ff].astype(F32) + theirs[:, :ff].astype(F32)) * factor
    up = (mine[:, ff : 2 * ff].astype(F32) + theirs[:, ff : 2 * ff].astype(F32)) * factor
    hidden = (gate / (1.0 + jnp.exp(-gate)) * up).astype(BF16)
    scr[...] = jnp.dot(hidden, weight[...], preferred_element_type=F32)
    rows = parts.shape[1]
    pool = parts.shape[0]
    for p in range(pool):
        parts[pool - 1 - p] = scr[p * rows : (p + 1) * rows, :].astype(BF16)


def final_kernel(own, parts, out):
    total = own[...]
    for p in range(parts.shape[0]):
        total = total + parts[p].astype(F32)
    out[...] = total.astype(BF16)


def flip(values, axis, step):
    size = lax.axis_size(axis)
    return lax.ppermute(values, axis, [(index, index ^ step) for index in range(size)])


def per_device_small(
    residual_in,
    query_new,
    key_new,
    value_new,
    key_cache,
    value_cache,
    block_table,
    lengths,
    out_weight,
    norm_gain,
    gate_weight,
    up_weight,
    down_weight,
):
    rows, width = residual_in.shape
    blocks = key_cache.shape[0]
    pool, mlp = 8, 4
    requests = rows * pool
    ff = gate_weight.shape[1]
    part_cols = out_weight.shape[1]
    packed_width = 2 * width + 128
    slots = blocks + rows + 1
    part_width = width + 128

    packed, new = call(
        prepare_kernel,
        "rotary",
        [((rows, packed_width), BF16), ((rows, 2 * width), BF16)],
        [block_table, lengths, query_new, key_new, value_new, residual_in, key_cache, value_cache],
        [pltpu.SMEM(block_table.shape, jnp.int32), pltpu.SMEM(lengths.shape, jnp.int32)]
        + [pltpu.VMEM((rows, width), BF16)] * 4
        + [pltpu.VMEM((8, width), F32), pltpu.SemaphoreType.DMA((6,))],
        hbm=range(8),
        limit=54 * 2**20,
    )

    packed_near, own = call(
        carry_kernel,
        "carry",
        [(packed.shape, BF16), ((slots, part_width), F32)],
        [packed, new],
    )

    def pool_gather(values, near, steps):
        (both,) = call(
            merge_kernel,
            "merge",
            [((2,) + values.shape, values.dtype)],
            [near, flip(values, "pool", 1)],
        )
        got = {step: flip(both, "pool", step) for step in steps}
        return [both] + [got[step] for step in steps]

    part, all_input, tables = call(
        attend_kernel,
        "attend",
        [((slots, width), BF16), ((requests, width), F32), ((requests, 128), F32)],
        pool_gather(packed, packed_near, (2, 6, 4)) + [own, key_cache, value_cache],
        [pltpu.VMEM((requests, packed_width), F32)],
    )
    (head_part,) = call(
        combine_kernel,
        "combine",
        [((requests, part_cols), BF16)],
        pool_gather(part, part, (2, 4, 6)) + [tables, out_weight],
        [
            pltpu.VMEM((pool * slots, width), F32),
            pltpu.VMEM((pool, slots, 128), F32),
        ],
    )
    (head_sum,) = call(
        sum_kernel,
        "head_sum",
        [((requests, part_cols), BF16)],
        [head_part] + [flip(head_part, "mlp", step) for step in (1, 2, 3)],
    )
    pieces = []
    for turn in range(2):
        route = []
        for m in range(mlp):
            by_distance = sorted(range(4), key=lambda z: (-abs(z - m), z))
            for z, step in zip(by_distance, (1, 0, 3, 2) if m % 2 == 0 else (0, 1, 2, 3)):
                for y in range(2):
                    source = (m * 2 + y) * mlp + (m ^ step)
                    route.append((source, (z * 2 + (y ^ turn)) * mlp + m))
        pieces.append(lax.ppermute(head_sum, ("pool", "mlp"), route))
    sums, own_residual = call(
        gate_up_kernel,
        "gate_up",
        [((requests, 2 * ff + 128), BF16), ((rows, width), F32)],
        pieces + [all_input, norm_gain.reshape(1, width), gate_weight, up_weight],
        [pltpu.VMEM((requests, width), F32)],
    )
    (core_sums,) = call(
        core_sum_kernel,
        "core_sum",
        [((requests, 2 * ff + 128), BF16)],
        [sums, flip(sums, "mlp", 1)],
    )
    (down,) = call(
        functools.partial(down_kernel, width * mlp),
        "down",
        [((pool, rows, width), BF16)],
        [core_sums, flip(core_sums, "mlp", 3), down_weight],
        [pltpu.VMEM((requests, width), F32)],
    )
    backwards = list(range(pool))[::-1]
    (out,) = call(
        final_kernel,
        "final",
        [((rows, width), BF16)],
        [own_residual, lax.all_to_all(down, "pool", 0, 0, axis_index_groups=[backwards])],
    )
    return out


def solution(mesh):
    in_specs = (
        P("pool", "mlp"),
        P("pool", "mlp"),
        P("pool", "mlp"),
        P("pool", "mlp"),
        P("pool", None, "mlp"),
        P("pool", None, "mlp"),
        P("pool", None),
        P("pool"),
        P("mlp", "pool"),
        P("mlp"),
        P("mlp", "pool"),
        P("mlp", "pool"),
        P("pool", "mlp"),
    )
    small = mesh.shape["pool"] == 8 and mesh.shape["mlp"] == 4
    per_device = per_device_small if small else per_device_wide
    return jax.shard_map(
        per_device, mesh=mesh, in_specs=in_specs, out_specs=P("pool", "mlp"), check_vma=False
    )
```

```python
import functools
import math

import jax
import jax.numpy as jnp
import numpy as np
from jax import lax
from jax.experimental import pallas as pl
from jax.experimental.pallas import tpu as pltpu
from jax.sharding import PartitionSpec as P

HD = 96
LOW = -1e30
CODE = 128


def rotate(values, positions):
    half_size = values.shape[-1] // 2
    inverse_freq = 10000.0 ** (-(2.0 * jnp.arange(half_size, dtype=jnp.float32)) / values.shape[-1])
    angles = positions.astype(jnp.float32)[:, None, None] * inverse_freq[None, None, :]
    cosine = jnp.cos(angles)
    sine_part = jnp.sin(angles)
    first = values[..., :half_size]
    second = values[..., half_size:]
    return jnp.concatenate(
        [first * cosine - second * sine_part, second * cosine + first * sine_part], -1
    )


def low(values):
    return lax.reduce_precision(values, 8, 7)


def split(values):
    high = low(values)
    return high.astype(jnp.bfloat16), (values - high).astype(jnp.bfloat16)


def encode(ints):
    return (ints // CODE).astype(jnp.bfloat16), (ints % CODE).astype(jnp.bfloat16)


def decode(high, rest):
    return high.astype(jnp.int32) * CODE + rest.astype(jnp.int32)


def gather(values, axis):
    copies = jnp.broadcast_to(values[None], (lax.axis_size(axis),) + values.shape)
    return lax.all_to_all(copies, axis, 0, 0)


def per_device_wide(
    residual_in,
    query_new,
    key_new,
    value_new,
    key_cache,
    value_cache,
    block_table,
    lengths,
    out_weight,
    norm_gain,
    gate_weight,
    up_weight,
    down_weight,
):
    rows, width = residual_in.shape
    heads = width // HD
    blocks, block_len = key_cache.shape[:2]
    most = block_table.shape[1]
    pool, mlp = lax.axis_size("pool"), lax.axis_size("mlp")
    pool_index = lax.axis_index("pool")
    requests = rows * pool
    score_scale = 1.0 / math.sqrt(HD)
    f32, bf16 = jnp.float32, jnp.bfloat16

    queries = rotate(query_new.astype(f32).reshape(rows, heads, HD), lengths).astype(bf16)
    new_keys = rotate(key_new.astype(f32).reshape(rows, heads, HD), lengths).astype(bf16)

    table_high, table_low = encode(block_table + 1)
    len_high, len_low = encode(lengths)
    packed = jnp.concatenate(
        [
            queries.reshape(rows, width),
            residual_in,
            table_high,
            table_low,
            len_high[:, None],
            len_low[:, None],
        ],
        1,
    )
    spare = -packed.shape[1] % 128
    packed = jnp.pad(packed, ((0, 0), (0, spare)))
    got = gather(packed, "pool").reshape(requests, packed.shape[1])
    all_queries = got[:, :width]
    all_input = got[:, width : 2 * width]
    tail = got[:, 2 * width :]
    tables = decode(tail[:, :most], tail[:, most : 2 * most]) - 1
    all_lengths = decode(tail[:, 2 * most], tail[:, 2 * most + 1])

    held_ids = pool_index * blocks + jnp.arange(blocks, dtype=jnp.int32)
    matches = tables[None, :, :] == held_ids[:, None, None]
    holder = jnp.any(matches, 2)
    block_index = jnp.sum(
        jnp.where(matches, jnp.arange(most, dtype=jnp.int32)[None, None, :], 0), (1, 2)
    )
    valid_len = jnp.sum(jnp.where(holder, all_lengths[None, :], 0), 1)
    block_query = jnp.dot(holder.astype(bf16), all_queries, preferred_element_type=f32)
    block_query = block_query.astype(bf16).reshape(blocks, heads, HD)
    key_rows = key_cache.reshape(blocks, block_len, heads, HD)
    value_rows = value_cache.reshape(blocks, block_len, heads, HD)
    scores = (
        jnp.einsum("bhd,bthd->bht", block_query, key_rows, preferred_element_type=f32)
        * score_scale
    )
    token_pos = block_index[:, None] * block_len + jnp.arange(block_len, dtype=jnp.int32)[None, :]
    valid = (token_pos < valid_len[:, None])[:, None, :]
    scores = jnp.where(valid, scores, LOW)
    shift = low(jnp.max(scores, 2))
    weights = jnp.where(valid, jnp.exp(scores - shift[:, :, None]), 0.0)
    totals = jnp.sum(weights, 2)
    numerator = jnp.einsum(
        "bht,bthd->bhd", weights.astype(bf16), value_rows, preferred_element_type=f32
    )
    self_score = jnp.sum(queries.astype(f32) * new_keys.astype(f32), -1) * score_scale
    self_shift = low(self_score)
    self_weight = jnp.exp(self_score - self_shift)
    self_numer = self_weight[:, :, None] * value_new.astype(f32).reshape(rows, heads, HD)

    own_total = jnp.concatenate([totals, self_weight], 0)
    total_high, total_low = split(own_total)
    part = jnp.concatenate(
        [
            jnp.concatenate([numerator, self_numer], 0)
            .astype(bf16)
            .reshape(blocks + rows, width),
            jnp.concatenate([shift, self_shift], 0).astype(bf16),
            total_high,
            total_low,
        ],
        1,
    )
    part = jnp.pad(part, ((0, 0), (0, -part.shape[1] % 128)))
    count = blocks + rows
    parts = gather(part, "pool").reshape(pool * count, part.shape[1])
    all_shift = parts[:, width : width + heads].astype(f32)
    all_total = parts[:, width + heads : width + 2 * heads].astype(f32) + parts[
        :, width + 2 * heads : width + 3 * heads
    ].astype(f32)
    place = jnp.arange(pool * count, dtype=jnp.int32)
    owner, slot = place // count, place % count
    is_block = slot < blocks
    block_id = jnp.where(is_block, owner * blocks + slot, -2)
    self_id = jnp.where(is_block, -2, owner * rows + slot - blocks)
    request_ids = jnp.arange(requests, dtype=jnp.int32)
    belongs = jnp.any(tables[:, None, :] == block_id[None, :, None], 2) | (
        request_ids[:, None] == self_id[None, :]
    )
    top = jnp.max(jnp.where(belongs[:, :, None], all_shift[None], LOW), 1)
    part_top = jnp.sum(jnp.where(belongs[:, :, None], top[:, None, :], 0.0), 0)
    scale = jnp.exp(all_shift - part_top)
    scaled = parts[:, :width].astype(f32).reshape(-1, heads, HD) * scale[:, :, None]
    mix = belongs.astype(f32)
    numer = jnp.dot(mix, scaled.reshape(-1, width), precision=lax.Precision.HIGHEST)
    denom = jnp.dot(mix, all_total * scale, precision=lax.Precision.HIGHEST)
    attended = (numer.reshape(requests, heads, HD) / denom[:, :, None]).astype(bf16)
    attended = attended.reshape(requests, width)

    head_part = jnp.dot(attended, out_weight, preferred_element_type=f32).astype(bf16)
    share = pool // mlp
    route = []
    for p in range(pool):
        for m in range(mlp):
            route.append((p * mlp + m, ((p % share) * mlp + m) * mlp + p // share))
    moved = lax.ppermute(head_part, ("pool", "mlp"), route)
    head_all = gather(moved, "pool").reshape(share, mlp, requests, -1)
    head_out = low(jnp.sum(head_all.astype(f32), 1))
    head_out = jnp.swapaxes(head_out, 0, 1).reshape(requests, width)
    residual = all_input.astype(f32) + head_out
    squares = jnp.sum(residual * residual, -1, keepdims=True)
    portion = (residual * norm_gain.astype(f32)).astype(bf16)

    ff = gate_weight.shape[1]
    square_high, square_low = split(squares)
    sums = jnp.concatenate(
        [
            jnp.dot(portion, gate_weight, preferred_element_type=f32).astype(bf16),
            jnp.dot(portion, up_weight, preferred_element_type=f32).astype(bf16),
            jnp.broadcast_to(square_high, (requests, 64)),
            jnp.broadcast_to(square_low, (requests, 64)),
        ],
        1,
    )
    summed = jnp.sum(gather(sums, "mlp").astype(f32), 0)
    mean_square = (summed[:, 2 * ff : 2 * ff + 1] + summed[:, 2 * ff + 64 : 2 * ff + 65]) / (
        width * mlp
    )
    factor = lax.rsqrt(mean_square + 1e-05)
    gate = summed[:, :ff] * factor
    up = summed[:, ff : 2 * ff] * factor
    hidden = (jax.nn.silu(gate) * up).astype(bf16)

    down = jnp.dot(hidden, down_weight, preferred_element_type=f32)
    down = lax.all_to_all(down.reshape(pool, rows, width), "pool", 0, 0)
    own = lax.dynamic_slice_in_dim(residual, pool_index * rows, rows, 0)
    return (own + jnp.sum(down, 0)).astype(bf16)


F32, BF16 = jnp.float32, jnp.bfloat16

ROUTES = (
    ((1, 1, 1, 1), (2, 0, 3, 1), (2, 3, 0, 1)),
    ((0, 0, 0, 1), (2, 0, 3, 1), (0, 3, 1, 2)),
    ((1, 1, 0, 1), (2, 3, 0, 1), (3, 1, 2, 0)),
    ((1, 1, 1, 1), (2, 3, 1, 0), (3, 2, 1, 0)),
)
VMEM = pl.BlockSpec(memory_space=pltpu.VMEM)
HBM = pl.BlockSpec(memory_space=pl.ANY)


def call(kernel, name, outs, args, scratch=(), hbm=(), limit=16 * 2**20):
    size = sum(math.prod(a.shape) * a.dtype.itemsize for a in args)
    return pl.pallas_call(
        kernel,
        out_shape=[jax.ShapeDtypeStruct(shape, dtype) for shape, dtype in outs],
        in_specs=[HBM if i in hbm else VMEM for i in range(len(args))],
        out_specs=[VMEM] * len(outs),
        scratch_shapes=list(scratch),
        compiler_params=pltpu.CompilerParams(vmem_limit_bytes=limit),
        cost_estimate=pl.CostEstimate(flops=0, bytes_accessed=size, transcendentals=0),
        name=name,
    )(*args)


def lanes(shape):
    return lax.broadcasted_iota(jnp.int32, shape, len(shape) - 1)


def in_order(pieces, index):
    for bit in (1, 2):
        odd = (index & bit) != 0
        pieces = [jnp.where(odd, pieces[s ^ bit], pieces[s]) for s in range(4)]
    return pieces


def rows_of(shape):
    return lax.broadcasted_iota(jnp.int32, shape, len(shape) - 2)


def round_low(values):
    return values.astype(BF16).astype(F32)


def head_start(shape):
    return rows_of(shape) * HD % 128


def flatten(tail, width):
    heads = tail.shape[0]
    spread = jnp.zeros((heads, width), F32)
    start = head_start((heads, width))
    for k in (0, 32, 64, 96):
        moved = pltpu.roll(tail, k, 1) if k else tail
        spread = jnp.where(start == k, jnp.concatenate([moved] * (width // 128), 1), spread)
    lane = lanes((heads, width))
    used = (lane // HD == rows_of((heads, width))) & (lane % HD < 24)
    return jnp.sum(jnp.where(used, spread, 0.0), 0, keepdims=True)


def unflatten(row, heads):
    width = row.shape[1]
    lane = lanes((heads, width))
    used = (lane // HD == rows_of((heads, width))) & (lane % HD < 24)
    spread = jnp.where(used, jnp.broadcast_to(row, (heads, width)), 0.0)
    folded = spread[:, :128]
    for at in range(128, width, 128):
        folded = folded + spread[:, at : at + 128]
    start = head_start((heads, 128))
    tail = jnp.where(start == 0, folded, 0.0)
    for k in (32, 64, 96):
        tail = jnp.where(start == k, pltpu.roll(folded, 128 - k, 1), tail)
    return tail


def prepare_kernel(*refs):
    sources, (packed, new), held = refs[:6], refs[8:10], refs[10:16]
    scr, sems = refs[16:]
    copies = [
        pltpu.make_async_copy(source, target, sems.at[i])
        for i, (source, target) in enumerate(zip(sources, held))
    ]
    for copy in copies:
        copy.start()
    table, length, query, key, value, residual = held
    rows, width = query.shape
    most = table.shape[1]
    period = 384
    turn = lanes((8, period)) % (HD // 2)
    freq = jnp.zeros((8, period), F32)
    for i in range(HD // 2):
        freq = jnp.where(turn == i, float(np.float32(10000.0 ** (-2.0 * i / HD))), freq)
    for copy in copies:
        copy.wait()
    scr[...] = jnp.zeros_like(scr)
    scr[0:rows, :] = query[...].astype(F32)
    scr[rows : 2 * rows, :] = key[...].astype(F32)
    values = scr[...]
    line = rows_of((8, period))
    where_at = jnp.zeros((8, period), F32)
    for r in range(rows):
        here = (line == r) | (line == rows + r)
        where_at = jnp.where(here, length[r].astype(F32), where_at)
    angles = where_at * freq
    cosine = jnp.concatenate([jnp.cos(angles)] * (width // period), 1)
    sine = jnp.concatenate([jnp.sin(angles)] * (width // period), 1)
    first = lanes((8, width)) % HD < HD // 2
    ahead = pltpu.roll(values, width - HD // 2, 1)
    behind = pltpu.roll(values, HD // 2, 1)
    scr[...] = values * cosine + jnp.where(first, -ahead, behind) * sine
    packed[:, :width] = scr[0:rows, :].astype(BF16)
    packed[:, width : 2 * width] = residual[...]
    tail = jnp.zeros((rows, 128), F32)
    at, row = lanes((rows, 128)), rows_of((rows, 128))
    for r in range(rows):
        codes = [table[r, k] + 1 for k in range(most)] + [length[r]]
        spots = [(k, most + k) for k in range(most)] + [(2 * most, 2 * most + 1)]
        for code, (high, rest) in zip(codes, spots):
            tail = jnp.where((row == r) & (at == high), (code >> 7).astype(F32), tail)
            tail = jnp.where((row == r) & (at == rest), (code & 127).astype(F32), tail)
    packed[:, 2 * width :] = tail.astype(BF16)
    new[:, :width] = scr[rows : 2 * rows, :].astype(BF16)
    new[:, width:] = value[...]


def carry_kernel(packed, new, packed_near, own):
    packed_near[...] = packed[...]
    rows, width = new.shape[0], new.shape[1] // 2
    blocks = own.shape[0] - rows - 1
    heads = width // HD
    head_mask = lanes((heads, width)) // HD == rows_of((heads, width))
    product = packed[:, :width].astype(F32) * new[:, :width].astype(F32)
    own[...] = jnp.zeros_like(own)
    spot = lanes((heads, 128))
    tail = jnp.zeros((heads, 128), F32)
    for r in range(rows):
        score = jnp.sum(
            jnp.where(head_mask, jnp.broadcast_to(product[r : r + 1], (heads, width)), 0.0),
            1,
            keepdims=True,
        ) * (1.0 / math.sqrt(HD))
        shift = round_low(score)
        weight = jnp.exp(score - shift)
        spread = jnp.sum(jnp.where(head_mask, round_low(weight), 0.0), 0, keepdims=True)
        own[blocks + r : blocks + r + 1, :width] = spread * new[r : r + 1, width:].astype(F32)
        high = round_low(weight)
        tail = jnp.where(spot == blocks + r, shift, tail)
        tail = jnp.where(spot == 8 + blocks + r, high, tail)
        tail = jnp.where(spot == 16 + blocks + r, weight - high, tail)
    own[:, width:] = tail


def merge_kernel(mine, theirs, both):
    y = lax.axis_index("pool") % 2
    both[y] = mine[...]
    both[1 - y] = theirs[...]


def attend_kernel(a0, a1, a2, a3, own, keys, values, part, residual, tables, scr):
    blocks, block_len, width = keys.shape
    rows = a0.shape[1]
    heads = width // HD
    most = 8
    me = lax.axis_index("pool")
    for y in range(2):
        pieces = [piece[y].astype(F32) for piece in (a0, a1, a2, a3)]
        for z, piece in enumerate(in_order(pieces, me // 2)):
            scr[(z * 2 + y) * rows : (z * 2 + y + 1) * rows, :] = piece
    queries = scr[:, :width]
    residual[...] = scr[:, width : 2 * width]
    tail = scr[:, 2 * width :]
    requests = tail.shape[0]
    table = tail * CODE + pltpu.roll(tail, 128 - most, 1) - 1.0
    length = tail[:, 2 * most : 2 * most + 1] * CODE + tail[:, 2 * most + 1 : 2 * most + 2]
    lane = lanes((requests, 128))
    table = jnp.where(lane < most, table, -2.0)
    tables[...] = table
    head_mask = lanes((heads, width)) // HD == rows_of((heads, width))
    spot = lanes((heads, 128))
    tail = own[:, width:]
    scores, limits = [], []
    for b in range(blocks):
        match = jnp.where(table == (me * blocks + b).astype(F32), 1.0, 0.0)
        holder = jnp.sum(match, 1, keepdims=True)
        place = jnp.sum(jnp.sum(match * lane.astype(F32), 1, keepdims=True), 0, keepdims=True)
        limit = jnp.sum(holder * length, 0, keepdims=True) - place * block_len
        limits.append(jnp.broadcast_to(limit, (heads, block_len)))
        query = jnp.sum(holder * queries, 0, keepdims=True)
        spread = jnp.where(head_mask, query, 0.0).astype(BF16)
        scores.append(
            lax.dot_general(
                spread, keys[b], (((1,), (1,)), ((), ())), preferred_element_type=F32
            )
        )
    scores = jnp.concatenate(scores, 0) * (1.0 / math.sqrt(HD))
    token = lanes((blocks * heads, block_len)).astype(F32)
    valid = token < jnp.concatenate(limits, 0)
    scores = jnp.where(valid, scores, LOW)
    shift = round_low(jnp.max(scores, 1, keepdims=True))
    weights = jnp.where(valid, jnp.exp(scores - shift), 0.0)
    total = jnp.sum(weights, 1, keepdims=True)
    high = round_low(total)
    rest = total - high
    numerators = []
    for b in range(blocks):
        mine = slice(b * heads, (b + 1) * heads)
        full = jnp.dot(weights[mine].astype(BF16), values[b], preferred_element_type=F32)
        numerators.append(jnp.sum(jnp.where(head_mask, full, 0.0), 0, keepdims=True))
        tail = jnp.where(spot == b, shift[mine], tail)
        tail = jnp.where(spot == 8 + b, high[mine], tail)
        tail = jnp.where(spot == 16 + b, rest[mine], tail)
    line = rows_of((8, width))
    numer = own[:, :width]
    for b in range(blocks):
        numer = jnp.where(line == b, numerators[b], numer)
    numer = jnp.where(line == 7, flatten(tail, width), numer)
    part[...] = numer.astype(BF16)


def combine_kernel(b0, b1, b2, b3, tables, weight, head_part, numer, tails, mix):
    requests = tables.shape[0]
    slots = b0.shape[1]
    width = weight.shape[0]
    heads = width // HD
    rows, blocks = 2, slots - 3
    me = lax.axis_index("pool")
    for step, piece in enumerate((b0, b1, b2, b3)):
        z = (me // 2) ^ step
        for y in range(2):
            owner = z * 2 + y
            values = piece[y].astype(F32)
            numer[pl.ds(pl.multiple_of(owner * slots, 8), slots), :] = values
            tails[owner] = unflatten(values[slots - 1 : slots], heads)
    lane8 = lanes((heads, 128))
    shifts = jnp.zeros((heads, 128), F32)
    totals = jnp.zeros((heads, 128), F32)
    for owner in range(8):
        tail = tails[owner]
        total = pltpu.roll(tail, 120, 1) + pltpu.roll(tail, 112, 1)
        tail, total = jnp.where(lane8 < 8, tail, 0.0), jnp.where(lane8 < 8, total, 0.0)
        if owner:
            tail, total = pltpu.roll(tail, 8 * owner, 1), pltpu.roll(total, 8 * owner, 1)
        shifts, totals = shifts + tail, totals + total
    lane = lanes((requests, 128))
    owner, slot = lane // slots, lane % slots
    block_id = jnp.where((slot < blocks) & (lane < 64), owner * blocks + slot, -5).astype(F32)
    self_id = jnp.where((slot >= blocks) & (slot < blocks + rows), owner * rows + slot - blocks, -5)
    table = tables[...]
    belongs = (self_id == rows_of((requests, 128))) & (lane < 64)
    for k in range(8):
        belongs = belongs | (table[:, k : k + 1] == block_id)
    for h in range(heads):
        shift = jnp.broadcast_to(shifts[h : h + 1], (requests, 128))
        top = jnp.max(jnp.where(belongs, shift, LOW), 1, keepdims=True)
        scale = jnp.where(belongs, jnp.exp(shift - top), 0.0)
        total = jnp.sum(scale * totals[h : h + 1], 1, keepdims=True)
        mix[h * requests : (h + 1) * requests, :] = scale / total
    full = jnp.dot(
        mix[:, : 8 * slots].astype(BF16), numer[...].astype(BF16), preferred_element_type=F32
    )
    head = lanes((requests, width)) // HD
    attended = jnp.zeros((requests, width), F32)
    for h in range(heads):
        attended = jnp.where(head == h, full[h * requests : (h + 1) * requests], attended)
    head_part[...] = jnp.dot(
        attended.astype(BF16), weight[...], preferred_element_type=F32
    ).astype(BF16)


def sum_kernel(p0, p1, p2, p3, total):
    total[...] = (
        (p0[...].astype(F32) + p1[...].astype(F32)) + (p2[...].astype(F32) + p3[...].astype(F32))
    ).astype(BF16)


def gate_up_kernel(second, first, all_input, gain, gate, up, sums, own, scr):
    me = lax.axis_index("pool")
    place = lax.axis_index("mlp") * 4 + me // 2
    crossed = functools.reduce(
        lambda found, at: jnp.where(place == at, 1, found),
        [m * 4 + z for m in range(4) for z in range(4) if ROUTES[m][0][z]],
        0,
    )
    swapped = (me % 2) ^ crossed == 1
    part = first.shape[1]
    ff = gate.shape[1]
    rows = own.shape[0]
    one, other = first[...].astype(F32), second[...].astype(F32)
    scr[:, :part] = all_input[:, :part] + jnp.where(swapped, other, one)
    scr[:, part:] = all_input[:, part:] + jnp.where(swapped, one, other)
    residual = scr[...]
    mine = scr[0:rows, :]
    for p in range(1, residual.shape[0] // rows):
        mine = jnp.where(me == p, scr[p * rows : (p + 1) * rows, :], mine)
    own[...] = mine
    square = jnp.sum(residual * residual, 1, keepdims=True)
    portion = (residual * gain[...].astype(F32)).astype(BF16)
    sums[:, :ff] = jnp.dot(portion, gate[...], preferred_element_type=F32).astype(BF16)
    sums[:, ff : 2 * ff] = jnp.dot(portion, up[...], preferred_element_type=F32).astype(BF16)
    lane = lanes((residual.shape[0], 128))
    high = round_low(square)
    tail = jnp.where(lane == 0, high, jnp.where(lane == 1, square - high, 0.0))
    sums[:, 2 * ff :] = tail.astype(BF16)


def core_sum_kernel(mine, theirs, total):
    ff2 = mine.shape[1] - 128
    total[:, :ff2] = (mine[:, :ff2].astype(F32) + theirs[:, :ff2].astype(F32)).astype(BF16)
    tail = mine[:, ff2:].astype(F32) + theirs[:, ff2:].astype(F32)
    square = jnp.sum(tail, 1, keepdims=True)
    lane = lanes(tail.shape)
    high = round_low(square)
    tail = jnp.where(lane == 0, high, jnp.where(lane == 1, square - high, 0.0))
    total[:, ff2:] = tail.astype(BF16)


def down_kernel(features, mine, theirs, weight, parts, scr):
    ff = weight.shape[0]
    tail = mine[:, 2 * ff :].astype(F32) + theirs[:, 2 * ff :].astype(F32)
    square = jnp.sum(tail, 1, keepdims=True)
    factor = lax.rsqrt(square * (1.0 / features) + 1e-05)
    gate = (mine[:, :ff].astype(F32) + theirs[:, :ff].astype(F32)) * factor
    up = (mine[:, ff : 2 * ff].astype(F32) + theirs[:, ff : 2 * ff].astype(F32)) * factor
    hidden = (gate / (1.0 + jnp.exp(-gate)) * up).astype(BF16)
    scr[...] = jnp.dot(hidden, weight[...], preferred_element_type=F32)
    rows = parts.shape[1]
    pool = parts.shape[0]
    for p in range(pool):
        parts[pool - 1 - p] = scr[p * rows : (p + 1) * rows, :].astype(BF16)


def final_kernel(own, parts, out):
    total = own[...]
    for p in range(parts.shape[0]):
        total = total + parts[p].astype(F32)
    out[...] = total.astype(BF16)


def flip(values, axis, step):
    size = lax.axis_size(axis)
    return lax.ppermute(values, axis, [(index, index ^ step) for index in range(size)])


def per_device_small(
    residual_in,
    query_new,
    key_new,
    value_new,
    key_cache,
    value_cache,
    block_table,
    lengths,
    out_weight,
    norm_gain,
    gate_weight,
    up_weight,
    down_weight,
):
    rows, width = residual_in.shape
    blocks = key_cache.shape[0]
    pool, mlp = 8, 4
    requests = rows * pool
    ff = gate_weight.shape[1]
    part_cols = out_weight.shape[1]
    packed_width = 2 * width + 128
    slots = blocks + rows + 1
    part_width = width + 128

    packed, new = call(
        prepare_kernel,
        "rotary",
        [((rows, packed_width), BF16), ((rows, 2 * width), BF16)],
        [block_table, lengths, query_new, key_new, value_new, residual_in, key_cache, value_cache],
        [pltpu.SMEM(block_table.shape, jnp.int32), pltpu.SMEM(lengths.shape, jnp.int32)]
        + [pltpu.VMEM((rows, width), BF16)] * 4
        + [pltpu.VMEM((8, width), F32), pltpu.SemaphoreType.DMA((6,))],
        hbm=range(8),
        limit=54 * 2**20,
    )

    packed_near, own = call(
        carry_kernel,
        "carry",
        [(packed.shape, BF16), ((slots, part_width), F32)],
        [packed, new],
    )

    def pool_gather(values, near):
        (both,) = call(
            merge_kernel,
            "merge",
            [((2,) + values.shape, values.dtype)],
            [near, flip(values, "pool", 1)],
        )
        return [both] + [flip(both, "pool", step) for step in (2, 4, 6)]

    part, all_input, tables = call(
        attend_kernel,
        "attend",
        [((slots, width), BF16), ((requests, width), F32), ((requests, 128), F32)],
        pool_gather(packed, packed_near) + [own, key_cache, value_cache],
        [pltpu.VMEM((requests, packed_width), F32)],
    )
    (head_part,) = call(
        combine_kernel,
        "combine",
        [((requests, part_cols), BF16)],
        pool_gather(part, part) + [tables, out_weight],
        [
            pltpu.VMEM((pool * slots, width), F32),
            pltpu.VMEM((pool, slots, 128), F32),
            pltpu.VMEM((requests * width // HD, 128), F32),
        ],
    )
    (head_sum,) = call(
        sum_kernel,
        "head_sum",
        [((requests, part_cols), BF16)],
        [head_part] + [flip(head_part, "mlp", step) for step in (1, 2, 3)],
    )
    pieces = []
    for turn in (1, 0):
        route = []
        for m, (crossing, *members) in enumerate(ROUTES):
            for z in range(4):
                for y in range(2):
                    source = (m * 2 + (y ^ crossing[z] ^ turn)) * mlp + members[turn][z]
                    route.append((source, (z * 2 + y) * mlp + m))
        pieces.append(lax.ppermute(head_sum, ("pool", "mlp"), route))
    sums, own_residual = call(
        gate_up_kernel,
        "gate_up",
        [((requests, 2 * ff + 128), BF16), ((rows, width), F32)],
        pieces + [all_input, norm_gain.reshape(1, width), gate_weight, up_weight],
        [pltpu.VMEM((requests, width), F32)],
    )
    (core_sums,) = call(
        core_sum_kernel,
        "core_sum",
        [((requests, 2 * ff + 128), BF16)],
        [sums, flip(sums, "mlp", 1)],
    )
    (down,) = call(
        functools.partial(down_kernel, width * mlp),
        "down",
        [((pool, rows, width), BF16)],
        [core_sums, flip(core_sums, "mlp", 3), down_weight],
        [pltpu.VMEM((requests, width), F32)],
    )
    backwards = list(range(pool))[::-1]
    (out,) = call(
        final_kernel,
        "final",
        [((rows, width), BF16)],
        [own_residual, lax.all_to_all(down, "pool", 0, 0, axis_index_groups=[backwards])],
    )
    return out


def solution(mesh):
    in_specs = (
        P("pool", "mlp"),
        P("pool", "mlp"),
        P("pool", "mlp"),
        P("pool", "mlp"),
        P("pool", None, "mlp"),
        P("pool", None, "mlp"),
        P("pool", None),
        P("pool"),
        P("mlp", "pool"),
        P("mlp"),
        P("mlp", "pool"),
        P("mlp", "pool"),
        P("pool", "mlp"),
    )
    small = mesh.shape["pool"] == 8 and mesh.shape["mlp"] == 4
    per_device = per_device_small if small else per_device_wide
    return jax.shard_map(
        per_device, mesh=mesh, in_specs=in_specs, out_specs=P("pool", "mlp"), check_vma=False
    )
```

```python
import functools
import math

import jax
import jax.numpy as jnp
import numpy as np
from jax import lax
from jax.experimental import pallas as pl
from jax.experimental.pallas import tpu as pltpu
from jax.sharding import PartitionSpec as P

HD = 96
LOW = -1e30
CODE = 128


def rotate(values, positions):
    half_size = values.shape[-1] // 2
    inverse_freq = 10000.0 ** (-(2.0 * jnp.arange(half_size, dtype=jnp.float32)) / values.shape[-1])
    angles = positions.astype(jnp.float32)[:, None, None] * inverse_freq[None, None, :]
    cosine = jnp.cos(angles)
    sine_part = jnp.sin(angles)
    first = values[..., :half_size]
    second = values[..., half_size:]
    return jnp.concatenate(
        [first * cosine - second * sine_part, second * cosine + first * sine_part], -1
    )


def low(values):
    return lax.reduce_precision(values, 8, 7)


def split(values):
    high = low(values)
    return high.astype(jnp.bfloat16), (values - high).astype(jnp.bfloat16)


def encode(ints):
    return (ints // CODE).astype(jnp.bfloat16), (ints % CODE).astype(jnp.bfloat16)


def decode(high, rest):
    return high.astype(jnp.int32) * CODE + rest.astype(jnp.int32)


def gather(values, axis):
    copies = jnp.broadcast_to(values[None], (lax.axis_size(axis),) + values.shape)
    return lax.all_to_all(copies, axis, 0, 0)


def per_device_wide(
    residual_in,
    query_new,
    key_new,
    value_new,
    key_cache,
    value_cache,
    block_table,
    lengths,
    out_weight,
    norm_gain,
    gate_weight,
    up_weight,
    down_weight,
):
    rows, width = residual_in.shape
    heads = width // HD
    blocks, block_len = key_cache.shape[:2]
    most = block_table.shape[1]
    pool, mlp = lax.axis_size("pool"), lax.axis_size("mlp")
    pool_index = lax.axis_index("pool")
    requests = rows * pool
    score_scale = 1.0 / math.sqrt(HD)
    f32, bf16 = jnp.float32, jnp.bfloat16

    queries = rotate(query_new.astype(f32).reshape(rows, heads, HD), lengths).astype(bf16)
    new_keys = rotate(key_new.astype(f32).reshape(rows, heads, HD), lengths).astype(bf16)

    table_high, table_low = encode(block_table + 1)
    len_high, len_low = encode(lengths)
    packed = jnp.concatenate(
        [
            queries.reshape(rows, width),
            residual_in,
            table_high,
            table_low,
            len_high[:, None],
            len_low[:, None],
        ],
        1,
    )
    spare = -packed.shape[1] % 128
    packed = jnp.pad(packed, ((0, 0), (0, spare)))
    got = gather(packed, "pool").reshape(requests, packed.shape[1])
    all_queries = got[:, :width]
    all_input = got[:, width : 2 * width]
    tail = got[:, 2 * width :]
    tables = decode(tail[:, :most], tail[:, most : 2 * most]) - 1
    all_lengths = decode(tail[:, 2 * most], tail[:, 2 * most + 1])

    held_ids = pool_index * blocks + jnp.arange(blocks, dtype=jnp.int32)
    matches = tables[None, :, :] == held_ids[:, None, None]
    holder = jnp.any(matches, 2)
    block_index = jnp.sum(
        jnp.where(matches, jnp.arange(most, dtype=jnp.int32)[None, None, :], 0), (1, 2)
    )
    valid_len = jnp.sum(jnp.where(holder, all_lengths[None, :], 0), 1)
    block_query = jnp.dot(holder.astype(bf16), all_queries, preferred_element_type=f32)
    block_query = block_query.astype(bf16).reshape(blocks, heads, HD)
    key_rows = key_cache.reshape(blocks, block_len, heads, HD)
    value_rows = value_cache.reshape(blocks, block_len, heads, HD)
    scores = (
        jnp.einsum("bhd,bthd->bht", block_query, key_rows, preferred_element_type=f32)
        * score_scale
    )
    token_pos = block_index[:, None] * block_len + jnp.arange(block_len, dtype=jnp.int32)[None, :]
    valid = (token_pos < valid_len[:, None])[:, None, :]
    scores = jnp.where(valid, scores, LOW)
    shift = low(jnp.max(scores, 2))
    weights = jnp.where(valid, jnp.exp(scores - shift[:, :, None]), 0.0)
    totals = jnp.sum(weights, 2)
    numerator = jnp.einsum(
        "bht,bthd->bhd", weights.astype(bf16), value_rows, preferred_element_type=f32
    )
    self_score = jnp.sum(queries.astype(f32) * new_keys.astype(f32), -1) * score_scale
    self_shift = low(self_score)
    self_weight = jnp.exp(self_score - self_shift)
    self_numer = self_weight[:, :, None] * value_new.astype(f32).reshape(rows, heads, HD)

    own_total = jnp.concatenate([totals, self_weight], 0)
    total_high, total_low = split(own_total)
    part = jnp.concatenate(
        [
            jnp.concatenate([numerator, self_numer], 0)
            .astype(bf16)
            .reshape(blocks + rows, width),
            jnp.concatenate([shift, self_shift], 0).astype(bf16),
            total_high,
            total_low,
        ],
        1,
    )
    part = jnp.pad(part, ((0, 0), (0, -part.shape[1] % 128)))
    count = blocks + rows
    parts = gather(part, "pool").reshape(pool * count, part.shape[1])
    all_shift = parts[:, width : width + heads].astype(f32)
    all_total = parts[:, width + heads : width + 2 * heads].astype(f32) + parts[
        :, width + 2 * heads : width + 3 * heads
    ].astype(f32)
    place = jnp.arange(pool * count, dtype=jnp.int32)
    owner, slot = place // count, place % count
    is_block = slot < blocks
    block_id = jnp.where(is_block, owner * blocks + slot, -2)
    self_id = jnp.where(is_block, -2, owner * rows + slot - blocks)
    request_ids = jnp.arange(requests, dtype=jnp.int32)
    belongs = jnp.any(tables[:, None, :] == block_id[None, :, None], 2) | (
        request_ids[:, None] == self_id[None, :]
    )
    top = jnp.max(jnp.where(belongs[:, :, None], all_shift[None], LOW), 1)
    part_top = jnp.sum(jnp.where(belongs[:, :, None], top[:, None, :], 0.0), 0)
    scale = jnp.exp(all_shift - part_top)
    scaled = parts[:, :width].astype(f32).reshape(-1, heads, HD) * scale[:, :, None]
    mix = belongs.astype(f32)
    numer = jnp.dot(mix, scaled.reshape(-1, width), precision=lax.Precision.HIGHEST)
    denom = jnp.dot(mix, all_total * scale, precision=lax.Precision.HIGHEST)
    attended = (numer.reshape(requests, heads, HD) / denom[:, :, None]).astype(bf16)
    attended = attended.reshape(requests, width)

    head_part = jnp.dot(attended, out_weight, preferred_element_type=f32).astype(bf16)
    share = pool // mlp
    route = []
    for p in range(pool):
        for m in range(mlp):
            route.append((p * mlp + m, ((p % share) * mlp + m) * mlp + p // share))
    moved = lax.ppermute(head_part, ("pool", "mlp"), route)
    head_all = gather(moved, "pool").reshape(share, mlp, requests, -1)
    head_out = low(jnp.sum(head_all.astype(f32), 1))
    head_out = jnp.swapaxes(head_out, 0, 1).reshape(requests, width)
    residual = all_input.astype(f32) + head_out
    squares = jnp.sum(residual * residual, -1, keepdims=True)
    portion = (residual * norm_gain.astype(f32)).astype(bf16)

    ff = gate_weight.shape[1]
    square_high, square_low = split(squares)
    sums = jnp.concatenate(
        [
            jnp.dot(portion, gate_weight, preferred_element_type=f32).astype(bf16),
            jnp.dot(portion, up_weight, preferred_element_type=f32).astype(bf16),
            jnp.broadcast_to(square_high, (requests, 64)),
            jnp.broadcast_to(square_low, (requests, 64)),
        ],
        1,
    )
    summed = jnp.sum(gather(sums, "mlp").astype(f32), 0)
    mean_square = (summed[:, 2 * ff : 2 * ff + 1] + summed[:, 2 * ff + 64 : 2 * ff + 65]) / (
        width * mlp
    )
    factor = lax.rsqrt(mean_square + 1e-05)
    gate = summed[:, :ff] * factor
    up = summed[:, ff : 2 * ff] * factor
    hidden = (jax.nn.silu(gate) * up).astype(bf16)

    down = jnp.dot(hidden, down_weight, preferred_element_type=f32)
    down = lax.all_to_all(down.reshape(pool, rows, width), "pool", 0, 0)
    own = lax.dynamic_slice_in_dim(residual, pool_index * rows, rows, 0)
    return (own + jnp.sum(down, 0)).astype(bf16)


F32, BF16 = jnp.float32, jnp.bfloat16
VMEM = pl.BlockSpec(memory_space=pltpu.VMEM)
HBM = pl.BlockSpec(memory_space=pl.ANY)


def call(kernel, name, outs, args, scratch=(), hbm=(), limit=16 * 2**20):
    size = sum(math.prod(a.shape) * a.dtype.itemsize for a in args)
    return pl.pallas_call(
        kernel,
        out_shape=[jax.ShapeDtypeStruct(shape, dtype) for shape, dtype in outs],
        in_specs=[HBM if i in hbm else VMEM for i in range(len(args))],
        out_specs=[VMEM] * len(outs),
        scratch_shapes=list(scratch),
        compiler_params=pltpu.CompilerParams(vmem_limit_bytes=limit),
        cost_estimate=pl.CostEstimate(flops=0, bytes_accessed=size, transcendentals=0),
        name=name,
    )(*args)


def lanes(shape):
    return lax.broadcasted_iota(jnp.int32, shape, len(shape) - 1)


def in_order(pieces, index):
    for bit in (1, 2):
        odd = (index & bit) != 0
        pieces = [jnp.where(odd, pieces[s ^ bit], pieces[s]) for s in range(4)]
    return pieces


def rows_of(shape):
    return lax.broadcasted_iota(jnp.int32, shape, len(shape) - 2)


def round_low(values):
    return values.astype(BF16).astype(F32)


def head_start(shape):
    return rows_of(shape) * HD % 128


def flatten(tail, width):
    heads = tail.shape[0]
    spread = jnp.zeros((heads, width), F32)
    start = head_start((heads, width))
    for k in (0, 32, 64, 96):
        moved = pltpu.roll(tail, k, 1) if k else tail
        spread = jnp.where(start == k, jnp.concatenate([moved] * (width // 128), 1), spread)
    lane = lanes((heads, width))
    used = (lane // HD == rows_of((heads, width))) & (lane % HD < 24)
    return jnp.sum(jnp.where(used, spread, 0.0), 0, keepdims=True)


def unflatten(row, heads):
    width = row.shape[1]
    lane = lanes((heads, width))
    used = (lane // HD == rows_of((heads, width))) & (lane % HD < 24)
    spread = jnp.where(used, jnp.broadcast_to(row, (heads, width)), 0.0)
    folded = spread[:, :128]
    for at in range(128, width, 128):
        folded = folded + spread[:, at : at + 128]
    start = head_start((heads, 128))
    tail = jnp.where(start == 0, folded, 0.0)
    for k in (32, 64, 96):
        tail = jnp.where(start == k, pltpu.roll(folded, 128 - k, 1), tail)
    return tail


def prepare_kernel(*refs):
    sources, (packed, new), held = refs[:6], refs[8:10], refs[10:16]
    scr, sems = refs[16:]
    copies = [
        pltpu.make_async_copy(source, target, sems.at[i])
        for i, (source, target) in enumerate(zip(sources, held))
    ]
    for copy in copies:
        copy.start()
    table, length, query, key, value, residual = held
    rows, width = query.shape
    most = table.shape[1]
    period = 384
    turn = lanes((8, period)) % (HD // 2)
    freq = jnp.zeros((8, period), F32)
    for i in range(HD // 2):
        freq = jnp.where(turn == i, float(np.float32(10000.0 ** (-2.0 * i / HD))), freq)
    for copy in copies:
        copy.wait()
    scr[...] = jnp.zeros_like(scr)
    scr[0:rows, :] = query[...].astype(F32)
    scr[rows : 2 * rows, :] = key[...].astype(F32)
    values = scr[...]
    line = rows_of((8, period))
    where_at = jnp.zeros((8, period), F32)
    for r in range(rows):
        here = (line == r) | (line == rows + r)
        where_at = jnp.where(here, length[r].astype(F32), where_at)
    angles = where_at * freq
    cosine = jnp.concatenate([jnp.cos(angles)] * (width // period), 1)
    sine = jnp.concatenate([jnp.sin(angles)] * (width // period), 1)
    first = lanes((8, width)) % HD < HD // 2
    ahead = pltpu.roll(values, width - HD // 2, 1)
    behind = pltpu.roll(values, HD // 2, 1)
    scr[...] = values * cosine + jnp.where(first, -ahead, behind) * sine
    packed[:, :width] = scr[0:rows, :].astype(BF16)
    packed[:, width : 2 * width] = residual[...]
    tail = jnp.zeros((rows, 128), F32)
    at, row = lanes((rows, 128)), rows_of((rows, 128))
    for r in range(rows):
        codes = [table[r, k] + 1 for k in range(most)] + [length[r]]
        spots = [(k, most + k) for k in range(most)] + [(2 * most, 2 * most + 1)]
        for code, (high, rest) in zip(codes, spots):
            tail = jnp.where((row == r) & (at == high), (code >> 7).astype(F32), tail)
            tail = jnp.where((row == r) & (at == rest), (code & 127).astype(F32), tail)
    packed[:, 2 * width :] = tail.astype(BF16)
    new[:, :width] = scr[rows : 2 * rows, :].astype(BF16)
    new[:, width:] = value[...]


def carry_kernel(packed, new, packed_near, own):
    packed_near[...] = packed[...]
    rows, width = new.shape[0], new.shape[1] // 2
    blocks = own.shape[0] - rows - 1
    heads = width // HD
    head_mask = lanes((heads, width)) // HD == rows_of((heads, width))
    product = packed[:, :width].astype(F32) * new[:, :width].astype(F32)
    own[...] = jnp.zeros_like(own)
    spot = lanes((heads, 128))
    tail = jnp.zeros((heads, 128), F32)
    for r in range(rows):
        score = jnp.sum(
            jnp.where(head_mask, jnp.broadcast_to(product[r : r + 1], (heads, width)), 0.0),
            1,
            keepdims=True,
        ) * (1.0 / math.sqrt(HD))
        shift = round_low(score)
        weight = jnp.exp(score - shift)
        spread = jnp.sum(jnp.where(head_mask, round_low(weight), 0.0), 0, keepdims=True)
        own[blocks + r : blocks + r + 1, :width] = spread * new[r : r + 1, width:].astype(F32)
        high = round_low(weight)
        tail = jnp.where(spot == blocks + r, shift, tail)
        tail = jnp.where(spot == 8 + blocks + r, high, tail)
        tail = jnp.where(spot == 16 + blocks + r, weight - high, tail)
    own[:, width:] = tail


def merge_kernel(mine, theirs, both):
    y = lax.axis_index("pool") % 2
    both[y] = mine[...]
    both[1 - y] = theirs[...]


def attend_kernel(a0, a1, a2, a3, own, keys, values, part, residual, tables, scr):
    blocks, block_len, width = keys.shape
    rows = a0.shape[1]
    heads = width // HD
    most = 8
    me = lax.axis_index("pool")
    for y in range(2):
        pieces = [piece[y].astype(F32) for piece in (a0, a1, a2, a3)]
        for z, piece in enumerate(in_order(pieces, me // 2)):
            scr[(z * 2 + y) * rows : (z * 2 + y + 1) * rows, :] = piece
    queries = scr[:, :width]
    residual[...] = scr[:, width : 2 * width]
    tail = scr[:, 2 * width :]
    requests = tail.shape[0]
    table = tail * CODE + pltpu.roll(tail, 128 - most, 1) - 1.0
    length = tail[:, 2 * most : 2 * most + 1] * CODE + tail[:, 2 * most + 1 : 2 * most + 2]
    lane = lanes((requests, 128))
    table = jnp.where(lane < most, table, -2.0)
    tables[...] = table
    head_mask = lanes((heads, width)) // HD == rows_of((heads, width))
    spot = lanes((heads, 128))
    tail = own[:, width:]
    scores, limits = [], []
    for b in range(blocks):
        match = jnp.where(table == (me * blocks + b).astype(F32), 1.0, 0.0)
        holder = jnp.sum(match, 1, keepdims=True)
        place = jnp.sum(jnp.sum(match * lane.astype(F32), 1, keepdims=True), 0, keepdims=True)
        limit = jnp.sum(holder * length, 0, keepdims=True) - place * block_len
        limits.append(jnp.broadcast_to(limit, (heads, block_len)))
        query = jnp.sum(holder * queries, 0, keepdims=True)
        spread = jnp.where(head_mask, query, 0.0).astype(BF16)
        scores.append(
            lax.dot_general(
                spread, keys[b], (((1,), (1,)), ((), ())), preferred_element_type=F32
            )
        )
    scores = jnp.concatenate(scores, 0) * (1.0 / math.sqrt(HD))
    token = lanes((blocks * heads, block_len)).astype(F32)
    valid = token < jnp.concatenate(limits, 0)
    scores = jnp.where(valid, scores, LOW)
    shift = round_low(jnp.max(scores, 1, keepdims=True))
    weights = jnp.where(valid, jnp.exp(scores - shift), 0.0)
    total = jnp.sum(weights, 1, keepdims=True)
    high = round_low(total)
    rest = total - high
    numerators = []
    for b in range(blocks):
        mine = slice(b * heads, (b + 1) * heads)
        full = jnp.dot(weights[mine].astype(BF16), values[b], preferred_element_type=F32)
        numerators.append(jnp.sum(jnp.where(head_mask, full, 0.0), 0, keepdims=True))
        tail = jnp.where(spot == b, shift[mine], tail)
        tail = jnp.where(spot == 8 + b, high[mine], tail)
        tail = jnp.where(spot == 16 + b, rest[mine], tail)
    line = rows_of((8, width))
    numer = own[:, :width]
    for b in range(blocks):
        numer = jnp.where(line == b, numerators[b], numer)
    numer = jnp.where(line == 7, flatten(tail, width), numer)
    part[...] = numer.astype(BF16)


def combine_kernel(b0, b1, b2, b3, tables, weight, head_part, numer, tails, mix):
    requests = tables.shape[0]
    slots = b0.shape[1]
    width = weight.shape[0]
    heads = width // HD
    rows, blocks = 2, slots - 3
    me = lax.axis_index("pool")
    for step, piece in enumerate((b0, b1, b2, b3)):
        z = (me // 2) ^ step
        for y in range(2):
            owner = z * 2 + y
            values = piece[y].astype(F32)
            numer[pl.ds(pl.multiple_of(owner * slots, 8), slots), :] = values
            tails[owner] = unflatten(values[slots - 1 : slots], heads)
    lane8 = lanes((heads, 128))
    shifts = jnp.zeros((heads, 128), F32)
    totals = jnp.zeros((heads, 128), F32)
    for owner in range(8):
        tail = tails[owner]
        total = pltpu.roll(tail, 120, 1) + pltpu.roll(tail, 112, 1)
        tail, total = jnp.where(lane8 < 8, tail, 0.0), jnp.where(lane8 < 8, total, 0.0)
        if owner:
            tail, total = pltpu.roll(tail, 8 * owner, 1), pltpu.roll(total, 8 * owner, 1)
        shifts, totals = shifts + tail, totals + total
    lane = lanes((requests, 128))
    owner, slot = lane // slots, lane % slots
    block_id = jnp.where((slot < blocks) & (lane < 64), owner * blocks + slot, -5).astype(F32)
    self_id = jnp.where((slot >= blocks) & (slot < blocks + rows), owner * rows + slot - blocks, -5)
    table = tables[...]
    belongs = (self_id == rows_of((requests, 128))) & (lane < 64)
    for k in range(8):
        belongs = belongs | (table[:, k : k + 1] == block_id)
    for h in range(heads):
        shift = jnp.broadcast_to(shifts[h : h + 1], (requests, 128))
        top = jnp.max(jnp.where(belongs, shift, LOW), 1, keepdims=True)
        scale = jnp.where(belongs, jnp.exp(shift - top), 0.0)
        total = jnp.sum(scale * totals[h : h + 1], 1, keepdims=True)
        mix[h * requests : (h + 1) * requests, :] = scale / total
    full = jnp.dot(
        mix[:, : 8 * slots].astype(BF16), numer[...].astype(BF16), preferred_element_type=F32
    )
    head = lanes((requests, width)) // HD
    attended = jnp.zeros((requests, width), F32)
    for h in range(heads):
        attended = jnp.where(head == h, full[h * requests : (h + 1) * requests], attended)
    head_part[...] = jnp.dot(
        attended.astype(BF16), weight[...], preferred_element_type=F32
    ).astype(BF16)


def sum_kernel(p0, p1, p2, p3, total):
    total[...] = (
        (p0[...].astype(F32) + p1[...].astype(F32)) + (p2[...].astype(F32) + p3[...].astype(F32))
    ).astype(BF16)


def gate_up_kernel(same, flip, all_input, gain, gate, up, sums, own, scr):
    me = lax.axis_index("pool")
    odd = me % 2 == 1
    part = same.shape[1]
    ff = gate.shape[1]
    rows = own.shape[0]
    near, far = same[...].astype(F32), flip[...].astype(F32)
    scr[:, :part] = all_input[:, :part] + jnp.where(odd, far, near)
    scr[:, part:] = all_input[:, part:] + jnp.where(odd, near, far)
    residual = scr[...]
    mine = scr[0:rows, :]
    for p in range(1, residual.shape[0] // rows):
        mine = jnp.where(me == p, scr[p * rows : (p + 1) * rows, :], mine)
    own[...] = mine
    square = jnp.sum(residual * residual, 1, keepdims=True)
    portion = (residual * gain[...].astype(F32)).astype(BF16)
    sums[:, :ff] = jnp.dot(portion, gate[...], preferred_element_type=F32).astype(BF16)
    sums[:, ff : 2 * ff] = jnp.dot(portion, up[...], preferred_element_type=F32).astype(BF16)
    lane = lanes((residual.shape[0], 128))
    high = round_low(square)
    tail = jnp.where(lane == 0, high, jnp.where(lane == 1, square - high, 0.0))
    sums[:, 2 * ff :] = tail.astype(BF16)


def down_kernel(features, p0, p1, p2, p3, weight, parts, scr):
    ff = weight.shape[0]

    def total(columns):
        a, b, c, d = (p[:, columns].astype(F32) for p in (p0, p1, p2, p3))
        return (a + b) + (c + d)

    square = jnp.sum(total(slice(2 * ff, None)), 1, keepdims=True)
    factor = lax.rsqrt(square * (1.0 / features) + 1e-05)
    gate = total(slice(0, ff)) * factor
    up = total(slice(ff, 2 * ff)) * factor
    hidden = (gate / (1.0 + jnp.exp(-gate)) * up).astype(BF16)
    scr[...] = jnp.dot(hidden, weight[...], preferred_element_type=F32)
    rows = parts.shape[1]
    pool = parts.shape[0]
    for p in range(pool):
        parts[pool - 1 - p] = scr[p * rows : (p + 1) * rows, :].astype(BF16)


def final_kernel(own, parts, out):
    total = own[...]
    for p in range(parts.shape[0]):
        total = total + parts[p].astype(F32)
    out[...] = total.astype(BF16)


def flip(values, axis, step):
    size = lax.axis_size(axis)
    return lax.ppermute(values, axis, [(index, index ^ step) for index in range(size)])


def per_device_small(
    residual_in,
    query_new,
    key_new,
    value_new,
    key_cache,
    value_cache,
    block_table,
    lengths,
    out_weight,
    norm_gain,
    gate_weight,
    up_weight,
    down_weight,
):
    rows, width = residual_in.shape
    blocks = key_cache.shape[0]
    pool, mlp = 8, 4
    requests = rows * pool
    ff = gate_weight.shape[1]
    part_cols = out_weight.shape[1]
    packed_width = 2 * width + 128
    slots = blocks + rows + 1
    part_width = width + 128

    packed, new = call(
        prepare_kernel,
        "rotary",
        [((rows, packed_width), BF16), ((rows, 2 * width), BF16)],
        [block_table, lengths, query_new, key_new, value_new, residual_in, key_cache, value_cache],
        [pltpu.SMEM(block_table.shape, jnp.int32), pltpu.SMEM(lengths.shape, jnp.int32)]
        + [pltpu.VMEM((rows, width), BF16)] * 4
        + [pltpu.VMEM((8, width), F32), pltpu.SemaphoreType.DMA((6,))],
        hbm=range(8),
        limit=54 * 2**20,
    )

    packed_near, own = call(
        carry_kernel,
        "carry",
        [(packed.shape, BF16), ((slots, part_width), F32)],
        [packed, new],
    )

    def pool_gather(values, near):
        (both,) = call(
            merge_kernel,
            "merge",
            [((2,) + values.shape, values.dtype)],
            [near, flip(values, "pool", 1)],
        )
        return [both] + [flip(both, "pool", step) for step in (2, 4, 6)]

    part, all_input, tables = call(
        attend_kernel,
        "attend",
        [((slots, width), BF16), ((requests, width), F32), ((requests, 128), F32)],
        pool_gather(packed, packed_near) + [own, key_cache, value_cache],
        [pltpu.VMEM((requests, packed_width), F32)],
    )
    (head_part,) = call(
        combine_kernel,
        "combine",
        [((requests, part_cols), BF16)],
        pool_gather(part, part) + [tables, out_weight],
        [
            pltpu.VMEM((pool * slots, width), F32),
            pltpu.VMEM((pool, slots, 128), F32),
            pltpu.VMEM((requests * width // HD, 128), F32),
        ],
    )
    (head_sum,) = call(
        sum_kernel,
        "head_sum",
        [((requests, part_cols), BF16)],
        [head_part] + [flip(head_part, "mlp", step) for step in (1, 2, 3)],
    )
    pieces = []
    for turn in range(2):
        route = []
        for m in range(mlp):
            by_distance = sorted(range(4), key=lambda z: (-abs(z - m), z))
            for z, step in zip(by_distance, (1, 0, 3, 2) if m % 2 == 0 else (0, 1, 2, 3)):
                for y in range(2):
                    source = (m * 2 + y) * mlp + (m ^ step)
                    route.append((source, (z * 2 + (y ^ turn)) * mlp + m))
        pieces.append(lax.ppermute(head_sum, ("pool", "mlp"), route))
    sums, own_residual = call(
        gate_up_kernel,
        "gate_up",
        [((requests, 2 * ff + 128), BF16), ((rows, width), F32)],
        pieces + [all_input, norm_gain.reshape(1, width), gate_weight, up_weight],
        [pltpu.VMEM((requests, width), F32)],
    )
    (down,) = call(
        functools.partial(down_kernel, width * mlp),
        "down",
        [((pool, rows, width), BF16)],
        [sums] + [flip(sums, "mlp", step) for step in (1, 2, 3)] + [down_weight],
        [pltpu.VMEM((requests, width), F32)],
    )
    backwards = list(range(pool))[::-1]
    (out,) = call(
        final_kernel,
        "final",
        [((rows, width), BF16)],
        [own_residual, lax.all_to_all(down, "pool", 0, 0, axis_index_groups=[backwards])],
    )
    return out


def solution(mesh):
    in_specs = (
        P("pool", "mlp"),
        P("pool", "mlp"),
        P("pool", "mlp"),
        P("pool", "mlp"),
        P("pool", None, "mlp"),
        P("pool", None, "mlp"),
        P("pool", None),
        P("pool"),
        P("mlp", "pool"),
        P("mlp"),
        P("mlp", "pool"),
        P("mlp", "pool"),
        P("pool", "mlp"),
    )
    small = mesh.shape["pool"] == 8 and mesh.shape["mlp"] == 4
    per_device = per_device_small if small else per_device_wide
    return jax.shard_map(
        per_device, mesh=mesh, in_specs=in_specs, out_specs=P("pool", "mlp"), check_vma=False
    )
```

```python
import functools
import math

import jax
import jax.numpy as jnp
import numpy as np
from jax import lax
from jax.experimental import pallas as pl
from jax.experimental.pallas import tpu as pltpu
from jax.sharding import PartitionSpec as P

HD = 96
LOW = -1e30
CODE = 128


def rotate(values, positions):
    half_size = values.shape[-1] // 2
    inverse_freq = 10000.0 ** (-(2.0 * jnp.arange(half_size, dtype=jnp.float32)) / values.shape[-1])
    angles = positions.astype(jnp.float32)[:, None, None] * inverse_freq[None, None, :]
    cosine = jnp.cos(angles)
    sine_part = jnp.sin(angles)
    first = values[..., :half_size]
    second = values[..., half_size:]
    return jnp.concatenate(
        [first * cosine - second * sine_part, second * cosine + first * sine_part], -1
    )


def low(values):
    return lax.reduce_precision(values, 8, 7)


def split(values):
    high = low(values)
    return high.astype(jnp.bfloat16), (values - high).astype(jnp.bfloat16)


def encode(ints):
    return (ints // CODE).astype(jnp.bfloat16), (ints % CODE).astype(jnp.bfloat16)


def decode(high, rest):
    return high.astype(jnp.int32) * CODE + rest.astype(jnp.int32)


def gather(values, axis):
    copies = jnp.broadcast_to(values[None], (lax.axis_size(axis),) + values.shape)
    return lax.all_to_all(copies, axis, 0, 0)


def per_device_wide(
    residual_in,
    query_new,
    key_new,
    value_new,
    key_cache,
    value_cache,
    block_table,
    lengths,
    out_weight,
    norm_gain,
    gate_weight,
    up_weight,
    down_weight,
):
    rows, width = residual_in.shape
    heads = width // HD
    blocks, block_len = key_cache.shape[:2]
    most = block_table.shape[1]
    pool, mlp = lax.axis_size("pool"), lax.axis_size("mlp")
    pool_index = lax.axis_index("pool")
    requests = rows * pool
    score_scale = 1.0 / math.sqrt(HD)
    f32, bf16 = jnp.float32, jnp.bfloat16

    queries = rotate(query_new.astype(f32).reshape(rows, heads, HD), lengths).astype(bf16)
    new_keys = rotate(key_new.astype(f32).reshape(rows, heads, HD), lengths).astype(bf16)

    table_high, table_low = encode(block_table + 1)
    len_high, len_low = encode(lengths)
    packed = jnp.concatenate(
        [
            queries.reshape(rows, width),
            residual_in,
            table_high,
            table_low,
            len_high[:, None],
            len_low[:, None],
        ],
        1,
    )
    spare = -packed.shape[1] % 128
    packed = jnp.pad(packed, ((0, 0), (0, spare)))
    got = gather(packed, "pool").reshape(requests, packed.shape[1])
    all_queries = got[:, :width]
    all_input = got[:, width : 2 * width]
    tail = got[:, 2 * width :]
    tables = decode(tail[:, :most], tail[:, most : 2 * most]) - 1
    all_lengths = decode(tail[:, 2 * most], tail[:, 2 * most + 1])

    held_ids = pool_index * blocks + jnp.arange(blocks, dtype=jnp.int32)
    matches = tables[None, :, :] == held_ids[:, None, None]
    holder = jnp.any(matches, 2)
    block_index = jnp.sum(
        jnp.where(matches, jnp.arange(most, dtype=jnp.int32)[None, None, :], 0), (1, 2)
    )
    valid_len = jnp.sum(jnp.where(holder, all_lengths[None, :], 0), 1)
    block_query = jnp.dot(holder.astype(bf16), all_queries, preferred_element_type=f32)
    block_query = block_query.astype(bf16).reshape(blocks, heads, HD)
    key_rows = key_cache.reshape(blocks, block_len, heads, HD)
    value_rows = value_cache.reshape(blocks, block_len, heads, HD)
    scores = (
        jnp.einsum("bhd,bthd->bht", block_query, key_rows, preferred_element_type=f32)
        * score_scale
    )
    token_pos = block_index[:, None] * block_len + jnp.arange(block_len, dtype=jnp.int32)[None, :]
    valid = (token_pos < valid_len[:, None])[:, None, :]
    scores = jnp.where(valid, scores, LOW)
    shift = low(jnp.max(scores, 2))
    weights = jnp.where(valid, jnp.exp(scores - shift[:, :, None]), 0.0)
    totals = jnp.sum(weights, 2)
    numerator = jnp.einsum(
        "bht,bthd->bhd", weights.astype(bf16), value_rows, preferred_element_type=f32
    )
    self_score = jnp.sum(queries.astype(f32) * new_keys.astype(f32), -1) * score_scale
    self_shift = low(self_score)
    self_weight = jnp.exp(self_score - self_shift)
    self_numer = self_weight[:, :, None] * value_new.astype(f32).reshape(rows, heads, HD)

    own_total = jnp.concatenate([totals, self_weight], 0)
    total_high, total_low = split(own_total)
    part = jnp.concatenate(
        [
            jnp.concatenate([numerator, self_numer], 0)
            .astype(bf16)
            .reshape(blocks + rows, width),
            jnp.concatenate([shift, self_shift], 0).astype(bf16),
            total_high,
            total_low,
        ],
        1,
    )
    part = jnp.pad(part, ((0, 0), (0, -part.shape[1] % 128)))
    count = blocks + rows
    parts = gather(part, "pool").reshape(pool * count, part.shape[1])
    all_shift = parts[:, width : width + heads].astype(f32)
    all_total = parts[:, width + heads : width + 2 * heads].astype(f32) + parts[
        :, width + 2 * heads : width + 3 * heads
    ].astype(f32)
    place = jnp.arange(pool * count, dtype=jnp.int32)
    owner, slot = place // count, place % count
    is_block = slot < blocks
    block_id = jnp.where(is_block, owner * blocks + slot, -2)
    self_id = jnp.where(is_block, -2, owner * rows + slot - blocks)
    request_ids = jnp.arange(requests, dtype=jnp.int32)
    belongs = jnp.any(tables[:, None, :] == block_id[None, :, None], 2) | (
        request_ids[:, None] == self_id[None, :]
    )
    top = jnp.max(jnp.where(belongs[:, :, None], all_shift[None], LOW), 1)
    part_top = jnp.sum(jnp.where(belongs[:, :, None], top[:, None, :], 0.0), 0)
    scale = jnp.exp(all_shift - part_top)
    scaled = parts[:, :width].astype(f32).reshape(-1, heads, HD) * scale[:, :, None]
    mix = belongs.astype(f32)
    numer = jnp.dot(mix, scaled.reshape(-1, width), precision=lax.Precision.HIGHEST)
    denom = jnp.dot(mix, all_total * scale, precision=lax.Precision.HIGHEST)
    attended = (numer.reshape(requests, heads, HD) / denom[:, :, None]).astype(bf16)
    attended = attended.reshape(requests, width)

    head_part = jnp.dot(attended, out_weight, preferred_element_type=f32).astype(bf16)
    share = pool // mlp
    route = []
    for p in range(pool):
        for m in range(mlp):
            route.append((p * mlp + m, ((p % share) * mlp + m) * mlp + p // share))
    moved = lax.ppermute(head_part, ("pool", "mlp"), route)
    head_all = gather(moved, "pool").reshape(share, mlp, requests, -1)
    head_out = low(jnp.sum(head_all.astype(f32), 1))
    head_out = jnp.swapaxes(head_out, 0, 1).reshape(requests, width)
    residual = all_input.astype(f32) + head_out
    squares = jnp.sum(residual * residual, -1, keepdims=True)
    portion = (residual * norm_gain.astype(f32)).astype(bf16)

    ff = gate_weight.shape[1]
    square_high, square_low = split(squares)
    sums = jnp.concatenate(
        [
            jnp.dot(portion, gate_weight, preferred_element_type=f32).astype(bf16),
            jnp.dot(portion, up_weight, preferred_element_type=f32).astype(bf16),
            jnp.broadcast_to(square_high, (requests, 64)),
            jnp.broadcast_to(square_low, (requests, 64)),
        ],
        1,
    )
    summed = jnp.sum(gather(sums, "mlp").astype(f32), 0)
    mean_square = (summed[:, 2 * ff : 2 * ff + 1] + summed[:, 2 * ff + 64 : 2 * ff + 65]) / (
        width * mlp
    )
    factor = lax.rsqrt(mean_square + 1e-05)
    gate = summed[:, :ff] * factor
    up = summed[:, ff : 2 * ff] * factor
    hidden = (jax.nn.silu(gate) * up).astype(bf16)

    down = jnp.dot(hidden, down_weight, preferred_element_type=f32)
    down = lax.all_to_all(down.reshape(pool, rows, width), "pool", 0, 0)
    own = lax.dynamic_slice_in_dim(residual, pool_index * rows, rows, 0)
    return (own + jnp.sum(down, 0)).astype(bf16)


F32, BF16 = jnp.float32, jnp.bfloat16
VMEM = pl.BlockSpec(memory_space=pltpu.VMEM)
HBM = pl.BlockSpec(memory_space=pl.ANY)


def call(kernel, name, outs, args, scratch=(), hbm=(), limit=16 * 2**20):
    size = sum(math.prod(a.shape) * a.dtype.itemsize for a in args)
    return pl.pallas_call(
        kernel,
        out_shape=[jax.ShapeDtypeStruct(shape, dtype) for shape, dtype in outs],
        in_specs=[HBM if i in hbm else VMEM for i in range(len(args))],
        out_specs=[VMEM] * len(outs),
        scratch_shapes=list(scratch),
        compiler_params=pltpu.CompilerParams(vmem_limit_bytes=limit),
        cost_estimate=pl.CostEstimate(flops=0, bytes_accessed=size, transcendentals=0),
        name=name,
    )(*args)


def lanes(shape):
    return lax.broadcasted_iota(jnp.int32, shape, len(shape) - 1)


def in_order(pieces, index):
    for bit in (1, 2):
        odd = (index & bit) != 0
        pieces = [jnp.where(odd, pieces[s ^ bit], pieces[s]) for s in range(4)]
    return pieces


def rows_of(shape):
    return lax.broadcasted_iota(jnp.int32, shape, len(shape) - 2)


def round_low(values):
    return values.astype(BF16).astype(F32)


def head_start(shape):
    return rows_of(shape) * HD % 128


def flatten(tail, width):
    heads = tail.shape[0]
    spread = jnp.zeros((heads, width), F32)
    start = head_start((heads, width))
    for k in (0, 32, 64, 96):
        moved = pltpu.roll(tail, k, 1) if k else tail
        spread = jnp.where(start == k, jnp.concatenate([moved] * (width // 128), 1), spread)
    lane = lanes((heads, width))
    used = (lane // HD == rows_of((heads, width))) & (lane % HD < 24)
    return jnp.sum(jnp.where(used, spread, 0.0), 0, keepdims=True)


def unflatten(row, heads):
    width = row.shape[1]
    lane = lanes((heads, width))
    used = (lane // HD == rows_of((heads, width))) & (lane % HD < 24)
    spread = jnp.where(used, jnp.broadcast_to(row, (heads, width)), 0.0)
    folded = spread[:, :128]
    for at in range(128, width, 128):
        folded = folded + spread[:, at : at + 128]
    start = head_start((heads, 128))
    tail = jnp.where(start == 0, folded, 0.0)
    for k in (32, 64, 96):
        tail = jnp.where(start == k, pltpu.roll(folded, 128 - k, 1), tail)
    return tail


def prepare_kernel(*refs):
    sources, (packed, new), held = refs[:6], refs[8:10], refs[10:16]
    scr, sems = refs[16:]
    copies = [
        pltpu.make_async_copy(source, target, sems.at[i])
        for i, (source, target) in enumerate(zip(sources, held))
    ]
    for copy in copies:
        copy.start()
    table, length, query, key, value, residual = held
    rows, width = query.shape
    most = table.shape[1]
    period = 384
    turn = lanes((8, period)) % (HD // 2)
    freq = jnp.zeros((8, period), F32)
    for i in range(HD // 2):
        freq = jnp.where(turn == i, float(np.float32(10000.0 ** (-2.0 * i / HD))), freq)
    for copy in copies:
        copy.wait()
    scr[...] = jnp.zeros_like(scr)
    scr[0:rows, :] = query[...].astype(F32)
    scr[rows : 2 * rows, :] = key[...].astype(F32)
    values = scr[...]
    line = rows_of((8, period))
    where_at = jnp.zeros((8, period), F32)
    for r in range(rows):
        here = (line == r) | (line == rows + r)
        where_at = jnp.where(here, length[r].astype(F32), where_at)
    angles = where_at * freq
    cosine = jnp.concatenate([jnp.cos(angles)] * (width // period), 1)
    sine = jnp.concatenate([jnp.sin(angles)] * (width // period), 1)
    first = lanes((8, width)) % HD < HD // 2
    ahead = pltpu.roll(values, width - HD // 2, 1)
    behind = pltpu.roll(values, HD // 2, 1)
    scr[...] = values * cosine + jnp.where(first, -ahead, behind) * sine
    packed[:, :width] = scr[0:rows, :].astype(BF16)
    packed[:, width : 2 * width] = residual[...]
    tail = jnp.zeros((rows, 128), F32)
    at, row = lanes((rows, 128)), rows_of((rows, 128))
    for r in range(rows):
        codes = [table[r, k] + 1 for k in range(most)] + [length[r]]
        spots = [(k, most + k) for k in range(most)] + [(2 * most, 2 * most + 1)]
        for code, (high, rest) in zip(codes, spots):
            tail = jnp.where((row == r) & (at == high), (code >> 7).astype(F32), tail)
            tail = jnp.where((row == r) & (at == rest), (code & 127).astype(F32), tail)
    packed[:, 2 * width :] = tail.astype(BF16)
    new[:, :width] = scr[rows : 2 * rows, :].astype(BF16)
    new[:, width:] = value[...]


def carry_kernel(packed, new, packed_near, own):
    packed_near[...] = packed[...]
    rows, width = new.shape[0], new.shape[1] // 2
    blocks = own.shape[0] - rows - 1
    heads = width // HD
    head_mask = lanes((heads, width)) // HD == rows_of((heads, width))
    product = packed[:, :width].astype(F32) * new[:, :width].astype(F32)
    own[...] = jnp.zeros_like(own)
    spot = lanes((heads, 128))
    tail = jnp.zeros((heads, 128), F32)
    for r in range(rows):
        score = jnp.sum(
            jnp.where(head_mask, jnp.broadcast_to(product[r : r + 1], (heads, width)), 0.0),
            1,
            keepdims=True,
        ) * (1.0 / math.sqrt(HD))
        shift = round_low(score)
        weight = jnp.exp(score - shift)
        spread = jnp.sum(jnp.where(head_mask, round_low(weight), 0.0), 0, keepdims=True)
        own[blocks + r : blocks + r + 1, :width] = spread * new[r : r + 1, width:].astype(F32)
        high = round_low(weight)
        tail = jnp.where(spot == blocks + r, shift, tail)
        tail = jnp.where(spot == 8 + blocks + r, high, tail)
        tail = jnp.where(spot == 16 + blocks + r, weight - high, tail)
    own[:, width:] = tail


def merge_kernel(mine, theirs, both):
    y = lax.axis_index("pool") % 2
    both[y] = mine[...]
    both[1 - y] = theirs[...]


def attend_kernel(a0, a1, a2, a3, own, keys, values, part, residual, tables, scr):
    blocks, block_len, width = keys.shape
    rows = a0.shape[1]
    heads = width // HD
    most = 8
    me = lax.axis_index("pool")
    for y in range(2):
        pieces = [piece[y].astype(F32) for piece in (a0, a1, a2, a3)]
        for z, piece in enumerate(in_order(pieces, me // 2)):
            scr[(z * 2 + y) * rows : (z * 2 + y + 1) * rows, :] = piece
    queries = scr[:, :width]
    residual[...] = scr[:, width : 2 * width]
    tail = scr[:, 2 * width :]
    requests = tail.shape[0]
    table = tail * CODE + pltpu.roll(tail, 128 - most, 1) - 1.0
    length = tail[:, 2 * most : 2 * most + 1] * CODE + tail[:, 2 * most + 1 : 2 * most + 2]
    lane = lanes((requests, 128))
    table = jnp.where(lane < most, table, -2.0)
    tables[...] = table
    head_mask = lanes((heads, width)) // HD == rows_of((heads, width))
    spot = lanes((heads, 128))
    tail = own[:, width:]
    scores, limits = [], []
    for b in range(blocks):
        match = jnp.where(table == (me * blocks + b).astype(F32), 1.0, 0.0)
        holder = jnp.sum(match, 1, keepdims=True)
        place = jnp.sum(jnp.sum(match * lane.astype(F32), 1, keepdims=True), 0, keepdims=True)
        limit = jnp.sum(holder * length, 0, keepdims=True) - place * block_len
        limits.append(jnp.broadcast_to(limit, (heads, block_len)))
        query = jnp.sum(holder * queries, 0, keepdims=True)
        scores.append(jnp.where(head_mask, query, 0.0))
    filler = jnp.zeros((128 - blocks * heads, width), F32)
    stacked = jnp.concatenate(scores + [filler], 0).astype(BF16)
    every = lax.dot_general(
        keys[...].reshape(blocks * block_len, width),
        stacked,
        (((1,), (1,)), ((), ())),
        preferred_element_type=F32,
    )
    scores = []
    for b in range(blocks):
        turned = jnp.transpose(every[b * block_len : (b + 1) * block_len])
        scores.append(turned[b * heads : (b + 1) * heads])
    scores = jnp.concatenate(scores, 0) * (1.0 / math.sqrt(HD))
    token = lanes((blocks * heads, block_len)).astype(F32)
    valid = token < jnp.concatenate(limits, 0)
    scores = jnp.where(valid, scores, LOW)
    shift = round_low(jnp.max(scores, 1, keepdims=True))
    weights = jnp.where(valid, jnp.exp(scores - shift), 0.0)
    total = jnp.sum(weights, 1, keepdims=True)
    high = round_low(total)
    rest = total - high
    numerators = []
    for b in range(blocks):
        mine = slice(b * heads, (b + 1) * heads)
        full = jnp.dot(weights[mine].astype(BF16), values[b], preferred_element_type=F32)
        numerators.append(jnp.sum(jnp.where(head_mask, full, 0.0), 0, keepdims=True))
        tail = jnp.where(spot == b, shift[mine], tail)
        tail = jnp.where(spot == 8 + b, high[mine], tail)
        tail = jnp.where(spot == 16 + b, rest[mine], tail)
    line = rows_of((8, width))
    numer = own[:, :width]
    for b in range(blocks):
        numer = jnp.where(line == b, numerators[b], numer)
    numer = jnp.where(line == 7, flatten(tail, width), numer)
    part[...] = numer.astype(BF16)


def combine_kernel(b0, b1, b2, b3, tables, weight, head_part, numer, tails, mix):
    requests = tables.shape[0]
    slots = b0.shape[1]
    width = weight.shape[0]
    heads = width // HD
    rows, blocks = 2, slots - 3
    me = lax.axis_index("pool")
    for step, piece in enumerate((b0, b1, b2, b3)):
        z = (me // 2) ^ step
        for y in range(2):
            owner = z * 2 + y
            values = piece[y].astype(F32)
            numer[pl.ds(pl.multiple_of(owner * slots, 8), slots), :] = values
            tails[owner] = unflatten(values[slots - 1 : slots], heads)
    lane8 = lanes((heads, 128))
    shifts = jnp.zeros((heads, 128), F32)
    totals = jnp.zeros((heads, 128), F32)
    for owner in range(8):
        tail = tails[owner]
        total = pltpu.roll(tail, 120, 1) + pltpu.roll(tail, 112, 1)
        tail, total = jnp.where(lane8 < 8, tail, 0.0), jnp.where(lane8 < 8, total, 0.0)
        if owner:
            tail, total = pltpu.roll(tail, 8 * owner, 1), pltpu.roll(total, 8 * owner, 1)
        shifts, totals = shifts + tail, totals + total
    lane = lanes((requests, 128))
    owner, slot = lane // slots, lane % slots
    block_id = jnp.where((slot < blocks) & (lane < 64), owner * blocks + slot, -5).astype(F32)
    self_id = jnp.where((slot >= blocks) & (slot < blocks + rows), owner * rows + slot - blocks, -5)
    table = tables[...]
    belongs = (self_id == rows_of((requests, 128))) & (lane < 64)
    for k in range(8):
        belongs = belongs | (table[:, k : k + 1] == block_id)
    for h in range(heads):
        shift = jnp.broadcast_to(shifts[h : h + 1], (requests, 128))
        top = jnp.max(jnp.where(belongs, shift, LOW), 1, keepdims=True)
        scale = jnp.where(belongs, jnp.exp(shift - top), 0.0)
        total = jnp.sum(scale * totals[h : h + 1], 1, keepdims=True)
        mix[h * requests : (h + 1) * requests, :] = scale / total
    full = jnp.dot(
        mix[:, : 8 * slots].astype(BF16), numer[...].astype(BF16), preferred_element_type=F32
    )
    head = lanes((requests, width)) // HD
    attended = jnp.zeros((requests, width), F32)
    for h in range(heads):
        attended = jnp.where(head == h, full[h * requests : (h + 1) * requests], attended)
    head_part[...] = jnp.dot(
        attended.astype(BF16), weight[...], preferred_element_type=F32
    ).astype(BF16)


def sum_kernel(p0, p1, p2, p3, total):
    total[...] = (
        (p0[...].astype(F32) + p1[...].astype(F32)) + (p2[...].astype(F32) + p3[...].astype(F32))
    ).astype(BF16)


def gate_up_kernel(same, flip, all_input, gain, gate, up, sums, own, scr):
    me = lax.axis_index("pool")
    odd = me % 2 == 1
    part = same.shape[1]
    ff = gate.shape[1]
    rows = own.shape[0]
    near, far = same[...].astype(F32), flip[...].astype(F32)
    scr[:, :part] = all_input[:, :part] + jnp.where(odd, far, near)
    scr[:, part:] = all_input[:, part:] + jnp.where(odd, near, far)
    residual = scr[...]
    mine = scr[0:rows, :]
    for p in range(1, residual.shape[0] // rows):
        mine = jnp.where(me == p, scr[p * rows : (p + 1) * rows, :], mine)
    own[...] = mine
    square = jnp.sum(residual * residual, 1, keepdims=True)
    portion = (residual * gain[...].astype(F32)).astype(BF16)
    sums[:, :ff] = jnp.dot(portion, gate[...], preferred_element_type=F32).astype(BF16)
    sums[:, ff : 2 * ff] = jnp.dot(portion, up[...], preferred_element_type=F32).astype(BF16)
    lane = lanes((residual.shape[0], 128))
    high = round_low(square)
    tail = jnp.where(lane == 0, high, jnp.where(lane == 1, square - high, 0.0))
    sums[:, 2 * ff :] = tail.astype(BF16)


def core_sum_kernel(mine, theirs, total):
    ff2 = mine.shape[1] - 128
    total[:, :ff2] = (mine[:, :ff2].astype(F32) + theirs[:, :ff2].astype(F32)).astype(BF16)
    tail = mine[:, ff2:].astype(F32) + theirs[:, ff2:].astype(F32)
    square = jnp.sum(tail, 1, keepdims=True)
    lane = lanes(tail.shape)
    high = round_low(square)
    tail = jnp.where(lane == 0, high, jnp.where(lane == 1, square - high, 0.0))
    total[:, ff2:] = tail.astype(BF16)


def down_kernel(features, mine, theirs, weight, parts, scr):
    ff = weight.shape[0]
    tail = mine[:, 2 * ff :].astype(F32) + theirs[:, 2 * ff :].astype(F32)
    square = jnp.sum(tail, 1, keepdims=True)
    factor = lax.rsqrt(square * (1.0 / features) + 1e-05)
    gate = (mine[:, :ff].astype(F32) + theirs[:, :ff].astype(F32)) * factor
    up = (mine[:, ff : 2 * ff].astype(F32) + theirs[:, ff : 2 * ff].astype(F32)) * factor
    hidden = (gate / (1.0 + jnp.exp(-gate)) * up).astype(BF16)
    scr[...] = jnp.dot(hidden, weight[...], preferred_element_type=F32)
    rows = parts.shape[1]
    pool = parts.shape[0]
    for p in range(pool):
        parts[pool - 1 - p] = scr[p * rows : (p + 1) * rows, :].astype(BF16)


def final_kernel(own, parts, out):
    total = own[...]
    for p in range(parts.shape[0]):
        total = total + parts[p].astype(F32)
    out[...] = total.astype(BF16)


def flip(values, axis, step):
    size = lax.axis_size(axis)
    return lax.ppermute(values, axis, [(index, index ^ step) for index in range(size)])


def per_device_small(
    residual_in,
    query_new,
    key_new,
    value_new,
    key_cache,
    value_cache,
    block_table,
    lengths,
    out_weight,
    norm_gain,
    gate_weight,
    up_weight,
    down_weight,
):
    rows, width = residual_in.shape
    blocks = key_cache.shape[0]
    pool, mlp = 8, 4
    requests = rows * pool
    ff = gate_weight.shape[1]
    part_cols = out_weight.shape[1]
    packed_width = 2 * width + 128
    slots = blocks + rows + 1
    part_width = width + 128

    packed, new = call(
        prepare_kernel,
        "rotary",
        [((rows, packed_width), BF16), ((rows, 2 * width), BF16)],
        [block_table, lengths, query_new, key_new, value_new, residual_in, key_cache, value_cache],
        [pltpu.SMEM(block_table.shape, jnp.int32), pltpu.SMEM(lengths.shape, jnp.int32)]
        + [pltpu.VMEM((rows, width), BF16)] * 4
        + [pltpu.VMEM((8, width), F32), pltpu.SemaphoreType.DMA((6,))],
        hbm=range(8),
        limit=54 * 2**20,
    )

    packed_near, own = call(
        carry_kernel,
        "carry",
        [(packed.shape, BF16), ((slots, part_width), F32)],
        [packed, new],
    )

    def pool_gather(values, near):
        (both,) = call(
            merge_kernel,
            "merge",
            [((2,) + values.shape, values.dtype)],
            [near, flip(values, "pool", 1)],
        )
        return [both] + [flip(both, "pool", step) for step in (2, 4, 6)]

    part, all_input, tables = call(
        attend_kernel,
        "attend",
        [((slots, width), BF16), ((requests, width), F32), ((requests, 128), F32)],
        pool_gather(packed, packed_near) + [own, key_cache, value_cache],
        [pltpu.VMEM((requests, packed_width), F32)],
    )
    (head_part,) = call(
        combine_kernel,
        "combine",
        [((requests, part_cols), BF16)],
        pool_gather(part, part) + [tables, out_weight],
        [
            pltpu.VMEM((pool * slots, width), F32),
            pltpu.VMEM((pool, slots, 128), F32),
            pltpu.VMEM((requests * width // HD, 128), F32),
        ],
    )
    (head_sum,) = call(
        sum_kernel,
        "head_sum",
        [((requests, part_cols), BF16)],
        [head_part] + [flip(head_part, "mlp", step) for step in (1, 2, 3)],
    )
    pieces = []
    for turn in range(2):
        route = []
        for m in range(mlp):
            by_distance = sorted(range(4), key=lambda z: (-abs(z - m), z))
            for z, step in zip(by_distance, (1, 0, 3, 2) if m % 2 == 0 else (0, 1, 2, 3)):
                for y in range(2):
                    source = (m * 2 + y) * mlp + (m ^ step)
                    route.append((source, (z * 2 + (y ^ turn)) * mlp + m))
        pieces.append(lax.ppermute(head_sum, ("pool", "mlp"), route))
    sums, own_residual = call(
        gate_up_kernel,
        "gate_up",
        [((requests, 2 * ff + 128), BF16), ((rows, width), F32)],
        pieces + [all_input, norm_gain.reshape(1, width), gate_weight, up_weight],
        [pltpu.VMEM((requests, width), F32)],
    )
    (core_sums,) = call(
        core_sum_kernel,
        "core_sum",
        [((requests, 2 * ff + 128), BF16)],
        [sums, flip(sums, "mlp", 1)],
    )
    (down,) = call(
        functools.partial(down_kernel, width * mlp),
        "down",
        [((pool, rows, width), BF16)],
        [core_sums, flip(core_sums, "mlp", 3), down_weight],
        [pltpu.VMEM((requests, width), F32)],
    )
    backwards = list(range(pool))[::-1]
    (out,) = call(
        final_kernel,
        "final",
        [((rows, width), BF16)],
        [own_residual, lax.all_to_all(down, "pool", 0, 0, axis_index_groups=[backwards])],
    )
    return out


def solution(mesh):
    in_specs = (
        P("pool", "mlp"),
        P("pool", "mlp"),
        P("pool", "mlp"),
        P("pool", "mlp"),
        P("pool", None, "mlp"),
        P("pool", None, "mlp"),
        P("pool", None),
        P("pool"),
        P("mlp", "pool"),
        P("mlp"),
        P("mlp", "pool"),
        P("mlp", "pool"),
        P("pool", "mlp"),
    )
    small = mesh.shape["pool"] == 8 and mesh.shape["mlp"] == 4
    per_device = per_device_small if small else per_device_wide
    return jax.shard_map(
        per_device, mesh=mesh, in_specs=in_specs, out_specs=P("pool", "mlp"), check_vma=False
    )
```

```python
import functools
import math

import jax
import jax.numpy as jnp
import numpy as np
from jax import lax
from jax.experimental import pallas as pl
from jax.experimental.pallas import tpu as pltpu
from jax.sharding import PartitionSpec as P

HD = 96
LOW = -1e30
CODE = 128


def rotate(values, positions):
    half_size = values.shape[-1] // 2
    inverse_freq = 10000.0 ** (-(2.0 * jnp.arange(half_size, dtype=jnp.float32)) / values.shape[-1])
    angles = positions.astype(jnp.float32)[:, None, None] * inverse_freq[None, None, :]
    cosine = jnp.cos(angles)
    sine_part = jnp.sin(angles)
    first = values[..., :half_size]
    second = values[..., half_size:]
    return jnp.concatenate(
        [first * cosine - second * sine_part, second * cosine + first * sine_part], -1
    )


def low(values):
    return lax.reduce_precision(values, 8, 7)


def split(values):
    high = low(values)
    return high.astype(jnp.bfloat16), (values - high).astype(jnp.bfloat16)


def encode(ints):
    return (ints // CODE).astype(jnp.bfloat16), (ints % CODE).astype(jnp.bfloat16)


def decode(high, rest):
    return high.astype(jnp.int32) * CODE + rest.astype(jnp.int32)


def gather(values, axis):
    copies = jnp.broadcast_to(values[None], (lax.axis_size(axis),) + values.shape)
    return lax.all_to_all(copies, axis, 0, 0)


def per_device_wide(
    residual_in,
    query_new,
    key_new,
    value_new,
    key_cache,
    value_cache,
    block_table,
    lengths,
    out_weight,
    norm_gain,
    gate_weight,
    up_weight,
    down_weight,
):
    rows, width = residual_in.shape
    heads = width // HD
    blocks, block_len = key_cache.shape[:2]
    most = block_table.shape[1]
    pool, mlp = lax.axis_size("pool"), lax.axis_size("mlp")
    pool_index = lax.axis_index("pool")
    requests = rows * pool
    score_scale = 1.0 / math.sqrt(HD)
    f32, bf16 = jnp.float32, jnp.bfloat16

    queries = rotate(query_new.astype(f32).reshape(rows, heads, HD), lengths).astype(bf16)
    new_keys = rotate(key_new.astype(f32).reshape(rows, heads, HD), lengths).astype(bf16)

    table_high, table_low = encode(block_table + 1)
    len_high, len_low = encode(lengths)
    packed = jnp.concatenate(
        [
            queries.reshape(rows, width),
            residual_in,
            table_high,
            table_low,
            len_high[:, None],
            len_low[:, None],
        ],
        1,
    )
    spare = -packed.shape[1] % 128
    packed = jnp.pad(packed, ((0, 0), (0, spare)))
    got = gather(packed, "pool").reshape(requests, packed.shape[1])
    all_queries = got[:, :width]
    all_input = got[:, width : 2 * width]
    tail = got[:, 2 * width :]
    tables = decode(tail[:, :most], tail[:, most : 2 * most]) - 1
    all_lengths = decode(tail[:, 2 * most], tail[:, 2 * most + 1])

    held_ids = pool_index * blocks + jnp.arange(blocks, dtype=jnp.int32)
    matches = tables[None, :, :] == held_ids[:, None, None]
    holder = jnp.any(matches, 2)
    block_index = jnp.sum(
        jnp.where(matches, jnp.arange(most, dtype=jnp.int32)[None, None, :], 0), (1, 2)
    )
    valid_len = jnp.sum(jnp.where(holder, all_lengths[None, :], 0), 1)
    block_query = jnp.dot(holder.astype(bf16), all_queries, preferred_element_type=f32)
    block_query = block_query.astype(bf16).reshape(blocks, heads, HD)
    key_rows = key_cache.reshape(blocks, block_len, heads, HD)
    value_rows = value_cache.reshape(blocks, block_len, heads, HD)
    scores = (
        jnp.einsum("bhd,bthd->bht", block_query, key_rows, preferred_element_type=f32)
        * score_scale
    )
    token_pos = block_index[:, None] * block_len + jnp.arange(block_len, dtype=jnp.int32)[None, :]
    valid = (token_pos < valid_len[:, None])[:, None, :]
    scores = jnp.where(valid, scores, LOW)
    shift = low(jnp.max(scores, 2))
    weights = jnp.where(valid, jnp.exp(scores - shift[:, :, None]), 0.0)
    totals = jnp.sum(weights, 2)
    numerator = jnp.einsum(
        "bht,bthd->bhd", weights.astype(bf16), value_rows, preferred_element_type=f32
    )
    self_score = jnp.sum(queries.astype(f32) * new_keys.astype(f32), -1) * score_scale
    self_shift = low(self_score)
    self_weight = jnp.exp(self_score - self_shift)
    self_numer = self_weight[:, :, None] * value_new.astype(f32).reshape(rows, heads, HD)

    own_total = jnp.concatenate([totals, self_weight], 0)
    total_high, total_low = split(own_total)
    part = jnp.concatenate(
        [
            jnp.concatenate([numerator, self_numer], 0)
            .astype(bf16)
            .reshape(blocks + rows, width),
            jnp.concatenate([shift, self_shift], 0).astype(bf16),
            total_high,
            total_low,
        ],
        1,
    )
    part = jnp.pad(part, ((0, 0), (0, -part.shape[1] % 128)))
    count = blocks + rows
    parts = gather(part, "pool").reshape(pool * count, part.shape[1])
    all_shift = parts[:, width : width + heads].astype(f32)
    all_total = parts[:, width + heads : width + 2 * heads].astype(f32) + parts[
        :, width + 2 * heads : width + 3 * heads
    ].astype(f32)
    place = jnp.arange(pool * count, dtype=jnp.int32)
    owner, slot = place // count, place % count
    is_block = slot < blocks
    block_id = jnp.where(is_block, owner * blocks + slot, -2)
    self_id = jnp.where(is_block, -2, owner * rows + slot - blocks)
    request_ids = jnp.arange(requests, dtype=jnp.int32)
    belongs = jnp.any(tables[:, None, :] == block_id[None, :, None], 2) | (
        request_ids[:, None] == self_id[None, :]
    )
    top = jnp.max(jnp.where(belongs[:, :, None], all_shift[None], LOW), 1)
    part_top = jnp.sum(jnp.where(belongs[:, :, None], top[:, None, :], 0.0), 0)
    scale = jnp.exp(all_shift - part_top)
    scaled = parts[:, :width].astype(f32).reshape(-1, heads, HD) * scale[:, :, None]
    mix = belongs.astype(f32)
    numer = jnp.dot(mix, scaled.reshape(-1, width), precision=lax.Precision.HIGHEST)
    denom = jnp.dot(mix, all_total * scale, precision=lax.Precision.HIGHEST)
    attended = (numer.reshape(requests, heads, HD) / denom[:, :, None]).astype(bf16)
    attended = attended.reshape(requests, width)

    head_part = jnp.dot(attended, out_weight, preferred_element_type=f32).astype(bf16)
    share = pool // mlp
    route = []
    for p in range(pool):
        for m in range(mlp):
            route.append((p * mlp + m, ((p % share) * mlp + m) * mlp + p // share))
    moved = lax.ppermute(head_part, ("pool", "mlp"), route)
    head_all = gather(moved, "pool").reshape(share, mlp, requests, -1)
    head_out = low(jnp.sum(head_all.astype(f32), 1))
    head_out = jnp.swapaxes(head_out, 0, 1).reshape(requests, width)
    residual = all_input.astype(f32) + head_out
    squares = jnp.sum(residual * residual, -1, keepdims=True)
    portion = (residual * norm_gain.astype(f32)).astype(bf16)

    ff = gate_weight.shape[1]
    square_high, square_low = split(squares)
    sums = jnp.concatenate(
        [
            jnp.dot(portion, gate_weight, preferred_element_type=f32).astype(bf16),
            jnp.dot(portion, up_weight, preferred_element_type=f32).astype(bf16),
            jnp.broadcast_to(square_high, (requests, 64)),
            jnp.broadcast_to(square_low, (requests, 64)),
        ],
        1,
    )
    summed = jnp.sum(gather(sums, "mlp").astype(f32), 0)
    mean_square = (summed[:, 2 * ff : 2 * ff + 1] + summed[:, 2 * ff + 64 : 2 * ff + 65]) / (
        width * mlp
    )
    factor = lax.rsqrt(mean_square + 1e-05)
    gate = summed[:, :ff] * factor
    up = summed[:, ff : 2 * ff] * factor
    hidden = (jax.nn.silu(gate) * up).astype(bf16)

    down = jnp.dot(hidden, down_weight, preferred_element_type=f32)
    down = lax.all_to_all(down.reshape(pool, rows, width), "pool", 0, 0)
    own = lax.dynamic_slice_in_dim(residual, pool_index * rows, rows, 0)
    return (own + jnp.sum(down, 0)).astype(bf16)


F32, BF16 = jnp.float32, jnp.bfloat16
VMEM = pl.BlockSpec(memory_space=pltpu.VMEM)
HBM = pl.BlockSpec(memory_space=pl.ANY)


def call(kernel, name, outs, args, scratch=(), hbm=(), limit=16 * 2**20):
    size = sum(math.prod(a.shape) * a.dtype.itemsize for a in args)
    return pl.pallas_call(
        kernel,
        out_shape=[jax.ShapeDtypeStruct(shape, dtype) for shape, dtype in outs],
        in_specs=[HBM if i in hbm else VMEM for i in range(len(args))],
        out_specs=[VMEM] * len(outs),
        scratch_shapes=list(scratch),
        compiler_params=pltpu.CompilerParams(vmem_limit_bytes=limit),
        cost_estimate=pl.CostEstimate(flops=0, bytes_accessed=size, transcendentals=0),
        name=name,
    )(*args)


def lanes(shape):
    return lax.broadcasted_iota(jnp.int32, shape, len(shape) - 1)


def in_order(pieces, index):
    for bit in (1, 2):
        odd = (index & bit) != 0
        pieces = [jnp.where(odd, pieces[s ^ bit], pieces[s]) for s in range(4)]
    return pieces


def rows_of(shape):
    return lax.broadcasted_iota(jnp.int32, shape, len(shape) - 2)


def round_low(values):
    return values.astype(BF16).astype(F32)


def head_start(shape):
    return rows_of(shape) * HD % 128


def flatten(tail, width):
    heads = tail.shape[0]
    spread = jnp.zeros((heads, width), F32)
    start = head_start((heads, width))
    for k in (0, 32, 64, 96):
        moved = pltpu.roll(tail, k, 1) if k else tail
        spread = jnp.where(start == k, jnp.concatenate([moved] * (width // 128), 1), spread)
    lane = lanes((heads, width))
    used = (lane // HD == rows_of((heads, width))) & (lane % HD < 24)
    return jnp.sum(jnp.where(used, spread, 0.0), 0, keepdims=True)


def unflatten(row, heads):
    width = row.shape[1]
    lane = lanes((heads, width))
    used = (lane // HD == rows_of((heads, width))) & (lane % HD < 24)
    spread = jnp.where(used, jnp.broadcast_to(row, (heads, width)), 0.0)
    folded = spread[:, :128]
    for at in range(128, width, 128):
        folded = folded + spread[:, at : at + 128]
    start = head_start((heads, 128))
    tail = jnp.where(start == 0, folded, 0.0)
    for k in (32, 64, 96):
        tail = jnp.where(start == k, pltpu.roll(folded, 128 - k, 1), tail)
    return tail


def prepare_kernel(*refs):
    sources, (packed, new), held = refs[:6], refs[8:10], refs[10:16]
    scr, sems = refs[16:]
    copies = [
        pltpu.make_async_copy(source, target, sems.at[i])
        for i, (source, target) in enumerate(zip(sources, held))
    ]
    for copy in copies:
        copy.start()
    table, length, query, key, value, residual = held
    rows, width = query.shape
    most = table.shape[1]
    period = 384
    turn = lanes((8, period)) % (HD // 2)
    freq = jnp.zeros((8, period), F32)
    for i in range(HD // 2):
        freq = jnp.where(turn == i, float(np.float32(10000.0 ** (-2.0 * i / HD))), freq)
    for copy in copies:
        copy.wait()
    scr[...] = jnp.zeros_like(scr)
    scr[0:rows, :] = query[...].astype(F32)
    scr[rows : 2 * rows, :] = key[...].astype(F32)
    values = scr[...]
    line = rows_of((8, period))
    where_at = jnp.zeros((8, period), F32)
    for r in range(rows):
        here = (line == r) | (line == rows + r)
        where_at = jnp.where(here, length[r].astype(F32), where_at)
    angles = where_at * freq
    cosine = jnp.concatenate([jnp.cos(angles)] * (width // period), 1)
    sine = jnp.concatenate([jnp.sin(angles)] * (width // period), 1)
    first = lanes((8, width)) % HD < HD // 2
    ahead = pltpu.roll(values, width - HD // 2, 1)
    behind = pltpu.roll(values, HD // 2, 1)
    scr[...] = values * cosine + jnp.where(first, -ahead, behind) * sine
    packed[:, :width] = scr[0:rows, :].astype(BF16)
    packed[:, width : 2 * width] = residual[...]
    tail = jnp.zeros((rows, 128), F32)
    at, row = lanes((rows, 128)), rows_of((rows, 128))
    for r in range(rows):
        codes = [table[r, k] + 1 for k in range(most)] + [length[r]]
        spots = [(k, most + k) for k in range(most)] + [(2 * most, 2 * most + 1)]
        for code, (high, rest) in zip(codes, spots):
            tail = jnp.where((row == r) & (at == high), (code >> 7).astype(F32), tail)
            tail = jnp.where((row == r) & (at == rest), (code & 127).astype(F32), tail)
    packed[:, 2 * width :] = tail.astype(BF16)
    new[:, :width] = scr[rows : 2 * rows, :].astype(BF16)
    new[:, width:] = value[...]


def carry_kernel(packed, new, packed_near, own):
    packed_near[...] = packed[...]
    rows, width = new.shape[0], new.shape[1] // 2
    blocks = own.shape[0] - rows - 1
    heads = width // HD
    head_mask = lanes((heads, width)) // HD == rows_of((heads, width))
    product = packed[:, :width].astype(F32) * new[:, :width].astype(F32)
    own[...] = jnp.zeros_like(own)
    spot = lanes((heads, 128))
    tail = jnp.zeros((heads, 128), F32)
    for r in range(rows):
        score = jnp.sum(
            jnp.where(head_mask, jnp.broadcast_to(product[r : r + 1], (heads, width)), 0.0),
            1,
            keepdims=True,
        ) * (1.0 / math.sqrt(HD))
        shift = round_low(score)
        weight = jnp.exp(score - shift)
        spread = jnp.sum(jnp.where(head_mask, round_low(weight), 0.0), 0, keepdims=True)
        own[blocks + r : blocks + r + 1, :width] = spread * new[r : r + 1, width:].astype(F32)
        high = round_low(weight)
        tail = jnp.where(spot == blocks + r, shift, tail)
        tail = jnp.where(spot == 8 + blocks + r, high, tail)
        tail = jnp.where(spot == 16 + blocks + r, weight - high, tail)
    own[:, width:] = tail


def merge_kernel(mine, theirs, both):
    y = lax.axis_index("pool") % 2
    both[y] = mine[...]
    both[1 - y] = theirs[...]


def attend_kernel(a0, a1, a2, a3, own, keys, values, part, residual, tables, scr):
    blocks, block_len, width = keys.shape
    rows = a0.shape[1]
    heads = width // HD
    most = 8
    me = lax.axis_index("pool")
    for y in range(2):
        pieces = [piece[y].astype(F32) for piece in (a0, a1, a2, a3)]
        for z, piece in enumerate(in_order(pieces, me // 2)):
            scr[(z * 2 + y) * rows : (z * 2 + y + 1) * rows, :] = piece
    queries = scr[:, :width]
    residual[...] = scr[:, width : 2 * width]
    tail = scr[:, 2 * width :]
    requests = tail.shape[0]
    table = tail * CODE + pltpu.roll(tail, 128 - most, 1) - 1.0
    length = tail[:, 2 * most : 2 * most + 1] * CODE + tail[:, 2 * most + 1 : 2 * most + 2]
    lane = lanes((requests, 128))
    table = jnp.where(lane < most, table, -2.0)
    tables[...] = table
    head_mask = lanes((heads, width)) // HD == rows_of((heads, width))
    spot = lanes((heads, 128))
    tail = own[:, width:]
    scores, limits = [], []
    for b in range(blocks):
        match = jnp.where(table == (me * blocks + b).astype(F32), 1.0, 0.0)
        holder = jnp.sum(match, 1, keepdims=True)
        place = jnp.sum(jnp.sum(match * lane.astype(F32), 1, keepdims=True), 0, keepdims=True)
        limit = jnp.sum(holder * length, 0, keepdims=True) - place * block_len
        limits.append(jnp.broadcast_to(limit, (heads, block_len)))
        query = jnp.sum(holder * queries, 0, keepdims=True)
        spread = jnp.where(head_mask, query, 0.0).astype(BF16)
        scores.append(
            lax.dot_general(
                spread, keys[b], (((1,), (1,)), ((), ())), preferred_element_type=F32
            )
        )
    scores = jnp.concatenate(scores, 0) * (1.0 / math.sqrt(HD))
    token = lanes((blocks * heads, block_len)).astype(F32)
    valid = token < jnp.concatenate(limits, 0)
    scores = jnp.where(valid, scores, LOW)
    shift = round_low(jnp.max(scores, 1, keepdims=True))
    weights = jnp.where(valid, jnp.exp(scores - shift), 0.0)
    total = jnp.sum(weights, 1, keepdims=True)
    high = round_low(total)
    rest = total - high
    numerators = []
    for b in range(blocks):
        mine = slice(b * heads, (b + 1) * heads)
        full = jnp.dot(weights[mine].astype(BF16), values[b], preferred_element_type=F32)
        numerators.append(jnp.sum(jnp.where(head_mask, full, 0.0), 0, keepdims=True))
        tail = jnp.where(spot == b, shift[mine], tail)
        tail = jnp.where(spot == 8 + b, high[mine], tail)
        tail = jnp.where(spot == 16 + b, rest[mine], tail)
    line = rows_of((8, width))
    numer = own[:, :width]
    for b in range(blocks):
        numer = jnp.where(line == b, numerators[b], numer)
    numer = jnp.where(line == 7, flatten(tail, width), numer)
    part[...] = numer.astype(BF16)


def combine_kernel(b0, b1, b2, b3, tables, weight, head_part, numer, tails, mix):
    requests = tables.shape[0]
    slots = b0.shape[1]
    width = weight.shape[0]
    heads = width // HD
    rows, blocks = 2, slots - 3
    me = lax.axis_index("pool")
    for step, piece in enumerate((b0, b1, b2, b3)):
        z = (me // 2) ^ step
        for y in range(2):
            owner = z * 2 + y
            values = piece[y].astype(F32)
            numer[pl.ds(pl.multiple_of(owner * slots, 8), slots), :] = values
            tails[owner] = unflatten(values[slots - 1 : slots], heads)
    lane8 = lanes((heads, 128))
    shifts = jnp.zeros((heads, 128), F32)
    totals = jnp.zeros((heads, 128), F32)
    for owner in range(8):
        tail = tails[owner]
        total = pltpu.roll(tail, 120, 1) + pltpu.roll(tail, 112, 1)
        tail, total = jnp.where(lane8 < 8, tail, 0.0), jnp.where(lane8 < 8, total, 0.0)
        if owner:
            tail, total = pltpu.roll(tail, 8 * owner, 1), pltpu.roll(total, 8 * owner, 1)
        shifts, totals = shifts + tail, totals + total
    lane = lanes((requests, 128))
    owner, slot = lane // slots, lane % slots
    block_id = jnp.where((slot < blocks) & (lane < 64), owner * blocks + slot, -5).astype(F32)
    self_id = jnp.where((slot >= blocks) & (slot < blocks + rows), owner * rows + slot - blocks, -5)
    table = tables[...]
    belongs = (self_id == rows_of((requests, 128))) & (lane < 64)
    for k in range(8):
        belongs = belongs | (table[:, k : k + 1] == block_id)
    for h in range(heads):
        shift = jnp.broadcast_to(shifts[h : h + 1], (requests, 128))
        top = jnp.max(jnp.where(belongs, shift, LOW), 1, keepdims=True)
        scale = jnp.where(belongs, jnp.exp(shift - top), 0.0)
        total = jnp.sum(scale * totals[h : h + 1], 1, keepdims=True)
        mix[h * requests : (h + 1) * requests, :] = scale / total
    full = jnp.dot(
        mix[:, : 8 * slots].astype(BF16), numer[...].astype(BF16), preferred_element_type=F32
    )
    head = lanes((requests, width)) // HD
    attended = jnp.zeros((requests, width), F32)
    for h in range(heads):
        attended = jnp.where(head == h, full[h * requests : (h + 1) * requests], attended)
    head_part[...] = jnp.dot(
        attended.astype(BF16), weight[...], preferred_element_type=F32
    ).astype(BF16)


def sum_kernel(p0, p1, p2, p3, total):
    total[...] = (
        (p0[...].astype(F32) + p1[...].astype(F32)) + (p2[...].astype(F32) + p3[...].astype(F32))
    ).astype(BF16)


def gate_up_kernel(same, flip, all_input, gain, gate, up, sums, own, scr):
    me = lax.axis_index("pool")
    odd = me % 2 == 1
    part = same.shape[1]
    ff = gate.shape[1]
    rows = own.shape[0]
    near, far = same[...].astype(F32), flip[...].astype(F32)
    scr[:, :part] = all_input[:, :part] + jnp.where(odd, far, near)
    scr[:, part:] = all_input[:, part:] + jnp.where(odd, near, far)
    residual = scr[...]
    mine = scr[0:rows, :]
    for p in range(1, residual.shape[0] // rows):
        mine = jnp.where(me == p, scr[p * rows : (p + 1) * rows, :], mine)
    own[...] = mine
    square = jnp.sum(residual * residual, 1, keepdims=True)
    portion = (residual * gain[...].astype(F32)).astype(BF16)
    sums[:, :ff] = jnp.dot(portion, gate[...], preferred_element_type=F32).astype(BF16)
    sums[:, ff : 2 * ff] = jnp.dot(portion, up[...], preferred_element_type=F32).astype(BF16)
    lane = lanes((residual.shape[0], 128))
    high = round_low(square)
    tail = jnp.where(lane == 0, high, jnp.where(lane == 1, square - high, 0.0))
    sums[:, 2 * ff :] = tail.astype(BF16)


def down_kernel(features, p0, p1, p2, p3, weight, parts, scr):
    ff = weight.shape[0]

    def total(columns):
        a, b, c, d = (p[:, columns].astype(F32) for p in (p0, p1, p2, p3))
        return (a + b) + (c + d)

    square = jnp.sum(total(slice(2 * ff, None)), 1, keepdims=True)
    factor = lax.rsqrt(square * (1.0 / features) + 1e-05)
    gate = total(slice(0, ff)) * factor
    up = total(slice(ff, 2 * ff)) * factor
    hidden = (gate / (1.0 + jnp.exp(-gate)) * up).astype(BF16)
    scr[...] = jnp.dot(hidden, weight[...], preferred_element_type=F32)
    rows = parts.shape[1]
    pool = parts.shape[0]
    for p in range(pool):
        parts[pool - 1 - p] = scr[p * rows : (p + 1) * rows, :].astype(BF16)


def final_kernel(own, parts, out):
    total = own[...]
    for p in range(parts.shape[0]):
        total = total + parts[p].astype(F32)
    out[...] = total.astype(BF16)


def flip(values, axis, step):
    size = lax.axis_size(axis)
    return lax.ppermute(values, axis, [(index, index ^ step) for index in range(size)])


def per_device_small(
    residual_in,
    query_new,
    key_new,
    value_new,
    key_cache,
    value_cache,
    block_table,
    lengths,
    out_weight,
    norm_gain,
    gate_weight,
    up_weight,
    down_weight,
):
    rows, width = residual_in.shape
    blocks = key_cache.shape[0]
    pool, mlp = 8, 4
    requests = rows * pool
    ff = gate_weight.shape[1]
    part_cols = out_weight.shape[1]
    packed_width = 2 * width + 128
    slots = blocks + rows + 1
    part_width = width + 128

    packed, new = call(
        prepare_kernel,
        "rotary",
        [((rows, packed_width), BF16), ((rows, 2 * width), BF16)],
        [block_table, lengths, query_new, key_new, value_new, residual_in, key_cache, value_cache],
        [pltpu.SMEM(block_table.shape, jnp.int32), pltpu.SMEM(lengths.shape, jnp.int32)]
        + [pltpu.VMEM((rows, width), BF16)] * 4
        + [pltpu.VMEM((8, width), F32), pltpu.SemaphoreType.DMA((6,))],
        hbm=range(8),
        limit=54 * 2**20,
    )

    packed_near, own = call(
        carry_kernel,
        "carry",
        [(packed.shape, BF16), ((slots, part_width), F32)],
        [packed, new],
    )

    def pool_gather(values, near):
        (both,) = call(
            merge_kernel,
            "merge",
            [((2,) + values.shape, values.dtype)],
            [near, flip(values, "pool", 1)],
        )
        return [both] + [flip(both, "pool", step) for step in (2, 4, 6)]

    part, all_input, tables = call(
        attend_kernel,
        "attend",
        [((slots, width), BF16), ((requests, width), F32), ((requests, 128), F32)],
        pool_gather(packed, packed_near) + [own, key_cache, value_cache],
        [pltpu.VMEM((requests, packed_width), F32)],
    )
    (head_part,) = call(
        combine_kernel,
        "combine",
        [((requests, part_cols), BF16)],
        pool_gather(part, part) + [tables, out_weight],
        [
            pltpu.VMEM((pool * slots, width), F32),
            pltpu.VMEM((pool, slots, 128), F32),
            pltpu.VMEM((requests * width // HD, 128), F32),
        ],
    )
    (head_sum,) = call(
        sum_kernel,
        "head_sum",
        [((requests, part_cols), BF16)],
        [head_part] + [flip(head_part, "mlp", step) for step in (1, 2, 3)],
    )
    pieces = []
    for turn in range(2):
        route = []
        for m in range(mlp):
            by_distance = sorted(range(4), key=lambda z: (-abs(z - m), z))
            for z, step in zip(by_distance, (1, 0, 3, 2) if m % 2 == 0 else (0, 1, 2, 3)):
                for y in range(2):
                    source = (m * 2 + y) * mlp + (m ^ step)
                    route.append((source, (z * 2 + (y ^ turn)) * mlp + m))
        pieces.append(lax.ppermute(head_sum, ("pool", "mlp"), route))
    sums, own_residual = call(
        gate_up_kernel,
        "gate_up",
        [((requests, 2 * ff + 128), BF16), ((rows, width), F32)],
        pieces + [all_input, norm_gain.reshape(1, width), gate_weight, up_weight],
        [pltpu.VMEM((requests, width), F32)],
    )
    (down,) = call(
        functools.partial(down_kernel, width * mlp),
        "down",
        [((pool, rows, width), BF16)],
        [sums] + [flip(sums, "mlp", step) for step in (1, 3, 2)] + [down_weight],
        [pltpu.VMEM((requests, width), F32)],
    )
    backwards = list(range(pool))[::-1]
    (out,) = call(
        final_kernel,
        "final",
        [((rows, width), BF16)],
        [own_residual, lax.all_to_all(down, "pool", 0, 0, axis_index_groups=[backwards])],
    )
    return out


def solution(mesh):
    in_specs = (
        P("pool", "mlp"),
        P("pool", "mlp"),
        P("pool", "mlp"),
        P("pool", "mlp"),
        P("pool", None, "mlp"),
        P("pool", None, "mlp"),
        P("pool", None),
        P("pool"),
        P("mlp", "pool"),
        P("mlp"),
        P("mlp", "pool"),
        P("mlp", "pool"),
        P("pool", "mlp"),
    )
    small = mesh.shape["pool"] == 8 and mesh.shape["mlp"] == 4
    per_device = per_device_small if small else per_device_wide
    return jax.shard_map(
        per_device, mesh=mesh, in_specs=in_specs, out_specs=P("pool", "mlp"), check_vma=False
    )
```

```python
import functools
import math

import jax
import jax.numpy as jnp
import numpy as np
from jax import lax
from jax.experimental import pallas as pl
from jax.experimental.pallas import tpu as pltpu
from jax.sharding import PartitionSpec as P

HD = 96
LOW = -1e30
CODE = 128


def rotate(values, positions):
    half_size = values.shape[-1] // 2
    inverse_freq = 10000.0 ** (-(2.0 * jnp.arange(half_size, dtype=jnp.float32)) / values.shape[-1])
    angles = positions.astype(jnp.float32)[:, None, None] * inverse_freq[None, None, :]
    cosine = jnp.cos(angles)
    sine_part = jnp.sin(angles)
    first = values[..., :half_size]
    second = values[..., half_size:]
    return jnp.concatenate(
        [first * cosine - second * sine_part, second * cosine + first * sine_part], -1
    )


def low(values):
    return lax.reduce_precision(values, 8, 7)


def split(values):
    high = low(values)
    return high.astype(jnp.bfloat16), (values - high).astype(jnp.bfloat16)


def encode(ints):
    return (ints // CODE).astype(jnp.bfloat16), (ints % CODE).astype(jnp.bfloat16)


def decode(high, rest):
    return high.astype(jnp.int32) * CODE + rest.astype(jnp.int32)


def gather(values, axis):
    copies = jnp.broadcast_to(values[None], (lax.axis_size(axis),) + values.shape)
    return lax.all_to_all(copies, axis, 0, 0)


def per_device_wide(
    residual_in,
    query_new,
    key_new,
    value_new,
    key_cache,
    value_cache,
    block_table,
    lengths,
    out_weight,
    norm_gain,
    gate_weight,
    up_weight,
    down_weight,
):
    rows, width = residual_in.shape
    heads = width // HD
    blocks, block_len = key_cache.shape[:2]
    most = block_table.shape[1]
    pool, mlp = lax.axis_size("pool"), lax.axis_size("mlp")
    pool_index = lax.axis_index("pool")
    requests = rows * pool
    score_scale = 1.0 / math.sqrt(HD)
    f32, bf16 = jnp.float32, jnp.bfloat16

    queries = rotate(query_new.astype(f32).reshape(rows, heads, HD), lengths).astype(bf16)
    new_keys = rotate(key_new.astype(f32).reshape(rows, heads, HD), lengths).astype(bf16)

    table_high, table_low = encode(block_table + 1)
    len_high, len_low = encode(lengths)
    packed = jnp.concatenate(
        [
            queries.reshape(rows, width),
            residual_in,
            table_high,
            table_low,
            len_high[:, None],
            len_low[:, None],
        ],
        1,
    )
    spare = -packed.shape[1] % 128
    packed = jnp.pad(packed, ((0, 0), (0, spare)))
    got = gather(packed, "pool").reshape(requests, packed.shape[1])
    all_queries = got[:, :width]
    all_input = got[:, width : 2 * width]
    tail = got[:, 2 * width :]
    tables = decode(tail[:, :most], tail[:, most : 2 * most]) - 1
    all_lengths = decode(tail[:, 2 * most], tail[:, 2 * most + 1])

    held_ids = pool_index * blocks + jnp.arange(blocks, dtype=jnp.int32)
    matches = tables[None, :, :] == held_ids[:, None, None]
    holder = jnp.any(matches, 2)
    block_index = jnp.sum(
        jnp.where(matches, jnp.arange(most, dtype=jnp.int32)[None, None, :], 0), (1, 2)
    )
    valid_len = jnp.sum(jnp.where(holder, all_lengths[None, :], 0), 1)
    block_query = jnp.dot(holder.astype(bf16), all_queries, preferred_element_type=f32)
    block_query = block_query.astype(bf16).reshape(blocks, heads, HD)
    key_rows = key_cache.reshape(blocks, block_len, heads, HD)
    value_rows = value_cache.reshape(blocks, block_len, heads, HD)
    scores = (
        jnp.einsum("bhd,bthd->bht", block_query, key_rows, preferred_element_type=f32)
        * score_scale
    )
    token_pos = block_index[:, None] * block_len + jnp.arange(block_len, dtype=jnp.int32)[None, :]
    valid = (token_pos < valid_len[:, None])[:, None, :]
    scores = jnp.where(valid, scores, LOW)
    shift = low(jnp.max(scores, 2))
    weights = jnp.where(valid, jnp.exp(scores - shift[:, :, None]), 0.0)
    totals = jnp.sum(weights, 2)
    numerator = jnp.einsum(
        "bht,bthd->bhd", weights.astype(bf16), value_rows, preferred_element_type=f32
    )
    self_score = jnp.sum(queries.astype(f32) * new_keys.astype(f32), -1) * score_scale
    self_shift = low(self_score)
    self_weight = jnp.exp(self_score - self_shift)
    self_numer = self_weight[:, :, None] * value_new.astype(f32).reshape(rows, heads, HD)

    own_total = jnp.concatenate([totals, self_weight], 0)
    total_high, total_low = split(own_total)
    part = jnp.concatenate(
        [
            jnp.concatenate([numerator, self_numer], 0)
            .astype(bf16)
            .reshape(blocks + rows, width),
            jnp.concatenate([shift, self_shift], 0).astype(bf16),
            total_high,
            total_low,
        ],
        1,
    )
    part = jnp.pad(part, ((0, 0), (0, -part.shape[1] % 128)))
    count = blocks + rows
    parts = gather(part, "pool").reshape(pool * count, part.shape[1])
    all_shift = parts[:, width : width + heads].astype(f32)
    all_total = parts[:, width + heads : width + 2 * heads].astype(f32) + parts[
        :, width + 2 * heads : width + 3 * heads
    ].astype(f32)
    place = jnp.arange(pool * count, dtype=jnp.int32)
    owner, slot = place // count, place % count
    is_block = slot < blocks
    block_id = jnp.where(is_block, owner * blocks + slot, -2)
    self_id = jnp.where(is_block, -2, owner * rows + slot - blocks)
    request_ids = jnp.arange(requests, dtype=jnp.int32)
    belongs = jnp.any(tables[:, None, :] == block_id[None, :, None], 2) | (
        request_ids[:, None] == self_id[None, :]
    )
    top = jnp.max(jnp.where(belongs[:, :, None], all_shift[None], LOW), 1)
    part_top = jnp.sum(jnp.where(belongs[:, :, None], top[:, None, :], 0.0), 0)
    scale = jnp.exp(all_shift - part_top)
    scaled = parts[:, :width].astype(f32).reshape(-1, heads, HD) * scale[:, :, None]
    mix = belongs.astype(f32)
    numer = jnp.dot(mix, scaled.reshape(-1, width), precision=lax.Precision.HIGHEST)
    denom = jnp.dot(mix, all_total * scale, precision=lax.Precision.HIGHEST)
    attended = (numer.reshape(requests, heads, HD) / denom[:, :, None]).astype(bf16)
    attended = attended.reshape(requests, width)

    head_part = jnp.dot(attended, out_weight, preferred_element_type=f32).astype(bf16)
    share = pool // mlp
    route = []
    for p in range(pool):
        for m in range(mlp):
            route.append((p * mlp + m, ((p % share) * mlp + m) * mlp + p // share))
    moved = lax.ppermute(head_part, ("pool", "mlp"), route)
    head_all = gather(moved, "pool").reshape(share, mlp, requests, -1)
    head_out = low(jnp.sum(head_all.astype(f32), 1))
    head_out = jnp.swapaxes(head_out, 0, 1).reshape(requests, width)
    residual = all_input.astype(f32) + head_out
    squares = jnp.sum(residual * residual, -1, keepdims=True)
    portion = (residual * norm_gain.astype(f32)).astype(bf16)

    ff = gate_weight.shape[1]
    square_high, square_low = split(squares)
    sums = jnp.concatenate(
        [
            jnp.dot(portion, gate_weight, preferred_element_type=f32).astype(bf16),
            jnp.dot(portion, up_weight, preferred_element_type=f32).astype(bf16),
            jnp.broadcast_to(square_high, (requests, 64)),
            jnp.broadcast_to(square_low, (requests, 64)),
        ],
        1,
    )
    summed = jnp.sum(gather(sums, "mlp").astype(f32), 0)
    mean_square = (summed[:, 2 * ff : 2 * ff + 1] + summed[:, 2 * ff + 64 : 2 * ff + 65]) / (
        width * mlp
    )
    factor = lax.rsqrt(mean_square + 1e-05)
    gate = summed[:, :ff] * factor
    up = summed[:, ff : 2 * ff] * factor
    hidden = (jax.nn.silu(gate) * up).astype(bf16)

    down = jnp.dot(hidden, down_weight, preferred_element_type=f32)
    down = lax.all_to_all(down.reshape(pool, rows, width), "pool", 0, 0)
    own = lax.dynamic_slice_in_dim(residual, pool_index * rows, rows, 0)
    return (own + jnp.sum(down, 0)).astype(bf16)


F32, BF16 = jnp.float32, jnp.bfloat16
VMEM = pl.BlockSpec(memory_space=pltpu.VMEM)
HBM = pl.BlockSpec(memory_space=pl.ANY)


def call(kernel, name, outs, args, scratch=(), hbm=(), limit=16 * 2**20):
    size = sum(math.prod(a.shape) * a.dtype.itemsize for a in args)
    return pl.pallas_call(
        kernel,
        out_shape=[jax.ShapeDtypeStruct(shape, dtype) for shape, dtype in outs],
        in_specs=[HBM if i in hbm else VMEM for i in range(len(args))],
        out_specs=[VMEM] * len(outs),
        scratch_shapes=list(scratch),
        compiler_params=pltpu.CompilerParams(vmem_limit_bytes=limit),
        cost_estimate=pl.CostEstimate(flops=0, bytes_accessed=size, transcendentals=0),
        name=name,
    )(*args)


def lanes(shape):
    return lax.broadcasted_iota(jnp.int32, shape, len(shape) - 1)


def in_order(pieces, index):
    for bit in (1, 2):
        odd = (index & bit) != 0
        pieces = [jnp.where(odd, pieces[s ^ bit], pieces[s]) for s in range(4)]
    return pieces


def rows_of(shape):
    return lax.broadcasted_iota(jnp.int32, shape, len(shape) - 2)


def round_low(values):
    return values.astype(BF16).astype(F32)


def head_start(shape):
    return rows_of(shape) * HD % 128


def flatten(tail, width):
    heads = tail.shape[0]
    spread = jnp.zeros((heads, width), F32)
    start = head_start((heads, width))
    for k in (0, 32, 64, 96):
        moved = pltpu.roll(tail, k, 1) if k else tail
        spread = jnp.where(start == k, jnp.concatenate([moved] * (width // 128), 1), spread)
    lane = lanes((heads, width))
    used = (lane // HD == rows_of((heads, width))) & (lane % HD < 24)
    return jnp.sum(jnp.where(used, spread, 0.0), 0, keepdims=True)


def unflatten(row, heads):
    width = row.shape[1]
    lane = lanes((heads, width))
    used = (lane // HD == rows_of((heads, width))) & (lane % HD < 24)
    spread = jnp.where(used, jnp.broadcast_to(row, (heads, width)), 0.0)
    folded = spread[:, :128]
    for at in range(128, width, 128):
        folded = folded + spread[:, at : at + 128]
    start = head_start((heads, 128))
    tail = jnp.where(start == 0, folded, 0.0)
    for k in (32, 64, 96):
        tail = jnp.where(start == k, pltpu.roll(folded, 128 - k, 1), tail)
    return tail


def prepare_kernel(*refs):
    sources, (packed, new), held = refs[:6], refs[8:10], refs[10:16]
    scr, sems = refs[16:]
    copies = [
        pltpu.make_async_copy(source, target, sems.at[i])
        for i, (source, target) in enumerate(zip(sources, held))
    ]
    for copy in copies:
        copy.start()
    table, length, query, key, value, residual = held
    rows, width = query.shape
    most = table.shape[1]
    period = 384
    turn = lanes((8, period)) % (HD // 2)
    freq = jnp.zeros((8, period), F32)
    for i in range(HD // 2):
        freq = jnp.where(turn == i, float(np.float32(10000.0 ** (-2.0 * i / HD))), freq)
    for copy in copies:
        copy.wait()
    scr[...] = jnp.zeros_like(scr)
    scr[0:rows, :] = query[...].astype(F32)
    scr[rows : 2 * rows, :] = key[...].astype(F32)
    values = scr[...]
    line = rows_of((8, period))
    where_at = jnp.zeros((8, period), F32)
    for r in range(rows):
        here = (line == r) | (line == rows + r)
        where_at = jnp.where(here, length[r].astype(F32), where_at)
    angles = where_at * freq
    cosine = jnp.concatenate([jnp.cos(angles)] * (width // period), 1)
    sine = jnp.concatenate([jnp.sin(angles)] * (width // period), 1)
    first = lanes((8, width)) % HD < HD // 2
    ahead = pltpu.roll(values, width - HD // 2, 1)
    behind = pltpu.roll(values, HD // 2, 1)
    scr[...] = values * cosine + jnp.where(first, -ahead, behind) * sine
    packed[:, :width] = scr[0:rows, :].astype(BF16)
    packed[:, width : 2 * width] = residual[...]
    tail = jnp.zeros((rows, 128), F32)
    at, row = lanes((rows, 128)), rows_of((rows, 128))
    for r in range(rows):
        codes = [table[r, k] + 1 for k in range(most)] + [length[r]]
        spots = [(k, most + k) for k in range(most)] + [(2 * most, 2 * most + 1)]
        for code, (high, rest) in zip(codes, spots):
            tail = jnp.where((row == r) & (at == high), (code >> 7).astype(F32), tail)
            tail = jnp.where((row == r) & (at == rest), (code & 127).astype(F32), tail)
    packed[:, 2 * width :] = tail.astype(BF16)
    new[:, :width] = scr[rows : 2 * rows, :].astype(BF16)
    new[:, width:] = value[...]


def carry_kernel(packed, new, packed_near, own):
    packed_near[...] = packed[...]
    rows, width = new.shape[0], new.shape[1] // 2
    blocks = own.shape[0] - rows - 1
    heads = width // HD
    head_mask = lanes((heads, width)) // HD == rows_of((heads, width))
    product = packed[:, :width].astype(F32) * new[:, :width].astype(F32)
    own[...] = jnp.zeros_like(own)
    spot = lanes((heads, 128))
    tail = jnp.zeros((heads, 128), F32)
    for r in range(rows):
        score = jnp.sum(
            jnp.where(head_mask, jnp.broadcast_to(product[r : r + 1], (heads, width)), 0.0),
            1,
            keepdims=True,
        ) * (1.0 / math.sqrt(HD))
        shift = round_low(score)
        weight = jnp.exp(score - shift)
        spread = jnp.sum(jnp.where(head_mask, round_low(weight), 0.0), 0, keepdims=True)
        own[blocks + r : blocks + r + 1, :width] = spread * new[r : r + 1, width:].astype(F32)
        high = round_low(weight)
        tail = jnp.where(spot == blocks + r, shift, tail)
        tail = jnp.where(spot == 8 + blocks + r, high, tail)
        tail = jnp.where(spot == 16 + blocks + r, weight - high, tail)
    own[:, width:] = tail


def merge_kernel(mine, theirs, both):
    y = lax.axis_index("pool") % 2
    both[y] = mine[...]
    both[1 - y] = theirs[...]


def attend_kernel(a0, a1, a2, a3, own, keys, values, part, residual, tables, scr):
    blocks, block_len, width = keys.shape
    rows = a0.shape[1]
    heads = width // HD
    most = 8
    me = lax.axis_index("pool")
    for y in range(2):
        pieces = [piece[y].astype(F32) for piece in (a0, a1, a2, a3)]
        for z, piece in enumerate(in_order(pieces, me // 2)):
            scr[(z * 2 + y) * rows : (z * 2 + y + 1) * rows, :] = piece
    queries = scr[:, :width]
    residual[...] = scr[:, width : 2 * width]
    tail = scr[:, 2 * width :]
    requests = tail.shape[0]
    table = tail * CODE + pltpu.roll(tail, 128 - most, 1) - 1.0
    length = tail[:, 2 * most : 2 * most + 1] * CODE + tail[:, 2 * most + 1 : 2 * most + 2]
    lane = lanes((requests, 128))
    table = jnp.where(lane < most, table, -2.0)
    tables[...] = table
    head_mask = lanes((heads, width)) // HD == rows_of((heads, width))
    spot = lanes((heads, 128))
    tail = own[:, width:]
    scores, limits = [], []
    for b in range(blocks):
        match = jnp.where(table == (me * blocks + b).astype(F32), 1.0, 0.0)
        holder = jnp.sum(match, 1, keepdims=True)
        place = jnp.sum(jnp.sum(match * lane.astype(F32), 1, keepdims=True), 0, keepdims=True)
        limit = jnp.sum(holder * length, 0, keepdims=True) - place * block_len
        limits.append(jnp.broadcast_to(limit, (heads, block_len)))
        query = jnp.sum(holder * queries, 0, keepdims=True)
        spread = jnp.where(head_mask, query, 0.0).astype(BF16)
        scores.append(
            lax.dot_general(
                spread, keys[b], (((1,), (1,)), ((), ())), preferred_element_type=F32
            )
        )
    scores = jnp.concatenate(scores, 0) * (1.0 / math.sqrt(HD))
    token = lanes((blocks * heads, block_len)).astype(F32)
    valid = token < jnp.concatenate(limits, 0)
    scores = jnp.where(valid, scores, LOW)
    shift = round_low(jnp.max(scores, 1, keepdims=True))
    weights = jnp.where(valid, jnp.exp(scores - shift), 0.0)
    total = jnp.sum(weights, 1, keepdims=True)
    high = round_low(total)
    rest = total - high
    numerators = []
    for b in range(blocks):
        mine = slice(b * heads, (b + 1) * heads)
        full = jnp.dot(weights[mine].astype(BF16), values[b], preferred_element_type=F32)
        numerators.append(jnp.sum(jnp.where(head_mask, full, 0.0), 0, keepdims=True))
        tail = jnp.where(spot == b, shift[mine], tail)
        tail = jnp.where(spot == 8 + b, high[mine], tail)
        tail = jnp.where(spot == 16 + b, rest[mine], tail)
    line = rows_of((8, width))
    numer = own[:, :width]
    for b in range(blocks):
        numer = jnp.where(line == b, numerators[b], numer)
    numer = jnp.where(line == 7, flatten(tail, width), numer)
    part[...] = numer.astype(BF16)


def combine_kernel(b0, b1, b2, b3, tables, weight, head_part, numer, tails, mix):
    requests = tables.shape[0]
    slots = b0.shape[1]
    width = weight.shape[0]
    heads = width // HD
    rows, blocks = 2, slots - 3
    me = lax.axis_index("pool")
    for step, piece in enumerate((b0, b1, b2, b3)):
        z = (me // 2) ^ step
        for y in range(2):
            owner = z * 2 + y
            values = piece[y].astype(F32)
            numer[pl.ds(pl.multiple_of(owner * slots, 8), slots), :] = values
            tails[owner] = unflatten(values[slots - 1 : slots], heads)
    lane8 = lanes((heads, 128))
    shifts = jnp.zeros((heads, 128), F32)
    totals = jnp.zeros((heads, 128), F32)
    for owner in range(8):
        tail = tails[owner]
        total = pltpu.roll(tail, 120, 1) + pltpu.roll(tail, 112, 1)
        tail, total = jnp.where(lane8 < 8, tail, 0.0), jnp.where(lane8 < 8, total, 0.0)
        if owner:
            tail, total = pltpu.roll(tail, 8 * owner, 1), pltpu.roll(total, 8 * owner, 1)
        shifts, totals = shifts + tail, totals + total
    lane = lanes((requests, 128))
    owner, slot = lane // slots, lane % slots
    block_id = jnp.where((slot < blocks) & (lane < 64), owner * blocks + slot, -5).astype(F32)
    self_id = jnp.where((slot >= blocks) & (slot < blocks + rows), owner * rows + slot - blocks, -5)
    table = tables[...]
    belongs = (self_id == rows_of((requests, 128))) & (lane < 64)
    for k in range(8):
        belongs = belongs | (table[:, k : k + 1] == block_id)
    for h in range(heads):
        shift = jnp.broadcast_to(shifts[h : h + 1], (requests, 128))
        top = jnp.max(jnp.where(belongs, shift, LOW), 1, keepdims=True)
        scale = jnp.where(belongs, jnp.exp(shift - top), 0.0)
        total = jnp.sum(scale * totals[h : h + 1], 1, keepdims=True)
        mix[h * requests : (h + 1) * requests, :] = scale / total
    full = jnp.dot(
        mix[:, : 8 * slots].astype(BF16), numer[...].astype(BF16), preferred_element_type=F32
    )
    head = lanes((requests, width)) // HD
    attended = jnp.zeros((requests, width), F32)
    for h in range(heads):
        attended = jnp.where(head == h, full[h * requests : (h + 1) * requests], attended)
    head_part[...] = jnp.dot(
        attended.astype(BF16), weight[...], preferred_element_type=F32
    ).astype(BF16)


def sum_kernel(p0, p1, p2, p3, total):
    total[...] = (
        (p0[...].astype(F32) + p1[...].astype(F32)) + (p2[...].astype(F32) + p3[...].astype(F32))
    ).astype(BF16)


def gate_up_kernel(same, flip, all_input, gain, gate, up, sums, own, scr):
    me = lax.axis_index("pool")
    odd = me % 2 == 1
    part = same.shape[1]
    ff = gate.shape[1]
    rows = own.shape[0]
    near, far = same[...].astype(F32), flip[...].astype(F32)
    scr[:, :part] = all_input[:, :part] + jnp.where(odd, far, near)
    scr[:, part:] = all_input[:, part:] + jnp.where(odd, near, far)
    residual = scr[...]
    mine = scr[0:rows, :]
    for p in range(1, residual.shape[0] // rows):
        mine = jnp.where(me == p, scr[p * rows : (p + 1) * rows, :], mine)
    own[...] = mine
    square = jnp.sum(residual * residual, 1, keepdims=True)
    portion = (residual * gain[...].astype(F32)).astype(BF16)
    sums[:, :ff] = jnp.dot(portion, gate[...], preferred_element_type=F32).astype(BF16)
    sums[:, ff : 2 * ff] = jnp.dot(portion, up[...], preferred_element_type=F32).astype(BF16)
    lane = lanes((residual.shape[0], 128))
    high = round_low(square)
    tail = jnp.where(lane == 0, high, jnp.where(lane == 1, square - high, 0.0))
    sums[:, 2 * ff :] = tail.astype(BF16)


def down_kernel(features, p0, p1, p2, p3, weight, parts, scr):
    ff = weight.shape[0]

    def total(columns):
        a, b, c, d = (p[:, columns].astype(F32) for p in (p0, p1, p2, p3))
        return (a + b) + (c + d)

    square = jnp.sum(total(slice(2 * ff, None)), 1, keepdims=True)
    factor = lax.rsqrt(square * (1.0 / features) + 1e-05)
    gate = total(slice(0, ff)) * factor
    up = total(slice(ff, 2 * ff)) * factor
    hidden = (gate / (1.0 + jnp.exp(-gate)) * up).astype(BF16)
    scr[...] = jnp.dot(hidden, weight[...], preferred_element_type=F32)
    rows = parts.shape[1]
    pool = parts.shape[0]
    for p in range(pool):
        parts[pool - 1 - p] = scr[p * rows : (p + 1) * rows, :].astype(BF16)


def final_kernel(own, parts, out):
    total = own[...]
    for p in range(parts.shape[0]):
        total = total + parts[p].astype(F32)
    out[...] = total.astype(BF16)


def flip(values, axis, step):
    size = lax.axis_size(axis)
    return lax.ppermute(values, axis, [(index, index ^ step) for index in range(size)])


def per_device_small(
    residual_in,
    query_new,
    key_new,
    value_new,
    key_cache,
    value_cache,
    block_table,
    lengths,
    out_weight,
    norm_gain,
    gate_weight,
    up_weight,
    down_weight,
):
    rows, width = residual_in.shape
    blocks = key_cache.shape[0]
    pool, mlp = 8, 4
    requests = rows * pool
    ff = gate_weight.shape[1]
    part_cols = out_weight.shape[1]
    packed_width = 2 * width + 128
    slots = blocks + rows + 1
    part_width = width + 128

    packed, new = call(
        prepare_kernel,
        "rotary",
        [((rows, packed_width), BF16), ((rows, 2 * width), BF16)],
        [block_table, lengths, query_new, key_new, value_new, residual_in, key_cache, value_cache],
        [pltpu.SMEM(block_table.shape, jnp.int32), pltpu.SMEM(lengths.shape, jnp.int32)]
        + [pltpu.VMEM((rows, width), BF16)] * 4
        + [pltpu.VMEM((8, width), F32), pltpu.SemaphoreType.DMA((6,))],
        hbm=range(8),
        limit=54 * 2**20,
    )

    packed_near, own = call(
        carry_kernel,
        "carry",
        [(packed.shape, BF16), ((slots, part_width), F32)],
        [packed, new],
    )

    def pool_gather(values, near):
        (both,) = call(
            merge_kernel,
            "merge",
            [((2,) + values.shape, values.dtype)],
            [near, flip(values, "pool", 1)],
        )
        return [both] + [flip(both, "pool", step) for step in (2, 4, 6)]

    part, all_input, tables = call(
        attend_kernel,
        "attend",
        [((slots, width), BF16), ((requests, width), F32), ((requests, 128), F32)],
        pool_gather(packed, packed_near) + [own, key_cache, value_cache],
        [pltpu.VMEM((requests, packed_width), F32)],
    )
    (head_part,) = call(
        combine_kernel,
        "combine",
        [((requests, part_cols), BF16)],
        pool_gather(part, part) + [tables, out_weight],
        [
            pltpu.VMEM((pool * slots, width), F32),
            pltpu.VMEM((pool, slots, 128), F32),
            pltpu.VMEM((requests * width // HD, 128), F32),
        ],
    )
    (head_sum,) = call(
        sum_kernel,
        "head_sum",
        [((requests, part_cols), BF16)],
        [head_part] + [flip(head_part, "mlp", step) for step in (1, 2, 3)],
    )
    pieces = []
    for turn in range(2):
        route = []
        for m in range(mlp):
            by_distance = sorted(range(4), key=lambda z: (-abs(z - m), z))
            for z, step in zip(by_distance, (1, 0, 3, 2) if m % 2 == 0 else (0, 1, 2, 3)):
                for y in range(2):
                    source = (m * 2 + y) * mlp + (m ^ step)
                    route.append((source, (z * 2 + (y ^ turn)) * mlp + m))
        pieces.append(lax.ppermute(head_sum, ("pool", "mlp"), route))
    sums, own_residual = call(
        gate_up_kernel,
        "gate_up",
        [((requests, 2 * ff + 128), BF16), ((rows, width), F32)],
        pieces + [all_input, norm_gain.reshape(1, width), gate_weight, up_weight],
        [pltpu.VMEM((requests, width), F32)],
    )
    (down,) = call(
        functools.partial(down_kernel, width * mlp),
        "down",
        [((pool, rows, width), BF16)],
        [sums] + [flip(sums, "mlp", step) for step in (3, 1, 2)] + [down_weight],
        [pltpu.VMEM((requests, width), F32)],
    )
    backwards = list(range(pool))[::-1]
    (out,) = call(
        final_kernel,
        "final",
        [((rows, width), BF16)],
        [own_residual, lax.all_to_all(down, "pool", 0, 0, axis_index_groups=[backwards])],
    )
    return out


def solution(mesh):
    in_specs = (
        P("pool", "mlp"),
        P("pool", "mlp"),
        P("pool", "mlp"),
        P("pool", "mlp"),
        P("pool", None, "mlp"),
        P("pool", None, "mlp"),
        P("pool", None),
        P("pool"),
        P("mlp", "pool"),
        P("mlp"),
        P("mlp", "pool"),
        P("mlp", "pool"),
        P("pool", "mlp"),
    )
    small = mesh.shape["pool"] == 8 and mesh.shape["mlp"] == 4
    per_device = per_device_small if small else per_device_wide
    return jax.shard_map(
        per_device, mesh=mesh, in_specs=in_specs, out_specs=P("pool", "mlp"), check_vma=False
    )
```
